32 devices in a mesh: tok: 32 (over z, y, x, core).
Axes of the slice: x: 2, y: 2, z: 4, core: 2. Of those that a mesh axis runs over, the one named last changes fastest.
Arguments:
- layer_in: bfloat16 [4096, 2048], P('tok'), may hold values from -6 to 6
- cotangent: bfloat16 [4096, 2048], P('tok'), may hold values from -6 to 6
- doc_lengths: int32 [2, 4], replicated, may hold values from 1 to 1024, 2048 in all within a row
- tile_slot: int32 [1536], replicated, may hold values from 0 to 1535, as said below
- pool_weight: float32 [1536, 128, 128], P('tok')
- pool_first: float32 [1536, 128, 128], P('tok'), may hold values from -112 to 112
- pool_second: float32 [1536, 128, 128], P('tok'), may hold values from 204.8 to 2867.2
- pool_left: float32 [1536, 128, 128], P('tok'), may hold values from -1 to 1
- pool_right: float32 [1536, 128, 128], P('tok'), may hold values from -1 to 1
- pool_left_stat: float32 [1536, 128, 128], P('tok'), may hold values from 0 to 209715.2
- pool_right_stat: float32 [1536, 128, 128], P('tok'), may hold values from 0 to 209715.2
- channel_weight: float32 [4096, 288], P('tok')
- channel_first: float32 [4096, 288], P('tok'), may hold values from -40 to 40
- channel_second: float32 [4096, 288], P('tok'), may hold values from 20.48 to 327.68
- channel_left: float32 [4096, 128], P('tok'), may hold values from -1 to 1
- channel_right: float32 [9216, 288], P('tok'), may hold values from -1 to 1
- channel_left_stat: float32 [4096, 128], P('tok'), may hold values from 0 to 1415577.6
- channel_right_stat: float32 [9216, 288], P('tok'), may hold values from 0 to 629145.6
- norm_gain: float32 [2048], P('tok'), may hold values from 0.5 to 1.5
- gain_first: float32 [2048], P('tok'), may hold values from -112 to 112
- gain_second: float32 [2048], P('tok'), may hold values from 204.8 to 2867.2
- channel_vectors: float32 [23, 4096], P(None, 'tok'), may hold values from -5 to 5
- vector_first: float32 [23, 4096], P(None, 'tok'), may hold values from -40 to 40
- vector_second: float32 [23, 4096], P(None, 'tok'), may hold values from 20.48 to 327.68
Outputs:
- layer_out: bfloat16 [4096, 2048], P('tok')
- input_grad: float32 [4096, 2048], P('tok')
- pool_first_next: float32 [1536, 128, 128], P('tok')
- pool_second_next: float32 [1536, 128, 128], P('tok')
- pool_weight_next: float32 [1536, 128, 128], P('tok')
- pool_left_next: float32 [1536, 128, 128], P('tok')
- pool_right_next: float32 [1536, 128, 128], P('tok')
- pool_lstat_next: float32 [1536, 128, 128], P('tok')
- pool_rstat_next: float32 [1536, 128, 128], P('tok')
- channel_first_next: float32 [4096, 288], P('tok')
- channel_second_next: float32 [4096, 288], P('tok')
- channel_weight_next: float32 [4096, 288], P('tok')
- channel_left_next: float32 [4096, 128], P('tok')
- channel_right_next: float32 [9216, 288], P('tok')
- channel_lstat_next: float32 [4096, 128], P('tok')
- channel_rstat_next: float32 [9216, 288], P('tok')
- gain_first_next: float32 [2048], P('tok')
- gain_second_next: float32 [2048], P('tok')
- gain_next: float32 [2048], P('tok')
- vector_first_next: float32 [23, 4096], P(None, 'tok')
- vector_second_next: float32 [23, 4096], P(None, 'tok')
- vector_next: float32 [23, 4096], P(None, 'tok')
The draws below stay inside these ranges and needn't reach their ends.
Inputs may be any that keep to these rules, and one draw needn't show every extreme that they name: `tile_slot`: a permutation; the device at index k of tok holds slots k * 48 to (k + 1) * 48 - 1. `doc_lengths`: each row's lengths sum to 2048, and the longest of each row is 1024.
All inputs are finite; a program needn't handle non-finite values.
Results may differ from the reference program's by a relative error of at most 0.0055.
The reference program's roundings to bfloat16 on the way count: a program that leaves them out, or rounds other values in their place, can miss the bound.
Values may be sent and summed in bfloat16 or wider, within the bound.
A program may use at most 576 MiB of HBM per device.

```python
import math
from functools import partial
import jax
import jax.numpy as jnp
import numpy as np
from jax import lax

D = 2048
E = 4096
N = 16
R = 128
K = 4
L = 2048
DOCS = 4
BLOCK = 16
P_SIZE = 128
STEP = 5
TOKENS = 4096
ROWS = 2
CH = 128
XW = 160
XR = 288
CP = 23
NT = 1536
NI = 1024


def tile_order(key):
    return jax.random.permutation(key, NT).astype(jnp.int32)


def orthogonal(key, batch, order):
    keys = jax.random.split(key, 4)
    row_keys = jax.random.split(keys[0], batch)
    column_keys = jax.random.split(keys[1], batch)
    row_order = jax.vmap(lambda one: jax.random.permutation(one, order))(row_keys).astype(jnp.float32)
    column_order = jax.vmap(lambda one: jax.random.permutation(one, order))(column_keys).astype(jnp.float32)
    row_signs = (2 * jax.random.randint(keys[2], (batch, order), 0, 2) - 1).astype(jnp.float32)
    column_signs = (2 * jax.random.randint(keys[3], (batch, order), 0, 2) - 1).astype(jnp.float32)
    angles = jnp.pi * (row_order[:, :, None] + 0.5) * (column_order[:, None, :] + 0.5) / order
    cosines = jnp.cos(angles) * (2.0 / order) ** 0.5
    return (cosines * row_signs[:, :, None] * column_signs[:, None, :]).astype(jnp.float32)


def diagonal_stats(key, batch, order, level):
    values = jax.random.uniform(key, (batch, order), jnp.float32, 1.0, 4.0) * level
    return values[:, :, None] * jnp.eye(order, dtype=jnp.float32)[None]


def draw_tile_slot(key, part):
    return tile_order(key)


def draw_pool_weight(key, part):
    order = tile_order(key)
    key = jax.random.fold_in(key, 11)
    holder = jnp.zeros((NT,), jnp.int32).at[order].set(jnp.arange(NT, dtype=jnp.int32))
    scales = jnp.where(holder < NI, D ** (-0.5), (E // 8) ** (-0.5)).astype(jnp.float32)
    return jax.random.normal(key, (NT, P_SIZE, P_SIZE), jnp.float32) * scales[:, None, None]


def draw_pool_left(key, part):
    key = jax.random.fold_in(key, 12)
    return orthogonal(key, NT, P_SIZE)


def draw_pool_right(key, part):
    key = jax.random.fold_in(key, 13)
    return orthogonal(key, NT, P_SIZE)


def draw_pool_left_stat(key, part):
    key = jax.random.fold_in(key, 14)
    return diagonal_stats(key, NT, P_SIZE, 0.1 * TOKENS * P_SIZE)


def draw_pool_right_stat(key, part):
    key = jax.random.fold_in(key, 15)
    return diagonal_stats(key, NT, P_SIZE, 0.1 * TOKENS * P_SIZE)


def draw_channel_weight(key, part):
    key = jax.random.fold_in(key, 21)
    columns = jnp.arange(XR)
    scales = jnp.where(columns < XW, E ** (-0.5), R ** (-0.5)).astype(jnp.float32)
    return jax.random.normal(key, (E, XR), jnp.float32) * scales[None, :]


def draw_channel_left(key, part):
    key = jax.random.fold_in(key, 22)
    return orthogonal(key, E // CH, CH).reshape(E, CH)


def draw_channel_right(key, part):
    key = jax.random.fold_in(key, 23)
    return orthogonal(key, E // CH, XR).reshape(E // CH * XR, XR)


def draw_channel_left_stat(key, part):
    key = jax.random.fold_in(key, 24)
    return diagonal_stats(key, E // CH, CH, 0.3 * TOKENS * XR).reshape(E, CH)


def draw_channel_right_stat(key, part):
    key = jax.random.fold_in(key, 25)
    return diagonal_stats(key, E // CH, XR, 0.3 * TOKENS * CH).reshape(E // CH * XR, XR)


def draw_channel_vectors(key, part):
    key = jax.random.fold_in(key, 31)
    subkeys = jax.random.split(key, 5)
    kernel_taps = jax.random.normal(subkeys[0], (K, E), jnp.float32) * 0.5
    conv_offset = jax.random.normal(subkeys[1], (1, E), jnp.float32) * 0.3
    step_bias = jax.random.uniform(subkeys[2], (1, E), jnp.float32, -5.0, -1.5)
    log_rates = jax.random.uniform(subkeys[3], (N, E), jnp.float32, -1.4, 2.0)
    skip_gain = jax.random.uniform(subkeys[4], (1, E), jnp.float32, 0.5, 1.5)
    return jnp.concatenate([kernel_taps, conv_offset, step_bias, log_rates, skip_gain], axis=0).astype(jnp.float32)


def levels(key, dims, cuts, least, largest):
    def one(dim, parts):
        steps = jax.random.uniform(jax.random.fold_in(jax.random.fold_in(key, 6), dim), (parts,), jnp.float32, least / len(cuts), largest / len(cuts))
        return jnp.repeat(jnp.exp(steps), dims[dim] // parts).reshape((-1,) + (1,) * (len(dims) - dim - 1))

    loudness = one(*cuts[0])
    for cut in cuts[1:]:
        loudness = loudness * one(*cut)
    return loudness


def profile(count, total, most, slope):
    weights = [(1 << 20) // math.isqrt(rank ** slope) + 1 for rank in range(2, count + 1)]
    spare, holding = total - most - (count - 1), [1] * (count - 1)
    while spare > 0:
        free = [i for i in range(count - 1) if holding[i] < most]
        whole, remaining = sum([weights[i] for i in free]), spare
        for i in free:
            extra = min(most - holding[i], max(1, remaining * weights[i] // whole), spare)
            holding[i] = holding[i] + extra
            spare = spare - extra
    return np.array([most] + holding)


def ragged(own_key, number_of, total, limit, lean):
    if number_of == 2:
        one = jax.random.randint(own_key, (), max(1, total - limit), min(limit, total - 1) + 1)
        return jnp.stack([one, total - one])
    sizes = jnp.asarray(profile(number_of, total, limit, lean), jnp.int32)
    twos = (number_of - 1) // 2
    source_of, receiver = sizes[1:1 + 2 * twos:2], sizes[2:2 + 2 * twos:2]
    margin = jnp.minimum(source_of - 1, limit - receiver)
    shifted = jax.random.randint(jax.random.fold_in(own_key, 1), (twos,), 0, 1 << 20) % (margin + 1)
    sizes = sizes.at[1:1 + 2 * twos:2].set(source_of - shifted).at[2:2 + 2 * twos:2].set(receiver + shifted)
    return sizes[jax.random.permutation(jax.random.fold_in(own_key, 2), number_of)]


def bell_draw(stream_key, dims, spread, limit, shards=(), kind=jnp.bfloat16):
    level = levels(stream_key, dims, shards, -0.22, 0.18) if shards else 1.0
    entries = jax.random.normal(stream_key, dims, jnp.float32) * spread * level
    return jnp.minimum(jnp.maximum(entries, -limit), limit).astype(kind)


def setup_inputs(seed: int = 0) -> dict:
    streams_of = jax.random.split(jax.random.key(seed), 25)
    layer_in = bell_draw(streams_of[0], (TOKENS, D), 1.0, 6.0, ((0, 32),))
    cotangent = bell_draw(streams_of[1], (TOKENS, D), 1.0, 6.0, ((0, 32),))
    doc_lengths = jax.vmap(lambda own: ragged(own, DOCS, L, L // 2, 2))(jax.random.split(streams_of[2], ROWS)).reshape((ROWS, DOCS)).astype(jnp.int32)
    tile_slot = draw_tile_slot(jax.random.fold_in(streams_of[24], 71), 0)
    pool_weight = draw_pool_weight(jax.random.fold_in(streams_of[24], 71), 0)
    pool_first = bell_draw(streams_of[5], (NT, P_SIZE, P_SIZE), (0.3 * TOKENS ** 0.5), 112.0, ((0, 32),), jnp.float32)
    pool_second = jnp.clip(jnp.exp(math.log(2867.2) - 2.6390573 * jax.random.uniform(streams_of[6], (NT, P_SIZE, P_SIZE), jnp.float32) ** levels(streams_of[6], (NT, P_SIZE, P_SIZE), ((0, 32),), -0.2, 0.2)), 204.8, 2867.2)
    pool_left = draw_pool_left(jax.random.fold_in(streams_of[24], 71), 0)
    pool_right = draw_pool_right(jax.random.fold_in(streams_of[24], 71), 0)
    pool_left_stat = draw_pool_left_stat(jax.random.fold_in(streams_of[24], 71), 0)
    pool_right_stat = draw_pool_right_stat(jax.random.fold_in(streams_of[24], 71), 0)
    channel_weight = draw_channel_weight(jax.random.fold_in(streams_of[24], 71), 0)
    channel_first = bell_draw(streams_of[12], (E, XR), (0.1 * TOKENS ** 0.5), 40.0, ((0, 32),), jnp.float32)
    channel_second = jnp.clip(jnp.exp(math.log(327.68) - 2.7725887 * jax.random.uniform(streams_of[13], (E, XR), jnp.float32) ** levels(streams_of[13], (E, XR), ((0, 32),), -0.2, 0.2)), 20.48, 327.68)
    channel_left = draw_channel_left(jax.random.fold_in(streams_of[24], 71), 0)
    channel_right = draw_channel_right(jax.random.fold_in(streams_of[24], 71), 0)
    channel_left_stat = draw_channel_left_stat(jax.random.fold_in(streams_of[24], 71), 0)
    channel_right_stat = draw_channel_right_stat(jax.random.fold_in(streams_of[24], 71), 0)
    norm_gain = jnp.clip(1.0 + 0.1 * jax.random.normal(streams_of[18], (D,), jnp.float32), 0.5, 1.5)
    gain_first = bell_draw(streams_of[19], (D,), (0.3 * TOKENS ** 0.5), 112.0, ((0, 32),), jnp.float32)
    gain_second = jnp.clip(jnp.exp(math.log(2867.2) - 2.6390573 * jax.random.uniform(streams_of[20], (D,), jnp.float32) ** levels(streams_of[20], (D,), ((0, 32),), -0.2, 0.2)), 204.8, 2867.2)
    channel_vectors = draw_channel_vectors(jax.random.fold_in(streams_of[24], 71), 0)
    vector_first = bell_draw(streams_of[22], (CP, E), (0.1 * TOKENS ** 0.5), 40.0, ((1, 32),), jnp.float32)
    vector_second = jnp.clip(jnp.exp(math.log(327.68) - 2.7725887 * jax.random.uniform(streams_of[23], (CP, E), jnp.float32) ** levels(streams_of[23], (CP, E), ((1, 32),), -0.2, 0.2)), 20.48, 327.68)
    return dict(layer_in=layer_in, cotangent=cotangent, doc_lengths=doc_lengths, tile_slot=tile_slot, pool_weight=pool_weight, pool_first=pool_first, pool_second=pool_second, pool_left=pool_left, pool_right=pool_right, pool_left_stat=pool_left_stat, pool_right_stat=pool_right_stat, channel_weight=channel_weight, channel_first=channel_first, channel_second=channel_second, channel_left=channel_left, channel_right=channel_right, channel_left_stat=channel_left_stat, channel_right_stat=channel_right_stat, norm_gain=norm_gain, gain_first=gain_first, gain_second=gain_second, channel_vectors=channel_vectors, vector_first=vector_first, vector_second=vector_second)


@jax.custom_vjp
def low(v):
    return lax.optimization_barrier(v.astype(jnp.bfloat16)).astype(jnp.float32)

@jax.custom_vjp
def low_back(v):
    return v

def low_keep(v):
    return (low(v), None)

def low_pass(kept, grad):
    return (grad,)

def back_keep(v):
    return (v, None)

def back_low(kept, grad):
    return (low(grad),)
low.defvjp(low_keep, low_pass)
low_back.defvjp(back_keep, back_low)
beta_first = 0.5
beta_second = 0.5
stat_decay = 0.5
learn_rate = 0.02
vector_rate = 0.2
weight_decay = 0.01
adam_epsilon = 1e-08
norm_epsilon = 1e-05
highest = lax.Precision.HIGHEST

def matmul(left, right):
    return jnp.dot(left, right, precision=highest)

def doc_positions(doc_lengths):
    starts = (jnp.cumsum(doc_lengths, axis=1) - doc_lengths).astype(jnp.int32)
    places = jnp.arange(L, dtype=jnp.int32)
    begun = jnp.where(starts[:, None, :] <= places[None, :, None], starts[:, None, :], 0)
    return (places[None, :] - lax.optimization_barrier(jnp.max(begun, axis=2))).astype(jnp.int32)

def conv_silu(signal, kernel_taps, conv_offset, doc_place):
    length = signal.shape[1]
    summed = conv_offset[:, None] + kernel_taps[K - 1][:, None] * signal
    for lagging in range(1, K):
        moved = jnp.pad(signal, ((0, 0), (lagging, 0)))[:, :length]
        summed = summed + jnp.where(doc_place[None, :] >= lagging, kernel_taps[K - 1 - lagging][:, None] * moved, 0.0)
    return jax.nn.silu(summed)

def ssm_scan(signal, stepsize, decay_rates, inject, readout, keeping):
    channels, length = signal.shape
    block_count = length // BLOCK

    def blocked(values):
        return values.reshape(channels, block_count, BLOCK).transpose(2, 1, 0)

    def blocked_rows(values):
        return values.reshape(block_count, BLOCK, values.shape[1]).transpose(1, 0, 2)
    signal_blocks = blocked(signal)
    step_blocks = blocked(stepsize)
    inject_blocks = blocked_rows(inject)
    read_blocks = blocked_rows(readout)
    keep_blocks = keeping.reshape(block_count, BLOCK).T

    def advance(hidden, pieces):
        signal_now, step_now, inject_now, read_now, keep_now = pieces
        factor = jnp.exp(-step_now[:, :, None] * decay_rates[None]) * keep_now[:, None, None]
        hidden = factor * hidden + (step_now * signal_now)[:, :, None] * inject_now[:, None, :]
        return (hidden, lax.optimization_barrier(jnp.sum(hidden * read_now[:, None, :], axis=2)))
    initial = jnp.zeros((block_count, channels, decay_rates.shape[1]), jnp.float32)
    finals, inside = lax.scan(advance, initial, (signal_blocks, step_blocks, inject_blocks, read_blocks, keep_blocks))
    cumulative = jnp.cumsum(step_blocks, axis=0)
    living = jnp.cumprod(keep_blocks, axis=0)
    through = jnp.exp(-cumulative[-1][:, :, None] * decay_rates[None]) * living[-1][:, None, None]

    def compose(earlier, latter):
        return (earlier[0] * latter[0], latter[0] * earlier[1] + latter[1])
    carried = lax.associative_scan(compose, (through, finals))[1]
    entering = jnp.concatenate([jnp.zeros_like(carried[:1]), carried[:-1]], axis=0)
    decays = jnp.exp(-cumulative[:, :, :, None] * decay_rates[None, None]) * living[:, :, None, None]
    incoming = lax.optimization_barrier(jnp.sum(decays * entering[None] * read_blocks[:, :, None, :], axis=3))
    return (inside + incoming).transpose(2, 1, 0).reshape(channels, length)

def mixer_row(inputs, doc_place, gain_low, input_low, select_low, step_low, output_low, vectors):
    inverse = lax.rsqrt(lax.optimization_barrier(jnp.mean(inputs * inputs, axis=1, keepdims=True)) + norm_epsilon)
    normed = low(inputs * inverse * gain_low)
    joint = low(low_back(matmul(normed, input_low)))
    gate_values = joint[:, E:].T
    filtered = low(conv_silu(joint[:, :E].T, vectors[:K], vectors[K], doc_place))
    for_select = low_back(filtered)
    projected = low(low_back(matmul(for_select.T, select_low)))
    raw_step = low_back(matmul(step_low, projected[:, :R].T))
    stepsize = jax.nn.softplus(raw_step + vectors[K + 1][:, None])
    decay_rates = jnp.exp(vectors[K + 2:K + 2 + N]).T
    keeping = (doc_place > 0).astype(jnp.float32)
    scanned = ssm_scan(filtered, stepsize, decay_rates, projected[:, R:R + N], projected[:, R + N:], keeping)
    mixed = low(low_back((scanned + vectors[K + 2 + N][:, None] * filtered) * jax.nn.silu(gate_values)))
    return inputs + matmul(mixed.T, output_low)

def layer(layer_input, gain_weight, input_weight, select_weight, step_weight, output_weight, vectors, doc_place):
    gain_low = low(gain_weight)
    input_low = low(input_weight)
    select_low = low(select_weight)
    step_low = low(step_weight)
    output_low = low(output_weight)

    def one_row(pieces):
        return mixer_row(pieces[0], pieces[1], gain_low, input_low, select_low, step_low, output_low, vectors)
    rows_out = lax.map(jax.checkpoint(one_row), (layer_input.reshape(ROWS, L, D), doc_place))
    return rows_out.reshape(ROWS * L, D)

def assemble(tiles, tall_tiles, wide_tiles):
    return tiles.reshape(tall_tiles, wide_tiles, P_SIZE, P_SIZE).transpose(0, 2, 1, 3).reshape(tall_tiles * P_SIZE, wide_tiles * P_SIZE)

def split_tiles(matrix):
    tall_tiles = matrix.shape[0] // P_SIZE
    wide_tiles = matrix.shape[1] // P_SIZE
    return matrix.reshape(tall_tiles, P_SIZE, wide_tiles, P_SIZE).transpose(0, 2, 1, 3).reshape(tall_tiles * wide_tiles, P_SIZE, P_SIZE)

def orthonormal(matrix):
    gram = jnp.einsum('bki,bkj->bij', matrix, matrix, precision=highest)
    factor = jnp.linalg.cholesky(gram)

    def solve_one(lower_factor, columns):
        return jax.scipy.linalg.solve_triangular(lower_factor, columns, lower=True)
    solved = jax.vmap(solve_one)(factor, jnp.swapaxes(matrix, 1, 2))
    return jnp.swapaxes(solved, 1, 2)

def renewal(stat, basis):
    shift_level = lax.optimization_barrier(jnp.sum(jnp.diagonal(stat, axis1=1, axis2=2), axis=1)) / stat.shape[1]
    return jnp.einsum('bik,bkj->bij', stat, basis, precision=highest) + shift_level[:, None, None] * basis

def soap_step(weight, gradient, first, second, left_basis, right_basis, left_stat, right_stat):
    turned = jnp.einsum('bki,bkj->bij', left_basis, jnp.einsum('bik,bkj->bij', gradient, right_basis, precision=highest), precision=highest)
    first_new = beta_first * first + (1.0 - beta_first) * turned
    second_new = beta_second * second + (1.0 - beta_second) * turned * turned
    direction = first_new / (1.0 - beta_first ** STEP) / (jnp.sqrt(second_new / (1.0 - beta_second ** STEP)) + adam_epsilon)
    returned = jnp.einsum('bik,bkj->bij', left_basis, jnp.einsum('bik,bjk->bij', direction, right_basis, precision=highest), precision=highest)
    weight_new = weight - learn_rate * (returned + weight_decay * weight)
    left_stat_new = stat_decay * left_stat + (1.0 - stat_decay) * jnp.einsum('bik,bjk->bij', gradient, gradient, precision=highest)
    right_stat_new = stat_decay * right_stat + (1.0 - stat_decay) * jnp.einsum('bki,bkj->bij', gradient, gradient, precision=highest)
    left_new = orthonormal(renewal(left_stat_new, left_basis))
    right_new = orthonormal(renewal(right_stat_new, right_basis))
    return (first_new, second_new, weight_new, left_new, right_new, left_stat_new, right_stat_new)

def adam_step(weight, gradient, first, second):
    first_new = beta_first * first + (1.0 - beta_first) * gradient
    second_new = beta_second * second + (1.0 - beta_second) * gradient * gradient
    direction = first_new / (1.0 - beta_first ** STEP) / (jnp.sqrt(second_new / (1.0 - beta_second ** STEP)) + adam_epsilon)
    return (first_new, second_new, weight - vector_rate * (direction + weight_decay * weight))

def reference(layer_in, cotangent, doc_lengths, tile_slot, pool_weight, pool_first, pool_second, pool_left, pool_right, pool_left_stat, pool_right_stat, channel_weight, channel_first, channel_second, channel_left, channel_right, channel_left_stat, channel_right_stat, norm_gain, gain_first, gain_second, channel_vectors, vector_first, vector_second):
    doc_place = doc_positions(doc_lengths)
    tiles = jnp.take(pool_weight, tile_slot, axis=0)
    input_weight = assemble(tiles[:NI], D // P_SIZE, 2 * E // P_SIZE)
    output_weight = assemble(tiles[NI:], E // P_SIZE, D // P_SIZE)
    output, pullback = jax.vjp(partial(layer, doc_place=doc_place), layer_in.astype(jnp.float32), norm_gain, input_weight, channel_weight[:, :XW], channel_weight[:, XW:], output_weight, channel_vectors)
    grads = pullback(cotangent.astype(jnp.float32))
    input_grad = grads[0]
    grad_tiles = jnp.concatenate([split_tiles(grads[2]), split_tiles(grads[5])], axis=0)
    pool_grad = jnp.zeros_like(grad_tiles).at[tile_slot].set(grad_tiles)
    pool_new = soap_step(pool_weight, pool_grad, pool_first, pool_second, pool_left, pool_right, pool_left_stat, pool_right_stat)
    blocks = E // CH
    channel_grad = jnp.concatenate([grads[3], grads[4]], axis=1).reshape(blocks, CH, XR)
    channel_new = soap_step(channel_weight.reshape(blocks, CH, XR), channel_grad, channel_first.reshape(blocks, CH, XR), channel_second.reshape(blocks, CH, XR), channel_left.reshape(blocks, CH, CH), channel_right.reshape(blocks, XR, XR), channel_left_stat.reshape(blocks, CH, CH), channel_right_stat.reshape(blocks, XR, XR))
    gain_new = adam_step(norm_gain, grads[1], gain_first, gain_second)
    vector_new = adam_step(channel_vectors, grads[6], vector_first, vector_second)
    return (output.astype(jnp.bfloat16), input_grad, pool_new[0], pool_new[1], pool_new[2], pool_new[3], pool_new[4], pool_new[5], pool_new[6], channel_new[0].reshape(E, XR), channel_new[1].reshape(E, XR), channel_new[2].reshape(E, XR), channel_new[3].reshape(E, CH), channel_new[4].reshape(blocks * XR, XR), channel_new[5].reshape(E, CH), channel_new[6].reshape(blocks * XR, XR), gain_new[0], gain_new[1], gain_new[2], vector_new[0], vector_new[1], vector_new[2])
```

```python
import functools

import jax
import jax.numpy as jnp
from jax import lax
from jax.experimental import pallas as pl
from jax.experimental.pallas import tpu as pltpu
from jax.sharding import PartitionSpec as P

N = 16
R = 128
K = 4
L = 2048
STEP = 5
GROUP = 16
LOG2E = 1.4426950408889634

beta_first = 0.5
beta_second = 0.5
stat_decay = 0.5
learn_rate = 0.02
vector_rate = 0.2
weight_decay = 0.01
adam_epsilon = 1e-08
norm_epsilon = 1e-05
highest = lax.Precision.HIGHEST


def dot_nt(left, right):
    return lax.dot_general(left, right, (((1,), (1,)), ((), ())), preferred_element_type=jnp.float32)

def dot_nn(left, right):
    return jnp.dot(left, right, preferred_element_type=jnp.float32)

def softplus(v):
    return jnp.maximum(v, 0.0) + jnp.log1p(jnp.exp(-jnp.abs(v)))

def split2(v):
    high = v.astype(jnp.bfloat16)
    return high, (v - high.astype(jnp.float32)).astype(jnp.bfloat16)

def own_token(dtype):
    token = lax.broadcasted_iota(jnp.int32, (GROUP, GROUP * N), 0)
    column = lax.broadcasted_iota(jnp.int32, (GROUP, GROUP * N), 1)
    return (column // N == token).astype(dtype)

def fwd_kernel(pair, chunk, f_ref, rank_ref, z_ref, gm_ref, start_ref, cols_ref, read_ref,
               stepw_ref, bias_ref, rate_ref, skip_ref,
               mixed_ref, dz_ref, keep_ref, state, step_s, drive_s, scan_s):
    groups = chunk // GROUP
    neg = rate_ref[...] * (-LOG2E)
    mine = own_token(jnp.float32)

    @pl.when(pl.program_id(1) == 0)
    def _():
        state[...] = jnp.zeros_like(state)

    for r in range(pair):
        raw = dot_nt(rank_ref[r], stepw_ref[...])
        step = softplus(raw + bias_ref[...])
        step_s[r] = step + start_ref[r].astype(jnp.float32)
        drive_s[r] = step * f_ref[r].astype(jnp.float32)
        keep_ref[r, 0] = state[r]

    def group(g, hidden):
        hidden = list(hidden)
        held = [[] for _ in range(pair)]
        base = pl.multiple_of(g * GROUP, GROUP)
        cols = [cols_ref[r, g] for r in range(pair)]
        for k in range(GROUP):
            for r in range(pair):
                factor = jnp.exp2(step_s[r, pl.ds(base + k, 1), :] * neg)
                hidden[r] = factor * hidden[r] + drive_s[r, pl.ds(base + k, 1), :] * cols[r][:N, k : k + 1]
                held[r].append(hidden[r].astype(jnp.bfloat16))
        for r in range(pair):
            states = jnp.concatenate(held[r], axis=0)
            scan_s[r, pl.ds(base, GROUP), :] = dot_nn((mine * read_ref[r, pl.ds(g, 1), :]).astype(jnp.bfloat16), states)
        return tuple(hidden)

    hidden = lax.fori_loop(0, groups, group, tuple(state[r] for r in range(pair)))
    for r in range(pair):
        state[r] = hidden[r]
        f = f_ref[r].astype(jnp.float32)
        z = z_ref[r].astype(jnp.float32)
        gate = 1.0 / (1.0 + jnp.exp(-z))
        summed = scan_s[r] + skip_ref[...] * f
        mixed_ref[r] = (summed * (z * gate)).astype(jnp.bfloat16)
        dz_ref[r] = (gm_ref[r].astype(jnp.float32) * summed * (gate * (1.0 + z * (1.0 - gate)))).astype(jnp.bfloat16)

def bwd_kernel(pair, chunk, f_ref, rank_ref, z_ref, gm_ref, start_ref, cols_ref, inj_ref,
               stepw_ref, bias_ref, rate_ref, skip_ref, keep_ref,
               draw_ref, dfm_ref, dinj_ref, dread_ref, drate_ref, dskip_ref, dbias_ref,
               carry_s, step_s, drive_s, dscan_s, raw_s, delta_s, a_s, ah_s, h_s, s1_s, s2_s):
    groups = chunk // GROUP
    rate = rate_ref[...]
    neg = rate * (-LOG2E)
    mine = own_token(jnp.float32)
    mine_f = mine

    @pl.when(pl.program_id(1) == 0)
    def _():
        carry_s[...] = jnp.zeros_like(carry_s)

    @pl.when((pl.program_id(1) == 0) & (pl.program_id(0) == 0))
    def _():
        drate_ref[...] = jnp.zeros_like(drate_ref)
        dskip_ref[...] = jnp.zeros_like(dskip_ref)
        dbias_ref[...] = jnp.zeros_like(dbias_ref)

    for r in range(pair):
        raw = dot_nt(rank_ref[r], stepw_ref[...]) + bias_ref[...]
        step = softplus(raw)
        raw_s[r] = raw
        delta_s[r] = step
        step_s[r] = step + start_ref[r].astype(jnp.float32)
        f = f_ref[r].astype(jnp.float32)
        drive_s[r] = step * f
        z = z_ref[r].astype(jnp.float32)
        gate = 1.0 / (1.0 + jnp.exp(-z))
        dscan = gm_ref[r].astype(jnp.float32) * (z * gate)
        dscan_s[r] = dscan
        dskip_ref[...] += jnp.sum(dscan * f, axis=0, keepdims=True)

    def forward(g, hidden):
        hidden = list(hidden)
        base = pl.multiple_of(g * GROUP, GROUP)
        cols = [cols_ref[r, g] for r in range(pair)]
        held = [[] for _ in range(pair)]
        for k in range(GROUP):
            for r in range(pair):
                factor = jnp.exp2(step_s[r, pl.ds(base + k, 1), :] * neg)
                kept = factor * hidden[r]
                hidden[r] = kept + drive_s[r, pl.ds(base + k, 1), :] * cols[r][:N, k : k + 1]
                a_s[r, base + k] = factor
                ah_s[r, base + k] = kept
                held[r].append(hidden[r].astype(jnp.bfloat16))
        for r in range(pair):
            h_s[r, g] = jnp.concatenate(held[r], axis=0)
        return tuple(hidden)

    lax.fori_loop(0, groups, forward, tuple(keep_ref[r, 0] for r in range(pair)))

    def backward(i, carried):
        g = groups - 1 - i
        base = pl.multiple_of(g * GROUP, GROUP)
        ag = list(carried[:pair])
        total = carried[pair]
        cols = [cols_ref[r, g] for r in range(pair)]
        gs = [[None] * GROUP for _ in range(pair)]
        qs = [[None] * GROUP for _ in range(pair)]
        for k in reversed(range(GROUP)):
            for r in range(pair):
                grad = dscan_s[r, pl.ds(base + k, 1), :] * cols[r][N:, k : k + 1] + ag[r]
                ag[r] = a_s[r, base + k] * grad
                q = grad * ah_s[r, base + k]
                total = total + delta_s[r, pl.ds(base + k, 1), :] * q
                gs[r][k] = grad.astype(jnp.bfloat16)
                qs[r][k] = (rate * q).astype(jnp.bfloat16)
        for r in range(pair):
            grads = jnp.concatenate(gs[r], axis=0)
            pulls = jnp.concatenate(qs[r], axis=0)
            s1_s[r, pl.ds(base, GROUP), :] = dot_nn((mine * inj_ref[r, pl.ds(g, 1), :]).astype(jnp.bfloat16), grads)
            s2_s[r, pl.ds(base, GROUP), :] = dot_nn(mine.astype(jnp.bfloat16), pulls)
            dh, dl = split2(dscan_s[r, pl.ds(base, GROUP), :])
            uh, ul = split2(drive_s[r, pl.ds(base, GROUP), :])
            dr = dot_nt(jnp.concatenate([dh, dl], axis=0), h_s[r, g])
            dread_ref[r, pl.ds(g, 1), :] = jnp.sum((dr[:GROUP] + dr[GROUP:]) * mine_f, axis=0, keepdims=True)
            di = dot_nt(jnp.concatenate([uh, ul], axis=0), grads)
            dinj_ref[r, pl.ds(g, 1), :] = jnp.sum((di[:GROUP] + di[GROUP:]) * mine_f, axis=0, keepdims=True)
        return tuple(ag) + (total,)

    out = lax.fori_loop(0, groups, backward, tuple(carry_s[r] for r in range(pair)) + (jnp.zeros_like(rate),))
    drate_ref[...] += out[pair]
    for r in range(pair):
        carry_s[r] = out[r]
        f = f_ref[r].astype(jnp.float32)
        draw = (f * s1_s[r] - s2_s[r]) / (1.0 + jnp.exp(-raw_s[r]))
        draw_ref[r] = draw.astype(jnp.bfloat16)
        dbias_ref[...] += jnp.sum(draw, axis=0, keepdims=True)
        dfm_ref[r] = delta_s[r] * s1_s[r] + skip_ref[...] * dscan_s[r]

def specs(pair, chunk, ch, rank, back, chunks):
    def at(i, j):
        return (i, chunks - 1 - j if back else j)
    tok = pl.BlockSpec((pair, chunk, ch), lambda i, j: at(i, j) + (0,))
    rk = pl.BlockSpec((pair, chunk, rank), lambda i, j: at(i, j) + (0,))
    cols = pl.BlockSpec((pair, chunk // GROUP, 2 * N, GROUP), lambda i, j: at(i, j) + (0, 0))
    flat = pl.BlockSpec((pair, chunk // GROUP, GROUP * N), lambda i, j: at(i, j) + (0,))
    keep = pl.BlockSpec((pair, 1, N, ch), lambda i, j: at(i, j) + (0, 0))
    def whole(a):
        return pl.BlockSpec(a.shape, lambda i, j: (0,) * a.ndim)
    return tok, rk, cols, flat, keep, whole

def scan_forward(f, rank, z, gm, start, cols, read, stepw, bias, rate, skip, chunk=128):
    rows, length, ch = f.shape
    pair = 2 if rows % 2 == 0 else 1
    chunks = length // chunk
    tok, rk, colb, flat, keep, whole = specs(pair, chunk, ch, rank.shape[2], False, chunks)
    return pl.pallas_call(
        functools.partial(fwd_kernel, pair, chunk),
        grid=(rows // pair, chunks),
        in_specs=[tok, rk, tok, tok, tok, colb, flat, whole(stepw), whole(bias), whole(rate), whole(skip)],
        out_specs=[tok, tok, keep],
        out_shape=[jax.ShapeDtypeStruct(f.shape, jnp.bfloat16), jax.ShapeDtypeStruct(f.shape, jnp.bfloat16),
                   jax.ShapeDtypeStruct((rows, chunks, N, ch), jnp.float32)],
        scratch_shapes=[pltpu.VMEM((pair, N, ch), jnp.float32)] + [pltpu.VMEM((pair, chunk, ch), jnp.float32)] * 3,
        compiler_params=pltpu.CompilerParams(vmem_limit_bytes=40 * 2**20),
    )(f, rank, z, gm, start, cols, read, stepw, bias, rate, skip)

def scan_backward(f, rank, z, gm, start, cols, inj, stepw, bias, rate, skip, kept, chunk=128):
    rows, length, ch = f.shape
    pair = 2 if rows % 2 == 0 else 1
    chunks = length // chunk
    tok, rk, colb, flat, keep, whole = specs(pair, chunk, ch, rank.shape[2], True, chunks)
    f32 = jnp.float32
    row = jax.ShapeDtypeStruct((1, ch), f32)
    return pl.pallas_call(
        functools.partial(bwd_kernel, pair, chunk),
        grid=(rows // pair, chunks),
        in_specs=[tok, rk, tok, tok, tok, colb, flat, whole(stepw), whole(bias), whole(rate), whole(skip), keep],
        out_specs=[tok, tok, flat, flat, whole(rate), whole(row), whole(row)],
        out_shape=[jax.ShapeDtypeStruct(f.shape, jnp.bfloat16), jax.ShapeDtypeStruct(f.shape, f32),
                   jax.ShapeDtypeStruct(inj.shape, f32), jax.ShapeDtypeStruct(inj.shape, f32),
                   jax.ShapeDtypeStruct(rate.shape, f32), row, row],
        scratch_shapes=[pltpu.VMEM((pair, N, ch), f32)] + [pltpu.VMEM((pair, chunk, ch), f32)] * 5
        + [pltpu.VMEM((pair, chunk, N, ch), f32)] * 2 + [pltpu.VMEM((pair, chunk // GROUP, GROUP * N, ch), jnp.bfloat16)]
        + [pltpu.VMEM((pair, chunk, ch), f32)] * 2,
        compiler_params=pltpu.CompilerParams(vmem_limit_bytes=40 * 2**20),
    )(f, rank, z, gm, start, cols, inj, stepw, bias, rate, skip, kept)


def chol_kernel(batch, order, gram_ref, out_ref, low_ref, inv_ref, piv_ref):
    tiles = order // 8
    rows8 = lax.broadcasted_iota(jnp.int32, (8, batch), 0)

    def load_slab(j, carry):
        low_ref[j, pl.ds(0, order), :] = gram_ref[pl.ds(j, batch, stride=order), :].T
        inv_ref[j] = jnp.zeros(inv_ref.shape[1:], jnp.float32)
        return carry

    lax.fori_loop(0, order, load_slab, 0)

    def bcast(ref, j, row):
        return jnp.broadcast_to(ref[j, pl.ds(row, 1), :], (8, batch))

    def block_column(block, carry):
        base = pl.multiple_of(block * 8, 8)

        def updated(tile_rows, seed):
            def one(j, accs):
                mult = [bcast(low_ref, j, base + k) for k in range(8)]
                out = []
                for s, rows in enumerate(tile_rows):
                    piece = low_ref[j, pl.ds(rows, 8), :]
                    out.extend(accs[s * 8 + k] - piece * mult[k] for k in range(8))
                return tuple(out)

            def eight(step, accs):
                for u in range(8):
                    accs = one(step * 8 + u, accs)
                return accs

            return list(lax.fori_loop(0, block, eight, tuple(seed)))

        accs = updated([base], [low_ref[base + k, pl.ds(base, 8), :] for k in range(8)])
        scales = []
        for k in range(8):
            scale = lax.rsqrt(jnp.broadcast_to(accs[k][k : k + 1, :], (8, batch)))
            scales.append(scale)
            accs[k] = jnp.where(rows8 >= k, accs[k] * scale, 0.0)
            for later in range(k + 1, 8):
                accs[later] = accs[later] - accs[k] * jnp.broadcast_to(
                    accs[k][later : later + 1, :], (8, batch)
                )
        for k in range(8):
            low_ref[base + k, pl.ds(base, 8), :] = accs[k]
            piv_ref[base + k] = scales[k]

        def pair(p, carry):
            first = pl.multiple_of(base + 8 + p * 16, 8)
            both = [first, pl.multiple_of(first + 8, 8)]
            accs = updated(
                both, [low_ref[base + k, pl.ds(rows, 8), :] for rows in both for k in range(8)]
            )
            for k in range(8):
                scale = piv_ref[base + k]
                for s in range(2):
                    accs[s * 8 + k] = accs[s * 8 + k] * scale
                for later in range(k + 1, 8):
                    mult = bcast(low_ref, base + k, base + later)
                    for s in range(2):
                        accs[s * 8 + later] = accs[s * 8 + later] - accs[s * 8 + k] * mult
            for s, rows in enumerate(both):
                for k in range(8):
                    low_ref[base + k, pl.ds(rows, 8), :] = accs[s * 8 + k]
            return carry

        lax.fori_loop(0, (tiles - block) // 2, pair, 0)
        return carry

    lax.fori_loop(0, tiles, block_column, 0)

    def block_row(block, carry):
        base = pl.multiple_of(block * 8, 8)

        def finish(accs, both):
            for k in range(8):
                scale = piv_ref[base + k]
                for s in range(len(both)):
                    accs[s * 8 + k] = accs[s * 8 + k] * scale
                for later in range(k + 1, 8):
                    mult = bcast(low_ref, base + k, base + later)
                    for s in range(len(both)):
                        accs[s * 8 + later] = accs[s * 8 + later] - accs[s * 8 + k] * mult
            for s, columns in enumerate(both):
                for k in range(8):
                    inv_ref[base + k, pl.ds(columns, 8), :] = accs[s * 8 + k]

        def pair(p, carry):
            first = pl.multiple_of(p * 16, 8)
            both = [first, pl.multiple_of(first + 8, 8)]

            def eight(step, accs):
                for u in range(8):
                    j = step * 8 + u
                    mult = [bcast(low_ref, j, base + k) for k in range(8)]
                    out = []
                    for s, columns in enumerate(both):
                        piece = inv_ref[j, pl.ds(columns, 8), :]
                        out.extend(accs[s * 8 + k] - piece * mult[k] for k in range(8))
                    accs = tuple(out)
                return accs

            accs = list(lax.fori_loop(
                p * 2, block, eight, (jnp.zeros((8, batch), jnp.float32),) * 16
            ))
            finish(accs, both)
            return carry

        lax.fori_loop(0, (block + 1) // 2, pair, 0)
        odd = block % 2

        def diagonal():
            accs = [jnp.where(rows8 == k, 1.0, 0.0) for k in range(8)]
            finish(accs, [base])

        diagonal()
        return carry

    lax.fori_loop(0, tiles, block_row, 0)

    def store_slab(i, carry):
        out_ref[pl.ds(i, batch, stride=order), :] = inv_ref[i, pl.ds(0, order), :].T
        return carry

    lax.fori_loop(0, order, store_slab, 0)

def inverse_factor(gram):
    batch, order, _ = gram.shape
    out = pl.pallas_call(
        functools.partial(chol_kernel, batch, order),
        out_shape=jax.ShapeDtypeStruct((batch * order, order), jnp.float32),
        in_specs=[pl.BlockSpec(memory_space=pltpu.VMEM)],
        out_specs=pl.BlockSpec(memory_space=pltpu.VMEM),
        scratch_shapes=[
            pltpu.VMEM((order, order + 8, batch), jnp.float32),
            pltpu.VMEM((order, order + 8, batch), jnp.float32),
            pltpu.VMEM((order, 8, batch), jnp.float32),
        ],
        compiler_params=pltpu.CompilerParams(vmem_limit_bytes=56 * 2**20),
    )(gram.reshape(batch * order, order))
    return out.reshape(batch, order, order)


def tile_product_kernel(many, steps, transposed, left_blocks, residual, idx_ref, *refs):
    left_ref, tiles = refs[0], refs[1 : 1 + many]
    refs = refs[1 + many :]
    if residual:
        res_ref, refs = refs[0], refs[1:]
    out_ref = refs[0]
    side = tiles[0].shape[1]
    total = None
    for u in range(0, many, 2):
        if left_blocks:
            left = jnp.concatenate([left_ref[u], left_ref[u + 1]], axis=1)
        else:
            left = left_ref[:, u * side : (u + 2) * side]
        if transposed:
            part = dot_nt(left, jnp.concatenate([tiles[u][0], tiles[u + 1][0]], axis=1))
        else:
            part = dot_nn(left, jnp.concatenate([tiles[u][0], tiles[u + 1][0]], axis=0))
        total = part if total is None else total + part

    def finish(value):
        if residual:
            value = value + res_ref[...].astype(jnp.float32)
        value = value.astype(out_ref.dtype)
        if len(out_ref.shape) == 3:
            out_ref[0] = value
        else:
            out_ref[...] = value

    if steps == 1:
        finish(total)
        return
    sum_ref = refs[1]
    step = pl.program_id(1)

    @pl.when(step == 0)
    def _():
        sum_ref[...] = total

    @pl.when((step > 0) & (step < steps - 1))
    def _():
        sum_ref[...] += total

    @pl.when(step == steps - 1)
    def _():
        finish(sum_ref[...] + total)


def tile_product(left, pool, index, transposed, dtype, flat_out, residual=None):
    outs, depth = index.shape
    many = 16
    steps = depth // many
    side = pool.shape[1]
    left_blocks = left.ndim == 3
    tok = left.shape[1] if left_blocks else left.shape[0]
    if left_blocks:
        left_spec = pl.BlockSpec((many, tok, side), lambda o, k, idx: (k, 0, 0))
    else:
        left_spec = pl.BlockSpec((tok, many * side), lambda o, k, idx: (0, k))

    def tile_spec(u):
        return pl.BlockSpec((1, side, side), lambda o, k, idx: (idx[(o * steps + k) * many + u], 0, 0))

    if flat_out:
        out_spec = pl.BlockSpec((tok, side), lambda o, k, idx: (0, o))
        out_shape = jax.ShapeDtypeStruct((tok, outs * side), dtype)
    else:
        out_spec = pl.BlockSpec((1, tok, side), lambda o, k, idx: (o, 0, 0))
        out_shape = jax.ShapeDtypeStruct((outs, tok, side), dtype)
    extra_specs = [pl.BlockSpec((tok, side), lambda o, k, idx: (0, o))] if residual is not None else []
    extra = [residual] if residual is not None else []
    return pl.pallas_call(
        functools.partial(tile_product_kernel, many, steps, transposed, left_blocks, residual is not None),
        grid_spec=pltpu.PrefetchScalarGridSpec(
            num_scalar_prefetch=1,
            grid=(outs, steps),
            in_specs=[left_spec] + [tile_spec(u) for u in range(many)] + extra_specs,
            out_specs=out_spec,
            scratch_shapes=[] if steps == 1 else [pltpu.VMEM((tok, side), jnp.float32)],
        ),
        out_shape=out_shape,
        cost_estimate=pl.CostEstimate(
            flops=2 * outs * depth * tok * side * side, bytes_accessed=outs * depth * side * side * 2, transcendentals=0
        ),
    )(index.reshape(-1).astype(jnp.int32), left, *([pool] * many), *extra)


def dot_tn(left, right):
    return lax.dot_general(left, right, (((0,), (0,)), ((), ())), preferred_element_type=jnp.float32)


def three(dot, left, right):
    return dot(left[0], right[0]) + (dot(left[0], right[1]) + dot(left[1], right[0]))


def soap_kernel(kind_ref, idx_ref, gx_ref, gz_ref, go_ref, weight_ref, first_ref, second_ref, left_ref, right_ref,
                lstat_ref, rstat_ref, first_out, second_out, weight_out, lstat_out, rstat_out, turned_out, gram_out):
    kind = kind_ref[pl.program_id(0)]
    grad = jnp.where(kind == 0, gx_ref[0], jnp.where(kind == 1, gz_ref[0], go_ref[0]))
    left = left_ref[0]
    right = right_ref[0]
    left2 = split2(left)
    right2 = split2(right)
    across = split2(dot_nn(grad, right2[0]) + dot_nn(grad, right2[1]))
    turned = three(dot_tn, left2, across)
    first = beta_first * first_ref[0] + (1.0 - beta_first) * turned
    second = beta_second * second_ref[0] + (1.0 - beta_second) * turned * turned
    first_out[0] = first
    second_out[0] = second
    direction = (
        first / (1.0 - beta_first**STEP) / (jnp.sqrt(second / (1.0 - beta_second**STEP)) + adam_epsilon)
    )
    returned = three(dot_nn, left2, split2(three(dot_nt, split2(direction), right2)))
    weight = weight_ref[0]
    weight_out[0] = weight - learn_rate * (returned + weight_decay * weight)
    side = left.shape[0]
    diagonal = lax.broadcasted_iota(jnp.int32, (side, side), 0) == lax.broadcasted_iota(jnp.int32, (side, side), 1)

    def renew(which, stat, product, basis, basis2, stat_out):
        stat = stat_decay * stat + (1.0 - stat_decay) * product
        stat_out[0] = stat
        trace = jnp.sum(jnp.sum(jnp.where(diagonal, stat, 0.0), axis=0, keepdims=True), axis=1, keepdims=True)
        turned = three(dot_nn, split2(stat), basis2) + (trace / side) * basis
        turned_out[0, which] = turned
        turned2 = split2(turned)
        gram_out[0, which] = three(dot_tn, turned2, turned2)

    renew(0, lstat_ref[0], dot_nt(grad, grad), left, left2, lstat_out)
    renew(1, rstat_ref[0], dot_tn(grad, grad), right, right2, rstat_out)


def soap_tiles(kind, index, grads, weight, first, second, left, right, lstat, rstat):
    count, side, _ = weight.shape
    one = pl.BlockSpec((1, side, side), lambda s, kind, idx: (s, 0, 0))
    two = pl.BlockSpec((1, 2, side, side), lambda s, kind, idx: (s, 0, 0, 0))

    def picked(which):
        return pl.BlockSpec((1, side, side), lambda s, kind, idx: (jnp.where(kind[s] == which, idx[s], 0), 0, 0))

    tile = jax.ShapeDtypeStruct(weight.shape, jnp.float32)
    pairs = jax.ShapeDtypeStruct((count, 2, side, side), jnp.float32)
    return pl.pallas_call(
        soap_kernel,
        grid_spec=pltpu.PrefetchScalarGridSpec(
            num_scalar_prefetch=2,
            grid=(count,),
            in_specs=[picked(0), picked(1), picked(2)] + [one] * 7,
            out_specs=[one] * 5 + [two] * 2,
        ),
        out_shape=[tile] * 5 + [pairs] * 2,
        cost_estimate=pl.CostEstimate(flops=count * 60 * side**3, bytes_accessed=count * 18 * 4 * side**2, transcendentals=0),
    )(kind, index, *grads, weight, first, second, left, right, lstat, rstat)


def renew_kernel(turned_ref, inv_ref, left_out, right_out):
    for which, out in ((0, left_out), (1, right_out)):
        out[0] = three(dot_nt, split2(turned_ref[0, which]), split2(inv_ref[0, which]))


def renew_bases(turned, inverse):
    count, _, side, _ = turned.shape
    one = pl.BlockSpec((1, side, side), lambda s: (s, 0, 0))
    two = pl.BlockSpec((1, 2, side, side), lambda s: (s, 0, 0, 0))
    tile = jax.ShapeDtypeStruct((count, side, side), jnp.float32)
    return pl.pallas_call(
        renew_kernel,
        grid=(count,),
        in_specs=[two, two],
        out_specs=[one, one],
        out_shape=[tile, tile],
    )(turned, inverse)


def doc_positions(doc_lengths):
    starts = jnp.cumsum(doc_lengths, axis=1) - doc_lengths
    places = jnp.arange(L, dtype=jnp.int32)
    begun = jnp.where(starts[:, None, :] <= places[None, :, None], starts[:, None, :], 0)
    return places[None, :] - jnp.max(begun, axis=2)


def orthonormal(matrix):
    gram = jnp.einsum("bki,bkj->bij", matrix, matrix, precision=highest)
    factor = jnp.linalg.cholesky(gram)

    def solve_one(lower_factor, columns):
        return jax.scipy.linalg.solve_triangular(lower_factor, columns, lower=True)

    solved = jax.vmap(solve_one)(factor, jnp.swapaxes(matrix, 1, 2))
    return jnp.swapaxes(solved, 1, 2)


def renewal(stat, basis):
    shift_level = jnp.sum(jnp.diagonal(stat, axis1=1, axis2=2), axis=1) / stat.shape[1]
    return (
        jnp.einsum("bik,bkj->bij", stat, basis, precision=highest)
        + shift_level[:, None, None] * basis
    )


def soap_step(weight, gradient, first, second, left_basis, right_basis, left_stat, right_stat):
    turned = jnp.einsum(
        "bki,bkj->bij",
        left_basis,
        jnp.einsum("bik,bkj->bij", gradient, right_basis, precision=highest),
        precision=highest,
    )
    first_new = beta_first * first + (1.0 - beta_first) * turned
    second_new = beta_second * second + (1.0 - beta_second) * turned * turned
    direction = (
        first_new
        / (1.0 - beta_first**STEP)
        / (jnp.sqrt(second_new / (1.0 - beta_second**STEP)) + adam_epsilon)
    )
    returned = jnp.einsum(
        "bik,bkj->bij",
        left_basis,
        jnp.einsum("bik,bjk->bij", direction, right_basis, precision=highest),
        precision=highest,
    )
    weight_new = weight - learn_rate * (returned + weight_decay * weight)
    left_stat_new = stat_decay * left_stat + (1.0 - stat_decay) * jnp.einsum(
        "bik,bjk->bij", gradient, gradient, precision=highest
    )
    right_stat_new = stat_decay * right_stat + (1.0 - stat_decay) * jnp.einsum(
        "bki,bkj->bij", gradient, gradient, precision=highest
    )
    left_new = orthonormal(renewal(left_stat_new, left_basis))
    right_new = orthonormal(renewal(right_stat_new, right_basis))
    return (first_new, second_new, weight_new, left_new, right_new, left_stat_new, right_stat_new)


def adam_step(weight, gradient, first, second):
    first_new = beta_first * first + (1.0 - beta_first) * gradient
    second_new = beta_second * second + (1.0 - beta_second) * gradient * gradient
    direction = (
        first_new
        / (1.0 - beta_first**STEP)
        / (jnp.sqrt(second_new / (1.0 - beta_second**STEP)) + adam_epsilon)
    )
    return (first_new, second_new, weight - vector_rate * (direction + weight_decay * weight))


def later(values, lag):
    return jnp.pad(values, ((lag, 0), (0, 0)))[: values.shape[0]]


def sooner(values, lag):
    return jnp.pad(values, ((0, lag), (0, 0)))[lag:]


def conv_pre(xs, taps, offset, place):
    total = offset[None] + taps[K - 1][None] * xs
    for lag in range(1, K):
        total = total + jnp.where(place >= lag, taps[K - 1 - lag][None] * later(xs, lag), 0.0)
    return total


def shards(
    layer_in,
    cotangent,
    doc_lengths,
    tile_slot,
    pool_weight,
    pool_first,
    pool_second,
    pool_left,
    pool_right,
    pool_left_stat,
    pool_right_stat,
    channel_weight,
    channel_first,
    channel_second,
    channel_left,
    channel_right,
    channel_left_stat,
    channel_right_stat,
    norm_gain,
    gain_first,
    gain_second,
    channel_vectors,
    vector_first,
    vector_second,
):
    bf16, f32 = jnp.bfloat16, jnp.float32
    devices = lax.axis_size("tok")
    me = lax.axis_index("tok")
    tok_rows, model_width = layer_in.shape
    tokens = tok_rows * devices
    rows = tokens // L
    channels = channel_vectors.shape[1]
    inner_width = channels * devices
    tiles_here, side, _ = pool_weight.shape
    tile_total = tiles_here * devices
    tall = model_width // side
    half = inner_width // side
    wide = 2 * half
    cut = side // channels
    input_tiles = tall * wide
    select_width = channel_weight.shape[1] - R
    select_here = channels * select_width
    gain_here = norm_gain.shape[0]
    per_device = tiles_here + -(-(select_here + gain_here) // (side * side))

    spare = (per_device - tiles_here) * side * side - select_here - gain_here
    tail = jnp.concatenate(
        [channel_weight[:, :select_width].reshape(-1), norm_gain, jnp.zeros((spare,), f32)]
    ).astype(bf16)
    packed = jnp.concatenate([pool_weight.astype(bf16), tail.reshape(-1, side, side)], axis=0)
    pool_all = lax.all_gather(packed, "tok", axis=0, tiled=True)
    tail_all = pool_all.reshape(devices, per_device, side, side)[:, tiles_here:].reshape(devices, -1)
    select_weight = tail_all[:, :select_here].reshape(inner_width, select_width)
    gain_float = tail_all[:, select_here : select_here + gain_here].reshape(-1).astype(f32)
    spot = tile_slot // tiles_here * per_device + tile_slot % tiles_here
    input_spot = spot[:input_tiles].reshape(tall, wide)
    output_spot = spot[input_tiles:].reshape(half, tall)

    input_float = layer_in.astype(f32)
    inverse = lax.rsqrt(jnp.mean(input_float * input_float, axis=1, keepdims=True) + norm_epsilon)
    normed = (input_float * inverse * gain_float).astype(bf16)

    def to_channels(blocks):
        lead = blocks.shape[:-3]
        parts = blocks.reshape(lead + (half, tok_rows, cut, channels))
        parts = jnp.swapaxes(parts, -3, -2).reshape(lead + (devices, tok_rows, channels))
        moved = lax.all_to_all(parts, "tok", split_axis=len(lead), concat_axis=len(lead), tiled=True)
        return moved.reshape(lead + (tokens, channels))

    def to_tokens(values):
        lead = values.shape[:-2]
        parts = values.reshape(lead + (devices, tok_rows, channels))
        moved = lax.all_to_all(parts, "tok", split_axis=len(lead), concat_axis=len(lead), tiled=True)
        moved = moved.reshape(lead + (half, cut, tok_rows, channels))
        return jnp.swapaxes(moved, -3, -2).reshape(lead + (half, tok_rows, side))

    joint = tile_product(normed, pool_all, input_spot.T, False, bf16, False)
    joint_chan = to_channels(joint.reshape(2, half, tok_rows, side))
    back_tokens = tile_product(cotangent, pool_all, output_spot, True, bf16, False)
    back_chan = to_channels(back_tokens)

    place = doc_positions(doc_lengths).reshape(-1, 1)
    taps, offset = channel_vectors[:K], channel_vectors[K]
    xs = joint_chan[0].astype(f32)
    filtered = jax.nn.silu(conv_pre(xs, taps, offset, place)).astype(bf16)
    filtered_tokens = to_tokens(filtered)
    projected = jnp.einsum(
        "gtc,gcf->tf",
        filtered_tokens,
        select_weight.reshape(half, side, select_width),
        preferred_element_type=f32,
    ).astype(bf16)
    projected_all = lax.all_gather(projected, "tok", axis=0, tiled=True)

    by_row = lambda values: values.reshape((rows, L) + values.shape[1:])
    rank_in = projected_all[:, :R]
    state_in = projected_all[:, R:].astype(f32)
    groups = L // GROUP
    columns = state_in.reshape(rows, groups, GROUP, 2 * N).transpose(0, 1, 3, 2)
    inject = state_in[:, :N].reshape(rows, groups, GROUP * N)
    readout = state_in[:, N:].reshape(rows, groups, GROUP * N)
    begins = by_row(jnp.broadcast_to(jnp.where(place == 0, 1e30, 0.0).astype(bf16), (tokens, channels)))
    step_local = channel_weight[:, select_width:].astype(bf16)
    rates = jnp.exp(channel_vectors[K + 2 : K + 2 + N])
    step_bias = channel_vectors[K + 1 : K + 2]
    skip_gain = channel_vectors[K + 2 + N :]
    scan_in = (by_row(filtered), by_row(rank_in), by_row(joint_chan[1]), by_row(back_chan), begins, columns)
    scan_params = (step_local, step_bias, rates, skip_gain)
    mixed, gate_grad, kept = scan_forward(*scan_in, readout, *scan_params)
    mixed = mixed.reshape(tokens, channels)
    gate_grad = gate_grad.reshape(tokens, channels)

    normed_all = lax.all_gather(normed, "tok", axis=0, tiled=True)
    cotangent_all = lax.all_gather(cotangent, "tok", axis=0, tiled=True)

    def gather_input_part(grad):
        part = jnp.einsum("td,tc->dc", normed_all, grad, preferred_element_type=f32).astype(bf16)
        every = lax.all_gather(part.reshape(tall, side, channels), "tok", axis=0)
        every = every.reshape(half, cut, tall, side, channels).transpose(0, 2, 3, 1, 4)
        return every.reshape(half * tall, side, side)

    output_part = jnp.einsum("tc,td->cd", mixed, cotangent_all, preferred_element_type=f32).astype(bf16)
    output_every = lax.all_gather(
        output_part.reshape(channels, tall, side).transpose(1, 0, 2), "tok", axis=0
    )
    output_every = (
        output_every.reshape(half, cut, tall, channels, side)
        .transpose(0, 2, 1, 3, 4)
        .reshape(half * tall, side, side)
    )
    gate_every = gather_input_part(gate_grad)

    mixed_tokens = to_tokens(mixed)
    layer_out = tile_product(mixed_tokens, pool_all, output_spot.T, False, bf16, True, layer_in)

    draw, filter_mix, inject_grad, read_grad, rate_sum, skip_grad, bias_grad = scan_backward(
        *scan_in, inject, *scan_params, kept
    )
    draw = draw.reshape(tokens, channels)
    step_grad = jnp.einsum("tc,tr->cr", draw, rank_in, preferred_element_type=f32)
    partial_sums = jnp.concatenate(
        [
            jnp.einsum("tc,cr->tr", draw, step_local, preferred_element_type=f32),
            inject_grad.reshape(tokens, N),
            read_grad.reshape(tokens, N),
        ],
        axis=1,
    )
    projected_grad = lax.psum_scatter(partial_sums, "tok", scatter_dimension=0, tiled=True).astype(bf16)
    projected_grad_all = lax.all_gather(projected_grad, "tok", axis=0, tiled=True)
    select_local = channel_weight[:, :select_width].astype(bf16)
    back_filter = jnp.einsum(
        "tf,cf->tc", projected_grad_all, select_local, preferred_element_type=f32
    ).astype(bf16)
    select_grad = jnp.einsum("tc,tf->cf", filtered, projected_grad_all, preferred_element_type=f32)
    pre = conv_pre(xs, taps, offset, place)
    gate = jax.nn.sigmoid(pre)
    dpre = (filter_mix.reshape(tokens, channels) + back_filter.astype(f32)) * (gate * (1.0 + pre * (1.0 - gate)))
    offset_grad = jnp.sum(dpre, axis=0)
    taps_grad = [jnp.sum(dpre * xs, axis=0)]
    xs_grad = taps[K - 1][None] * dpre
    for lag in range(1, K):
        masked = jnp.where(place >= lag, dpre, 0.0)
        xs_grad = xs_grad + taps[K - 1 - lag][None] * sooner(masked, lag)
        taps_grad.insert(0, jnp.sum(masked * later(xs, lag), axis=0))
    xs_grad = xs_grad.astype(bf16)
    xs_every = gather_input_part(xs_grad)

    joint_grad = to_tokens(jnp.stack([xs_grad, gate_grad])).reshape(wide, tok_rows, side)
    normed_grad = tile_product(joint_grad, pool_all, input_spot, True, f32, True)
    scaled = normed_grad * gain_float
    input_grad = (
        cotangent.astype(f32)
        + inverse * scaled
        - input_float * inverse**3 * jnp.mean(scaled * input_float, axis=1, keepdims=True)
    )
    gain_part = jnp.sum(normed_grad * input_float * inverse, axis=0).reshape(devices, gain_here)
    gain_grad = jnp.sum(lax.all_to_all(gain_part, "tok", split_axis=0, concat_axis=0, tiled=True), axis=0)

    slot_tile = jnp.zeros((tile_total,), jnp.int32).at[tile_slot].set(jnp.arange(tile_total, dtype=jnp.int32))
    own = lax.dynamic_slice(slot_tile, (me * tiles_here,), (tiles_here,))
    tile_row, tile_column = own // wide, own % wide
    kind = jnp.where(own >= input_tiles, 2, jnp.where(tile_column >= half, 1, 0))
    index = jnp.where(own >= input_tiles, own - input_tiles, tile_column % half * tall + tile_row)
    first_next, second_next, weight_next, lstat_next, rstat_next, turned, gram = soap_tiles(
        kind,
        index,
        (xs_every, gate_every, output_every),
        pool_weight,
        pool_first,
        pool_second,
        pool_left,
        pool_right,
        pool_left_stat,
        pool_right_stat,
    )
    inverse_low = inverse_factor(gram.reshape(2 * tiles_here, side, side)).reshape(gram.shape)
    left_next, right_next = renew_bases(turned, inverse_low)

    channel_new = soap_step(
        channel_weight[None],
        jnp.concatenate([select_grad, step_grad], axis=1)[None],
        channel_first[None],
        channel_second[None],
        channel_left[None],
        channel_right[None],
        channel_left_stat[None],
        channel_right_stat[None],
    )
    gain_new = adam_step(norm_gain, gain_grad, gain_first, gain_second)
    vector_grad = jnp.concatenate(
        [jnp.stack(taps_grad), offset_grad[None], bias_grad, -rates * rate_sum, skip_grad], axis=0
    )
    vector_new = adam_step(channel_vectors, vector_grad, vector_first, vector_second)
    return (
        layer_out,
        input_grad,
        first_next,
        second_next,
        weight_next,
        left_next,
        right_next,
        lstat_next,
        rstat_next,
        *(value[0] for value in channel_new),
        *gain_new,
        *vector_new,
    )


def solution(mesh):
    line, flat, cube, column = P("tok"), P("tok", None), P("tok", None, None), P(None, "tok")
    in_specs = (flat, flat, P(), P()) + (cube,) * 7 + (flat,) * 7 + (line,) * 3 + (column,) * 3
    out_specs = (flat, flat) + (cube,) * 7 + (flat,) * 7 + (line,) * 3 + (column,) * 3
    return jax.shard_map(shards, mesh=mesh, in_specs=in_specs, out_specs=out_specs, check_vma=False)
```

```python
import functools

import jax
import jax.numpy as jnp
from jax import lax
from jax.experimental import pallas as pl
from jax.experimental.pallas import tpu as pltpu
from jax.sharding import PartitionSpec as P

N = 16
R = 128
K = 4
L = 2048
STEP = 5
GROUP = 16
LOG2E = 1.4426950408889634

beta_first = 0.5
beta_second = 0.5
stat_decay = 0.5
learn_rate = 0.02
vector_rate = 0.2
weight_decay = 0.01
adam_epsilon = 1e-08
norm_epsilon = 1e-05
highest = lax.Precision.HIGHEST


def dot_nt(left, right):
    return lax.dot_general(left, right, (((1,), (1,)), ((), ())), preferred_element_type=jnp.float32)

def dot_nn(left, right):
    return jnp.dot(left, right, preferred_element_type=jnp.float32)

def softplus(v):
    return jnp.maximum(v, 0.0) + jnp.log1p(jnp.exp(-jnp.abs(v)))

def split2(v):
    high = v.astype(jnp.bfloat16)
    return high, (v - high.astype(jnp.float32)).astype(jnp.bfloat16)

def own_token(dtype):
    token = lax.broadcasted_iota(jnp.int32, (GROUP, GROUP * N), 0)
    column = lax.broadcasted_iota(jnp.int32, (GROUP, GROUP * N), 1)
    return (column // N == token).astype(dtype)

def fwd_kernel(pair, chunk, f_ref, rank_ref, z_ref, gm_ref, start_ref, cols_ref, read_ref,
               stepw_ref, bias_ref, rate_ref, skip_ref,
               mixed_ref, dz_ref, keep_ref, state, step_s, drive_s, scan_s):
    groups = chunk // GROUP
    neg = rate_ref[...] * (-LOG2E)
    mine = own_token(jnp.float32)

    @pl.when(pl.program_id(1) == 0)
    def _():
        state[...] = jnp.zeros_like(state)

    for r in range(pair):
        raw = dot_nt(rank_ref[r], stepw_ref[...])
        step = softplus(raw + bias_ref[...])
        step_s[r] = step + start_ref[r].astype(jnp.float32)
        drive_s[r] = step * f_ref[r].astype(jnp.float32)
        keep_ref[r, 0] = state[r]

    def group(g, hidden):
        hidden = list(hidden)
        held = [[] for _ in range(pair)]
        base = pl.multiple_of(g * GROUP, GROUP)
        cols = [cols_ref[r, g] for r in range(pair)]
        for k in range(GROUP):
            for r in range(pair):
                factor = jnp.exp2(step_s[r, pl.ds(base + k, 1), :] * neg)
                hidden[r] = factor * hidden[r] + drive_s[r, pl.ds(base + k, 1), :] * cols[r][:N, k : k + 1]
                held[r].append(hidden[r].astype(jnp.bfloat16))
        for r in range(pair):
            states = jnp.concatenate(held[r], axis=0)
            scan_s[r, pl.ds(base, GROUP), :] = dot_nn((mine * read_ref[r, pl.ds(g, 1), :]).astype(jnp.bfloat16), states)
        return tuple(hidden)

    hidden = lax.fori_loop(0, groups, group, tuple(state[r] for r in range(pair)))
    for r in range(pair):
        state[r] = hidden[r]
        f = f_ref[r].astype(jnp.float32)
        z = z_ref[r].astype(jnp.float32)
        gate = 1.0 / (1.0 + jnp.exp(-z))
        summed = scan_s[r] + skip_ref[...] * f
        mixed_ref[r] = (summed * (z * gate)).astype(jnp.bfloat16)
        dz_ref[r] = (gm_ref[r].astype(jnp.float32) * summed * (gate * (1.0 + z * (1.0 - gate)))).astype(jnp.bfloat16)

def bwd_kernel(pair, chunk, f_ref, rank_ref, z_ref, gm_ref, start_ref, cols_ref, inj_ref,
               stepw_ref, bias_ref, rate_ref, skip_ref, keep_ref,
               draw_ref, dfm_ref, dinj_ref, dread_ref, drate_ref, dskip_ref, dbias_ref,
               carry_s, step_s, drive_s, dscan_s, raw_s, delta_s, a_s, ah_s, h_s, s1_s, s2_s):
    groups = chunk // GROUP
    rate = rate_ref[...]
    neg = rate * (-LOG2E)
    mine = own_token(jnp.float32)
    mine_f = mine

    @pl.when(pl.program_id(1) == 0)
    def _():
        carry_s[...] = jnp.zeros_like(carry_s)

    @pl.when((pl.program_id(1) == 0) & (pl.program_id(0) == 0))
    def _():
        drate_ref[...] = jnp.zeros_like(drate_ref)
        dskip_ref[...] = jnp.zeros_like(dskip_ref)
        dbias_ref[...] = jnp.zeros_like(dbias_ref)

    for r in range(pair):
        raw = dot_nt(rank_ref[r], stepw_ref[...]) + bias_ref[...]
        step = softplus(raw)
        raw_s[r] = raw
        delta_s[r] = step
        step_s[r] = step + start_ref[r].astype(jnp.float32)
        f = f_ref[r].astype(jnp.float32)
        drive_s[r] = step * f
        z = z_ref[r].astype(jnp.float32)
        gate = 1.0 / (1.0 + jnp.exp(-z))
        dscan = gm_ref[r].astype(jnp.float32) * (z * gate)
        dscan_s[r] = dscan
        dskip_ref[...] += jnp.sum(dscan * f, axis=0, keepdims=True)

    def forward(g, hidden):
        hidden = list(hidden)
        base = pl.multiple_of(g * GROUP, GROUP)
        cols = [cols_ref[r, g] for r in range(pair)]
        held = [[] for _ in range(pair)]
        for k in range(GROUP):
            for r in range(pair):
                factor = jnp.exp2(step_s[r, pl.ds(base + k, 1), :] * neg)
                kept = factor * hidden[r]
                hidden[r] = kept + drive_s[r, pl.ds(base + k, 1), :] * cols[r][:N, k : k + 1]
                a_s[r, base + k] = factor
                ah_s[r, base + k] = kept
                held[r].append(hidden[r].astype(jnp.bfloat16))
        for r in range(pair):
            h_s[r, g] = jnp.concatenate(held[r], axis=0)
        return tuple(hidden)

    lax.fori_loop(0, groups, forward, tuple(keep_ref[r, 0] for r in range(pair)))

    def backward(i, carried):
        g = groups - 1 - i
        base = pl.multiple_of(g * GROUP, GROUP)
        ag = list(carried[:pair])
        total = carried[pair]
        cols = [cols_ref[r, g] for r in range(pair)]
        gs = [[None] * GROUP for _ in range(pair)]
        qs = [[None] * GROUP for _ in range(pair)]
        for k in reversed(range(GROUP)):
            for r in range(pair):
                grad = dscan_s[r, pl.ds(base + k, 1), :] * cols[r][N:, k : k + 1] + ag[r]
                ag[r] = a_s[r, base + k] * grad
                q = grad * ah_s[r, base + k]
                total = total + delta_s[r, pl.ds(base + k, 1), :] * q
                gs[r][k] = grad.astype(jnp.bfloat16)
                qs[r][k] = (rate * q).astype(jnp.bfloat16)
        for r in range(pair):
            grads = jnp.concatenate(gs[r], axis=0)
            pulls = jnp.concatenate(qs[r], axis=0)
            s1_s[r, pl.ds(base, GROUP), :] = dot_nn((mine * inj_ref[r, pl.ds(g, 1), :]).astype(jnp.bfloat16), grads)
            s2_s[r, pl.ds(base, GROUP), :] = dot_nn(mine.astype(jnp.bfloat16), pulls)
            dh, dl = split2(dscan_s[r, pl.ds(base, GROUP), :])
            uh, ul = split2(drive_s[r, pl.ds(base, GROUP), :])
            dr = dot_nt(jnp.concatenate([dh, dl], axis=0), h_s[r, g])
            dread_ref[r, pl.ds(g, 1), :] = jnp.sum((dr[:GROUP] + dr[GROUP:]) * mine_f, axis=0, keepdims=True)
            di = dot_nt(jnp.concatenate([uh, ul], axis=0), grads)
            dinj_ref[r, pl.ds(g, 1), :] = jnp.sum((di[:GROUP] + di[GROUP:]) * mine_f, axis=0, keepdims=True)
        return tuple(ag) + (total,)

    out = lax.fori_loop(0, groups, backward, tuple(carry_s[r] for r in range(pair)) + (jnp.zeros_like(rate),))
    drate_ref[...] += out[pair]
    for r in range(pair):
        carry_s[r] = out[r]
        f = f_ref[r].astype(jnp.float32)
        draw = (f * s1_s[r] - s2_s[r]) / (1.0 + jnp.exp(-raw_s[r]))
        draw_ref[r] = draw.astype(jnp.bfloat16)
        dbias_ref[...] += jnp.sum(draw, axis=0, keepdims=True)
        dfm_ref[r] = delta_s[r] * s1_s[r] + skip_ref[...] * dscan_s[r]

def specs(pair, chunk, ch, rank, back, chunks):
    def at(i, j):
        return (i, chunks - 1 - j if back else j)
    tok = pl.BlockSpec((pair, chunk, ch), lambda i, j: at(i, j) + (0,))
    rk = pl.BlockSpec((pair, chunk, rank), lambda i, j: at(i, j) + (0,))
    cols = pl.BlockSpec((pair, chunk // GROUP, 2 * N, GROUP), lambda i, j: at(i, j) + (0, 0))
    flat = pl.BlockSpec((pair, chunk // GROUP, GROUP * N), lambda i, j: at(i, j) + (0,))
    keep = pl.BlockSpec((pair, 1, N, ch), lambda i, j: at(i, j) + (0, 0))
    def whole(a):
        return pl.BlockSpec(a.shape, lambda i, j: (0,) * a.ndim)
    return tok, rk, cols, flat, keep, whole

def scan_forward(f, rank, z, gm, start, cols, read, stepw, bias, rate, skip, chunk=128):
    rows, length, ch = f.shape
    pair = 2 if rows % 2 == 0 else 1
    chunks = length // chunk
    tok, rk, colb, flat, keep, whole = specs(pair, chunk, ch, rank.shape[2], False, chunks)
    return pl.pallas_call(
        functools.partial(fwd_kernel, pair, chunk),
        grid=(rows // pair, chunks),
        in_specs=[tok, rk, tok, tok, tok, colb, flat, whole(stepw), whole(bias), whole(rate), whole(skip)],
        out_specs=[tok, tok, keep],
        out_shape=[jax.ShapeDtypeStruct(f.shape, jnp.bfloat16), jax.ShapeDtypeStruct(f.shape, jnp.bfloat16),
                   jax.ShapeDtypeStruct((rows, chunks, N, ch), jnp.float32)],
        scratch_shapes=[pltpu.VMEM((pair, N, ch), jnp.float32)] + [pltpu.VMEM((pair, chunk, ch), jnp.float32)] * 3,
        compiler_params=pltpu.CompilerParams(vmem_limit_bytes=40 * 2**20),
        cost_estimate=pl.CostEstimate(flops=4 * 10**10, bytes_accessed=8 * 10**6, transcendentals=0),
    )(f, rank, z, gm, start, cols, read, stepw, bias, rate, skip)

def scan_backward(f, rank, z, gm, start, cols, inj, stepw, bias, rate, skip, kept, chunk=128):
    rows, length, ch = f.shape
    pair = 2 if rows % 2 == 0 else 1
    chunks = length // chunk
    tok, rk, colb, flat, keep, whole = specs(pair, chunk, ch, rank.shape[2], True, chunks)
    f32 = jnp.float32
    row = jax.ShapeDtypeStruct((1, ch), f32)
    return pl.pallas_call(
        functools.partial(bwd_kernel, pair, chunk),
        grid=(rows // pair, chunks),
        in_specs=[tok, rk, tok, tok, tok, colb, flat, whole(stepw), whole(bias), whole(rate), whole(skip), keep],
        out_specs=[tok, tok, flat, flat, whole(rate), whole(row), whole(row)],
        out_shape=[jax.ShapeDtypeStruct(f.shape, jnp.bfloat16), jax.ShapeDtypeStruct(f.shape, f32),
                   jax.ShapeDtypeStruct(inj.shape, f32), jax.ShapeDtypeStruct(inj.shape, f32),
                   jax.ShapeDtypeStruct(rate.shape, f32), row, row],
        scratch_shapes=[pltpu.VMEM((pair, N, ch), f32)] + [pltpu.VMEM((pair, chunk, ch), f32)] * 5
        + [pltpu.VMEM((pair, chunk, N, ch), f32)] * 2 + [pltpu.VMEM((pair, chunk // GROUP, GROUP * N, ch), jnp.bfloat16)]
        + [pltpu.VMEM((pair, chunk, ch), f32)] * 2,
        compiler_params=pltpu.CompilerParams(vmem_limit_bytes=40 * 2**20),
        cost_estimate=pl.CostEstimate(flops=7 * 10**10, bytes_accessed=8 * 10**6, transcendentals=0),
    )(f, rank, z, gm, start, cols, inj, stepw, bias, rate, skip, kept)


def chol_kernel(batch, order, gram_ref, out_ref, low_ref, inv_ref, piv_ref):
    tiles = order // 8
    rows8 = lax.broadcasted_iota(jnp.int32, (8, batch), 0)

    def load_slab(j, carry):
        low_ref[j, pl.ds(0, order), :] = gram_ref[pl.ds(j, batch, stride=order), :].T
        inv_ref[j] = jnp.zeros(inv_ref.shape[1:], jnp.float32)
        return carry

    lax.fori_loop(0, order, load_slab, 0, unroll=8)

    def bcast(ref, j, row):
        return jnp.broadcast_to(ref[j, pl.ds(row, 1), :], (8, batch))

    def block_column(block, carry):
        base = pl.multiple_of(block * 8, 8)

        def updated(tile_rows, seed):
            def one(j, accs):
                mult = [bcast(low_ref, j, base + k) for k in range(8)]
                out = []
                for s, rows in enumerate(tile_rows):
                    piece = low_ref[j, pl.ds(rows, 8), :]
                    out.extend(accs[s * 8 + k] - piece * mult[k] for k in range(8))
                return tuple(out)

            def eight(step, accs):
                for u in range(8):
                    accs = one(step * 8 + u, accs)
                return accs

            return list(lax.fori_loop(0, block, eight, tuple(seed)))

        accs = updated([base], [low_ref[base + k, pl.ds(base, 8), :] for k in range(8)])
        scales = []
        for k in range(8):
            scale = lax.rsqrt(jnp.broadcast_to(accs[k][k : k + 1, :], (8, batch)))
            scales.append(scale)
            accs[k] = jnp.where(rows8 >= k, accs[k] * scale, 0.0)
            for later in range(k + 1, 8):
                accs[later] = accs[later] - accs[k] * jnp.broadcast_to(
                    accs[k][later : later + 1, :], (8, batch)
                )
        for k in range(8):
            low_ref[base + k, pl.ds(base, 8), :] = accs[k]
            piv_ref[base + k] = scales[k]

        def pair(p, carry):
            first = pl.multiple_of(base + 8 + p * 16, 8)
            both = [first, pl.multiple_of(first + 8, 8)]
            accs = updated(
                both, [low_ref[base + k, pl.ds(rows, 8), :] for rows in both for k in range(8)]
            )
            for k in range(8):
                scale = piv_ref[base + k]
                for s in range(2):
                    accs[s * 8 + k] = accs[s * 8 + k] * scale
                for later in range(k + 1, 8):
                    mult = bcast(low_ref, base + k, base + later)
                    for s in range(2):
                        accs[s * 8 + later] = accs[s * 8 + later] - accs[s * 8 + k] * mult
            for s, rows in enumerate(both):
                for k in range(8):
                    low_ref[base + k, pl.ds(rows, 8), :] = accs[s * 8 + k]
            return carry

        lax.fori_loop(0, (tiles - block) // 2, pair, 0)
        return carry

    lax.fori_loop(0, tiles, block_column, 0)

    def block_row(block, carry):
        base = pl.multiple_of(block * 8, 8)

        def finish(accs, both):
            for k in range(8):
                scale = piv_ref[base + k]
                for s in range(len(both)):
                    accs[s * 8 + k] = accs[s * 8 + k] * scale
                for later in range(k + 1, 8):
                    mult = bcast(low_ref, base + k, base + later)
                    for s in range(len(both)):
                        accs[s * 8 + later] = accs[s * 8 + later] - accs[s * 8 + k] * mult
            for s, columns in enumerate(both):
                for k in range(8):
                    inv_ref[base + k, pl.ds(columns, 8), :] = accs[s * 8 + k]

        def pair(p, carry):
            first = pl.multiple_of(p * 16, 8)
            both = [first, pl.multiple_of(first + 8, 8)]

            def eight(step, accs):
                for u in range(8):
                    j = step * 8 + u
                    mult = [bcast(low_ref, j, base + k) for k in range(8)]
                    out = []
                    for s, columns in enumerate(both):
                        piece = inv_ref[j, pl.ds(columns, 8), :]
                        out.extend(accs[s * 8 + k] - piece * mult[k] for k in range(8))
                    accs = tuple(out)
                return accs

            accs = list(lax.fori_loop(
                p * 2, block, eight, (jnp.zeros((8, batch), jnp.float32),) * 16
            ))
            finish(accs, both)
            return carry

        lax.fori_loop(0, (block + 1) // 2, pair, 0)
        odd = block % 2

        def diagonal():
            accs = [jnp.where(rows8 == k, 1.0, 0.0) for k in range(8)]
            finish(accs, [base])

        diagonal()
        return carry

    lax.fori_loop(0, tiles, block_row, 0)

    def store_slab(i, carry):
        out_ref[pl.ds(i, batch, stride=order), :] = inv_ref[i, pl.ds(0, order), :].T
        return carry

    lax.fori_loop(0, order, store_slab, 0, unroll=8)

def inverse_factor(gram):
    batch, order, _ = gram.shape
    out = pl.pallas_call(
        functools.partial(chol_kernel, batch, order),
        out_shape=jax.ShapeDtypeStruct((batch * order, order), jnp.float32),
        in_specs=[pl.BlockSpec(memory_space=pltpu.VMEM)],
        out_specs=pl.BlockSpec(memory_space=pltpu.VMEM),
        scratch_shapes=[
            pltpu.VMEM((order, order + 8, batch), jnp.float32),
            pltpu.VMEM((order, order + 8, batch), jnp.float32),
            pltpu.VMEM((order, 8, batch), jnp.float32),
        ],
        compiler_params=pltpu.CompilerParams(vmem_limit_bytes=56 * 2**20),
        cost_estimate=pl.CostEstimate(flops=5 * 10**10, bytes_accessed=12 * 10**6, transcendentals=0),
    )(gram.reshape(batch * order, order))
    return out.reshape(batch, order, order)


DEPTH = 4
BATCH = 16


def tile_product_kernel(pairs, steps, transposed, residual, idx_ref, left_ref, pool_ref, *refs):
    if residual:
        res_ref, refs = refs[0], refs[1:]
    out_ref, slots, sems = refs
    side = slots.shape[2]
    total_steps = pairs * steps

    def fetch(step):
        for u in range(BATCH):
            pltpu.make_async_copy(
                pool_ref.at[idx_ref[step * BATCH + u]], slots.at[step % DEPTH, u], sems.at[step % DEPTH]
            ).start()

    for step in range(min(DEPTH - 1, total_steps)):
        fetch(step)

    def one_pair(o, carry):
        total = jnp.zeros((left_ref.shape[1], 2 * side), jnp.float32)
        for k in range(steps):
            step = o * steps + k

            @pl.when(step + DEPTH - 1 < total_steps)
            def _():
                fetch(step + DEPTH - 1)

            slot = step % DEPTH
            pltpu.make_async_copy(slots.at[slot], slots.at[slot], sems.at[slot]).wait()
            for u in range(0, BATCH, 4):
                at = k * (BATCH // 2) + u // 2
                left = jnp.concatenate([left_ref[at], left_ref[at + 1]], axis=1)
                tile = [slots[slot, u + v] for v in range(4)]
                if transposed:
                    right = jnp.concatenate(
                        [jnp.concatenate([tile[0], tile[2]], axis=1), jnp.concatenate([tile[1], tile[3]], axis=1)], axis=0
                    )
                    total += dot_nt(left, right)
                else:
                    right = jnp.concatenate(
                        [jnp.concatenate([tile[0], tile[1]], axis=1), jnp.concatenate([tile[2], tile[3]], axis=1)], axis=0
                    )
                    total += dot_nn(left, right)
        columns = pl.ds(pl.multiple_of(o * 2 * side, side), 2 * side)
        if residual:
            total += res_ref[:, columns].astype(jnp.float32)
        out_ref[:, columns] = total.astype(out_ref.dtype)
        return carry

    lax.fori_loop(0, pairs, one_pair, 0)


def tile_product(left, pool, index, transposed, dtype, residual=None):
    outs, depth = index.shape
    pairs, steps = outs // 2, 2 * depth // BATCH
    side = pool.shape[1]
    tok = left.shape[1]
    vmem = pl.BlockSpec(memory_space=pltpu.VMEM)
    extra = [residual] if residual is not None else []
    order = index.reshape(pairs, 2, depth).transpose(0, 2, 1).reshape(-1).astype(jnp.int32)
    return pl.pallas_call(
        functools.partial(tile_product_kernel, pairs, steps, transposed, residual is not None),
        in_specs=[pl.BlockSpec(memory_space=pltpu.SMEM), vmem, pl.BlockSpec(memory_space=pl.ANY)] + [vmem] * len(extra),
        out_specs=vmem,
        out_shape=jax.ShapeDtypeStruct((tok, outs * side), dtype),
        scratch_shapes=[pltpu.VMEM((DEPTH, BATCH, side, side), pool.dtype), pltpu.SemaphoreType.DMA((DEPTH,))],
        compiler_params=pltpu.CompilerParams(vmem_limit_bytes=40 * 2**20),
        cost_estimate=pl.CostEstimate(
            flops=2 * outs * depth * tok * side * side, bytes_accessed=outs * depth * side * side * 2, transcendentals=0
        ),
    )(order, left, pool, *extra)


def dot_tn(left, right):
    return lax.dot_general(left, right, (((0,), (0,)), ((), ())), preferred_element_type=jnp.float32)


def three(dot, left, right):
    left_axis, right_axis = {dot_nn: (1, 0), dot_nt: (1, 1), dot_tn: (0, 0)}[dot]
    return dot(
        jnp.concatenate([left[0], left[0], left[1]], axis=left_axis),
        jnp.concatenate([right[0], right[1], right[0]], axis=right_axis),
    )


def soap_kernel(sources, many, kind_ref, idx_ref, *refs):
    grad_refs, refs = refs[: sources * many], refs[sources * many :]
    weight_ref, first_ref, second_ref, left_ref, right_ref, lstat_ref, rstat_ref = refs[:7]
    first_out, second_out, weight_out, lstat_out, rstat_out, turned_out, gram_out = refs[7:]
    side = weight_ref.shape[1]
    diagonal = lax.broadcasted_iota(jnp.int32, (side, side), 0) == lax.broadcasted_iota(jnp.int32, (side, side), 1)
    every = range(many)
    grads, lefts, rights = [], [], []
    for u in every:
        kind = kind_ref[pl.program_id(0) * many + u]
        grad = grad_refs[u * sources][0]
        for which in range(1, sources):
            grad = jnp.where(kind == which, grad_refs[u * sources + which][0], grad)
        grads.append(grad)
        lefts.append(split2(left_ref[u]))
        rights.append(split2(right_ref[u]))
    across = [split2(dot_nn(grads[u], rights[u][0]) + dot_nn(grads[u], rights[u][1])) for u in every]
    turned = [three(dot_tn, lefts[u], across[u]) for u in every]
    products = [(dot_nt(grads[u], grads[u]), dot_tn(grads[u], grads[u])) for u in every]
    directions = []
    for u in every:
        first = beta_first * first_ref[u] + (1.0 - beta_first) * turned[u]
        second = beta_second * second_ref[u] + (1.0 - beta_second) * turned[u] * turned[u]
        first_out[u] = first
        second_out[u] = second
        directions.append(split2(
            first / (1.0 - beta_first**STEP) / (jnp.sqrt(second / (1.0 - beta_second**STEP)) + adam_epsilon)
        ))
    renewed = []
    for u in every:
        for which, (stat_ref, basis_ref, basis2, stat_out) in enumerate(
            ((lstat_ref, left_ref, lefts[u], lstat_out), (rstat_ref, right_ref, rights[u], rstat_out))
        ):
            stat = stat_decay * stat_ref[u] + (1.0 - stat_decay) * products[u][which]
            stat_out[u] = stat
            trace = jnp.sum(jnp.sum(jnp.where(diagonal, stat, 0.0), axis=0, keepdims=True), axis=1, keepdims=True)
            value = three(dot_nn, split2(stat), basis2) + (trace / side) * basis_ref[u]
            turned_out[u, which] = value
            renewed.append(split2(value))
    back = [split2(three(dot_nt, directions[u], rights[u])) for u in every]
    for u in every:
        for which in range(2):
            gram_out[u, which] = three(dot_tn, renewed[u * 2 + which], renewed[u * 2 + which])
    for u in every:
        weight = weight_ref[u]
        weight_out[u] = weight - learn_rate * (three(dot_nn, lefts[u], back[u]) + weight_decay * weight)


def soap_tiles(kind, index, grads, weight, first, second, left, right, lstat, rstat, many=4):
    count, side, _ = weight.shape
    one = pl.BlockSpec((many, side, side), lambda s, kind, idx: (s, 0, 0))
    two = pl.BlockSpec((many, 2, side, side), lambda s, kind, idx: (s, 0, 0, 0))

    def picked(u, which):
        def at(s, kind, idx):
            return (jnp.where(kind[s * many + u] == which, idx[s * many + u], 0), 0, 0)

        return pl.BlockSpec((1, side, side), at)

    tile = jax.ShapeDtypeStruct(weight.shape, jnp.float32)
    pairs = jax.ShapeDtypeStruct((count, 2, side, side), jnp.float32)
    sources = len(grads)
    return pl.pallas_call(
        functools.partial(soap_kernel, sources, many),
        grid_spec=pltpu.PrefetchScalarGridSpec(
            num_scalar_prefetch=2,
            grid=(count // many,),
            in_specs=[picked(u, which) for u in range(many) for which in range(sources)] + [one] * 7,
            out_specs=[one] * 5 + [two] * 2,
        ),
        out_shape=[tile] * 5 + [pairs] * 2,
        compiler_params=pltpu.CompilerParams(vmem_limit_bytes=40 * 2**20),
        cost_estimate=pl.CostEstimate(flops=count * 60 * side**3, bytes_accessed=count * 18 * 4 * side**2, transcendentals=0),
    )(kind, index, *(list(grads) * many), weight, first, second, left, right, lstat, rstat)


def renew_kernel(many, turned_ref, inv_ref, left_out, right_out):
    for u in range(many):
        for which, out in ((0, left_out), (1, right_out)):
            out[u] = three(dot_nt, split2(turned_ref[u, which]), split2(inv_ref[u, which]))


def renew_bases(turned, inverse, many=6):
    count, _, side, _ = turned.shape
    one = pl.BlockSpec((many, side, side), lambda s: (s, 0, 0))
    two = pl.BlockSpec((many, 2, side, side), lambda s: (s, 0, 0, 0))
    tile = jax.ShapeDtypeStruct((count, side, side), jnp.float32)
    return pl.pallas_call(
        functools.partial(renew_kernel, many),
        grid=(count // many,),
        in_specs=[two, two],
        out_specs=[one, one],
        out_shape=[tile, tile],
        compiler_params=pltpu.CompilerParams(vmem_limit_bytes=40 * 2**20),
    )(turned, inverse)


def norm_joint_kernel(channels, x_ref, gain_ref, weight_ref, normed_ref, xs_ref, gate_ref):
    x = x_ref[...].astype(jnp.float32)
    inverse = lax.rsqrt(jnp.mean(x * x, axis=1, keepdims=True) + norm_epsilon)
    normed = (x * inverse * gain_ref[...]).astype(jnp.bfloat16)
    normed_ref[...] = normed
    joint = dot_nn(normed, weight_ref[...]).astype(jnp.bfloat16)
    xs_ref[...] = joint[:, :channels]
    gate_ref[...] = joint[:, channels:]


def norm_joint(x, gain, weight, block=256):
    tokens, width = x.shape
    channels = weight.shape[1] // 2
    wide = pl.BlockSpec((block, width), lambda i: (i, 0))
    thin = pl.BlockSpec((block, channels), lambda i: (i, 0))
    half = jax.ShapeDtypeStruct((tokens, channels), jnp.bfloat16)
    return pl.pallas_call(
        functools.partial(norm_joint_kernel, channels),
        grid=(tokens // block,),
        in_specs=[
            wide,
            pl.BlockSpec((1, width), lambda i: (0, 0)),
            pl.BlockSpec((width, 2 * channels), lambda i: (0, 0)),
        ],
        out_specs=[wide, thin, thin],
        out_shape=[jax.ShapeDtypeStruct(x.shape, jnp.bfloat16), half, half],
        compiler_params=pltpu.CompilerParams(vmem_limit_bytes=32 * 2**20),
        cost_estimate=pl.CostEstimate(
            flops=4 * tokens * width * channels, bytes_accessed=4 * tokens * width, transcendentals=0
        ),
    )(x, gain, weight)


def plain_three(dot, left, right):
    return dot(left[0], right[0]) + (dot(left[0], right[1]) + dot(left[1], right[0]))


def channel_kernel(weight_ref, grad_ref, first_ref, second_ref, left_ref, right_ref, lstat_ref, rstat_ref,
                   first_out, second_out, weight_out, lstat_out, rstat_out, lturn_out, rturn_out, lgram_out, rgram_out):
    grad = split2(grad_ref[...])
    left, right = split2(left_ref[...]), split2(right_ref[...])
    turned = plain_three(dot_tn, left, split2(plain_three(dot_nn, grad, right)))
    first = beta_first * first_ref[...] + (1.0 - beta_first) * turned
    second = beta_second * second_ref[...] + (1.0 - beta_second) * turned * turned
    first_out[...] = first
    second_out[...] = second
    direction = split2(
        first / (1.0 - beta_first**STEP) / (jnp.sqrt(second / (1.0 - beta_second**STEP)) + adam_epsilon)
    )
    returned = plain_three(dot_nn, left, split2(plain_three(dot_nt, direction, right)))
    weight = weight_ref[...]
    weight_out[...] = weight - learn_rate * (returned + weight_decay * weight)
    for basis_ref, basis, stat_ref, product, stat_out, turn_out, gram_out in (
        (left_ref, left, lstat_ref, plain_three(dot_nt, grad, grad), lstat_out, lturn_out, lgram_out),
        (right_ref, right, rstat_ref, plain_three(dot_tn, grad, grad), rstat_out, rturn_out, rgram_out),
    ):
        order = basis_ref.shape[0]
        diagonal = lax.broadcasted_iota(jnp.int32, (order, order), 0) == lax.broadcasted_iota(
            jnp.int32, (order, order), 1
        )
        stat = stat_decay * stat_ref[...] + (1.0 - stat_decay) * product
        stat_out[...] = stat
        trace = jnp.sum(jnp.sum(jnp.where(diagonal, stat, 0.0), axis=0, keepdims=True), axis=1, keepdims=True)
        value = plain_three(dot_nn, split2(stat), basis) + (trace / order) * basis_ref[...]
        turn_out[...] = value
        value = split2(value)
        gram_out[...] = plain_three(dot_tn, value, value)


def channel_moments(weight, grad, first, second, left, right, lstat, rstat):
    f32 = jnp.float32
    rows = jax.ShapeDtypeStruct(weight.shape, f32)
    small = jax.ShapeDtypeStruct(left.shape, f32)
    large = jax.ShapeDtypeStruct(right.shape, f32)
    return pl.pallas_call(
        channel_kernel,
        out_shape=[rows] * 3 + [small, large] * 3,
        compiler_params=pltpu.CompilerParams(vmem_limit_bytes=40 * 2**20),
        cost_estimate=pl.CostEstimate(flops=8 * 10**9, bytes_accessed=6 * 10**6, transcendentals=0),
    )(weight, grad, first, second, left, right, lstat, rstat)


PANEL = 32


def factor_inverse(block):
    order = block.shape[0]
    rows = lax.broadcasted_iota(jnp.int32, (order, 2 * order), 0)
    columns = lax.broadcasted_iota(jnp.int32, (order, 2 * order), 1)
    both = jnp.concatenate([block, jnp.zeros_like(block)], axis=1) + jnp.where(columns == rows + order, 1.0, 0.0)
    for k in range(order):
        scale = lax.rsqrt(both[k : k + 1, k : k + 1])
        row = both[k : k + 1, :] * scale
        column = both[:, k : k + 1] * scale
        both = jnp.where(rows == k, row, jnp.where(rows > k, both - column * row, both))
    return both[:, order:]


def solve_kernel(count, *refs):
    grams, sides, outs = refs[:count], refs[count : 2 * count], refs[2 * count : 3 * count]
    works = refs[3 * count :]
    for i in range(count):
        order = grams[i].shape[0]
        gram, side = works[2 * i], works[2 * i + 1]
        gram[...] = grams[i][...]
        side[...] = sides[i][...]
        for start in range(0, order, PANEL):
            stop = start + PANEL
            low = split2(factor_inverse(gram[start:stop, start:stop]))
            upper = split2(plain_three(dot_nn, low, split2(gram[start:stop, :])))
            solved = plain_three(dot_nn, low, split2(side[start:stop, :]))
            outs[i][start:stop, :] = solved
            if stop < order:
                gram[stop:, :] -= plain_three(dot_tn, upper, upper)[stop:]
                side[stop:, :] -= plain_three(dot_tn, upper, split2(solved))[stop:]


def solve_factors(grams, sides):
    count = len(grams)
    shapes = [jax.ShapeDtypeStruct(s.shape, jnp.float32) for s in sides]
    scratch = []
    for g, s in zip(grams, sides):
        scratch += [pltpu.VMEM(g.shape, jnp.float32), pltpu.VMEM(s.shape, jnp.float32)]
    return pl.pallas_call(
        functools.partial(solve_kernel, count),
        out_shape=shapes,
        scratch_shapes=scratch,
        compiler_params=pltpu.CompilerParams(vmem_limit_bytes=40 * 2**20),
        cost_estimate=pl.CostEstimate(flops=4 * 10**10, bytes_accessed=3 * 10**6, transcendentals=0),
    )(*grams, *sides)


def doc_positions(doc_lengths):
    starts = jnp.cumsum(doc_lengths, axis=1) - doc_lengths
    places = jnp.arange(L, dtype=jnp.int32)
    begun = jnp.where(starts[:, None, :] <= places[None, :, None], starts[:, None, :], 0)
    return places[None, :] - jnp.max(begun, axis=2)


def adam_step(weight, gradient, first, second):
    first_new = beta_first * first + (1.0 - beta_first) * gradient
    second_new = beta_second * second + (1.0 - beta_second) * gradient * gradient
    direction = (
        first_new
        / (1.0 - beta_first**STEP)
        / (jnp.sqrt(second_new / (1.0 - beta_second**STEP)) + adam_epsilon)
    )
    return (first_new, second_new, weight - vector_rate * (direction + weight_decay * weight))


def later(values, lag):
    return jnp.pad(values, ((lag, 0), (0, 0)))[: values.shape[0]]


def sooner(values, lag):
    return jnp.pad(values, ((0, lag), (0, 0)))[lag:]


def conv_pre(xs, taps, offset, place):
    total = offset[None] + taps[K - 1][None] * xs
    for lag in range(1, K):
        total = total + jnp.where(place >= lag, taps[K - 1 - lag][None] * later(xs, lag), 0.0)
    return total


def rank_within(key):
    count = key.shape[0]
    earlier = jnp.arange(count)[None, :] < jnp.arange(count)[:, None]
    return jnp.sum(((key[None, :] == key[:, None]) & earlier).astype(jnp.int32), axis=1)


def table(size, target, chosen, value):
    hit = (target[None, :] == jnp.arange(size)[:, None]) & chosen[None, :]
    return jnp.sum(jnp.where(hit, value[None, :], 0), axis=1)


LINES = 4
CAP_LINE = {3: 26, 2: 22, 1: 15}
CAP_PLANE = {3: 18, 2: 15, 1: 11}


class Routes:
    def __init__(self, tile_slot, devices, tiles_here, tall, half):
        count = tile_slot.shape[0]
        self.plane = devices // LINES
        self.tiles_here = tiles_here
        wide = 2 * half
        tile = jnp.arange(count, dtype=jnp.int32)
        output = tile >= tall * wide
        relative = tile - tall * wide
        column = tile % wide
        self.slot = tile_slot
        source = tile_slot // tiles_here
        self.source = source
        self.source_line, self.source_plane = source // self.plane, source % self.plane
        self.target = jnp.where(output, relative // tall, column % half)
        self.target_line, self.target_plane = self.target // self.plane, self.target % self.plane
        self.kind = jnp.where(output, 2, column // half)
        self.place = jnp.where(output, 2 * tall + relative % tall, column // half * tall + tile // wide)
        line_key = source * LINES + self.target_line
        plane_key = (self.target_line * self.plane + self.source_plane) * self.plane + self.target_plane
        self.ranks = {}
        fits = True
        late = self.kind == 0
        for name, group, large, small in (("all", jnp.zeros_like(source), 3, 3), ("xs", late.astype(jnp.int32), 2, 1)):
            ranks = []
            for key, caps in ((line_key, CAP_LINE), (plane_key, CAP_PLANE)):
                rank = rank_within(key * 2 + group)
                fits = fits & jnp.all(rank < jnp.where(late, caps[small], caps[large]))
                ranks.append(rank)
            self.ranks[name] = ranks
        self.fits = fits


def routed(values, groups, index):
    members, cap = index.shape
    packed = jnp.take(values, index.reshape(-1), axis=0)
    return lax.all_to_all(packed, "tok", split_axis=0, concat_axis=0, tiled=True, axis_index_groups=groups)


def device_groups(devices):
    plane = devices // LINES
    lines = [[z * plane + p for z in range(LINES)] for p in range(plane)]
    planes = [[z * plane + p for p in range(plane)] for z in range(LINES)]
    return lines, planes


def spread(value, devices):
    lines, planes = device_groups(devices)
    plane = devices // LINES
    step = lax.all_to_all(
        jnp.broadcast_to(value, (LINES,) + value.shape), "tok", 0, 0, tiled=True, axis_index_groups=lines
    )
    step = lax.all_to_all(
        jnp.broadcast_to(step, (plane,) + step.shape), "tok", 0, 0, tiled=True, axis_index_groups=planes
    )
    return jnp.swapaxes(step, 0, 1).reshape((devices * value.shape[0],) + value.shape[1:])


def fold(values, devices):
    lines, planes = device_groups(devices)
    plane = devices // LINES
    rows = values.shape[0] // devices
    parts = jnp.swapaxes(values.reshape((LINES, plane, rows) + values.shape[1:]), 0, 1).astype(jnp.bfloat16)
    parts = lax.all_to_all(parts, "tok", 0, 0, tiled=True, axis_index_groups=planes)
    parts = jnp.sum(parts.astype(jnp.float32), axis=0)
    parts = lax.all_to_all(parts, "tok", 0, 0, tiled=True, axis_index_groups=lines)
    return jnp.sum(parts, axis=0)


def core(
    routes,
    fast,
    layer_in,
    cotangent,
    doc_lengths,
    tile_slot,
    pool_weight,
    pool_first,
    pool_second,
    pool_left,
    pool_right,
    pool_left_stat,
    pool_right_stat,
    channel_weight,
    channel_first,
    channel_second,
    channel_left,
    channel_right,
    channel_left_stat,
    channel_right_stat,
    norm_gain,
    gain_first,
    gain_second,
    channel_vectors,
    vector_first,
    vector_second,
):
    bf16, f32 = jnp.bfloat16, jnp.float32
    devices = lax.axis_size("tok")
    me = lax.axis_index("tok")
    lines, planes = device_groups(devices)
    plane = devices // LINES
    my_line, my_plane = me // plane, me % plane
    tok_rows, model_width = layer_in.shape
    tokens = tok_rows * devices
    rows = tokens // L
    channels = channel_vectors.shape[1]
    inner_width = channels * devices
    tiles_here, side, _ = pool_weight.shape
    tall = model_width // side
    half = inner_width // side
    wide = 2 * half
    cut = side // channels
    input_tiles = tall * wide
    select_width = channel_weight.shape[1] - R
    select_here = channels * select_width
    gain_here = norm_gain.shape[0]

    x_all = lax.all_gather(layer_in, "tok", axis=0, tiled=True)
    small = spread(
        jnp.concatenate([channel_weight[:, :select_width].reshape(-1), norm_gain]).astype(bf16)[None], devices
    )
    select_weight = small[:, :select_here].reshape(inner_width, select_width)
    gain_float = small[:, select_here:].reshape(1, model_width).astype(f32)
    pool_low = pool_weight.astype(bf16)
    slot_here = lambda target: target - me * tiles_here

    def forward_tiles():
        line_rank, plane_rank = routes.ranks["all"]
        cap_line, cap_plane = CAP_LINE[3], CAP_PLANE[3]
        index = table(
            LINES * cap_line, routes.target_line * cap_line + line_rank, routes.source == me,
            routes.slot - me * tiles_here,
        )
        middle = routed(pool_low, lines, index.reshape(LINES, cap_line))
        here = (routes.target_line == my_line) & (routes.source_plane == my_plane)
        index = table(
            plane * cap_plane, routes.target_plane * cap_plane + plane_rank, here,
            routes.source_line * cap_line + line_rank,
        )
        last = routed(middle, planes, index.reshape(plane, cap_plane))
        index = table(
            3 * tall, routes.place, routes.target == me, routes.source_plane * cap_plane + plane_rank
        )
        return jnp.take(last, index, axis=0)

    def backward_tiles(name, chosen, first, tiles):
        size = 2 if tiles.shape[0] > tall else 1
        line_rank, plane_rank = routes.ranks[name]
        cap_line, cap_plane = CAP_LINE[size], CAP_PLANE[size]
        index = table(
            plane * cap_plane, routes.source_plane * cap_plane + plane_rank, chosen & (routes.target == me),
            routes.place - first,
        )
        middle = routed(tiles, planes, index.reshape(plane, cap_plane))
        here = chosen & (routes.target_line == my_line) & (routes.source_plane == my_plane)
        index = table(
            LINES * cap_line, routes.source_line * cap_line + line_rank, here,
            routes.target_plane * cap_plane + plane_rank,
        )
        return routed(middle, lines, index.reshape(LINES, cap_line))

    is_out, is_xs = routes.kind == 2, routes.kind == 0
    if fast:
        tiles_own = forward_tiles()
        input_own, output_own = tiles_own[: 2 * tall], tiles_own[2 * tall :]
    else:
        pool_all = lax.all_gather(pool_low, "tok", axis=0, tiled=True)
        columns = me // cut
        input_slots = tile_slot[:input_tiles].reshape(tall, 2, half)
        input_own = jnp.take(
            pool_all, lax.dynamic_index_in_dim(input_slots, columns, 2, False).T.reshape(-1), axis=0
        )
        output_slots = tile_slot[input_tiles:].reshape(half, tall)
        output_own = jnp.take(pool_all, lax.dynamic_index_in_dim(output_slots, columns, 0, False), axis=0)
    offset = me % cut * channels
    input_local = input_own.reshape(2, tall, side, side)
    output_local = output_own
    if cut > 1:
        input_local = lax.dynamic_slice_in_dim(input_local, offset, channels, axis=3)
        output_local = lax.dynamic_slice_in_dim(output_local, offset, channels, axis=1)
    input_local = input_local.transpose(1, 2, 0, 3).reshape(model_width, 2 * channels)
    output_local = output_local.transpose(1, 0, 2).reshape(channels, model_width)

    cotangent_later, input_local = lax.optimization_barrier((cotangent, input_local))
    normed_all, xs_low, gates = norm_joint(x_all, gain_float, input_local)
    cotangent_all = lax.all_gather(cotangent_later, "tok", axis=0, tiled=True)

    def to_tokens(values):
        lead = values.shape[:-2]
        parts = values.reshape(lead + (devices, tok_rows, channels))
        moved = lax.all_to_all(parts, "tok", split_axis=len(lead), concat_axis=len(lead), tiled=True)
        moved = moved.reshape(lead + (half, cut, tok_rows, channels))
        return jnp.swapaxes(moved, -3, -2).reshape(lead + (half, tok_rows, side))

    place = doc_positions(doc_lengths).reshape(-1, 1)
    taps, offset = channel_vectors[:K], channel_vectors[K]
    xs = xs_low.astype(f32)
    filtered = jax.nn.silu(conv_pre(xs, taps, offset, place)).astype(bf16)
    filtered_tokens = to_tokens(filtered)
    projected = jnp.einsum(
        "gtc,gcf->tf",
        filtered_tokens,
        select_weight.reshape(half, side, select_width),
        preferred_element_type=f32,
    ).astype(bf16)
    projected_all = spread(projected, devices)
    back_chan = jnp.einsum("td,cd->tc", cotangent_all, output_local, preferred_element_type=f32).astype(bf16)

    if fast:
        pool_low, projected_all = lax.optimization_barrier((pool_low, projected_all))
        pool_all = lax.all_gather(pool_low, "tok", axis=0, tiled=True)

    by_row = lambda values: values.reshape((rows, L) + values.shape[1:])
    rank_in = projected_all[:, :R]
    state_in = projected_all[:, R:].astype(f32)
    groups = L // GROUP
    columns = state_in.reshape(rows, groups, GROUP, 2 * N).transpose(0, 1, 3, 2)
    inject = state_in[:, :N].reshape(rows, groups, GROUP * N)
    readout = state_in[:, N:].reshape(rows, groups, GROUP * N)
    begins = by_row(jnp.broadcast_to(jnp.where(place == 0, 1e30, 0.0).astype(bf16), (tokens, channels)))
    step_local = channel_weight[:, select_width:].astype(bf16)
    rates = jnp.exp(channel_vectors[K + 2 : K + 2 + N])
    step_bias = channel_vectors[K + 1 : K + 2]
    skip_gain = channel_vectors[K + 2 + N :]
    scan_in = (by_row(filtered), by_row(rank_in), by_row(gates), by_row(back_chan), begins, columns)
    scan_params = (step_local, step_bias, rates, skip_gain)
    mixed, gate_grad, kept = scan_forward(*scan_in, readout, *scan_params)
    mixed = mixed.reshape(tokens, channels)
    gate_grad = gate_grad.reshape(tokens, channels)

    def input_part(grad):
        part = jnp.einsum("td,tc->dc", normed_all, grad, preferred_element_type=f32)
        return part.astype(bf16).reshape(tall, side, channels)

    output_part = jnp.einsum("tc,td->cd", mixed, cotangent_all, preferred_element_type=f32).astype(bf16)
    output_part = output_part.reshape(channels, tall, side).transpose(1, 0, 2)
    gate_part = input_part(gate_grad)

    def every_input(part):
        every = lax.all_gather(part, "tok", axis=0)
        every = every.reshape(half, cut, tall, side, channels).transpose(0, 2, 3, 1, 4)
        return every.reshape(half * tall, side, side)

    if fast:
        first_parts = jnp.concatenate([gate_part, output_part], axis=0)
        first_parts, kept = lax.optimization_barrier((first_parts, kept))
        early = backward_tiles("xs", ~is_xs, tall, first_parts)
    else:
        output_every = lax.all_gather(output_part, "tok", axis=0)
        output_every = (
            output_every.reshape(half, cut, tall, channels, side)
            .transpose(0, 2, 1, 3, 4)
            .reshape(half * tall, side, side)
        )
        gate_every = every_input(gate_part)

    mixed_tokens = to_tokens(mixed)

    draw, filter_mix, inject_grad, read_grad, rate_sum, skip_grad, bias_grad = scan_backward(
        *scan_in, inject, *scan_params, kept
    )
    draw = draw.reshape(tokens, channels)
    step_grad = jnp.einsum("tc,tr->cr", draw, rank_in, preferred_element_type=f32)
    partial_sums = jnp.concatenate(
        [
            jnp.einsum("tc,cr->tr", draw, step_local, preferred_element_type=f32),
            inject_grad.reshape(tokens, N),
            read_grad.reshape(tokens, N),
        ],
        axis=1,
    )
    projected_grad_all = spread(fold(partial_sums, devices).astype(bf16), devices)
    select_local = channel_weight[:, :select_width].astype(bf16)
    back_filter = jnp.einsum(
        "tf,cf->tc", projected_grad_all, select_local, preferred_element_type=f32
    ).astype(bf16)
    select_grad = jnp.einsum("tc,tf->cf", filtered, projected_grad_all, preferred_element_type=f32)
    pre = conv_pre(xs, taps, offset, place)
    gate = jax.nn.sigmoid(pre)
    dpre = (filter_mix.reshape(tokens, channels) + back_filter.astype(f32)) * (gate * (1.0 + pre * (1.0 - gate)))
    offset_grad = jnp.sum(dpre, axis=0)
    taps_grad = [jnp.sum(dpre * xs, axis=0)]
    xs_grad = taps[K - 1][None] * dpre
    for lag in range(1, K):
        masked = jnp.where(place >= lag, dpre, 0.0)
        xs_grad = xs_grad + taps[K - 1 - lag][None] * sooner(masked, lag)
        taps_grad.insert(0, jnp.sum(masked * later(xs, lag), axis=0))
    xs_grad = xs_grad.astype(bf16)
    xs_part = input_part(xs_grad)
    if fast:
        late = backward_tiles("xs", is_xs, 0, xs_part)
    else:
        xs_every = every_input(xs_part)

    own_slot = tile_slot - me * tiles_here
    every_tile = jnp.full(tile_slot.shape, True)
    if fast:
        grads = (late, early)
        line_rank = routes.ranks["xs"][0]
        cap = jnp.where(is_xs, CAP_LINE[1], CAP_LINE[2])
        kind = table(tiles_here, own_slot, every_tile, (~is_xs).astype(jnp.int32))
        index = table(tiles_here, own_slot, every_tile, routes.target_line * cap + line_rank)
    else:
        grads = (xs_every, gate_every, output_every)
        tile = jnp.arange(tile_slot.shape[0], dtype=jnp.int32)
        kind = table(tiles_here, own_slot, every_tile, routes.kind)
        spot = jnp.where(is_out, tile - input_tiles, tile % wide % half * tall + tile // wide)
        index = table(tiles_here, own_slot, every_tile, spot)
    first_next, second_next, weight_next, lstat_next, rstat_next, turned, gram = soap_tiles(
        kind,
        index,
        grads,
        pool_weight,
        pool_first,
        pool_second,
        pool_left,
        pool_right,
        pool_left_stat,
        pool_right_stat,
    )
    inverse_low = inverse_factor(gram.reshape(2 * tiles_here, side, side)).reshape(gram.shape)
    left_next, right_next = renew_bases(turned, inverse_low)

    joint_grad = to_tokens(jnp.stack([xs_grad, gate_grad])).reshape(wide, tok_rows, side)
    layer_out = tile_product(
        mixed_tokens, pool_all, tile_slot[input_tiles:].reshape(half, tall).T, False, bf16, layer_in
    )
    normed_grad = tile_product(
        joint_grad, pool_all, tile_slot[:input_tiles].reshape(tall, wide), True, f32
    )
    input_float = layer_in.astype(f32)
    inverse = lax.rsqrt(jnp.mean(input_float * input_float, axis=1, keepdims=True) + norm_epsilon)
    scaled = normed_grad * gain_float
    input_grad = (
        cotangent.astype(f32)
        + inverse * scaled
        - input_float * inverse**3 * jnp.mean(scaled * input_float, axis=1, keepdims=True)
    )
    gain_part = jnp.sum(normed_grad * input_float * inverse, axis=0).reshape(devices, gain_here)
    gain_grad = jnp.sum(lax.all_to_all(gain_part, "tok", split_axis=0, concat_axis=0, tiled=True), axis=0)

    first_c, second_c, weight_c, lstat_c, rstat_c, left_turned, right_turned, left_gram, right_gram = channel_moments(
        channel_weight,
        jnp.concatenate([select_grad, step_grad], axis=1),
        channel_first,
        channel_second,
        channel_left,
        channel_right,
        channel_left_stat,
        channel_right_stat,
    )
    left_c, right_c = solve_factors((left_gram, right_gram), (left_turned.T, right_turned.T))
    channel_new = (first_c, second_c, weight_c, left_c.T, right_c.T, lstat_c, rstat_c)
    gain_new = adam_step(norm_gain, gain_grad, gain_first, gain_second)
    vector_grad = jnp.concatenate(
        [jnp.stack(taps_grad), offset_grad[None], bias_grad, -rates * rate_sum, skip_grad], axis=0
    )
    vector_new = adam_step(channel_vectors, vector_grad, vector_first, vector_second)
    return (
        layer_out,
        input_grad,
        first_next,
        second_next,
        weight_next,
        left_next,
        right_next,
        lstat_next,
        rstat_next,
        *channel_new,
        *gain_new,
        *vector_new,
    )


def shards(*args):
    devices = lax.axis_size("tok")
    layer_in, tile_slot, pool_weight, channel_vectors = args[0], args[3], args[4], args[21]
    tiles_here, side, _ = pool_weight.shape
    channels = channel_vectors.shape[1]
    routes = Routes(tile_slot, devices, tiles_here, layer_in.shape[1] // side, channels * devices // side)
    if channels != side or devices % LINES:
        return core(routes, False, *args)
    return lax.cond(routes.fits, functools.partial(core, routes, True), functools.partial(core, routes, False), *args)


def solution(mesh):
    line, flat, cube, column = P("tok"), P("tok", None), P("tok", None, None), P(None, "tok")
    in_specs = (flat, flat, P(), P()) + (cube,) * 7 + (flat,) * 7 + (line,) * 3 + (column,) * 3
    out_specs = (flat, flat) + (cube,) * 7 + (flat,) * 7 + (line,) * 3 + (column,) * 3
    return jax.shard_map(shards, mesh=mesh, in_specs=in_specs, out_specs=out_specs, check_vma=False)
```

```python
import functools

import jax
import jax.numpy as jnp
from jax import lax
from jax.experimental import pallas as pl
from jax.experimental.pallas import tpu as pltpu
from jax.sharding import PartitionSpec as P

N = 16
R = 128
K = 4
L = 2048
STEP = 5
GROUP = 16
LOG2E = 1.4426950408889634

beta_first = 0.5
beta_second = 0.5
stat_decay = 0.5
learn_rate = 0.02
vector_rate = 0.2
weight_decay = 0.01
adam_epsilon = 1e-08
norm_epsilon = 1e-05
highest = lax.Precision.HIGHEST


LINES = 4
MESH = pl.DeviceIdType.MESH


def greet(line, spot, plane):
    barrier = pltpu.get_barrier_semaphore()
    for k in range(1, LINES):
        pl.semaphore_signal(barrier, inc=1, device_id=((line + k) % LINES * plane + spot,), device_id_type=MESH)
    for k in range(1, plane):
        pl.semaphore_signal(barrier, inc=1, device_id=(line * plane + (spot + k) % plane,), device_id_type=MESH)
    pl.semaphore_wait(barrier, LINES + plane - 2)


def remote(source, target, send, recv, device):
    return pltpu.make_async_remote_copy(
        src_ref=source, dst_ref=target, send_sem=send, recv_sem=recv, device_id=(device,), device_id_type=MESH
    )


def route_copies(cap_line, cap_plane, plane, source, out, sems):
    line_send, line_recv, plane_send, plane_recv, own = sems
    me = lax.axis_index("tok")
    line, spot = me // plane, me % plane
    start = LINES * cap_line

    def to_line(place):
        return pl.ds(place * cap_line, cap_line)

    def to_plane(place):
        return pl.ds(start + place * cap_plane, cap_plane)

    copies = [
        pltpu.make_async_copy(source.at[to_line(line)], out.at[to_line(line)], own.at[0]),
        pltpu.make_async_copy(source.at[to_plane(spot)], out.at[to_plane(spot)], own.at[1]),
    ]
    for k in range(1, LINES):
        place = (line + k) % LINES
        copies.append(
            remote(source.at[to_line(place)], out.at[to_line(line)], line_send.at[k], line_recv.at[k], place * plane + spot)
        )
    for k in range(1, plane):
        place = (spot + k) % plane
        copies.append(
            remote(source.at[to_plane(place)], out.at[to_plane(spot)], plane_send.at[k], plane_recv.at[k], line * plane + place)
        )
    return copies


def route_sems(plane):
    return [pltpu.SemaphoreType.DMA((LINES,))] * 2 + [pltpu.SemaphoreType.DMA((plane,))] * 2 + [pltpu.SemaphoreType.DMA((2,))]


def route_kernel(cap_line, cap_plane, plane, source, out, *sems):
    me = lax.axis_index("tok")
    greet(me // plane, me % plane, plane)
    copies = route_copies(cap_line, cap_plane, plane, source, out, sems)
    for copy in copies:
        copy.start()
    for copy in copies:
        copy.wait()


HBM = pl.BlockSpec(memory_space=pl.ANY)


def route_stage(packed, cap_line, cap_plane, plane, number):
    return pl.pallas_call(
        functools.partial(route_kernel, cap_line, cap_plane, plane),
        in_specs=[HBM],
        out_specs=HBM,
        out_shape=jax.ShapeDtypeStruct(packed.shape, packed.dtype),
        scratch_shapes=route_sems(plane),
        compiler_params=pltpu.CompilerParams(collective_id=number, has_side_effects=True),
    )(packed)


def everyone_kernel(devices, source, out, send, recv, own):
    me = lax.axis_index("tok")
    barrier = pltpu.get_barrier_semaphore()
    for k in range(1, devices):
        pl.semaphore_signal(barrier, inc=1, device_id=((me + k) % devices,), device_id_type=MESH)
    pl.semaphore_wait(barrier, devices - 1)
    copies = [pltpu.make_async_copy(source.at[me], out.at[me], own.at[0])]
    for k in range(1, devices):
        target = (me + k) % devices
        copies.append(remote(source.at[target], out.at[me], send.at[k], recv.at[k], target))
    for copy in copies:
        copy.start()
    for copy in copies:
        copy.wait()


def everyone(values, number):
    devices = values.shape[0]
    return pl.pallas_call(
        functools.partial(everyone_kernel, devices),
        in_specs=[HBM],
        out_specs=HBM,
        out_shape=jax.ShapeDtypeStruct(values.shape, values.dtype),
        scratch_shapes=[pltpu.SemaphoreType.DMA((devices,))] * 2 + [pltpu.SemaphoreType.DMA((1,))],
        compiler_params=pltpu.CompilerParams(collective_id=number, has_side_effects=True),
    )(values)


def spread_steps(plane, block, out, sems):
    line_send, line_recv, plane_send, plane_recv, own = sems
    me = lax.axis_index("tok")
    line, spot = me // plane, me % plane
    copies = [pltpu.make_async_copy(block, out.at[line, spot], own.at[0])]
    arrivals = []
    for k in range(1, LINES):
        place = (line + k) % LINES
        arrivals.append(remote(block, out.at[line, spot], line_send.at[k], line_recv.at[k], place * plane + spot))
    for k in range(1, plane):
        place = (spot + k) % plane
        copies.append(
            remote(block, out.at[line, spot], plane_send.at[0, k], plane_recv.at[0, k], line * plane + place)
        )
    for copy in arrivals + copies:
        copy.start()
    for k in range(1, LINES):
        arrivals[k - 1].wait_recv()
        origin = (line + LINES - k) % LINES
        for j in range(1, plane):
            place = (spot + j) % plane
            copy = remote(
                out.at[origin, spot], out.at[origin, spot], plane_send.at[k, j], plane_recv.at[k, j], line * plane + place
            )
            copy.start()
            copies.append(copy)
    for copy in arrivals:
        copy.wait_send()
    for copy in copies:
        copy.wait()


def spread_sems(plane):
    return (
        [pltpu.SemaphoreType.DMA((LINES,))] * 2
        + [pltpu.SemaphoreType.DMA((LINES, plane))] * 2
        + [pltpu.SemaphoreType.DMA((1,))]
    )


def spread_kernel(plane, block, out, *sems):
    me = lax.axis_index("tok")
    greet(me // plane, me % plane, plane)
    spread_steps(plane, block, out, sems)


def spread_blocks(block, plane, number):
    return pl.pallas_call(
        functools.partial(spread_kernel, plane),
        in_specs=[HBM],
        out_specs=HBM,
        out_shape=jax.ShapeDtypeStruct((LINES, plane) + block.shape, block.dtype),
        scratch_shapes=spread_sems(plane),
        compiler_params=pltpu.CompilerParams(collective_id=number, has_side_effects=True),
    )(block)


def fold_kernel(plane, parts, out, got, sent, last, block, plane_send, plane_recv, line_send, line_recv, own, *sems):
    me = lax.axis_index("tok")
    line, spot = me // plane, me % plane
    greet(line, spot, plane)
    copies = [pltpu.make_async_copy(parts.at[:, spot], got.at[spot], own.at[0])]
    for k in range(1, plane):
        place = (spot + k) % plane
        copies.append(
            remote(parts.at[:, place], got.at[spot], plane_send.at[k], plane_recv.at[k], line * plane + place)
        )
    for copy in copies:
        copy.start()
    for copy in copies:
        copy.wait()
    for z in range(LINES):
        total = got[0, z].astype(jnp.float32)
        for k in range(1, plane):
            total = total + got[k, z].astype(jnp.float32)
        sent[z] = total
    copies = [pltpu.make_async_copy(sent.at[line], last.at[line], own.at[1])]
    for k in range(1, LINES):
        place = (line + k) % LINES
        copies.append(remote(sent.at[place], last.at[line], line_send.at[k], line_recv.at[k], place * plane + spot))
    for copy in copies:
        copy.start()
    for copy in copies:
        copy.wait()
    block[...] = ((last[0] + last[1]) + (last[2] + last[3])).astype(block.dtype)
    spread_steps(plane, block, out, sems)


def fold_and_spread(parts, plane, number):
    shape = parts.shape[2:]
    return pl.pallas_call(
        functools.partial(fold_kernel, plane),
        in_specs=[HBM],
        out_specs=HBM,
        out_shape=jax.ShapeDtypeStruct(parts.shape, parts.dtype),
        scratch_shapes=[
            pltpu.VMEM((plane, LINES) + shape, parts.dtype),
            pltpu.VMEM((LINES,) + shape, jnp.float32),
            pltpu.VMEM((LINES,) + shape, jnp.float32),
            pltpu.VMEM(shape, parts.dtype),
        ]
        + [pltpu.SemaphoreType.DMA((plane,))] * 2
        + [pltpu.SemaphoreType.DMA((LINES,))] * 2
        + [pltpu.SemaphoreType.DMA((2,))]
        + spread_sems(plane),
        compiler_params=pltpu.CompilerParams(collective_id=number, has_side_effects=True, vmem_limit_bytes=16 * 2**20),
    )(parts)


def dot_nt(left, right):
    return lax.dot_general(left, right, (((1,), (1,)), ((), ())), preferred_element_type=jnp.float32)

def dot_nn(left, right):
    return jnp.dot(left, right, preferred_element_type=jnp.float32)

def softplus(v):
    return jnp.maximum(v, 0.0) + jnp.log1p(jnp.exp(-jnp.abs(v)))

def split2(v):
    high = v.astype(jnp.bfloat16)
    return high, (v - high.astype(jnp.float32)).astype(jnp.bfloat16)

def own_token(dtype):
    token = lax.broadcasted_iota(jnp.int32, (GROUP, GROUP * N), 0)
    column = lax.broadcasted_iota(jnp.int32, (GROUP, GROUP * N), 1)
    return (column // N == token).astype(dtype)

def fwd_kernel(pair, chunk, f_ref, rank_ref, z_ref, gm_ref, start_ref, cols_ref, read_ref,
               stepw_ref, bias_ref, rate_ref, skip_ref,
               mixed_ref, dz_ref, keep_ref, state, step_s, drive_s, scan_s):
    groups = chunk // GROUP
    neg = rate_ref[...] * (-LOG2E)
    mine = own_token(jnp.float32)

    @pl.when(pl.program_id(1) == 0)
    def _():
        state[...] = jnp.zeros_like(state)

    for r in range(pair):
        raw = dot_nt(rank_ref[r], stepw_ref[...])
        step = softplus(raw + bias_ref[...])
        step_s[r] = step + start_ref[r].astype(jnp.float32)
        drive_s[r] = step * f_ref[r].astype(jnp.float32)
        keep_ref[r, 0] = state[r]

    def group(g, hidden):
        hidden = list(hidden)
        held = [[] for _ in range(pair)]
        base = pl.multiple_of(g * GROUP, GROUP)
        cols = [cols_ref[r, g] for r in range(pair)]
        for k in range(GROUP):
            for r in range(pair):
                factor = jnp.exp2(step_s[r, pl.ds(base + k, 1), :] * neg)
                hidden[r] = factor * hidden[r] + drive_s[r, pl.ds(base + k, 1), :] * cols[r][:N, k : k + 1]
                held[r].append(hidden[r].astype(jnp.bfloat16))
        for r in range(pair):
            states = jnp.concatenate(held[r], axis=0)
            scan_s[r, pl.ds(base, GROUP), :] = dot_nn((mine * read_ref[r, pl.ds(g, 1), :]).astype(jnp.bfloat16), states)
        return tuple(hidden)

    hidden = lax.fori_loop(0, groups, group, tuple(state[r] for r in range(pair)))
    for r in range(pair):
        state[r] = hidden[r]
        f = f_ref[r].astype(jnp.float32)
        z = z_ref[r].astype(jnp.float32)
        gate = 1.0 / (1.0 + jnp.exp(-z))
        summed = scan_s[r] + skip_ref[...] * f
        mixed_ref[r] = (summed * (z * gate)).astype(jnp.bfloat16)
        dz_ref[r] = (gm_ref[r].astype(jnp.float32) * summed * (gate * (1.0 + z * (1.0 - gate)))).astype(jnp.bfloat16)

def bwd_kernel(pair, chunk, route, f_ref, rank_ref, z_ref, gm_ref, start_ref, cols_ref, inj_ref,
               stepw_ref, bias_ref, rate_ref, skip_ref, keep_ref, *refs):
    if route is not None:
        packed_ref, refs = refs[0], refs[1:]
    draw_ref, dfm_ref, dinj_ref, dread_ref, drate_ref, dskip_ref, dbias_ref = refs[:7]
    refs = refs[7:]
    if route is not None:
        moved_ref, refs = refs[0], refs[1:]
    carry_s, step_s, drive_s, dscan_s, raw_s, delta_s, a_s, ah_s, h_s, s1_s, s2_s = refs[:11]
    if route is not None:
        @pl.when((pl.program_id(0) == 0) & (pl.program_id(1) == 0))
        def _():
            me = lax.axis_index("tok")
            greet(me // route[2], me % route[2], route[2])
            for copy in route_copies(*route, packed_ref, moved_ref, refs[11:]):
                copy.start()

    groups = chunk // GROUP
    rate = rate_ref[...]
    neg = rate * (-LOG2E)
    mine = own_token(jnp.float32)
    mine_f = mine

    @pl.when(pl.program_id(1) == 0)
    def _():
        carry_s[...] = jnp.zeros_like(carry_s)

    @pl.when((pl.program_id(1) == 0) & (pl.program_id(0) == 0))
    def _():
        drate_ref[...] = jnp.zeros_like(drate_ref)
        dskip_ref[...] = jnp.zeros_like(dskip_ref)
        dbias_ref[...] = jnp.zeros_like(dbias_ref)

    for r in range(pair):
        raw = dot_nt(rank_ref[r], stepw_ref[...]) + bias_ref[...]
        step = softplus(raw)
        raw_s[r] = raw
        delta_s[r] = step
        step_s[r] = step + start_ref[r].astype(jnp.float32)
        f = f_ref[r].astype(jnp.float32)
        drive_s[r] = step * f
        z = z_ref[r].astype(jnp.float32)
        gate = 1.0 / (1.0 + jnp.exp(-z))
        dscan = gm_ref[r].astype(jnp.float32) * (z * gate)
        dscan_s[r] = dscan
        dskip_ref[...] += jnp.sum(dscan * f, axis=0, keepdims=True)

    def forward(g, hidden):
        hidden = list(hidden)
        base = pl.multiple_of(g * GROUP, GROUP)
        cols = [cols_ref[r, g] for r in range(pair)]
        held = [[] for _ in range(pair)]
        for k in range(GROUP):
            for r in range(pair):
                factor = jnp.exp2(step_s[r, pl.ds(base + k, 1), :] * neg)
                kept = factor * hidden[r]
                hidden[r] = kept + drive_s[r, pl.ds(base + k, 1), :] * cols[r][:N, k : k + 1]
                a_s[r, base + k] = factor
                ah_s[r, base + k] = kept
                held[r].append(hidden[r].astype(jnp.bfloat16))
        for r in range(pair):
            h_s[r, g] = jnp.concatenate(held[r], axis=0)
        return tuple(hidden)

    lax.fori_loop(0, groups, forward, tuple(keep_ref[r, 0] for r in range(pair)))

    def backward(i, carried):
        g = groups - 1 - i
        base = pl.multiple_of(g * GROUP, GROUP)
        ag = list(carried[:pair])
        total = carried[pair]
        cols = [cols_ref[r, g] for r in range(pair)]
        gs = [[None] * GROUP for _ in range(pair)]
        qs = [[None] * GROUP for _ in range(pair)]
        for k in reversed(range(GROUP)):
            for r in range(pair):
                grad = dscan_s[r, pl.ds(base + k, 1), :] * cols[r][N:, k : k + 1] + ag[r]
                ag[r] = a_s[r, base + k] * grad
                q = grad * ah_s[r, base + k]
                total = total + delta_s[r, pl.ds(base + k, 1), :] * q
                gs[r][k] = grad.astype(jnp.bfloat16)
                qs[r][k] = (rate * q).astype(jnp.bfloat16)
        for r in range(pair):
            grads = jnp.concatenate(gs[r], axis=0)
            pulls = jnp.concatenate(qs[r], axis=0)
            s1_s[r, pl.ds(base, GROUP), :] = dot_nn((mine * inj_ref[r, pl.ds(g, 1), :]).astype(jnp.bfloat16), grads)
            s2_s[r, pl.ds(base, GROUP), :] = dot_nn(mine.astype(jnp.bfloat16), pulls)
            dh, dl = split2(dscan_s[r, pl.ds(base, GROUP), :])
            uh, ul = split2(drive_s[r, pl.ds(base, GROUP), :])
            dr = dot_nt(jnp.concatenate([dh, dl], axis=0), h_s[r, g])
            dread_ref[r, pl.ds(g, 1), :] = jnp.sum((dr[:GROUP] + dr[GROUP:]) * mine_f, axis=0, keepdims=True)
            di = dot_nt(jnp.concatenate([uh, ul], axis=0), grads)
            dinj_ref[r, pl.ds(g, 1), :] = jnp.sum((di[:GROUP] + di[GROUP:]) * mine_f, axis=0, keepdims=True)
        return tuple(ag) + (total,)

    out = lax.fori_loop(0, groups, backward, tuple(carry_s[r] for r in range(pair)) + (jnp.zeros_like(rate),))
    drate_ref[...] += out[pair]
    for r in range(pair):
        carry_s[r] = out[r]
        f = f_ref[r].astype(jnp.float32)
        draw = (f * s1_s[r] - s2_s[r]) / (1.0 + jnp.exp(-raw_s[r]))
        draw_ref[r] = draw.astype(jnp.bfloat16)
        dbias_ref[...] += jnp.sum(draw, axis=0, keepdims=True)
        dfm_ref[r] = delta_s[r] * s1_s[r] + skip_ref[...] * dscan_s[r]

    if route is not None:
        @pl.when((pl.program_id(0) == pl.num_programs(0) - 1) & (pl.program_id(1) == pl.num_programs(1) - 1))
        def _():
            for copy in route_copies(*route, packed_ref, moved_ref, refs[11:]):
                copy.wait()

def specs(pair, chunk, ch, rank, back, chunks):
    def at(i, j):
        return (i, chunks - 1 - j if back else j)
    tok = pl.BlockSpec((pair, chunk, ch), lambda i, j: at(i, j) + (0,))
    rk = pl.BlockSpec((pair, chunk, rank), lambda i, j: at(i, j) + (0,))
    cols = pl.BlockSpec((pair, chunk // GROUP, 2 * N, GROUP), lambda i, j: at(i, j) + (0, 0))
    flat = pl.BlockSpec((pair, chunk // GROUP, GROUP * N), lambda i, j: at(i, j) + (0,))
    keep = pl.BlockSpec((pair, 1, N, ch), lambda i, j: at(i, j) + (0, 0))
    def whole(a):
        return pl.BlockSpec(a.shape, lambda i, j: (0,) * a.ndim)
    return tok, rk, cols, flat, keep, whole

def scan_forward(f, rank, z, gm, start, cols, read, stepw, bias, rate, skip, chunk=128):
    rows, length, ch = f.shape
    pair = 2 if rows % 2 == 0 else 1
    chunks = length // chunk
    tok, rk, colb, flat, keep, whole = specs(pair, chunk, ch, rank.shape[2], False, chunks)
    return pl.pallas_call(
        functools.partial(fwd_kernel, pair, chunk),
        grid=(rows // pair, chunks),
        in_specs=[tok, rk, tok, tok, tok, colb, flat, whole(stepw), whole(bias), whole(rate), whole(skip)],
        out_specs=[tok, tok, keep],
        out_shape=[jax.ShapeDtypeStruct(f.shape, jnp.bfloat16), jax.ShapeDtypeStruct(f.shape, jnp.bfloat16),
                   jax.ShapeDtypeStruct((rows, chunks, N, ch), jnp.float32)],
        scratch_shapes=[pltpu.VMEM((pair, N, ch), jnp.float32)] + [pltpu.VMEM((pair, chunk, ch), jnp.float32)] * 3,
        compiler_params=pltpu.CompilerParams(vmem_limit_bytes=40 * 2**20),
        cost_estimate=pl.CostEstimate(flops=4 * 10**10, bytes_accessed=8 * 10**6, transcendentals=0),
    )(f, rank, z, gm, start, cols, read, stepw, bias, rate, skip)

def scan_backward(f, rank, z, gm, start, cols, inj, stepw, bias, rate, skip, kept, packed=None, route=None, number=None, chunk=128):
    rows, length, ch = f.shape
    pair = 2 if rows % 2 == 0 else 1
    chunks = length // chunk
    tok, rk, colb, flat, keep, whole = specs(pair, chunk, ch, rank.shape[2], True, chunks)
    f32 = jnp.float32
    row = jax.ShapeDtypeStruct((1, ch), f32)
    in_specs = [tok, rk, tok, tok, tok, colb, flat, whole(stepw), whole(bias), whole(rate), whole(skip), keep]
    out_specs = [tok, tok, flat, flat, whole(rate), whole(row), whole(row)]
    out_shape = [jax.ShapeDtypeStruct(f.shape, jnp.bfloat16), jax.ShapeDtypeStruct(f.shape, f32),
                 jax.ShapeDtypeStruct(inj.shape, f32), jax.ShapeDtypeStruct(inj.shape, f32),
                 jax.ShapeDtypeStruct(rate.shape, f32), row, row]
    scratch = ([pltpu.VMEM((pair, N, ch), f32)] + [pltpu.VMEM((pair, chunk, ch), f32)] * 5
               + [pltpu.VMEM((pair, chunk, N, ch), f32)] * 2
               + [pltpu.VMEM((pair, chunk // GROUP, GROUP * N, ch), jnp.bfloat16)]
               + [pltpu.VMEM((pair, chunk, ch), f32)] * 2)
    values = (f, rank, z, gm, start, cols, inj, stepw, bias, rate, skip, kept)
    params = dict(vmem_limit_bytes=40 * 2**20)
    if route is not None:
        in_specs, out_specs = in_specs + [HBM], out_specs + [HBM]
        out_shape = out_shape + [jax.ShapeDtypeStruct(packed.shape, packed.dtype)]
        scratch = scratch + route_sems(route[2])
        values = values + (packed,)
        params.update(collective_id=number, has_side_effects=True)
    return pl.pallas_call(
        functools.partial(bwd_kernel, pair, chunk, route),
        grid=(rows // pair, chunks),
        in_specs=in_specs,
        out_specs=out_specs,
        out_shape=out_shape,
        scratch_shapes=scratch,
        compiler_params=pltpu.CompilerParams(**params),
        cost_estimate=pl.CostEstimate(flops=7 * 10**10, bytes_accessed=8 * 10**6, transcendentals=0),
    )(*values)


def chol_kernel(batch, order, gram_ref, out_ref, low_ref, inv_ref, piv_ref):
    tiles = order // 8
    rows8 = lax.broadcasted_iota(jnp.int32, (8, batch), 0)

    def load_slab(j, carry):
        low_ref[j, pl.ds(0, order), :] = gram_ref[pl.ds(j, batch, stride=order), :].T
        inv_ref[j] = jnp.zeros(inv_ref.shape[1:], jnp.float32)
        return carry

    lax.fori_loop(0, order, load_slab, 0, unroll=8)

    def bcast(ref, j, row):
        return jnp.broadcast_to(ref[j, pl.ds(row, 1), :], (8, batch))

    def block_column(block, carry):
        base = pl.multiple_of(block * 8, 8)

        def updated(tile_rows, seed):
            def one(j, accs):
                mult = [bcast(low_ref, j, base + k) for k in range(8)]
                out = []
                for s, rows in enumerate(tile_rows):
                    piece = low_ref[j, pl.ds(rows, 8), :]
                    out.extend(accs[s * 8 + k] - piece * mult[k] for k in range(8))
                return tuple(out)

            def eight(step, accs):
                for u in range(8):
                    accs = one(step * 8 + u, accs)
                return accs

            return list(lax.fori_loop(0, block, eight, tuple(seed)))

        accs = updated([base], [low_ref[base + k, pl.ds(base, 8), :] for k in range(8)])
        scales = []
        for k in range(8):
            scale = lax.rsqrt(jnp.broadcast_to(accs[k][k : k + 1, :], (8, batch)))
            scales.append(scale)
            accs[k] = jnp.where(rows8 >= k, accs[k] * scale, 0.0)
            for later in range(k + 1, 8):
                accs[later] = accs[later] - accs[k] * jnp.broadcast_to(
                    accs[k][later : later + 1, :], (8, batch)
                )
        for k in range(8):
            low_ref[base + k, pl.ds(base, 8), :] = accs[k]
            piv_ref[base + k] = scales[k]

        def pair(p, carry):
            first = pl.multiple_of(base + 8 + p * 16, 8)
            both = [first, pl.multiple_of(first + 8, 8)]
            accs = updated(
                both, [low_ref[base + k, pl.ds(rows, 8), :] for rows in both for k in range(8)]
            )
            for k in range(8):
                scale = piv_ref[base + k]
                for s in range(2):
                    accs[s * 8 + k] = accs[s * 8 + k] * scale
                for later in range(k + 1, 8):
                    mult = bcast(low_ref, base + k, base + later)
                    for s in range(2):
                        accs[s * 8 + later] = accs[s * 8 + later] - accs[s * 8 + k] * mult
            for s, rows in enumerate(both):
                for k in range(8):
                    low_ref[base + k, pl.ds(rows, 8), :] = accs[s * 8 + k]
            return carry

        lax.fori_loop(0, (tiles - block) // 2, pair, 0)
        return carry

    lax.fori_loop(0, tiles, block_column, 0)

    def block_row(block, carry):
        base = pl.multiple_of(block * 8, 8)

        def finish(accs, both):
            for k in range(8):
                scale = piv_ref[base + k]
                for s in range(len(both)):
                    accs[s * 8 + k] = accs[s * 8 + k] * scale
                for later in range(k + 1, 8):
                    mult = bcast(low_ref, base + k, base + later)
                    for s in range(len(both)):
                        accs[s * 8 + later] = accs[s * 8 + later] - accs[s * 8 + k] * mult
            for s, columns in enumerate(both):
                for k in range(8):
                    inv_ref[base + k, pl.ds(columns, 8), :] = accs[s * 8 + k]

        def pair(p, carry):
            first = pl.multiple_of(p * 16, 8)
            both = [first, pl.multiple_of(first + 8, 8)]

            def eight(step, accs):
                for u in range(8):
                    j = step * 8 + u
                    mult = [bcast(low_ref, j, base + k) for k in range(8)]
                    out = []
                    for s, columns in enumerate(both):
                        piece = inv_ref[j, pl.ds(columns, 8), :]
                        out.extend(accs[s * 8 + k] - piece * mult[k] for k in range(8))
                    accs = tuple(out)
                return accs

            accs = list(lax.fori_loop(
                p * 2, block, eight, (jnp.zeros((8, batch), jnp.float32),) * 16
            ))
            finish(accs, both)
            return carry

        lax.fori_loop(0, (block + 1) // 2, pair, 0)
        odd = block % 2

        def diagonal():
            accs = [jnp.where(rows8 == k, 1.0, 0.0) for k in range(8)]
            finish(accs, [base])

        diagonal()
        return carry

    lax.fori_loop(0, tiles, block_row, 0)

    def store_slab(i, carry):
        out_ref[pl.ds(i, batch, stride=order), :] = inv_ref[i, pl.ds(0, order), :].T
        return carry

    lax.fori_loop(0, order, store_slab, 0, unroll=8)

def inverse_factor(gram):
    batch, order, _ = gram.shape
    out = pl.pallas_call(
        functools.partial(chol_kernel, batch, order),
        out_shape=jax.ShapeDtypeStruct((batch * order, order), jnp.float32),
        in_specs=[pl.BlockSpec(memory_space=pltpu.VMEM)],
        out_specs=pl.BlockSpec(memory_space=pltpu.VMEM),
        scratch_shapes=[
            pltpu.VMEM((order, order + 8, batch), jnp.float32),
            pltpu.VMEM((order, order + 8, batch), jnp.float32),
            pltpu.VMEM((order, 8, batch), jnp.float32),
        ],
        compiler_params=pltpu.CompilerParams(vmem_limit_bytes=56 * 2**20),
        cost_estimate=pl.CostEstimate(flops=5 * 10**10, bytes_accessed=12 * 10**6, transcendentals=0),
    )(gram.reshape(batch * order, order))
    return out.reshape(batch, order, order)


DEPTH = 4
BATCH = 16


def tile_product_kernel(pairs, steps, transposed, residual, idx_ref, left_ref, pool_ref, *refs):
    if residual:
        res_ref, refs = refs[0], refs[1:]
    out_ref, slots, sems = refs
    side = slots.shape[2]
    total_steps = pairs * steps

    def fetch(step):
        for u in range(BATCH):
            pltpu.make_async_copy(
                pool_ref.at[idx_ref[step * BATCH + u]], slots.at[step % DEPTH, u], sems.at[step % DEPTH]
            ).start()

    for step in range(min(DEPTH - 1, total_steps)):
        fetch(step)

    def one_pair(o, carry):
        total = jnp.zeros((left_ref.shape[1], 2 * side), jnp.float32)
        for k in range(steps):
            step = o * steps + k

            @pl.when(step + DEPTH - 1 < total_steps)
            def _():
                fetch(step + DEPTH - 1)

            slot = step % DEPTH
            pltpu.make_async_copy(slots.at[slot], slots.at[slot], sems.at[slot]).wait()
            for u in range(0, BATCH, 4):
                at = k * (BATCH // 2) + u // 2
                left = jnp.concatenate([left_ref[at], left_ref[at + 1]], axis=1)
                tile = [slots[slot, u + v] for v in range(4)]
                if transposed:
                    right = jnp.concatenate(
                        [jnp.concatenate([tile[0], tile[2]], axis=1), jnp.concatenate([tile[1], tile[3]], axis=1)], axis=0
                    )
                    total += dot_nt(left, right)
                else:
                    right = jnp.concatenate(
                        [jnp.concatenate([tile[0], tile[1]], axis=1), jnp.concatenate([tile[2], tile[3]], axis=1)], axis=0
                    )
                    total += dot_nn(left, right)
        columns = pl.ds(pl.multiple_of(o * 2 * side, side), 2 * side)
        if residual:
            total += res_ref[:, columns].astype(jnp.float32)
        out_ref[:, columns] = total.astype(out_ref.dtype)
        return carry

    lax.fori_loop(0, pairs, one_pair, 0)


def tile_product(left, pool, index, transposed, dtype, residual=None):
    outs, depth = index.shape
    pairs, steps = outs // 2, 2 * depth // BATCH
    side = pool.shape[1]
    tok = left.shape[1]
    vmem = pl.BlockSpec(memory_space=pltpu.VMEM)
    extra = [residual] if residual is not None else []
    order = index.reshape(pairs, 2, depth).transpose(0, 2, 1).reshape(-1).astype(jnp.int32)
    return pl.pallas_call(
        functools.partial(tile_product_kernel, pairs, steps, transposed, residual is not None),
        in_specs=[pl.BlockSpec(memory_space=pltpu.SMEM), vmem, pl.BlockSpec(memory_space=pl.ANY)] + [vmem] * len(extra),
        out_specs=vmem,
        out_shape=jax.ShapeDtypeStruct((tok, outs * side), dtype),
        scratch_shapes=[pltpu.VMEM((DEPTH, BATCH, side, side), pool.dtype), pltpu.SemaphoreType.DMA((DEPTH,))],
        compiler_params=pltpu.CompilerParams(vmem_limit_bytes=40 * 2**20),
        cost_estimate=pl.CostEstimate(
            flops=2 * outs * depth * tok * side * side, bytes_accessed=outs * depth * side * side * 2, transcendentals=0
        ),
    )(order, left, pool, *extra)


def dot_tn(left, right):
    return lax.dot_general(left, right, (((0,), (0,)), ((), ())), preferred_element_type=jnp.float32)


def three(dot, left, right):
    left_axis, right_axis = {dot_nn: (1, 0), dot_nt: (1, 1), dot_tn: (0, 0)}[dot]
    return dot(
        jnp.concatenate([left[0], left[0], left[1]], axis=left_axis),
        jnp.concatenate([right[0], right[1], right[0]], axis=right_axis),
    )


def soap_kernel(sources, many, kind_ref, idx_ref, *refs):
    grad_refs, refs = refs[: sources * many], refs[sources * many :]
    weight_ref, first_ref, second_ref, left_ref, right_ref, lstat_ref, rstat_ref = refs[:7]
    first_out, second_out, weight_out, lstat_out, rstat_out, turned_out, gram_out = refs[7:]
    side = weight_ref.shape[1]
    diagonal = lax.broadcasted_iota(jnp.int32, (side, side), 0) == lax.broadcasted_iota(jnp.int32, (side, side), 1)
    every = range(many)
    grads, lefts, rights = [], [], []
    for u in every:
        kind = kind_ref[pl.program_id(0) * many + u]
        grad = grad_refs[u * sources][0]
        for which in range(1, sources):
            grad = jnp.where(kind == which, grad_refs[u * sources + which][0], grad)
        grads.append(grad)
        lefts.append(split2(left_ref[u]))
        rights.append(split2(right_ref[u]))
    across = [split2(dot_nn(grads[u], rights[u][0]) + dot_nn(grads[u], rights[u][1])) for u in every]
    turned = [three(dot_tn, lefts[u], across[u]) for u in every]
    products = [(dot_nt(grads[u], grads[u]), dot_tn(grads[u], grads[u])) for u in every]
    directions = []
    for u in every:
        first = beta_first * first_ref[u] + (1.0 - beta_first) * turned[u]
        second = beta_second * second_ref[u] + (1.0 - beta_second) * turned[u] * turned[u]
        first_out[u] = first
        second_out[u] = second
        directions.append(split2(
            first / (1.0 - beta_first**STEP) / (jnp.sqrt(second / (1.0 - beta_second**STEP)) + adam_epsilon)
        ))
    renewed = []
    for u in every:
        for which, (stat_ref, basis_ref, basis2, stat_out) in enumerate(
            ((lstat_ref, left_ref, lefts[u], lstat_out), (rstat_ref, right_ref, rights[u], rstat_out))
        ):
            stat = stat_decay * stat_ref[u] + (1.0 - stat_decay) * products[u][which]
            stat_out[u] = stat
            trace = jnp.sum(jnp.sum(jnp.where(diagonal, stat, 0.0), axis=0, keepdims=True), axis=1, keepdims=True)
            value = three(dot_nn, split2(stat), basis2) + (trace / side) * basis_ref[u]
            turned_out[u, which] = value
            renewed.append(split2(value))
    back = [split2(three(dot_nt, directions[u], rights[u])) for u in every]
    for u in every:
        for which in range(2):
            gram_out[u, which] = three(dot_tn, renewed[u * 2 + which], renewed[u * 2 + which])
    for u in every:
        weight = weight_ref[u]
        weight_out[u] = weight - learn_rate * (three(dot_nn, lefts[u], back[u]) + weight_decay * weight)


def soap_tiles(kind, index, grads, weight, first, second, left, right, lstat, rstat, many=4):
    count, side, _ = weight.shape
    one = pl.BlockSpec((many, side, side), lambda s, kind, idx: (s, 0, 0))
    two = pl.BlockSpec((many, 2, side, side), lambda s, kind, idx: (s, 0, 0, 0))

    def picked(u, which):
        def at(s, kind, idx):
            return (jnp.where(kind[s * many + u] == which, idx[s * many + u], 0), 0, 0)

        return pl.BlockSpec((1, side, side), at)

    tile = jax.ShapeDtypeStruct(weight.shape, jnp.float32)
    pairs = jax.ShapeDtypeStruct((count, 2, side, side), jnp.float32)
    sources = len(grads)
    return pl.pallas_call(
        functools.partial(soap_kernel, sources, many),
        grid_spec=pltpu.PrefetchScalarGridSpec(
            num_scalar_prefetch=2,
            grid=(count // many,),
            in_specs=[picked(u, which) for u in range(many) for which in range(sources)] + [one] * 7,
            out_specs=[one] * 5 + [two] * 2,
        ),
        out_shape=[tile] * 5 + [pairs] * 2,
        compiler_params=pltpu.CompilerParams(vmem_limit_bytes=40 * 2**20),
        cost_estimate=pl.CostEstimate(flops=count * 60 * side**3, bytes_accessed=count * 18 * 4 * side**2, transcendentals=0),
    )(kind, index, *(list(grads) * many), weight, first, second, left, right, lstat, rstat)


def renew_kernel(many, turned_ref, inv_ref, left_out, right_out):
    for u in range(many):
        for which, out in ((0, left_out), (1, right_out)):
            out[u] = three(dot_nt, split2(turned_ref[u, which]), split2(inv_ref[u, which]))


def renew_bases(turned, inverse, many=6):
    count, _, side, _ = turned.shape
    one = pl.BlockSpec((many, side, side), lambda s: (s, 0, 0))
    two = pl.BlockSpec((many, 2, side, side), lambda s: (s, 0, 0, 0))
    tile = jax.ShapeDtypeStruct((count, side, side), jnp.float32)
    return pl.pallas_call(
        functools.partial(renew_kernel, many),
        grid=(count // many,),
        in_specs=[two, two],
        out_specs=[one, one],
        out_shape=[tile, tile],
        compiler_params=pltpu.CompilerParams(vmem_limit_bytes=40 * 2**20),
    )(turned, inverse)


def norm_joint_kernel(channels, x_ref, gain_ref, weight_ref, normed_ref, xs_ref, gate_ref):
    width = x_ref.shape[2]
    x = x_ref[...].astype(jnp.float32).reshape(-1, width)
    inverse = lax.rsqrt(jnp.mean(x * x, axis=1, keepdims=True) + norm_epsilon)
    normed = (x * inverse * gain_ref[...]).astype(jnp.bfloat16)
    normed_ref[...] = normed
    joint = dot_nn(normed, weight_ref[...]).astype(jnp.bfloat16)
    xs_ref[...] = joint[:, :channels]
    gate_ref[...] = joint[:, channels:]


def norm_joint(x, rows, gain, weight, many=2):
    devices, _, width = x.shape
    tokens, block = devices * rows, many * rows
    channels = weight.shape[1] // 2
    wide = pl.BlockSpec((block, width), lambda i: (i, 0))
    thin = pl.BlockSpec((block, channels), lambda i: (i, 0))
    half = jax.ShapeDtypeStruct((tokens, channels), jnp.bfloat16)
    return pl.pallas_call(
        functools.partial(norm_joint_kernel, channels),
        grid=(tokens // block,),
        in_specs=[
            pl.BlockSpec((many, rows, width), lambda i: (i, 0, 0)),
            pl.BlockSpec((1, width), lambda i: (0, 0)),
            pl.BlockSpec((width, 2 * channels), lambda i: (0, 0)),
        ],
        out_specs=[wide, thin, thin],
        out_shape=[jax.ShapeDtypeStruct((tokens, width), jnp.bfloat16), half, half],
        compiler_params=pltpu.CompilerParams(vmem_limit_bytes=32 * 2**20),
        cost_estimate=pl.CostEstimate(
            flops=4 * tokens * width * channels, bytes_accessed=4 * tokens * width, transcendentals=0
        ),
    )(x, gain, weight)


def plain_three(dot, left, right):
    return dot(left[0], right[0]) + (dot(left[0], right[1]) + dot(left[1], right[0]))


def channel_kernel(weight_ref, grad_ref, first_ref, second_ref, left_ref, right_ref, lstat_ref, rstat_ref,
                   first_out, second_out, weight_out, lstat_out, rstat_out, lturn_out, rturn_out, lgram_out, rgram_out):
    grad = split2(grad_ref[...])
    left, right = split2(left_ref[...]), split2(right_ref[...])
    turned = plain_three(dot_tn, left, split2(plain_three(dot_nn, grad, right)))
    first = beta_first * first_ref[...] + (1.0 - beta_first) * turned
    second = beta_second * second_ref[...] + (1.0 - beta_second) * turned * turned
    first_out[...] = first
    second_out[...] = second
    direction = split2(
        first / (1.0 - beta_first**STEP) / (jnp.sqrt(second / (1.0 - beta_second**STEP)) + adam_epsilon)
    )
    returned = plain_three(dot_nn, left, split2(plain_three(dot_nt, direction, right)))
    weight = weight_ref[...]
    weight_out[...] = weight - learn_rate * (returned + weight_decay * weight)
    for basis_ref, basis, stat_ref, product, stat_out, turn_out, gram_out in (
        (left_ref, left, lstat_ref, plain_three(dot_nt, grad, grad), lstat_out, lturn_out, lgram_out),
        (right_ref, right, rstat_ref, plain_three(dot_tn, grad, grad), rstat_out, rturn_out, rgram_out),
    ):
        order = basis_ref.shape[0]
        diagonal = lax.broadcasted_iota(jnp.int32, (order, order), 0) == lax.broadcasted_iota(
            jnp.int32, (order, order), 1
        )
        stat = stat_decay * stat_ref[...] + (1.0 - stat_decay) * product
        stat_out[...] = stat
        trace = jnp.sum(jnp.sum(jnp.where(diagonal, stat, 0.0), axis=0, keepdims=True), axis=1, keepdims=True)
        value = plain_three(dot_nn, split2(stat), basis) + (trace / order) * basis_ref[...]
        turn_out[...] = value
        value = split2(value)
        gram_out[...] = plain_three(dot_tn, value, value)


def channel_moments(weight, grad, first, second, left, right, lstat, rstat):
    f32 = jnp.float32
    rows = jax.ShapeDtypeStruct(weight.shape, f32)
    small = jax.ShapeDtypeStruct(left.shape, f32)
    large = jax.ShapeDtypeStruct(right.shape, f32)
    return pl.pallas_call(
        channel_kernel,
        out_shape=[rows] * 3 + [small, large] * 3,
        compiler_params=pltpu.CompilerParams(vmem_limit_bytes=40 * 2**20),
        cost_estimate=pl.CostEstimate(flops=8 * 10**9, bytes_accessed=6 * 10**6, transcendentals=0),
    )(weight, grad, first, second, left, right, lstat, rstat)


PANEL = 32


def factor_inverse(block):
    order = block.shape[0]
    rows = lax.broadcasted_iota(jnp.int32, (order, 2 * order), 0)
    columns = lax.broadcasted_iota(jnp.int32, (order, 2 * order), 1)
    both = jnp.concatenate([block, jnp.zeros_like(block)], axis=1) + jnp.where(columns == rows + order, 1.0, 0.0)
    for k in range(order):
        scale = lax.rsqrt(both[k : k + 1, k : k + 1])
        row = both[k : k + 1, :] * scale
        column = both[:, k : k + 1] * scale
        both = jnp.where(rows == k, row, jnp.where(rows > k, both - column * row, both))
    return both[:, order:]


def solve_kernel(count, *refs):
    grams, sides, outs = refs[:count], refs[count : 2 * count], refs[2 * count : 3 * count]
    works = refs[3 * count :]
    for i in range(count):
        order = grams[i].shape[0]
        gram, side = works[2 * i], works[2 * i + 1]
        gram[...] = grams[i][...]
        side[...] = sides[i][...]
        for start in range(0, order, PANEL):
            stop = start + PANEL
            low = split2(factor_inverse(gram[start:stop, start:stop]))
            upper = split2(plain_three(dot_nn, low, split2(gram[start:stop, :])))
            solved = plain_three(dot_nn, low, split2(side[start:stop, :]))
            outs[i][start:stop, :] = solved
            if stop < order:
                gram[stop:, :] -= plain_three(dot_tn, upper, upper)[stop:]
                side[stop:, :] -= plain_three(dot_tn, upper, split2(solved))[stop:]


def solve_factors(grams, sides):
    count = len(grams)
    shapes = [jax.ShapeDtypeStruct(s.shape, jnp.float32) for s in sides]
    scratch = []
    for g, s in zip(grams, sides):
        scratch += [pltpu.VMEM(g.shape, jnp.float32), pltpu.VMEM(s.shape, jnp.float32)]
    return pl.pallas_call(
        functools.partial(solve_kernel, count),
        out_shape=shapes,
        scratch_shapes=scratch,
        compiler_params=pltpu.CompilerParams(vmem_limit_bytes=40 * 2**20),
        cost_estimate=pl.CostEstimate(flops=4 * 10**10, bytes_accessed=3 * 10**6, transcendentals=0),
    )(*grams, *sides)


def doc_positions(doc_lengths):
    starts = jnp.cumsum(doc_lengths, axis=1) - doc_lengths
    places = jnp.arange(L, dtype=jnp.int32)
    begun = jnp.where(starts[:, None, :] <= places[None, :, None], starts[:, None, :], 0)
    return places[None, :] - jnp.max(begun, axis=2)


def adam_step(weight, gradient, first, second):
    first_new = beta_first * first + (1.0 - beta_first) * gradient
    second_new = beta_second * second + (1.0 - beta_second) * gradient * gradient
    direction = (
        first_new
        / (1.0 - beta_first**STEP)
        / (jnp.sqrt(second_new / (1.0 - beta_second**STEP)) + adam_epsilon)
    )
    return (first_new, second_new, weight - vector_rate * (direction + weight_decay * weight))


def later(values, lag):
    return jnp.pad(values, ((lag, 0), (0, 0)))[: values.shape[0]]


def sooner(values, lag):
    return jnp.pad(values, ((0, lag), (0, 0)))[lag:]


def conv_pre(xs, taps, offset, place):
    total = offset[None] + taps[K - 1][None] * xs
    for lag in range(1, K):
        total = total + jnp.where(place >= lag, taps[K - 1 - lag][None] * later(xs, lag), 0.0)
    return total


def rank_within(key):
    count = key.shape[0]
    earlier = jnp.arange(count)[None, :] < jnp.arange(count)[:, None]
    return jnp.sum(((key[None, :] == key[:, None]) & earlier).astype(jnp.int32), axis=1)


def table(size, target, chosen, value):
    hit = (target[None, :] == jnp.arange(size)[:, None]) & chosen[None, :]
    return jnp.sum(jnp.where(hit, value[None, :], 0), axis=1)


CAPS = {"all": (18, 13), "early": (15, 11), "late": (11, 8)}


class Routes:
    def __init__(self, tile_slot, devices, tiles_here, tall, half):
        count = tile_slot.shape[0]
        plane = devices // LINES
        wide = 2 * half
        tile = jnp.arange(count, dtype=jnp.int32)
        output = tile >= tall * wide
        relative = tile - tall * wide
        column = tile % wide
        self.plane = plane
        self.local = tile_slot % tiles_here
        self.owner = tile_slot // tiles_here
        self.target = jnp.where(output, relative // tall, column % half)
        self.kind = jnp.where(output, 2, column // half)
        self.place = jnp.where(output, 2 * tall + relative % tall, column // half * tall + tile // wide)
        self.odd = self.place % 2 == 1
        self.late = self.kind == 0
        self.owner_line, self.owner_spot = self.owner // plane, self.owner % plane
        self.target_line, self.target_spot = self.target // plane, self.target % plane
        self.middle = jnp.where(
            self.odd,
            self.owner_line * plane + self.target_spot,
            self.target_line * plane + self.owner_spot,
        )
        line_key = (self.owner_line * LINES + self.target_line) * plane + self.middle % plane
        plane_key = (self.owner_spot * plane + self.target_spot) * LINES + self.middle // plane
        line_key = line_key * 4 + 2 * self.odd.astype(jnp.int32)
        plane_key = plane_key * 4 + 2 * self.odd.astype(jnp.int32)
        late = self.late.astype(jnp.int32)
        self.forward = rank_within(line_key), rank_within(plane_key)
        self.backward = rank_within(line_key + late), rank_within(plane_key + late)
        self.fits = jnp.all((self.forward[0] < CAPS["all"][0]) & (self.forward[1] < CAPS["all"][1]))
        for which in range(2):
            cap = jnp.where(self.late, CAPS["late"][which], CAPS["early"][which])
            self.fits = self.fits & jnp.all(self.backward[which] < cap)

    def spots(self, ranks, caps, line_member, spot_member):
        by_line = line_member * caps[0] + ranks[0]
        by_plane = LINES * caps[0] + spot_member * caps[1] + ranks[1]
        return by_line, by_plane

    def to_targets(self, me):
        caps = CAPS["all"]
        size = LINES * caps[0] + self.plane * caps[1]
        out_line, out_plane = self.spots(self.forward, caps, self.target_line, self.target_spot)
        in_line, in_plane = self.spots(self.forward, caps, self.owner_line, self.owner_spot)
        first = table(size, jnp.where(self.odd, out_plane, out_line), self.owner == me, self.local)
        second = table(
            size, jnp.where(self.odd, out_line, out_plane), self.middle == me, jnp.where(self.odd, in_plane, in_line)
        )
        landed = jnp.where(self.odd, in_line, in_plane)
        return first, second, landed

    def to_owners(self, me, name, begin):
        caps = CAPS[name]
        chosen = self.late if name == "late" else ~self.late
        size = LINES * caps[0] + self.plane * caps[1]
        out_line, out_plane = self.spots(self.backward, caps, self.owner_line, self.owner_spot)
        in_line, in_plane = self.spots(self.backward, caps, self.target_line, self.target_spot)
        first = table(
            size, jnp.where(self.odd, out_line, out_plane), chosen & (self.target == me), self.place - begin
        )
        second = table(
            size, jnp.where(self.odd, out_plane, out_line), chosen & (self.middle == me),
            jnp.where(self.odd, in_line, in_plane),
        )
        landed = jnp.where(self.odd, in_plane, in_line)
        return first, second, landed


def device_groups(devices):
    plane = devices // LINES
    lines = [[z * plane + p for z in range(LINES)] for p in range(plane)]
    planes = [[z * plane + p for p in range(plane)] for z in range(LINES)]
    return lines, planes


def spread(value, devices):
    lines, planes = device_groups(devices)
    plane = devices // LINES
    step = lax.all_to_all(
        jnp.broadcast_to(value, (LINES,) + value.shape), "tok", 0, 0, tiled=True, axis_index_groups=lines
    )
    step = lax.all_to_all(
        jnp.broadcast_to(step, (plane,) + step.shape), "tok", 0, 0, tiled=True, axis_index_groups=planes
    )
    return jnp.swapaxes(step, 0, 1).reshape((devices * value.shape[0],) + value.shape[1:])


def fold(values, devices):
    lines, planes = device_groups(devices)
    plane = devices // LINES
    rows = values.shape[0] // devices
    parts = jnp.swapaxes(values.reshape((LINES, plane, rows) + values.shape[1:]), 0, 1).astype(jnp.bfloat16)
    parts = lax.all_to_all(parts, "tok", 0, 0, tiled=True, axis_index_groups=planes)
    parts = jnp.sum(parts.astype(jnp.float32), axis=0)
    parts = lax.all_to_all(parts, "tok", 0, 0, tiled=True, axis_index_groups=lines)
    return jnp.sum(parts, axis=0)


def core(
    routes,
    fast,
    layer_in,
    cotangent,
    doc_lengths,
    tile_slot,
    pool_weight,
    pool_first,
    pool_second,
    pool_left,
    pool_right,
    pool_left_stat,
    pool_right_stat,
    channel_weight,
    channel_first,
    channel_second,
    channel_left,
    channel_right,
    channel_left_stat,
    channel_right_stat,
    norm_gain,
    gain_first,
    gain_second,
    channel_vectors,
    vector_first,
    vector_second,
):
    bf16, f32 = jnp.bfloat16, jnp.float32
    devices = lax.axis_size("tok")
    me = lax.axis_index("tok")
    lines, planes = device_groups(devices)
    plane = devices // LINES
    my_line, my_plane = me // plane, me % plane
    tok_rows, model_width = layer_in.shape
    tokens = tok_rows * devices
    rows = tokens // L
    channels = channel_vectors.shape[1]
    inner_width = channels * devices
    tiles_here, side, _ = pool_weight.shape
    tall = model_width // side
    half = inner_width // side
    wide = 2 * half
    cut = side // channels
    input_tiles = tall * wide
    select_width = channel_weight.shape[1] - R
    select_here = channels * select_width
    gain_here = norm_gain.shape[0]

    select_rows = -(-select_here // model_width)
    tail_rows = -(-(1 + select_rows) // 16) * 16
    tail = jnp.zeros((tail_rows, model_width), bf16)
    tail = tail.at[0, :gain_here].set(norm_gain.astype(bf16))
    select_flat = jnp.pad(
        channel_weight[:, :select_width].astype(bf16).reshape(-1), (0, select_rows * model_width - select_here)
    )
    tail = tail.at[1 : 1 + select_rows].set(select_flat.reshape(select_rows, model_width))
    x_all = lax.all_gather(jnp.concatenate([layer_in, tail], axis=0), "tok", axis=0)
    gain_float = x_all[:, tok_rows, :gain_here].reshape(1, model_width).astype(f32)
    select_weight = x_all[:, tok_rows + 1 : tok_rows + 1 + select_rows].reshape(devices, -1)[:, :select_here]
    select_weight = select_weight.reshape(inner_width, select_width)
    pool_low = pool_weight.astype(bf16)
    slot_here = lambda target: target - me * tiles_here

    is_out = routes.kind == 2
    if fast:
        caps = CAPS["all"]
        first, second, landed = routes.to_targets(me)
        middle = route_stage(jnp.take(pool_low, first, axis=0), *caps, plane, 1)
        last = route_stage(jnp.take(middle, second, axis=0), *caps, plane, 2)
        tiles_own = jnp.take(last, table(3 * tall, routes.place, routes.target == me, landed), axis=0)
        input_own, output_own = tiles_own[: 2 * tall], tiles_own[2 * tall :]
    else:
        pool_all = lax.all_gather(pool_low, "tok", axis=0, tiled=True)
        columns = me // cut
        input_slots = tile_slot[:input_tiles].reshape(tall, 2, half)
        input_own = jnp.take(
            pool_all, lax.dynamic_index_in_dim(input_slots, columns, 2, False).T.reshape(-1), axis=0
        )
        output_slots = tile_slot[input_tiles:].reshape(half, tall)
        output_own = jnp.take(pool_all, lax.dynamic_index_in_dim(output_slots, columns, 0, False), axis=0)
    offset = me % cut * channels
    input_local = input_own.reshape(2, tall, side, side)
    output_local = output_own
    if cut > 1:
        input_local = lax.dynamic_slice_in_dim(input_local, offset, channels, axis=3)
        output_local = lax.dynamic_slice_in_dim(output_local, offset, channels, axis=1)
    input_local = input_local.transpose(1, 2, 0, 3).reshape(model_width, 2 * channels)
    output_local = output_local.transpose(1, 0, 2).reshape(channels, model_width)

    cotangent_later, input_local = lax.optimization_barrier((cotangent, input_local))
    normed_all, xs_low, gates = norm_joint(x_all, tok_rows, gain_float, input_local)
    cotangent_all = lax.all_gather(cotangent_later, "tok", axis=0, tiled=True)

    def to_tokens(values, number=None):
        lead = values.shape[:-2]
        parts = values.reshape(lead + (devices, tok_rows, channels))
        if fast and number is not None:
            moved = everyone(parts, number)
        else:
            moved = lax.all_to_all(parts, "tok", split_axis=len(lead), concat_axis=len(lead), tiled=True)
        moved = moved.reshape(lead + (half, cut, tok_rows, channels))
        return jnp.swapaxes(moved, -3, -2).reshape(lead + (half, tok_rows, side))

    place = doc_positions(doc_lengths).reshape(-1, 1)
    taps, offset = channel_vectors[:K], channel_vectors[K]
    xs = xs_low.astype(f32)
    filtered = jax.nn.silu(conv_pre(xs, taps, offset, place)).astype(bf16)
    filtered_tokens = to_tokens(filtered, 3)
    select_blocks = select_weight.reshape(half, side, select_width)
    if fast:
        block = jnp.concatenate(
            [
                jnp.einsum("gtc,gcf->tf", filtered_tokens, select_blocks[..., :R], preferred_element_type=f32),
                jnp.einsum("gtc,gcf->ft", filtered_tokens, select_blocks[..., R:], preferred_element_type=f32),
            ],
            axis=0,
        ).astype(bf16)
        blocks = spread_blocks(block, plane, 4).reshape(devices, tok_rows + 2 * N, R)
        rank_in = blocks[:, :tok_rows].reshape(tokens, R)
        state_in = blocks[:, tok_rows:].astype(f32)
        columns = state_in.reshape(devices, 2 * N, tok_rows // GROUP, GROUP).transpose(0, 2, 1, 3)
        state_in = state_in.transpose(0, 2, 1).reshape(tokens, 2 * N)
    else:
        projected = jnp.einsum("gtc,gcf->tf", filtered_tokens, select_blocks, preferred_element_type=f32)
        projected_all = spread(projected.astype(bf16), devices)
        rank_in = projected_all[:, :R]
        state_in = projected_all[:, R:].astype(f32)
        columns = state_in.reshape(tokens // GROUP, GROUP, 2 * N).transpose(0, 2, 1)
    back_chan = jnp.einsum("td,cd->tc", cotangent_all, output_local, preferred_element_type=f32).astype(bf16)

    if fast:
        pool_low, state_in = lax.optimization_barrier((pool_low, state_in))
        pool_all = lax.all_gather(pool_low, "tok", axis=0, tiled=True)

    by_row = lambda values: values.reshape((rows, L) + values.shape[1:])
    groups = L // GROUP
    columns = columns.reshape(rows, groups, 2 * N, GROUP)
    inject = state_in[:, :N].reshape(rows, groups, GROUP * N)
    readout = state_in[:, N:].reshape(rows, groups, GROUP * N)
    begins = by_row(jnp.broadcast_to(jnp.where(place == 0, 1e30, 0.0).astype(bf16), (tokens, channels)))
    step_local = channel_weight[:, select_width:].astype(bf16)
    rates = jnp.exp(channel_vectors[K + 2 : K + 2 + N])
    step_bias = channel_vectors[K + 1 : K + 2]
    skip_gain = channel_vectors[K + 2 + N :]
    scan_in = (by_row(filtered), by_row(rank_in), by_row(gates), by_row(back_chan), begins, columns)
    scan_params = (step_local, step_bias, rates, skip_gain)
    mixed, gate_grad, kept = scan_forward(*scan_in, readout, *scan_params)
    mixed = mixed.reshape(tokens, channels)
    gate_grad = gate_grad.reshape(tokens, channels)

    def input_part(grad):
        part = jnp.einsum("td,tc->dc", normed_all, grad, preferred_element_type=f32)
        return part.astype(bf16).reshape(tall, side, channels)

    output_part = jnp.einsum("tc,td->cd", mixed, cotangent_all, preferred_element_type=f32).astype(bf16)
    output_part = output_part.reshape(channels, tall, side).transpose(1, 0, 2)
    gate_part = input_part(gate_grad)

    def every_input(part):
        every = lax.all_gather(part, "tok", axis=0)
        every = every.reshape(half, cut, tall, side, channels).transpose(0, 2, 3, 1, 4)
        return every.reshape(half * tall, side, side)

    if fast:
        first_parts = jnp.concatenate([gate_part, output_part], axis=0)
        first_parts, kept = lax.optimization_barrier((first_parts, kept))
        early_first, early_second, early_landed = routes.to_owners(me, "early", tall)
        early_packed = jnp.take(first_parts, early_first, axis=0)
    else:
        output_every = lax.all_gather(output_part, "tok", axis=0)
        output_every = (
            output_every.reshape(half, cut, tall, channels, side)
            .transpose(0, 2, 1, 3, 4)
            .reshape(half * tall, side, side)
        )
        gate_every = every_input(gate_part)

    mixed_tokens = to_tokens(mixed)

    if fast:
        *scan_grads, early_middle = scan_backward(
            *scan_in, inject, *scan_params, kept, early_packed, CAPS["early"] + (plane,), 6
        )
        early = route_stage(jnp.take(early_middle, early_second, axis=0), *CAPS["early"], plane, 7)
    else:
        scan_grads = scan_backward(*scan_in, inject, *scan_params, kept)
    draw, filter_mix, inject_grad, read_grad, rate_sum, skip_grad, bias_grad = scan_grads
    draw = draw.reshape(tokens, channels)
    step_grad = jnp.einsum("tc,tr->cr", draw, rank_in, preferred_element_type=f32)
    rank_part = jnp.einsum("tc,cr->tr", draw, step_local, preferred_element_type=f32)
    state_part = jnp.concatenate([inject_grad.reshape(tokens, N), read_grad.reshape(tokens, N)], axis=1)
    if fast:
        parts = jnp.concatenate(
            [
                rank_part.astype(bf16).reshape(devices, tok_rows, R),
                state_part.astype(bf16).reshape(devices, tok_rows, 2 * N).transpose(0, 2, 1),
            ],
            axis=1,
        )
        blocks = fold_and_spread(parts.reshape(LINES, plane, tok_rows + 2 * N, R), plane, 5)
        blocks = blocks.reshape(devices, tok_rows + 2 * N, R)
        projected_grad_all = jnp.concatenate(
            [
                blocks[:, :tok_rows].reshape(tokens, R),
                blocks[:, tok_rows:].transpose(0, 2, 1).reshape(tokens, 2 * N),
            ],
            axis=1,
        )
    else:
        partial_sums = jnp.concatenate([rank_part, state_part], axis=1)
        projected_grad_all = spread(fold(partial_sums, devices).astype(bf16), devices)
    select_local = channel_weight[:, :select_width].astype(bf16)
    back_filter = jnp.einsum(
        "tf,cf->tc", projected_grad_all, select_local, preferred_element_type=f32
    ).astype(bf16)
    select_grad = jnp.einsum("tc,tf->cf", filtered, projected_grad_all, preferred_element_type=f32)
    pre = conv_pre(xs, taps, offset, place)
    gate = jax.nn.sigmoid(pre)
    dpre = (filter_mix.reshape(tokens, channels) + back_filter.astype(f32)) * (gate * (1.0 + pre * (1.0 - gate)))
    offset_grad = jnp.sum(dpre, axis=0)
    taps_grad = [jnp.sum(dpre * xs, axis=0)]
    xs_grad = taps[K - 1][None] * dpre
    for lag in range(1, K):
        masked = jnp.where(place >= lag, dpre, 0.0)
        xs_grad = xs_grad + taps[K - 1 - lag][None] * sooner(masked, lag)
        taps_grad.insert(0, jnp.sum(masked * later(xs, lag), axis=0))
    xs_grad = xs_grad.astype(bf16)
    xs_part = input_part(xs_grad)
    if fast:
        late_first, late_second, late_landed = routes.to_owners(me, "late", 0)
        late_middle = route_stage(jnp.take(xs_part, late_first, axis=0), *CAPS["late"], plane, 8)
        late = route_stage(jnp.take(late_middle, late_second, axis=0), *CAPS["late"], plane, 9)
    else:
        xs_every = every_input(xs_part)

    own_slot = tile_slot - me * tiles_here
    every_tile = jnp.full(tile_slot.shape, True)
    if fast:
        grads = (late, early)
        kind = table(tiles_here, own_slot, every_tile, (~routes.late).astype(jnp.int32))
        index = table(tiles_here, own_slot, every_tile, jnp.where(routes.late, late_landed, early_landed))
    else:
        grads = (xs_every, gate_every, output_every)
        tile = jnp.arange(tile_slot.shape[0], dtype=jnp.int32)
        kind = table(tiles_here, own_slot, every_tile, routes.kind)
        spot = jnp.where(is_out, tile - input_tiles, tile % wide % half * tall + tile // wide)
        index = table(tiles_here, own_slot, every_tile, spot)
    first_next, second_next, weight_next, lstat_next, rstat_next, turned, gram = soap_tiles(
        kind,
        index,
        grads,
        pool_weight,
        pool_first,
        pool_second,
        pool_left,
        pool_right,
        pool_left_stat,
        pool_right_stat,
    )
    inverse_low = inverse_factor(gram.reshape(2 * tiles_here, side, side)).reshape(gram.shape)
    left_next, right_next = renew_bases(turned, inverse_low)

    joint_grad = to_tokens(jnp.stack([xs_grad, gate_grad])).reshape(wide, tok_rows, side)
    layer_out = tile_product(
        mixed_tokens, pool_all, tile_slot[input_tiles:].reshape(half, tall).T, False, bf16, layer_in
    )
    normed_grad = tile_product(
        joint_grad, pool_all, tile_slot[:input_tiles].reshape(tall, wide), True, f32
    )
    input_float = layer_in.astype(f32)
    inverse = lax.rsqrt(jnp.mean(input_float * input_float, axis=1, keepdims=True) + norm_epsilon)
    scaled = normed_grad * gain_float
    input_grad = (
        cotangent.astype(f32)
        + inverse * scaled
        - input_float * inverse**3 * jnp.mean(scaled * input_float, axis=1, keepdims=True)
    )
    gain_part = jnp.sum(normed_grad * input_float * inverse, axis=0).reshape(devices, gain_here)
    gain_grad = jnp.sum(lax.all_to_all(gain_part, "tok", split_axis=0, concat_axis=0, tiled=True), axis=0)

    first_c, second_c, weight_c, lstat_c, rstat_c, left_turned, right_turned, left_gram, right_gram = channel_moments(
        channel_weight,
        jnp.concatenate([select_grad, step_grad], axis=1),
        channel_first,
        channel_second,
        channel_left,
        channel_right,
        channel_left_stat,
        channel_right_stat,
    )
    left_c, right_c = solve_factors((left_gram, right_gram), (left_turned.T, right_turned.T))
    channel_new = (first_c, second_c, weight_c, left_c.T, right_c.T, lstat_c, rstat_c)
    gain_new = adam_step(norm_gain, gain_grad, gain_first, gain_second)
    vector_grad = jnp.concatenate(
        [jnp.stack(taps_grad), offset_grad[None], bias_grad, -rates * rate_sum, skip_grad], axis=0
    )
    vector_new = adam_step(channel_vectors, vector_grad, vector_first, vector_second)
    return (
        layer_out,
        input_grad,
        first_next,
        second_next,
        weight_next,
        left_next,
        right_next,
        lstat_next,
        rstat_next,
        *channel_new,
        *gain_new,
        *vector_new,
    )


def shards(*args):
    devices = lax.axis_size("tok")
    layer_in, tile_slot, pool_weight, channel_vectors = args[0], args[3], args[4], args[21]
    tiles_here, side, _ = pool_weight.shape
    channels = channel_vectors.shape[1]
    routes = Routes(tile_slot, devices, tiles_here, layer_in.shape[1] // side, channels * devices // side)
    if channels != side or devices % LINES or layer_in.shape[0] != R:
        return core(routes, False, *args)
    return lax.cond(routes.fits, functools.partial(core, routes, True), functools.partial(core, routes, False), *args)


def solution(mesh):
    line, flat, cube, column = P("tok"), P("tok", None), P("tok", None, None), P(None, "tok")
    in_specs = (flat, flat, P(), P()) + (cube,) * 7 + (flat,) * 7 + (line,) * 3 + (column,) * 3
    out_specs = (flat, flat) + (cube,) * 7 + (flat,) * 7 + (line,) * 3 + (column,) * 3
    return jax.shard_map(shards, mesh=mesh, in_specs=in_specs, out_specs=out_specs, check_vma=False)
```

```python
import functools

import jax
import jax.numpy as jnp
from jax import lax
from jax.experimental import pallas as pl
from jax.experimental.pallas import tpu as pltpu
from jax.sharding import PartitionSpec as P

N = 16
R = 128
K = 4
L = 2048
STEP = 5
GROUP = 16
LOG2E = 1.4426950408889634

beta_first = 0.5
beta_second = 0.5
stat_decay = 0.5
learn_rate = 0.02
vector_rate = 0.2
weight_decay = 0.01
adam_epsilon = 1e-08
norm_epsilon = 1e-05
highest = lax.Precision.HIGHEST


LINES = 4
MESH = pl.DeviceIdType.MESH


def greet(line, spot, plane):
    barrier = pltpu.get_barrier_semaphore()
    for k in range(1, LINES):
        pl.semaphore_signal(barrier, inc=1, device_id=((line + k) % LINES * plane + spot,), device_id_type=MESH)
    for k in range(1, plane):
        pl.semaphore_signal(barrier, inc=1, device_id=(line * plane + (spot + k) % plane,), device_id_type=MESH)
    pl.semaphore_wait(barrier, LINES + plane - 2)


def remote(source, target, send, recv, device):
    return pltpu.make_async_remote_copy(
        src_ref=source, dst_ref=target, send_sem=send, recv_sem=recv, device_id=(device,), device_id_type=MESH
    )


def ride_copies(spec, source, out, sems):
    kind, plane = spec[:2]
    me = lax.axis_index("tok")
    line, spot = me // plane, me % plane
    if kind == "line":
        send, recv, own = sems
        copies = [pltpu.make_async_copy(source.at[line], out.at[line], own.at[0])]
        for k in range(1, LINES):
            place = (line + k) % LINES
            copies.append(remote(source.at[place], out.at[line], send.at[k], recv.at[k], place * plane + spot))
        return copies
    if kind == "plane":
        send, recv, own = sems
        copies = [pltpu.make_async_copy(source.at[:, spot], out.at[spot], own.at[0])]
        for k in range(1, plane):
            place = (spot + k) % plane
            copies.append(remote(source.at[:, place], out.at[spot], send.at[k], recv.at[k], line * plane + place))
        return copies
    cap_line, cap_plane = spec[2:]
    line_send, line_recv, plane_send, plane_recv, own = sems
    start = LINES * cap_line

    def to_line(place):
        return pl.ds(place * cap_line, cap_line)

    def to_plane(place):
        return pl.ds(start + place * cap_plane, cap_plane)

    copies = [
        pltpu.make_async_copy(source.at[to_line(line)], out.at[to_line(line)], own.at[0]),
        pltpu.make_async_copy(source.at[to_plane(spot)], out.at[to_plane(spot)], own.at[1]),
    ]
    for k in range(1, LINES):
        place = (line + k) % LINES
        copies.append(
            remote(source.at[to_line(place)], out.at[to_line(line)], line_send.at[k], line_recv.at[k], place * plane + spot)
        )
    for k in range(1, plane):
        place = (spot + k) % plane
        copies.append(
            remote(source.at[to_plane(place)], out.at[to_plane(spot)], plane_send.at[k], plane_recv.at[k], line * plane + place)
        )
    return copies


def ride_sems(spec):
    kind, plane = spec[:2]
    if kind == "line":
        return [pltpu.SemaphoreType.DMA((LINES,))] * 2 + [pltpu.SemaphoreType.DMA((1,))]
    if kind == "plane":
        return [pltpu.SemaphoreType.DMA((plane,))] * 2 + [pltpu.SemaphoreType.DMA((1,))]
    return [pltpu.SemaphoreType.DMA((LINES,))] * 2 + [pltpu.SemaphoreType.DMA((plane,))] * 2 + [pltpu.SemaphoreType.DMA((2,))]


def ride_shape(spec, value):
    shape = value.shape
    if spec[0] == "plane":
        shape = (shape[1], shape[0]) + shape[2:]
    return jax.ShapeDtypeStruct(shape, value.dtype)


class Riders:
    def __init__(self, specs):
        self.specs = tuple(specs)

    def all_copies(self, sources, outs, sems):
        copies, at = [], 0
        for spec, source, out in zip(self.specs, sources, outs):
            count = len(ride_sems(spec))
            copies += ride_copies(spec, source, out, sems[at : at + count])
            at += count
        return copies

    def begin(self, sources, outs, sems):
        plane = self.specs[0][1]
        me = lax.axis_index("tok")
        greet(me // plane, me % plane, plane)
        for copy in self.all_copies(sources, outs, sems):
            copy.start()

    def end(self, sources, outs, sems):
        for copy in self.all_copies(sources, outs, sems):
            copy.wait()

    def sems(self):
        return [sem for spec in self.specs for sem in ride_sems(spec)]

    def shapes(self, values):
        return [ride_shape(spec, value) for spec, value in zip(self.specs, values)]


def riders_kernel(riders, *refs):
    count = len(riders.specs)
    sources, outs, sems = refs[:count], refs[count : 2 * count], refs[2 * count :]
    riders.begin(sources, outs, sems)
    riders.end(sources, outs, sems)


HBM = pl.BlockSpec(memory_space=pl.ANY)


def exchange(specs, values, number):
    riders = Riders(specs)
    return pl.pallas_call(
        functools.partial(riders_kernel, riders),
        in_specs=[HBM] * len(values),
        out_specs=[HBM] * len(values),
        out_shape=riders.shapes(values),
        scratch_shapes=riders.sems(),
        compiler_params=pltpu.CompilerParams(collective_id=number, has_side_effects=True),
    )(*values)


def everyone_kernel(devices, source, out, send, recv, own):
    me = lax.axis_index("tok")
    barrier = pltpu.get_barrier_semaphore()
    for k in range(1, devices):
        pl.semaphore_signal(barrier, inc=1, device_id=((me + k) % devices,), device_id_type=MESH)
    pl.semaphore_wait(barrier, devices - 1)
    copies = [pltpu.make_async_copy(source.at[me], out.at[me], own.at[0])]
    for k in range(1, devices):
        target = (me + k) % devices
        copies.append(remote(source.at[target], out.at[me], send.at[k], recv.at[k], target))
    for copy in copies:
        copy.start()
    for copy in copies:
        copy.wait()


def everyone(values, number):
    devices = values.shape[0]
    return pl.pallas_call(
        functools.partial(everyone_kernel, devices),
        in_specs=[HBM],
        out_specs=HBM,
        out_shape=jax.ShapeDtypeStruct(values.shape, values.dtype),
        scratch_shapes=[pltpu.SemaphoreType.DMA((devices,))] * 2 + [pltpu.SemaphoreType.DMA((1,))],
        compiler_params=pltpu.CompilerParams(collective_id=number, has_side_effects=True),
    )(values)


def spread_steps(plane, block, out, sems):
    line_send, line_recv, plane_send, plane_recv, own = sems
    me = lax.axis_index("tok")
    line, spot = me // plane, me % plane
    copies = [pltpu.make_async_copy(block, out.at[line, spot], own.at[0])]
    arrivals = []
    for k in range(1, LINES):
        place = (line + k) % LINES
        arrivals.append(remote(block, out.at[line, spot], line_send.at[k], line_recv.at[k], place * plane + spot))
    for k in range(1, plane):
        place = (spot + k) % plane
        copies.append(
            remote(block, out.at[line, spot], plane_send.at[0, k], plane_recv.at[0, k], line * plane + place)
        )
    for copy in arrivals + copies:
        copy.start()
    for k in range(1, LINES):
        arrivals[k - 1].wait_recv()
        origin = (line + LINES - k) % LINES
        for j in range(1, plane):
            place = (spot + j) % plane
            copy = remote(
                out.at[origin, spot], out.at[origin, spot], plane_send.at[k, j], plane_recv.at[k, j], line * plane + place
            )
            copy.start()
            copies.append(copy)
    for copy in arrivals:
        copy.wait_send()
    for copy in copies:
        copy.wait()


def spread_sems(plane):
    return (
        [pltpu.SemaphoreType.DMA((LINES,))] * 2
        + [pltpu.SemaphoreType.DMA((LINES, plane))] * 2
        + [pltpu.SemaphoreType.DMA((1,))]
    )


def spread_kernel(plane, block, out, *sems):
    me = lax.axis_index("tok")
    greet(me // plane, me % plane, plane)
    spread_steps(plane, block, out, sems)


def spread_blocks(block, plane, number):
    return pl.pallas_call(
        functools.partial(spread_kernel, plane),
        in_specs=[HBM],
        out_specs=HBM,
        out_shape=jax.ShapeDtypeStruct((LINES, plane) + block.shape, block.dtype),
        scratch_shapes=spread_sems(plane),
        compiler_params=pltpu.CompilerParams(collective_id=number, has_side_effects=True),
    )(block)


def fold_kernel(plane, riders, parts, *refs):
    count = len(riders.specs)
    sources, out, outs = refs[:count], refs[count], refs[count + 1 : 2 * count + 1]
    got, sent, last, block, plane_send, plane_recv, line_send, line_recv, own = refs[2 * count + 1 : 2 * count + 10]
    own_sems = len(spread_sems(plane))
    sems, ride = refs[2 * count + 10 : 2 * count + 10 + own_sems], refs[2 * count + 10 + own_sems :]
    me = lax.axis_index("tok")
    line, spot = me // plane, me % plane
    greet(line, spot, plane)
    copies = [pltpu.make_async_copy(parts.at[:, spot], got.at[spot], own.at[0])]
    for k in range(1, plane):
        place = (spot + k) % plane
        copies.append(
            remote(parts.at[:, place], got.at[spot], plane_send.at[k], plane_recv.at[k], line * plane + place)
        )
    for copy in copies:
        copy.start()
    guests = riders.all_copies(sources, outs, ride)
    for copy in guests:
        copy.start()
    for copy in copies:
        copy.wait()
    for z in range(LINES):
        total = got[0, z].astype(jnp.float32)
        for k in range(1, plane):
            total = total + got[k, z].astype(jnp.float32)
        sent[z] = total
    copies = [pltpu.make_async_copy(sent.at[line], last.at[line], own.at[1])]
    for k in range(1, LINES):
        place = (line + k) % LINES
        copies.append(remote(sent.at[place], last.at[line], line_send.at[k], line_recv.at[k], place * plane + spot))
    for copy in copies:
        copy.start()
    for copy in copies:
        copy.wait()
    block[...] = ((last[0] + last[1]) + (last[2] + last[3])).astype(block.dtype)
    spread_steps(plane, block, out, sems)
    for copy in guests:
        copy.wait()


def fold_and_spread(parts, plane, number, specs=(), values=()):
    shape = parts.shape[2:]
    riders = Riders(specs)
    return pl.pallas_call(
        functools.partial(fold_kernel, plane, riders),
        in_specs=[HBM] * (1 + len(values)),
        out_specs=[HBM] * (1 + len(values)),
        out_shape=[jax.ShapeDtypeStruct(parts.shape, parts.dtype)] + riders.shapes(values),
        scratch_shapes=[
            pltpu.VMEM((plane, LINES) + shape, parts.dtype),
            pltpu.VMEM((LINES,) + shape, jnp.float32),
            pltpu.VMEM((LINES,) + shape, jnp.float32),
            pltpu.VMEM(shape, parts.dtype),
        ]
        + [pltpu.SemaphoreType.DMA((plane,))] * 2
        + [pltpu.SemaphoreType.DMA((LINES,))] * 2
        + [pltpu.SemaphoreType.DMA((2,))]
        + spread_sems(plane)
        + riders.sems(),
        compiler_params=pltpu.CompilerParams(collective_id=number, has_side_effects=True, vmem_limit_bytes=16 * 2**20),
    )(parts, *values)


def dot_nt(left, right):
    return lax.dot_general(left, right, (((1,), (1,)), ((), ())), preferred_element_type=jnp.float32)

def dot_nn(left, right):
    return jnp.dot(left, right, preferred_element_type=jnp.float32)

def softplus(v):
    return jnp.maximum(v, 0.0) + jnp.log1p(jnp.exp(-jnp.abs(v)))

def split2(v):
    high = v.astype(jnp.bfloat16)
    return high, (v - high.astype(jnp.float32)).astype(jnp.bfloat16)

def own_token(dtype):
    token = lax.broadcasted_iota(jnp.int32, (GROUP, GROUP * N), 0)
    column = lax.broadcasted_iota(jnp.int32, (GROUP, GROUP * N), 1)
    return (column // N == token).astype(dtype)

def slice_columns(block_ref, cols_s, r, chunk):
    values = block_ref[0, chunk:].astype(jnp.float32)
    for g in range(chunk // GROUP):
        cols_s[r, g] = values[:, g * GROUP : (g + 1) * GROUP]


def lay_out(block_ref, inject_s, read_s, r, chunk):
    token = lax.broadcasted_iota(jnp.int32, (chunk, GROUP * N), 0) % GROUP
    column = lax.broadcasted_iota(jnp.int32, (chunk, GROUP * N), 1)
    mine = column // N == token
    for start, rows_s in ((chunk, inject_s), (chunk + N, read_s)):
        if rows_s is not None:
            rows_s[r] = jnp.where(mine, repeat_columns(block_ref[0, start : start + N]), 0).astype(jnp.bfloat16)


def repeat_columns(values):
    state = lax.broadcasted_iota(jnp.int32, (N, GROUP * N), 0)
    column = lax.broadcasted_iota(jnp.int32, (N, GROUP * N), 1)
    chosen = (column % N == state).astype(jnp.bfloat16)
    product = lax.dot_general(
        values, chosen, (((0,), (0,)), ((), ())), preferred_element_type=jnp.float32
    )
    return product


def fwd_kernel(pair, chunk, f_ref, z_ref, start_ref, *refs):
    block_refs, refs = refs[:pair], refs[pair:]
    stepw_ref, bias_ref, rate_ref, skip_ref, mixed_ref, dz_ref, keep_ref, state, step_s, drive_s, scan_s, cols_s, read_s = refs
    groups = chunk // GROUP
    neg = rate_ref[...] * (-LOG2E)
    @pl.when(pl.program_id(1) == 0)
    def _():
        state[...] = jnp.zeros_like(state)

    for r in range(pair):
        raw = dot_nt(block_refs[r][0, :chunk], stepw_ref[...])
        step = softplus(raw + bias_ref[...])
        slice_columns(block_refs[r], cols_s, r, chunk)
        lay_out(block_refs[r], None, read_s, r, chunk)
        step_s[r] = step + start_ref[r].astype(jnp.float32)
        drive_s[r] = step * f_ref[r].astype(jnp.float32)
        keep_ref[r, 0] = state[r]

    def group(g, hidden):
        hidden = list(hidden)
        held = [[] for _ in range(pair)]
        base = pl.multiple_of(g * GROUP, GROUP)
        cols = [cols_s[r, g] for r in range(pair)]
        for k in range(GROUP):
            for r in range(pair):
                factor = jnp.exp2(step_s[r, pl.ds(base + k, 1), :] * neg)
                hidden[r] = factor * hidden[r] + drive_s[r, pl.ds(base + k, 1), :] * cols[r][:N, k : k + 1]
                held[r].append(hidden[r].astype(jnp.bfloat16))
        for r in range(pair):
            states = jnp.concatenate(held[r], axis=0)
            scan_s[r, pl.ds(base, GROUP), :] = dot_nn(read_s[r, pl.ds(base, GROUP), :], states)
        return tuple(hidden)

    hidden = lax.fori_loop(0, groups, group, tuple(state[r] for r in range(pair)), unroll=groups)
    for r in range(pair):
        state[r] = hidden[r]
        f = f_ref[r].astype(jnp.float32)
        z = z_ref[r].astype(jnp.float32)
        gate = 1.0 / (1.0 + jnp.exp(-z))
        summed = scan_s[r] + skip_ref[...] * f
        mixed_ref[r] = (summed * (z * gate)).astype(jnp.bfloat16)
        dz_ref[r] = summed * (gate * (1.0 + z * (1.0 - gate)))

def bwd_kernel(pair, chunk, riders, f_ref, z_ref, gm_ref, start_ref, *refs):
    block_refs, refs = refs[:pair], refs[pair:]
    stepw_ref, bias_ref, rate_ref, skip_ref, keep_ref = refs[:5]
    refs = refs[5:]
    count = len(riders.specs)
    sources, refs = refs[:count], refs[count:]
    draw_ref, dfm_ref, dinj_ref, dread_ref, drate_ref, dskip_ref, dbias_ref = refs[:7]
    outs, refs = refs[7 : 7 + count], refs[7 + count :]
    carry_s, step_s, drive_s, dscan_s, raw_s, delta_s, a_s, ah_s, h_s, s1_s, s2_s, cols_s, inject_s = refs[:13]
    if count:

        @pl.when((pl.program_id(0) == 0) & (pl.program_id(1) == 0))
        def _():
            riders.begin(sources, outs, refs[13:])

    groups = chunk // GROUP
    rate = rate_ref[...]
    neg = rate * (-LOG2E)
    mine = own_token(jnp.bfloat16)
    mine_f = own_token(jnp.float32)

    @pl.when(pl.program_id(1) == 0)
    def _():
        carry_s[...] = jnp.zeros_like(carry_s)

    @pl.when((pl.program_id(1) == 0) & (pl.program_id(0) == 0))
    def _():
        drate_ref[...] = jnp.zeros_like(drate_ref)
        dskip_ref[...] = jnp.zeros_like(dskip_ref)
        dbias_ref[...] = jnp.zeros_like(dbias_ref)

    for r in range(pair):
        raw = dot_nt(block_refs[r][0, :chunk], stepw_ref[...]) + bias_ref[...]
        slice_columns(block_refs[r], cols_s, r, chunk)
        lay_out(block_refs[r], inject_s, None, r, chunk)
        step = softplus(raw)
        raw_s[r] = raw
        delta_s[r] = step
        step_s[r] = step + start_ref[r].astype(jnp.float32)
        f = f_ref[r].astype(jnp.float32)
        drive_s[r] = step * f
        z = z_ref[r].astype(jnp.float32)
        gate = 1.0 / (1.0 + jnp.exp(-z))
        dscan = gm_ref[r].astype(jnp.float32) * (z * gate)
        dscan_s[r] = dscan
        dskip_ref[...] += jnp.sum(dscan * f, axis=0, keepdims=True)

    def forward(g, hidden):
        hidden = list(hidden)
        base = pl.multiple_of(g * GROUP, GROUP)
        cols = [cols_s[r, g] for r in range(pair)]
        held = [[] for _ in range(pair)]
        for k in range(GROUP):
            for r in range(pair):
                factor = jnp.exp2(step_s[r, pl.ds(base + k, 1), :] * neg)
                kept = factor * hidden[r]
                hidden[r] = kept + drive_s[r, pl.ds(base + k, 1), :] * cols[r][:N, k : k + 1]
                a_s[r, base + k] = factor
                ah_s[r, base + k] = kept
                held[r].append(hidden[r].astype(jnp.bfloat16))
        for r in range(pair):
            h_s[r, g] = jnp.concatenate(held[r], axis=0)
        return tuple(hidden)

    lax.fori_loop(0, groups, forward, tuple(keep_ref[r, 0] for r in range(pair)), unroll=groups)

    def backward(i, carried):
        g = groups - 1 - i
        base = pl.multiple_of(g * GROUP, GROUP)
        ag = list(carried[:pair])
        total = carried[pair]
        cols = [cols_s[r, g] for r in range(pair)]
        gs = [[None] * GROUP for _ in range(pair)]
        qs = [[None] * GROUP for _ in range(pair)]
        for k in reversed(range(GROUP)):
            for r in range(pair):
                grad = dscan_s[r, pl.ds(base + k, 1), :] * cols[r][N:, k : k + 1] + ag[r]
                ag[r] = a_s[r, base + k] * grad
                q = grad * ah_s[r, base + k]
                total = total + delta_s[r, pl.ds(base + k, 1), :] * q
                gs[r][k] = grad.astype(jnp.bfloat16)
                qs[r][k] = (rate * q).astype(jnp.bfloat16)
        for r in range(pair):
            grads = jnp.concatenate(gs[r], axis=0)
            pulls = jnp.concatenate(qs[r], axis=0)
            s1_s[r, pl.ds(base, GROUP), :] = dot_nn(inject_s[r, pl.ds(base, GROUP), :], grads)
            s2_s[r, pl.ds(base, GROUP), :] = dot_nn(mine, pulls)
            dh, dl = split2(dscan_s[r, pl.ds(base, GROUP), :])
            uh, ul = split2(drive_s[r, pl.ds(base, GROUP), :])
            dr = dot_nt(jnp.concatenate([dh, dl], axis=0), h_s[r, g])
            dread_ref[r, pl.ds(g, 1), :] = jnp.sum((dr[:GROUP] + dr[GROUP:]) * mine_f, axis=0, keepdims=True)
            di = dot_nt(jnp.concatenate([uh, ul], axis=0), grads)
            dinj_ref[r, pl.ds(g, 1), :] = jnp.sum((di[:GROUP] + di[GROUP:]) * mine_f, axis=0, keepdims=True)
        return tuple(ag) + (total,)

    out = lax.fori_loop(
        0, groups, backward, tuple(carry_s[r] for r in range(pair)) + (jnp.zeros_like(rate),), unroll=groups
    )
    drate_ref[...] += out[pair]
    for r in range(pair):
        carry_s[r] = out[r]
        f = f_ref[r].astype(jnp.float32)
        draw = (f * s1_s[r] - s2_s[r]) / (1.0 + jnp.exp(-raw_s[r]))
        draw_ref[r] = draw.astype(jnp.bfloat16)
        dbias_ref[...] += jnp.sum(draw, axis=0, keepdims=True)
        dfm_ref[r] = delta_s[r] * s1_s[r] + skip_ref[...] * dscan_s[r]

    if count:

        @pl.when((pl.program_id(0) == pl.num_programs(0) - 1) & (pl.program_id(1) == pl.num_programs(1) - 1))
        def _():
            riders.end(sources, outs, refs[13:])


def specs(pair, chunk, ch, blocks, back, chunks):
    def at(i, j):
        return (i, chunks - 1 - j if back else j)
    tok = pl.BlockSpec((pair, chunk, ch), lambda i, j: at(i, j) + (0,))
    flat = pl.BlockSpec((pair, chunk // GROUP, GROUP * N), lambda i, j: at(i, j) + (0,))
    keep = pl.BlockSpec((pair, 1, N, ch), lambda i, j: at(i, j) + (0, 0))
    def block(r):
        def index(i, j):
            i, j = at(i, j)
            return ((i * pair + r) * chunks + j, 0, 0)
        return pl.BlockSpec((1,) + blocks.shape[1:], index)
    def whole(a):
        return pl.BlockSpec(a.shape, lambda i, j: (0,) * a.ndim)
    return tok, [block(r) for r in range(pair)], flat, keep, whole

def scan_forward(f, z, start, blocks, stepw, bias, rate, skip):
    chunk = blocks.shape[1] - 2 * N
    rows, length, ch = f.shape
    pair = 2 if rows % 2 == 0 else 1
    chunks = length // chunk
    tok, block_specs, flat, keep, whole = specs(pair, chunk, ch, blocks, False, chunks)
    return pl.pallas_call(
        functools.partial(fwd_kernel, pair, chunk),
        grid=(rows // pair, chunks),
        in_specs=[tok, tok, tok] + block_specs + [whole(stepw), whole(bias), whole(rate), whole(skip)],
        out_specs=[tok, tok, keep],
        out_shape=[jax.ShapeDtypeStruct(f.shape, jnp.bfloat16), jax.ShapeDtypeStruct(f.shape, jnp.float32),
                   jax.ShapeDtypeStruct((rows, chunks, N, ch), jnp.float32)],
        scratch_shapes=[pltpu.VMEM((pair, N, ch), jnp.float32)] + [pltpu.VMEM((pair, chunk, ch), jnp.float32)] * 3
        + [pltpu.VMEM((pair, chunk // GROUP, 2 * N, GROUP), jnp.float32)]
        + [pltpu.VMEM((pair, chunk, GROUP * N), jnp.bfloat16)],
        compiler_params=pltpu.CompilerParams(vmem_limit_bytes=40 * 2**20),
        cost_estimate=pl.CostEstimate(flops=4 * 10**10, bytes_accessed=8 * 10**6, transcendentals=0),
    )(f, z, start, *([blocks] * pair), stepw, bias, rate, skip)

def scan_backward(f, z, gm, start, blocks, stepw, bias, rate, skip, kept, rides=(), guests=(), number=None):
    chunk = blocks.shape[1] - 2 * N
    rows, length, ch = f.shape
    pair = 2 if rows % 2 == 0 else 1
    chunks = length // chunk
    tok, block_specs, flat, keep, whole = specs(pair, chunk, ch, blocks, True, chunks)
    f32 = jnp.float32
    row = jax.ShapeDtypeStruct((1, ch), f32)
    in_specs = [tok, tok, tok, tok] + block_specs + [whole(stepw), whole(bias), whole(rate), whole(skip), keep]
    inj = jax.ShapeDtypeStruct((rows, length // GROUP, GROUP * N), f32)
    out_specs = [tok, tok, flat, flat, whole(rate), whole(row), whole(row)]
    out_shape = [jax.ShapeDtypeStruct(f.shape, jnp.bfloat16), jax.ShapeDtypeStruct(f.shape, f32),
                 jax.ShapeDtypeStruct(inj.shape, f32), jax.ShapeDtypeStruct(inj.shape, f32),
                 jax.ShapeDtypeStruct(rate.shape, f32), row, row]
    scratch = ([pltpu.VMEM((pair, N, ch), f32)] + [pltpu.VMEM((pair, chunk, ch), f32)] * 5
               + [pltpu.VMEM((pair, chunk, N, ch), f32)] * 2
               + [pltpu.VMEM((pair, chunk // GROUP, GROUP * N, ch), jnp.bfloat16)]
               + [pltpu.VMEM((pair, chunk, ch), f32)] * 2
               + [pltpu.VMEM((pair, chunk // GROUP, 2 * N, GROUP), f32)]
               + [pltpu.VMEM((pair, chunk, GROUP * N), jnp.bfloat16)])
    values = (f, z, gm, start, *([blocks] * pair), stepw, bias, rate, skip, kept)
    params = dict(vmem_limit_bytes=40 * 2**20)
    riders = Riders(rides)
    if guests:
        in_specs, out_specs = in_specs + [HBM] * len(guests), out_specs + [HBM] * len(guests)
        out_shape = out_shape + riders.shapes(guests)
        scratch = scratch + riders.sems()
        values = values + tuple(guests)
        params.update(collective_id=number, has_side_effects=True)
    return pl.pallas_call(
        functools.partial(bwd_kernel, pair, chunk, riders),
        grid=(rows // pair, chunks),
        in_specs=in_specs,
        out_specs=out_specs,
        out_shape=out_shape,
        scratch_shapes=scratch,
        compiler_params=pltpu.CompilerParams(**params),
        cost_estimate=pl.CostEstimate(flops=7 * 10**10, bytes_accessed=8 * 10**6, transcendentals=0),
    )(*values)


DEPTH = 4
BATCH = 16


def tile_product_kernel(pairs, steps, transposed, residual, idx_ref, left_ref, pool_ref, *refs):
    if residual:
        res_ref, refs = refs[0], refs[1:]
    out_ref, slots, sems = refs
    side = slots.shape[2]
    total_steps = pairs * steps

    def fetch(step):
        for u in range(BATCH):
            pltpu.make_async_copy(
                pool_ref.at[idx_ref[step * BATCH + u]], slots.at[step % DEPTH, u], sems.at[step % DEPTH]
            ).start()

    for step in range(min(DEPTH - 1, total_steps)):
        fetch(step)

    def one_pair(o, carry):
        total = jnp.zeros((left_ref.shape[1], 2 * side), jnp.float32)
        for k in range(steps):
            step = o * steps + k

            @pl.when(step + DEPTH - 1 < total_steps)
            def _():
                fetch(step + DEPTH - 1)

            slot = step % DEPTH
            pltpu.make_async_copy(slots.at[slot], slots.at[slot], sems.at[slot]).wait()
            for u in range(0, BATCH, 4):
                at = k * (BATCH // 2) + u // 2
                left = jnp.concatenate([left_ref[at], left_ref[at + 1]], axis=1)
                tile = [slots[slot, u + v] for v in range(4)]
                if transposed:
                    right = jnp.concatenate(
                        [jnp.concatenate([tile[0], tile[2]], axis=1), jnp.concatenate([tile[1], tile[3]], axis=1)], axis=0
                    )
                    total += dot_nt(left, right)
                else:
                    right = jnp.concatenate(
                        [jnp.concatenate([tile[0], tile[1]], axis=1), jnp.concatenate([tile[2], tile[3]], axis=1)], axis=0
                    )
                    total += dot_nn(left, right)
        columns = pl.ds(pl.multiple_of(o * 2 * side, side), 2 * side)
        if residual:
            total += res_ref[:, columns].astype(jnp.float32)
        out_ref[:, columns] = total.astype(out_ref.dtype)
        return carry

    lax.fori_loop(0, pairs, one_pair, 0)


def tile_product(left, pool, index, transposed, dtype, residual=None):
    outs, depth = index.shape
    pairs, steps = outs // 2, 2 * depth // BATCH
    side = pool.shape[1]
    tok = left.shape[1]
    vmem = pl.BlockSpec(memory_space=pltpu.VMEM)
    extra = [residual] if residual is not None else []
    order = index.reshape(pairs, 2, depth).transpose(0, 2, 1).reshape(-1).astype(jnp.int32)
    return pl.pallas_call(
        functools.partial(tile_product_kernel, pairs, steps, transposed, residual is not None),
        in_specs=[pl.BlockSpec(memory_space=pltpu.SMEM), vmem, pl.BlockSpec(memory_space=pl.ANY)] + [vmem] * len(extra),
        out_specs=vmem,
        out_shape=jax.ShapeDtypeStruct((tok, outs * side), dtype),
        scratch_shapes=[pltpu.VMEM((DEPTH, BATCH, side, side), pool.dtype), pltpu.SemaphoreType.DMA((DEPTH,))],
        compiler_params=pltpu.CompilerParams(vmem_limit_bytes=40 * 2**20),
        cost_estimate=pl.CostEstimate(
            flops=2 * outs * depth * tok * side * side, bytes_accessed=outs * depth * side * side * 2, transcendentals=0
        ),
    )(order, left, pool, *extra)


def dot_tn(left, right):
    return lax.dot_general(left, right, (((0,), (0,)), ((), ())), preferred_element_type=jnp.float32)


def three(dot, left, right):
    left_axis, right_axis = {dot_nn: (1, 0), dot_nt: (1, 1), dot_tn: (0, 0)}[dot]
    return dot(
        jnp.concatenate([left[0], left[0], left[1]], axis=left_axis),
        jnp.concatenate([right[0], right[1], right[0]], axis=right_axis),
    )


def soap_kernel(sources, many, kind_ref, idx_ref, *refs):
    grad_refs, refs = refs[: sources * many], refs[sources * many :]
    weight_ref, first_ref, second_ref, left_ref, right_ref, lstat_ref, rstat_ref = refs[:7]
    first_out, second_out, weight_out, lstat_out, rstat_out, turned_out, gram_out = refs[7:]
    side = weight_ref.shape[1]
    diagonal = lax.broadcasted_iota(jnp.int32, (side, side), 0) == lax.broadcasted_iota(jnp.int32, (side, side), 1)
    every = range(many)
    grads, lefts, rights = [], [], []
    for u in every:
        kind = kind_ref[pl.program_id(0) * many + u]
        grad = grad_refs[u * sources][0]
        for which in range(1, sources):
            grad = jnp.where(kind == which, grad_refs[u * sources + which][0], grad)
        grads.append(grad)
        lefts.append(split2(left_ref[u]))
        rights.append(split2(right_ref[u]))
    across = [split2(dot_nn(grads[u], rights[u][0]) + dot_nn(grads[u], rights[u][1])) for u in every]
    turned = [three(dot_tn, lefts[u], across[u]) for u in every]
    products = [(dot_nt(grads[u], grads[u]), dot_tn(grads[u], grads[u])) for u in every]
    directions = []
    for u in every:
        first = beta_first * first_ref[u] + (1.0 - beta_first) * turned[u]
        second = beta_second * second_ref[u] + (1.0 - beta_second) * turned[u] * turned[u]
        first_out[u] = first
        second_out[u] = second
        directions.append(split2(
            first / (1.0 - beta_first**STEP) / (jnp.sqrt(second / (1.0 - beta_second**STEP)) + adam_epsilon)
        ))
    renewed = []
    for u in every:
        for which, (stat_ref, basis_ref, basis2, stat_out) in enumerate(
            ((lstat_ref, left_ref, lefts[u], lstat_out), (rstat_ref, right_ref, rights[u], rstat_out))
        ):
            stat = stat_decay * stat_ref[u] + (1.0 - stat_decay) * products[u][which]
            stat_out[u] = stat
            trace = jnp.sum(jnp.sum(jnp.where(diagonal, stat, 0.0), axis=0, keepdims=True), axis=1, keepdims=True)
            value = three(dot_nn, split2(stat), basis2) + (trace / side) * basis_ref[u]
            turned_out[u, which] = value
            renewed.append(split2(value))
    back = [split2(three(dot_nt, directions[u], rights[u])) for u in every]
    for u in every:
        for which in range(2):
            gram_out[u, which] = three(dot_tn, renewed[u * 2 + which], renewed[u * 2 + which])
    for u in every:
        weight = weight_ref[u]
        weight_out[u] = weight - learn_rate * (three(dot_nn, lefts[u], back[u]) + weight_decay * weight)


def soap_tiles(kind, index, grads, weight, first, second, left, right, lstat, rstat, many=4):
    count, side, _ = weight.shape
    one = pl.BlockSpec((many, side, side), lambda s, kind, idx: (s, 0, 0))
    two = pl.BlockSpec((many, 2, side, side), lambda s, kind, idx: (s, 0, 0, 0))

    def picked(u, which):
        def at(s, kind, idx):
            return (jnp.where(kind[s * many + u] == which, idx[s * many + u], 0), 0, 0)

        return pl.BlockSpec((1, side, side), at)

    tile = jax.ShapeDtypeStruct(weight.shape, jnp.float32)
    pairs = jax.ShapeDtypeStruct((count, 2, side, side), jnp.float32)
    sources = len(grads)
    return pl.pallas_call(
        functools.partial(soap_kernel, sources, many),
        grid_spec=pltpu.PrefetchScalarGridSpec(
            num_scalar_prefetch=2,
            grid=(count // many,),
            in_specs=[picked(u, which) for u in range(many) for which in range(sources)] + [one] * 7,
            out_specs=[one] * 5 + [two] * 2,
        ),
        out_shape=[tile] * 5 + [pairs] * 2,
        compiler_params=pltpu.CompilerParams(vmem_limit_bytes=40 * 2**20),
        cost_estimate=pl.CostEstimate(flops=count * 60 * side**3, bytes_accessed=count * 18 * 4 * side**2, transcendentals=0),
    )(kind, index, *(list(grads) * many), weight, first, second, left, right, lstat, rstat)


def chol_kernel(batch, order, riders, gram_ref, turned_ref, *refs):
    count = len(riders.specs)
    sources, basis_refs, outs = refs[:count], refs[count : count + 2], refs[count + 2 : 2 * count + 2]
    low_ref, inv_ref, piv_ref, out_ref = refs[2 * count + 2 : 2 * count + 6]
    ride_sems_here = refs[2 * count + 6 :]
    if count:
        riders.begin(sources, outs, ride_sems_here)
    tiles = order // 8
    rows8 = lax.broadcasted_iota(jnp.int32, (8, batch), 0)

    def load_slab(j, carry):
        low_ref[j, pl.ds(0, order), :] = gram_ref[pl.ds(j, batch, stride=order), :].T
        inv_ref[j] = jnp.zeros(inv_ref.shape[1:], jnp.float32)
        return carry

    lax.fori_loop(0, order, load_slab, 0, unroll=8)

    def bcast(ref, j, row):
        return jnp.broadcast_to(ref[j, pl.ds(row, 1), :], (8, batch))

    def block_column(block, carry):
        base = pl.multiple_of(block * 8, 8)

        def updated(tile_rows, seed):
            def one(j, accs):
                mult = [bcast(low_ref, j, base + k) for k in range(8)]
                out = []
                for s, rows in enumerate(tile_rows):
                    piece = low_ref[j, pl.ds(rows, 8), :]
                    out.extend(accs[s * 8 + k] - piece * mult[k] for k in range(8))
                return tuple(out)

            def eight(step, accs):
                for u in range(8):
                    accs = one(step * 8 + u, accs)
                return accs

            return list(lax.fori_loop(0, block, eight, tuple(seed)))

        accs = updated([base], [low_ref[base + k, pl.ds(base, 8), :] for k in range(8)])
        scales = []
        for k in range(8):
            scale = lax.rsqrt(jnp.broadcast_to(accs[k][k : k + 1, :], (8, batch)))
            scales.append(scale)
            accs[k] = jnp.where(rows8 >= k, accs[k] * scale, 0.0)
            for later in range(k + 1, 8):
                accs[later] = accs[later] - accs[k] * jnp.broadcast_to(
                    accs[k][later : later + 1, :], (8, batch)
                )
        for k in range(8):
            low_ref[base + k, pl.ds(base, 8), :] = accs[k]
            piv_ref[base + k] = scales[k]

        def pair(p, carry):
            first = pl.multiple_of(base + 8 + p * 16, 8)
            both = [first, pl.multiple_of(first + 8, 8)]
            accs = updated(
                both, [low_ref[base + k, pl.ds(rows, 8), :] for rows in both for k in range(8)]
            )
            for k in range(8):
                scale = piv_ref[base + k]
                for s in range(2):
                    accs[s * 8 + k] = accs[s * 8 + k] * scale
                for later in range(k + 1, 8):
                    mult = bcast(low_ref, base + k, base + later)
                    for s in range(2):
                        accs[s * 8 + later] = accs[s * 8 + later] - accs[s * 8 + k] * mult
            for s, rows in enumerate(both):
                for k in range(8):
                    low_ref[base + k, pl.ds(rows, 8), :] = accs[s * 8 + k]
            return carry

        lax.fori_loop(0, (tiles - block) // 2, pair, 0)
        return carry

    lax.fori_loop(0, tiles, block_column, 0)

    def block_row(block, carry):
        base = pl.multiple_of(block * 8, 8)

        def finish(accs, both):
            for k in range(8):
                scale = piv_ref[base + k]
                for s in range(len(both)):
                    accs[s * 8 + k] = accs[s * 8 + k] * scale
                for later in range(k + 1, 8):
                    mult = bcast(low_ref, base + k, base + later)
                    for s in range(len(both)):
                        accs[s * 8 + later] = accs[s * 8 + later] - accs[s * 8 + k] * mult
            for s, columns in enumerate(both):
                for k in range(8):
                    inv_ref[base + k, pl.ds(columns, 8), :] = accs[s * 8 + k]

        def pair(p, carry):
            first = pl.multiple_of(p * 16, 8)
            both = [first, pl.multiple_of(first + 8, 8)]

            def eight(step, accs):
                for u in range(8):
                    j = step * 8 + u
                    mult = [bcast(low_ref, j, base + k) for k in range(8)]
                    out = []
                    for s, columns in enumerate(both):
                        piece = inv_ref[j, pl.ds(columns, 8), :]
                        out.extend(accs[s * 8 + k] - piece * mult[k] for k in range(8))
                    accs = tuple(out)
                return accs

            accs = list(lax.fori_loop(
                p * 2, block, eight, (jnp.zeros((8, batch), jnp.float32),) * 16
            ))
            finish(accs, both)
            return carry

        lax.fori_loop(0, (block + 1) // 2, pair, 0)
        odd = block % 2

        def diagonal():
            accs = [jnp.where(rows8 == k, 1.0, 0.0) for k in range(8)]
            finish(accs, [base])

        diagonal()
        return carry

    lax.fori_loop(0, tiles, block_row, 0)

    def store_slab(i, carry):
        out_ref[pl.ds(i, batch, stride=order), :] = inv_ref[i, pl.ds(0, order), :].T
        return carry

    lax.fori_loop(0, order, store_slab, 0, unroll=8)

    many = 4

    def renew(step, carry):
        for u in range(many):
            for which in range(2):
                at = (step * many + u) * 2 + which
                inverse = out_ref[pl.ds(pl.multiple_of(at * order, order), order), :]
                basis_refs[which][step * many + u] = three(dot_nt, split2(turned_ref[at]), split2(inverse))
        return carry

    lax.fori_loop(0, batch // (2 * many), renew, 0)
    if count:
        riders.end(sources, outs, ride_sems_here)

def renewed_bases(gram, turned, rides=(), guests=(), number=None):
    count, _, order, _ = gram.shape
    batch = 2 * count
    riders = Riders(rides)
    params = dict(vmem_limit_bytes=58 * 2**20)
    if guests:
        params.update(collective_id=number, has_side_effects=True)
    vmem = pl.BlockSpec(memory_space=pltpu.VMEM)
    basis = jax.ShapeDtypeStruct((count, order, order), jnp.float32)
    return pl.pallas_call(
        functools.partial(chol_kernel, batch, order, riders),
        out_shape=[basis, basis] + riders.shapes(guests),
        in_specs=[vmem, vmem] + [HBM] * len(guests),
        out_specs=[vmem, vmem] + [HBM] * len(guests),
        scratch_shapes=[
            pltpu.VMEM((order, order + 8, batch), jnp.float32),
            pltpu.VMEM((order, order + 8, batch), jnp.float32),
            pltpu.VMEM((order, 8, batch), jnp.float32),
            pltpu.VMEM((batch * order, order), jnp.float32),
        ]
        + riders.sems(),
        compiler_params=pltpu.CompilerParams(**params),
        cost_estimate=pl.CostEstimate(flops=5 * 10**10, bytes_accessed=12 * 10**6, transcendentals=0),
    )(gram.reshape(batch * order, order), turned.reshape(batch, order, order), *guests)


def norm_joint_kernel(channels, x_ref, gain_ref, weight_ref, normed_ref, xs_ref, gate_ref):
    width = x_ref.shape[2]
    x = x_ref[...].astype(jnp.float32).reshape(-1, width)
    inverse = lax.rsqrt(jnp.mean(x * x, axis=1, keepdims=True) + norm_epsilon)
    normed = (x * inverse * gain_ref[...]).astype(jnp.bfloat16)
    normed_ref[...] = normed
    joint = dot_nn(normed, weight_ref[...]).astype(jnp.bfloat16)
    xs_ref[...] = joint[:, :channels]
    gate_ref[...] = joint[:, channels:]


def norm_joint(x, rows, gain, weight, many=2):
    devices, _, width = x.shape
    tokens, block = devices * rows, many * rows
    channels = weight.shape[1] // 2
    wide = pl.BlockSpec((block, width), lambda i: (i, 0))
    thin = pl.BlockSpec((block, channels), lambda i: (i, 0))
    half = jax.ShapeDtypeStruct((tokens, channels), jnp.bfloat16)
    return pl.pallas_call(
        functools.partial(norm_joint_kernel, channels),
        grid=(tokens // block,),
        in_specs=[
            pl.BlockSpec((many, rows, width), lambda i: (i, 0, 0)),
            pl.BlockSpec((1, width), lambda i: (0, 0)),
            pl.BlockSpec((width, 2 * channels), lambda i: (0, 0)),
        ],
        out_specs=[wide, thin, thin],
        out_shape=[jax.ShapeDtypeStruct((tokens, width), jnp.bfloat16), half, half],
        compiler_params=pltpu.CompilerParams(vmem_limit_bytes=32 * 2**20),
        cost_estimate=pl.CostEstimate(
            flops=4 * tokens * width * channels, bytes_accessed=4 * tokens * width, transcendentals=0
        ),
    )(x, gain, weight)


def plane_product_kernel(count, many, weight_ref, *refs):
    lefts, out_ref, total_ref = refs[:count], refs[count], refs[count + 1]
    step = pl.program_id(0)
    left = jnp.concatenate([ref[u] for u in range(many) for ref in lefts], axis=1)
    part = dot_nt(left, jnp.concatenate([weight_ref[u] for u in range(many)], axis=1))

    @pl.when(step == 0)
    def _():
        total_ref[...] = part

    @pl.when(step > 0)
    def _():
        total_ref[...] += part

    @pl.when(step == pl.num_programs(0) - 1)
    def _():
        out_ref[...] = total_ref[...].astype(out_ref.dtype)


def plane_product(lefts, weight, block, many=4):
    members, tokens, channels = lefts[0].shape
    rows, width = len(lefts) * channels, weight.shape[1]
    return pl.pallas_call(
        functools.partial(plane_product_kernel, len(lefts), many),
        grid=(members // many,),
        in_specs=[pl.BlockSpec((many, width, rows), lambda p: (p, 0, block))]
        + [pl.BlockSpec((many, tokens, channels), lambda p: (p, 0, 0))] * len(lefts),
        out_specs=pl.BlockSpec((tokens, width), lambda p: (0, 0)),
        out_shape=jax.ShapeDtypeStruct((tokens, width), jnp.bfloat16),
        scratch_shapes=[pltpu.VMEM((tokens, width), jnp.float32)],
        compiler_params=pltpu.CompilerParams(vmem_limit_bytes=48 * 2**20),
        cost_estimate=pl.CostEstimate(
            flops=2 * members * tokens * rows * width, bytes_accessed=2 * members * rows * width, transcendentals=0
        ),
    )(weight, *lefts)


def plain_three(dot, left, right):
    return dot(left[0], right[0]) + (dot(left[0], right[1]) + dot(left[1], right[0]))


def channel_kernel(weight_ref, grad_ref, first_ref, second_ref, left_ref, right_ref, lstat_ref, rstat_ref,
                   first_out, second_out, weight_out, lstat_out, rstat_out, lturn_out, rturn_out, lgram_out, rgram_out):
    grad = split2(grad_ref[...])
    left, right = split2(left_ref[...]), split2(right_ref[...])
    turned = plain_three(dot_tn, left, split2(plain_three(dot_nn, grad, right)))
    first = beta_first * first_ref[...] + (1.0 - beta_first) * turned
    second = beta_second * second_ref[...] + (1.0 - beta_second) * turned * turned
    first_out[...] = first
    second_out[...] = second
    direction = split2(
        first / (1.0 - beta_first**STEP) / (jnp.sqrt(second / (1.0 - beta_second**STEP)) + adam_epsilon)
    )
    returned = plain_three(dot_nn, left, split2(plain_three(dot_nt, direction, right)))
    weight = weight_ref[...]
    weight_out[...] = weight - learn_rate * (returned + weight_decay * weight)
    for basis_ref, basis, stat_ref, product, stat_out, turn_out, gram_out in (
        (left_ref, left, lstat_ref, plain_three(dot_nt, grad, grad), lstat_out, lturn_out, lgram_out),
        (right_ref, right, rstat_ref, plain_three(dot_tn, grad, grad), rstat_out, rturn_out, rgram_out),
    ):
        order = basis_ref.shape[0]
        diagonal = lax.broadcasted_iota(jnp.int32, (order, order), 0) == lax.broadcasted_iota(
            jnp.int32, (order, order), 1
        )
        stat = stat_decay * stat_ref[...] + (1.0 - stat_decay) * product
        stat_out[...] = stat
        trace = jnp.sum(jnp.sum(jnp.where(diagonal, stat, 0.0), axis=0, keepdims=True), axis=1, keepdims=True)
        value = plain_three(dot_nn, split2(stat), basis) + (trace / order) * basis_ref[...]
        turn_out[...] = value
        value = split2(value)
        gram_out[...] = plain_three(dot_tn, value, value)


def channel_moments(weight, grad, first, second, left, right, lstat, rstat):
    f32 = jnp.float32
    rows = jax.ShapeDtypeStruct(weight.shape, f32)
    small = jax.ShapeDtypeStruct(left.shape, f32)
    large = jax.ShapeDtypeStruct(right.shape, f32)
    return pl.pallas_call(
        channel_kernel,
        out_shape=[rows] * 3 + [small, large] * 3,
        compiler_params=pltpu.CompilerParams(vmem_limit_bytes=40 * 2**20),
        cost_estimate=pl.CostEstimate(flops=8 * 10**9, bytes_accessed=6 * 10**6, transcendentals=0),
    )(weight, grad, first, second, left, right, lstat, rstat)


PANEL = 32


def factor_inverse(block):
    order = block.shape[0]
    rows = lax.broadcasted_iota(jnp.int32, (order, 2 * order), 0)
    columns = lax.broadcasted_iota(jnp.int32, (order, 2 * order), 1)
    both = jnp.concatenate([block, jnp.zeros_like(block)], axis=1) + jnp.where(columns == rows + order, 1.0, 0.0)
    for k in range(order):
        scale = lax.rsqrt(both[k : k + 1, k : k + 1])
        row = both[k : k + 1, :] * scale
        column = both[:, k : k + 1] * scale
        both = jnp.where(rows == k, row, jnp.where(rows > k, both - column * row, both))
    return both[:, order:]


def solve_kernel(count, riders, *refs):
    guests = len(riders.specs)
    grams, sides, refs = refs[:count], refs[count : 2 * count], refs[2 * count :]
    sources, outs, refs = refs[:guests], refs[guests : guests + count], refs[guests + count :]
    arrived, works, ride = refs[:guests], refs[guests : guests + 2 * count], refs[guests + 2 * count :]
    if guests:
        riders.begin(sources, arrived, ride)
    for i in range(count):
        order = grams[i].shape[0]
        gram, side = works[2 * i], works[2 * i + 1]
        gram[...] = grams[i][...]
        side[...] = sides[i][...]
        for start in range(0, order, PANEL):
            stop = start + PANEL
            low = split2(factor_inverse(gram[start:stop, start:stop]))
            upper = split2(plain_three(dot_nn, low, split2(gram[start:stop, :])))
            solved = plain_three(dot_nn, low, split2(side[start:stop, :]))
            outs[i][start:stop, :] = solved
            if stop < order:
                gram[stop:, :] -= plain_three(dot_tn, upper, upper)[stop:]
                side[stop:, :] -= plain_three(dot_tn, upper, split2(solved))[stop:]
    if guests:
        riders.end(sources, arrived, ride)


def solve_factors(grams, sides, rides=(), guests=(), number=None):
    count = len(grams)
    riders = Riders(rides)
    params = dict(vmem_limit_bytes=40 * 2**20)
    if guests:
        params.update(collective_id=number, has_side_effects=True)
    shapes = [jax.ShapeDtypeStruct(s.shape, jnp.float32) for s in sides]
    scratch = []
    for g, s in zip(grams, sides):
        scratch += [pltpu.VMEM(g.shape, jnp.float32), pltpu.VMEM(s.shape, jnp.float32)]
    vmem = pl.BlockSpec(memory_space=pltpu.VMEM)
    return pl.pallas_call(
        functools.partial(solve_kernel, count, riders),
        in_specs=[vmem] * (2 * count) + [HBM] * len(guests),
        out_specs=[vmem] * count + [HBM] * len(guests),
        out_shape=shapes + riders.shapes(guests),
        scratch_shapes=scratch + riders.sems(),
        compiler_params=pltpu.CompilerParams(**params),
        cost_estimate=pl.CostEstimate(flops=4 * 10**10, bytes_accessed=3 * 10**6, transcendentals=0),
    )(*grams, *sides, *guests)


def doc_positions(doc_lengths):
    starts = jnp.cumsum(doc_lengths, axis=1) - doc_lengths
    places = jnp.arange(L, dtype=jnp.int32)
    begun = jnp.where(starts[:, None, :] <= places[None, :, None], starts[:, None, :], 0)
    return places[None, :] - jnp.max(begun, axis=2)


def adam_step(weight, gradient, first, second):
    first_new = beta_first * first + (1.0 - beta_first) * gradient
    second_new = beta_second * second + (1.0 - beta_second) * gradient * gradient
    direction = (
        first_new
        / (1.0 - beta_first**STEP)
        / (jnp.sqrt(second_new / (1.0 - beta_second**STEP)) + adam_epsilon)
    )
    return (first_new, second_new, weight - vector_rate * (direction + weight_decay * weight))


def later(values, lag):
    return jnp.pad(values, ((lag, 0), (0, 0)))[: values.shape[0]]


def sooner(values, lag):
    return jnp.pad(values, ((0, lag), (0, 0)))[lag:]


def conv_pre(xs, taps, offset, place):
    total = offset[None] + taps[K - 1][None] * xs
    for lag in range(1, K):
        total = total + jnp.where(place >= lag, taps[K - 1 - lag][None] * later(xs, lag), 0.0)
    return total


def rank_within(key):
    count = key.shape[0]
    earlier = jnp.arange(count)[None, :] < jnp.arange(count)[:, None]
    return jnp.sum(((key[None, :] == key[:, None]) & earlier).astype(jnp.int32), axis=1)


def table(size, target, chosen, value):
    hit = (target[None, :] == jnp.arange(size)[:, None]) & chosen[None, :]
    return jnp.sum(jnp.where(hit, value[None, :], 0), axis=1)


CAPS = {"all": (13, 9), "early": (10, 7), "late": (7, 6)}


class Routes:
    def __init__(self, tile_slot, devices, tiles_here, tall, half):
        count = tile_slot.shape[0]
        plane = devices // LINES
        wide = 2 * half
        tile = jnp.arange(count, dtype=jnp.int32)
        output = tile >= tall * wide
        relative = tile - tall * wide
        column = tile % wide
        self.plane = plane
        self.local = tile_slot % tiles_here
        self.owner = tile_slot // tiles_here
        self.target = jnp.where(output, relative // tall, column % half)
        self.kind = jnp.where(output, 2, column // half)
        self.place = jnp.where(output, 2 * tall + relative % tall, column // half * tall + tile // wide)
        self.late = self.kind == 0
        self.owner_line, self.owner_spot = self.owner // plane, self.owner % plane
        self.target_line, self.target_spot = self.target // plane, self.target % plane
        group = self.late.astype(jnp.int32)
        back_caps = [jnp.where(self.late, CAPS["late"][which], CAPS["early"][which]) for which in range(2)]
        self.forward, fits = self.settle(jnp.zeros_like(group), CAPS["all"])
        self.backward, back_fits = self.settle(group, back_caps)
        self.fits = fits & back_fits

    def settle(self, group, caps):
        odd = self.place % 2 == 1
        for attempt in range(2):
            middle = jnp.where(
                odd, self.owner_line * self.plane + self.target_spot, self.target_line * self.plane + self.owner_spot
            )
            kind = 2 * odd.astype(jnp.int32) + group
            line_key = (self.owner_line * LINES + self.target_line) * self.plane + middle % self.plane
            plane_key = (self.owner_spot * self.plane + self.target_spot) * LINES + middle // self.plane
            ranks = rank_within(line_key * 4 + kind), rank_within(plane_key * 4 + kind)
            full = (ranks[0] >= caps[0]) | (ranks[1] >= caps[1])
            if attempt == 0:
                odd = odd ^ full
        return (odd, middle, *ranks), ~jnp.any(full)

    def spots(self, ways, caps, line_member, spot_member):
        by_line = line_member * caps[0] + ways[2]
        by_plane = LINES * caps[0] + spot_member * caps[1] + ways[3]
        return by_line, by_plane

    def to_targets(self, me):
        caps = CAPS["all"]
        odd, middle = self.forward[:2]
        size = LINES * caps[0] + self.plane * caps[1]
        out_line, out_plane = self.spots(self.forward, caps, self.target_line, self.target_spot)
        in_line, in_plane = self.spots(self.forward, caps, self.owner_line, self.owner_spot)
        first = table(size, jnp.where(odd, out_plane, out_line), self.owner == me, self.local)
        second = table(size, jnp.where(odd, out_line, out_plane), middle == me, jnp.where(odd, in_plane, in_line))
        landed = jnp.where(odd, in_line, in_plane)
        return first, second, landed

    def to_owners(self, me, name, begin):
        caps = CAPS[name]
        odd, middle = self.backward[:2]
        chosen = self.late if name == "late" else ~self.late
        size = LINES * caps[0] + self.plane * caps[1]
        out_line, out_plane = self.spots(self.backward, caps, self.owner_line, self.owner_spot)
        in_line, in_plane = self.spots(self.backward, caps, self.target_line, self.target_spot)
        first = table(size, jnp.where(odd, out_line, out_plane), chosen & (self.target == me), self.place - begin)
        second = table(
            size, jnp.where(odd, out_plane, out_line), chosen & (middle == me), jnp.where(odd, in_line, in_plane)
        )
        landed = jnp.where(odd, in_plane, in_line)
        return first, second, landed


def pick(values, index):
    return values.at[index].get(mode="clip")


def device_groups(devices):
    plane = devices // LINES
    lines = [[z * plane + p for z in range(LINES)] for p in range(plane)]
    planes = [[z * plane + p for p in range(plane)] for z in range(LINES)]
    return lines, planes


def spread(value, devices):
    lines, planes = device_groups(devices)
    plane = devices // LINES
    step = lax.all_to_all(
        jnp.broadcast_to(value, (LINES,) + value.shape), "tok", 0, 0, tiled=True, axis_index_groups=lines
    )
    step = lax.all_to_all(
        jnp.broadcast_to(step, (plane,) + step.shape), "tok", 0, 0, tiled=True, axis_index_groups=planes
    )
    return jnp.swapaxes(step, 0, 1).reshape((devices * value.shape[0],) + value.shape[1:])


def fold(values, devices):
    lines, planes = device_groups(devices)
    plane = devices // LINES
    rows = values.shape[0] // devices
    parts = jnp.swapaxes(values.reshape((LINES, plane, rows) + values.shape[1:]), 0, 1).astype(jnp.bfloat16)
    parts = lax.all_to_all(parts, "tok", 0, 0, tiled=True, axis_index_groups=planes)
    parts = jnp.sum(parts.astype(jnp.float32), axis=0)
    parts = lax.all_to_all(parts, "tok", 0, 0, tiled=True, axis_index_groups=lines)
    return jnp.sum(parts, axis=0)


def core(
    routes,
    fast,
    x_all,
    weights,
    layer_in,
    cotangent,
    doc_lengths,
    tile_slot,
    pool_weight,
    pool_first,
    pool_second,
    pool_left,
    pool_right,
    pool_left_stat,
    pool_right_stat,
    channel_weight,
    channel_first,
    channel_second,
    channel_left,
    channel_right,
    channel_left_stat,
    channel_right_stat,
    norm_gain,
    gain_first,
    gain_second,
    channel_vectors,
    vector_first,
    vector_second,
):
    bf16, f32 = jnp.bfloat16, jnp.float32
    devices = lax.axis_size("tok")
    me = lax.axis_index("tok")
    lines, planes = device_groups(devices)
    plane = devices // LINES
    my_line, my_plane = me // plane, me % plane
    tok_rows, model_width = layer_in.shape
    tokens = tok_rows * devices
    rows = tokens // L
    channels = channel_vectors.shape[1]
    inner_width = channels * devices
    tiles_here, side, _ = pool_weight.shape
    tall = model_width // side
    half = inner_width // side
    wide = 2 * half
    cut = side // channels
    input_tiles = tall * wide
    select_width = channel_weight.shape[1] - R
    select_here = channels * select_width
    gain_here = norm_gain.shape[0]

    select_rows = -(-select_here // model_width)
    gain_float = x_all[:, tok_rows, :gain_here].reshape(1, model_width).astype(f32)
    select_weight = x_all[:, tok_rows + 1 : tok_rows + 1 + select_rows].reshape(devices, -1)[:, :select_here]
    select_weight = select_weight.reshape(inner_width, select_width)
    if not fast:
        pool_low = pool_weight.astype(bf16)

    is_out = routes.kind == 2
    if fast:
        input_local, output_local, plane_own = weights
    else:
        pool_all = lax.all_gather(pool_low, "tok", axis=0, tiled=True)
        columns = me // cut
        input_slots = tile_slot[:input_tiles].reshape(tall, 2, half)
        input_own = jnp.take(
            pool_all, lax.dynamic_index_in_dim(input_slots, columns, 2, False).T.reshape(-1), axis=0
        )
        output_slots = tile_slot[input_tiles:].reshape(half, tall)
        output_own = jnp.take(pool_all, lax.dynamic_index_in_dim(output_slots, columns, 0, False), axis=0)
        offset = me % cut * channels
        input_local = input_own.reshape(2, tall, side, side)
        output_local = output_own
        if cut > 1:
            input_local = lax.dynamic_slice_in_dim(input_local, offset, channels, axis=3)
            output_local = lax.dynamic_slice_in_dim(output_local, offset, channels, axis=1)
        input_local = input_local.transpose(1, 2, 0, 3).reshape(model_width, 2 * channels)
        output_local = output_local.transpose(1, 0, 2).reshape(channels, model_width)

    cotangent_later, input_local = lax.optimization_barrier((cotangent, input_local))
    normed_all, xs_low, gates = norm_joint(x_all, tok_rows, gain_float, input_local)
    cotangent_all = lax.all_gather(cotangent_later, "tok", axis=0, tiled=True)

    def to_tokens(values, number=None):
        lead = values.shape[:-2]
        parts = values.reshape(lead + (devices, tok_rows, channels))
        if fast and number is not None:
            moved = everyone(parts, number)
        else:
            moved = lax.all_to_all(parts, "tok", split_axis=len(lead), concat_axis=len(lead), tiled=True)
        moved = moved.reshape(lead + (half, cut, tok_rows, channels))
        return jnp.swapaxes(moved, -3, -2).reshape(lead + (half, tok_rows, side))

    place = doc_positions(doc_lengths).reshape(-1, 1)
    taps, offset = channel_vectors[:K], channel_vectors[K]
    xs = xs_low.astype(f32)
    filtered = jax.nn.silu(conv_pre(xs, taps, offset, place)).astype(bf16)
    filtered_tokens = to_tokens(filtered, 3)
    select_blocks = select_weight.reshape(half, side, select_width)
    block = jnp.concatenate(
        [
            jnp.einsum("gtc,gcf->tf", filtered_tokens, select_blocks[..., :R], preferred_element_type=f32),
            jnp.einsum("gtc,gcf->ft", filtered_tokens, select_blocks[..., R:], preferred_element_type=f32),
        ],
        axis=0,
    ).astype(bf16)
    if fast:
        blocks = spread_blocks(block, plane, 4).reshape(devices, tok_rows + 2 * N, R)
    else:
        blocks = spread(block[None], devices)

    if fast:
        def share(values):
            return values.reshape(LINES, plane, tok_rows, channels)

        def across(blocks, which):
            blocks = [values.reshape(plane, LINES * tok_rows, channels) for values in blocks]
            return plane_product(blocks, plane_weight, which).reshape(LINES, tok_rows, model_width)

    by_row = lambda values: values.reshape((rows, L) + values.shape[1:])
    begins = by_row(jnp.broadcast_to(jnp.where(place == 0, 1e30, 0.0).astype(bf16), (tokens, channels)))
    step_local = channel_weight[:, select_width:].astype(bf16)
    rates = jnp.exp(channel_vectors[K + 2 : K + 2 + N])
    step_bias = channel_vectors[K + 1 : K + 2]
    skip_gain = channel_vectors[K + 2 + N :]
    scan_params = (step_local, step_bias, rates, skip_gain)
    mixed, gate_slope, kept = scan_forward(
        by_row(filtered), by_row(gates), begins, blocks, *scan_params
    )
    mixed = mixed.reshape(tokens, channels)

    back_chan = jnp.einsum("td,cd->tc", cotangent_all, output_local, preferred_element_type=f32).astype(bf16)
    back_chan = lax.optimization_barrier(back_chan)
    gate_grad = (back_chan.astype(f32) * gate_slope.reshape(tokens, channels)).astype(bf16)

    def input_part(grad):
        part = jnp.einsum("td,tc->dc", normed_all, grad, preferred_element_type=f32)
        return part.astype(bf16).reshape(tall, side, channels)

    output_part = jnp.einsum("tc,td->cd", mixed, cotangent_all, preferred_element_type=f32).astype(bf16)
    output_part = output_part.reshape(channels, tall, side).transpose(1, 0, 2)
    gate_part = input_part(gate_grad)

    def every_input(part):
        every = lax.all_gather(part, "tok", axis=0)
        every = every.reshape(half, cut, tall, side, channels).transpose(0, 2, 3, 1, 4)
        return every.reshape(half * tall, side, side)

    if fast:
        plane_own, mixed, back_chan = lax.optimization_barrier((plane_own, mixed, back_chan))
        plane_weight = lax.all_gather(plane_own, "tok", axis=0, axis_index_groups=planes)
        mixed_plane = lax.all_to_all(
            jnp.swapaxes(share(mixed), 0, 1), "tok", 0, 0, tiled=True, axis_index_groups=planes
        )
        first_parts = jnp.concatenate([gate_part, output_part], axis=0)
        early_first, early_second, early_landed = routes.to_owners(me, "early", tall)
        early_packed = pick(first_parts, early_first)
    else:
        output_every = lax.all_gather(output_part, "tok", axis=0)
        output_every = (
            output_every.reshape(half, cut, tall, channels, side)
            .transpose(0, 2, 1, 3, 4)
            .reshape(half * tall, side, side)
        )
        gate_every = every_input(gate_part)

    scan_in = (by_row(filtered), by_row(gates), by_row(back_chan), begins, blocks)
    if fast:
        early_route = ("route", plane, *CAPS["early"])
        *scan_grads, early_middle, gate_plane = scan_backward(
            *scan_in,
            *scan_params,
            kept,
            [early_route, ("plane", plane)],
            [early_packed, share(gate_grad)],
            6,
        )
    else:
        scan_grads = scan_backward(*scan_in, *scan_params, kept)
    draw, filter_mix, inject_grad, read_grad, rate_sum, skip_grad, bias_grad = scan_grads
    draw = draw.reshape(tokens, channels)
    rank_in = blocks[:, :tok_rows].reshape(tokens, R)
    step_grad = jnp.einsum("tc,tr->cr", draw, rank_in, preferred_element_type=f32)
    rank_part = jnp.einsum("tc,cr->tr", draw, step_local, preferred_element_type=f32)
    state_part = jnp.concatenate([inject_grad.reshape(tokens, N), read_grad.reshape(tokens, N)], axis=1)
    if fast:
        parts = jnp.concatenate(
            [
                rank_part.astype(bf16).reshape(devices, tok_rows, R),
                state_part.astype(bf16).reshape(devices, tok_rows, 2 * N).transpose(0, 2, 1),
            ],
            axis=1,
        )
        grad_blocks, early = fold_and_spread(
            parts.reshape(LINES, plane, tok_rows + 2 * N, R),
            plane,
            5,
            [early_route],
            [pick(early_middle, early_second)],
        )
        grad_blocks = grad_blocks.reshape(devices, tok_rows + 2 * N, R)
        projected_grad_all = jnp.concatenate(
            [
                grad_blocks[:, :tok_rows].reshape(tokens, R),
                grad_blocks[:, tok_rows:].transpose(0, 2, 1).reshape(tokens, 2 * N),
            ],
            axis=1,
        )
    else:
        partial_sums = jnp.concatenate([rank_part, state_part], axis=1)
        projected_grad_all = spread(fold(partial_sums, devices).astype(bf16), devices)
    select_local = channel_weight[:, :select_width].astype(bf16)
    back_filter = jnp.einsum(
        "tf,cf->tc", projected_grad_all, select_local, preferred_element_type=f32
    ).astype(bf16)
    select_grad = jnp.einsum("tc,tf->cf", filtered, projected_grad_all, preferred_element_type=f32)
    pre = conv_pre(xs, taps, offset, place)
    gate = jax.nn.sigmoid(pre)
    dpre = (filter_mix.reshape(tokens, channels) + back_filter.astype(f32)) * (gate * (1.0 + pre * (1.0 - gate)))
    offset_grad = jnp.sum(dpre, axis=0)
    taps_grad = [jnp.sum(dpre * xs, axis=0)]
    xs_grad = taps[K - 1][None] * dpre
    for lag in range(1, K):
        masked = jnp.where(place >= lag, dpre, 0.0)
        xs_grad = xs_grad + taps[K - 1 - lag][None] * sooner(masked, lag)
        taps_grad.insert(0, jnp.sum(masked * later(xs, lag), axis=0))
    xs_grad = xs_grad.astype(bf16)
    xs_part = input_part(xs_grad)
    if fast:
        late_first, late_second, late_landed = routes.to_owners(me, "late", 0)
        late_route = ("route", plane, *CAPS["late"])
        layer_parts = across([mixed_plane], 2)
        rides = [late_route, ("plane", plane), ("line", plane)]
        guests = [pick(xs_part, late_first), share(xs_grad), layer_parts[..., : model_width // 2]]
    else:
        xs_every = every_input(xs_part)
        rides, guests = [], []

    first_c, second_c, weight_c, lstat_c, rstat_c, left_turned, right_turned, left_gram, right_gram = channel_moments(
        channel_weight,
        jnp.concatenate([select_grad, step_grad], axis=1),
        channel_first,
        channel_second,
        channel_left,
        channel_right,
        channel_left_stat,
        channel_right_stat,
    )
    left_c, right_c, *arrived = solve_factors(
        (left_gram, right_gram), (left_turned.T, right_turned.T), rides, guests, 8
    )
    channel_new = (first_c, second_c, weight_c, left_c.T, right_c.T, lstat_c, rstat_c)
    if fast:
        late_middle, xs_plane, layer_left = arrived
        (late,) = exchange([late_route], [pick(late_middle, late_second)], 9)
        normed_parts = across([xs_plane, gate_plane], 0)
        rides = [("line", plane), ("line", plane)]
        guests = [normed_parts, layer_parts[..., model_width // 2 :]]

    own_slot = tile_slot - me * tiles_here
    every_tile = jnp.full(tile_slot.shape, True)
    if fast:
        grads = (late, early)
        kind = table(tiles_here, own_slot, every_tile, (~routes.late).astype(jnp.int32))
        index = table(tiles_here, own_slot, every_tile, jnp.where(routes.late, late_landed, early_landed))
    else:
        grads = (xs_every, gate_every, output_every)
        tile = jnp.arange(tile_slot.shape[0], dtype=jnp.int32)
        kind = table(tiles_here, own_slot, every_tile, routes.kind)
        spot = jnp.where(is_out, tile - input_tiles, tile % wide % half * tall + tile // wide)
        index = table(tiles_here, own_slot, every_tile, spot)
    first_next, second_next, weight_next, lstat_next, rstat_next, turned, gram = soap_tiles(
        kind,
        index,
        grads,
        pool_weight,
        pool_first,
        pool_second,
        pool_left,
        pool_right,
        pool_left_stat,
        pool_right_stat,
    )
    left_next, right_next, *arrived = renewed_bases(gram, turned, rides, guests, 10)

    if fast:
        layer_sum = jnp.concatenate(
            [jnp.sum(layer_left.astype(f32), axis=0), jnp.sum(arrived[1].astype(f32), axis=0)], axis=1
        )
        layer_out = (layer_in.astype(f32) + layer_sum).astype(bf16)
        normed_grad = jnp.sum(arrived[0].astype(f32), axis=0)
    else:
        mixed_tokens = to_tokens(mixed)
        joint_grad = to_tokens(jnp.stack([xs_grad, gate_grad])).reshape(wide, tok_rows, side)
        layer_out = tile_product(
            mixed_tokens, pool_all, tile_slot[input_tiles:].reshape(half, tall).T, False, bf16, layer_in
        )
        normed_grad = tile_product(
            joint_grad, pool_all, tile_slot[:input_tiles].reshape(tall, wide), True, f32
        )
    input_float = layer_in.astype(f32)
    inverse = lax.rsqrt(jnp.mean(input_float * input_float, axis=1, keepdims=True) + norm_epsilon)
    scaled = normed_grad * gain_float
    input_grad = (
        cotangent.astype(f32)
        + inverse * scaled
        - input_float * inverse**3 * jnp.mean(scaled * input_float, axis=1, keepdims=True)
    )
    gain_part = jnp.sum(normed_grad * input_float * inverse, axis=0).reshape(devices, gain_here)
    gain_grad = jnp.sum(lax.all_to_all(gain_part, "tok", split_axis=0, concat_axis=0, tiled=True), axis=0)

    gain_new = adam_step(norm_gain, gain_grad, gain_first, gain_second)
    vector_grad = jnp.concatenate(
        [jnp.stack(taps_grad), offset_grad[None], bias_grad, -rates * rate_sum, skip_grad], axis=0
    )
    vector_new = adam_step(channel_vectors, vector_grad, vector_first, vector_second)
    return (
        layer_out,
        input_grad,
        first_next,
        second_next,
        weight_next,
        left_next,
        right_next,
        lstat_next,
        rstat_next,
        *channel_new,
        *gain_new,
        *vector_new,
    )


def shards(*args):
    bf16 = jnp.bfloat16
    devices = lax.axis_size("tok")
    me = lax.axis_index("tok")
    layer_in, tile_slot, pool_weight, channel_weight = args[0], args[3], args[4], args[11]
    norm_gain, channel_vectors = args[18], args[21]
    tok_rows, model_width = layer_in.shape
    tiles_here, side, _ = pool_weight.shape
    tall = model_width // side
    channels = channel_vectors.shape[1]
    select_width = channel_weight.shape[1] - R
    select_here = channels * select_width
    select_rows = -(-select_here // model_width)
    tail_rows = -(-(1 + select_rows) // 16) * 16
    tail = jnp.zeros((tail_rows, model_width), bf16)
    tail = tail.at[0, : norm_gain.shape[0]].set(norm_gain.astype(bf16))
    select_flat = jnp.pad(
        channel_weight[:, :select_width].astype(bf16).reshape(-1), (0, select_rows * model_width - select_here)
    )
    tail = tail.at[1 : 1 + select_rows].set(select_flat.reshape(select_rows, model_width))
    x_all = lax.all_gather(jnp.concatenate([layer_in, tail], axis=0), "tok", axis=0)
    routes = Routes(tile_slot, devices, tiles_here, tall, channels * devices // side)
    if channels != side or devices % LINES:
        return core(routes, False, x_all, None, *args)
    plane = devices // LINES
    route = ("route", plane, *CAPS["all"])
    first, second, landed = routes.to_targets(me)
    (middle,) = exchange([route], [pick(pool_weight.astype(bf16), first)], 1)
    (last,) = exchange([route], [pick(middle, second)], 2)
    tiles_own = pick(last, table(3 * tall, routes.place, routes.target == me, landed))
    input_own, output_own = tiles_own[: 2 * tall], tiles_own[2 * tall :]
    input_local = input_own.reshape(2, tall, side, side).transpose(1, 2, 0, 3).reshape(model_width, 2 * channels)
    output_local = output_own.transpose(1, 0, 2).reshape(channels, model_width)
    plane_own = jnp.concatenate([input_local, output_own.transpose(0, 2, 1).reshape(model_width, channels)], axis=1)
    weights = lax.optimization_barrier((input_local, output_local, plane_own))
    return lax.cond(
        routes.fits, functools.partial(core, routes, True), functools.partial(core, routes, False), x_all, weights, *args
    )


def solution(mesh):
    line, flat, cube, column = P("tok"), P("tok", None), P("tok", None, None), P(None, "tok")
    in_specs = (flat, flat, P(), P()) + (cube,) * 7 + (flat,) * 7 + (line,) * 3 + (column,) * 3
    out_specs = (flat, flat) + (cube,) * 7 + (flat,) * 7 + (line,) * 3 + (column,) * 3
    return jax.shard_map(shards, mesh=mesh, in_specs=in_specs, out_specs=out_specs, check_vma=False)
```

```python
import functools

import jax
import jax.numpy as jnp
from jax import lax
from jax.experimental import pallas as pl
from jax.experimental.pallas import tpu as pltpu
from jax.sharding import PartitionSpec as P

N = 16
R = 128
K = 4
L = 2048
STEP = 5
GROUP = 16
LOG2E = 1.4426950408889634

beta_first = 0.5
beta_second = 0.5
stat_decay = 0.5
learn_rate = 0.02
vector_rate = 0.2
weight_decay = 0.01
adam_epsilon = 1e-08
norm_epsilon = 1e-05
highest = lax.Precision.HIGHEST


LINES = 4
MESH = pl.DeviceIdType.MESH


def greet(line, spot, plane):
    barrier = pltpu.get_barrier_semaphore()
    for k in range(1, LINES):
        pl.semaphore_signal(barrier, inc=1, device_id=((line + k) % LINES * plane + spot,), device_id_type=MESH)
    for k in range(1, plane):
        pl.semaphore_signal(barrier, inc=1, device_id=(line * plane + (spot + k) % plane,), device_id_type=MESH)
    pl.semaphore_wait(barrier, LINES + plane - 2)


def greet_all(me, devices):
    barrier = pltpu.get_barrier_semaphore()
    for k in range(1, devices):
        pl.semaphore_signal(barrier, inc=1, device_id=((me + k) % devices,), device_id_type=MESH)
    pl.semaphore_wait(barrier, devices - 1)


def remote(source, target, send, recv, device):
    return pltpu.make_async_remote_copy(
        src_ref=source, dst_ref=target, send_sem=send, recv_sem=recv, device_id=(device,), device_id_type=MESH
    )


def ride_copies(spec, source, out, sems):
    kind, plane = spec[:2]
    me = lax.axis_index("tok")
    line, spot = me // plane, me % plane
    if kind in ("line", "line_gather"):
        send, recv, own = sems
        part = lambda place: source if kind == "line_gather" else source.at[place]
        copies = [pltpu.make_async_copy(part(line), out.at[line], own.at[0])]
        for k in range(1, LINES):
            place = (line + k) % LINES
            copies.append(remote(part(place), out.at[line], send.at[k], recv.at[k], place * plane + spot))
        return copies
    if kind.startswith("plane"):
        send, recv, own = sems
        part = {
            "plane": lambda place: source.at[:, place],
            "plane_gather": lambda place: source,
            "plane_rows": lambda place: source.at[place],
            "plane_back": lambda place: source.at[place],
        }[kind]
        target = out.at[:, spot] if kind == "plane_back" else out.at[spot]
        copies = [pltpu.make_async_copy(part(spot), target, own.at[0])]
        for k in range(1, plane):
            place = (spot + k) % plane
            copies.append(remote(part(place), target, send.at[k], recv.at[k], line * plane + place))
        return copies
    if kind == "all":
        send, recv, own = sems
        devices = LINES * plane
        copies = [pltpu.make_async_copy(source.at[me], out.at[me], own.at[0])]
        for k in range(1, devices):
            target = (me + k) % devices
            copies.append(remote(source.at[target], out.at[me], send.at[k], recv.at[k], target))
        return copies
    cap_line, cap_plane = spec[2:]
    line_send, line_recv, plane_send, plane_recv, own = sems
    start = LINES * cap_line

    def to_line(place):
        return pl.ds(place * cap_line, cap_line)

    def to_plane(place):
        return pl.ds(start + place * cap_plane, cap_plane)

    copies = [
        pltpu.make_async_copy(source.at[to_line(line)], out.at[to_line(line)], own.at[0]),
        pltpu.make_async_copy(source.at[to_plane(spot)], out.at[to_plane(spot)], own.at[1]),
    ]
    for k in range(1, LINES):
        place = (line + k) % LINES
        copies.append(
            remote(source.at[to_line(place)], out.at[to_line(line)], line_send.at[k], line_recv.at[k], place * plane + spot)
        )
    for k in range(1, plane):
        place = (spot + k) % plane
        copies.append(
            remote(source.at[to_plane(place)], out.at[to_plane(spot)], plane_send.at[k], plane_recv.at[k], line * plane + place)
        )
    return copies


def ride_sems(spec):
    kind, plane = spec[:2]
    if kind == "route":
        return (
            [pltpu.SemaphoreType.DMA((LINES,))] * 2
            + [pltpu.SemaphoreType.DMA((plane,))] * 2
            + [pltpu.SemaphoreType.DMA((2,))]
        )
    members = LINES if kind.startswith("line") else plane if kind.startswith("plane") else LINES * plane
    return [pltpu.SemaphoreType.DMA((members,))] * 2 + [pltpu.SemaphoreType.DMA((1,))]


def ride_shape(spec, value):
    kind, plane = spec[:2]
    shape = value.shape
    if kind in ("plane", "plane_back"):
        shape = (shape[1], shape[0]) + shape[2:]
    if kind.endswith("gather"):
        shape = (LINES if kind == "line_gather" else plane,) + shape
    return jax.ShapeDtypeStruct(shape, value.dtype)


class Riders:
    def __init__(self, specs):
        self.specs = tuple(specs)

    def all_copies(self, sources, outs, sems):
        copies, at = [], 0
        for spec, source, out in zip(self.specs, sources, outs):
            count = len(ride_sems(spec))
            copies += ride_copies(spec, source, out, sems[at : at + count])
            at += count
        return copies

    def begin(self, sources, outs, sems):
        plane = self.specs[0][1]
        me = lax.axis_index("tok")
        if any(spec[0] == "all" for spec in self.specs):
            greet_all(me, LINES * plane)
        else:
            greet(me // plane, me % plane, plane)
        for copy in self.all_copies(sources, outs, sems):
            copy.start()

    def end(self, sources, outs, sems):
        for copy in self.all_copies(sources, outs, sems):
            copy.wait()

    def sems(self):
        return [sem for spec in self.specs for sem in ride_sems(spec)]

    def shapes(self, values):
        return [ride_shape(spec, value) for spec, value in zip(self.specs, values)]


def riders_kernel(riders, *refs):
    count = len(riders.specs)
    sources, outs, sems = refs[:count], refs[count : 2 * count], refs[2 * count :]
    riders.begin(sources, outs, sems)
    riders.end(sources, outs, sems)


HBM = pl.BlockSpec(memory_space=pl.ANY)


def exchange(specs, values, number):
    riders = Riders(specs)
    return pl.pallas_call(
        functools.partial(riders_kernel, riders),
        in_specs=[HBM] * len(values),
        out_specs=[HBM] * len(values),
        out_shape=riders.shapes(values),
        scratch_shapes=riders.sems(),
        compiler_params=pltpu.CompilerParams(collective_id=number, has_side_effects=True),
    )(*values)


def everyone_kernel(devices, source, out, send, recv, own):
    me = lax.axis_index("tok")
    greet_all(me, devices)
    copies = [pltpu.make_async_copy(source.at[me], out.at[me], own.at[0])]
    for k in range(1, devices):
        target = (me + k) % devices
        copies.append(remote(source.at[target], out.at[me], send.at[k], recv.at[k], target))
    for copy in copies:
        copy.start()
    for copy in copies:
        copy.wait()


def everyone(values, number):
    devices = values.shape[0]
    return pl.pallas_call(
        functools.partial(everyone_kernel, devices),
        in_specs=[HBM],
        out_specs=HBM,
        out_shape=jax.ShapeDtypeStruct(values.shape, values.dtype),
        scratch_shapes=[pltpu.SemaphoreType.DMA((devices,))] * 2 + [pltpu.SemaphoreType.DMA((1,))],
        compiler_params=pltpu.CompilerParams(collective_id=number, has_side_effects=True),
    )(values)


def spread_steps(plane, block, out, sems):
    line_send, line_recv, plane_send, plane_recv, own = sems
    me = lax.axis_index("tok")
    line, spot = me // plane, me % plane
    copies = [pltpu.make_async_copy(block, out.at[line, spot], own.at[0])]
    arrivals = []
    for k in range(1, LINES):
        place = (line + k) % LINES
        arrivals.append(remote(block, out.at[line, spot], line_send.at[k], line_recv.at[k], place * plane + spot))
    for k in range(1, plane):
        place = (spot + k) % plane
        copies.append(
            remote(block, out.at[line, spot], plane_send.at[0, k], plane_recv.at[0, k], line * plane + place)
        )
    for copy in arrivals + copies:
        copy.start()
    for k in range(1, LINES):
        arrivals[k - 1].wait_recv()
        origin = (line + LINES - k) % LINES
        for j in range(1, plane):
            place = (spot + j) % plane
            copy = remote(
                out.at[origin, spot], out.at[origin, spot], plane_send.at[k, j], plane_recv.at[k, j], line * plane + place
            )
            copy.start()
            copies.append(copy)
    for copy in arrivals:
        copy.wait_send()
    for copy in copies:
        copy.wait()


def spread_sems(plane):
    return (
        [pltpu.SemaphoreType.DMA((LINES,))] * 2
        + [pltpu.SemaphoreType.DMA((LINES, plane))] * 2
        + [pltpu.SemaphoreType.DMA((1,))]
    )


def spread_kernel(plane, riders, block, *refs):
    count, own_sems = len(riders.specs), len(spread_sems(plane))
    sources, out, outs = refs[:count], refs[count], refs[count + 1 : 2 * count + 1]
    sems, ride = refs[2 * count + 1 : 2 * count + 1 + own_sems], refs[2 * count + 1 + own_sems :]
    me = lax.axis_index("tok")
    greet(me // plane, me % plane, plane)
    guests = riders.all_copies(sources, outs, ride)
    for copy in guests:
        copy.start()
    spread_steps(plane, block, out, sems)
    for copy in guests:
        copy.wait()


def spread_blocks(block, plane, number, specs=(), values=()):
    riders = Riders(specs)
    return pl.pallas_call(
        functools.partial(spread_kernel, plane, riders),
        in_specs=[HBM] * (1 + len(values)),
        out_specs=[HBM] * (1 + len(values)),
        out_shape=[jax.ShapeDtypeStruct((LINES, plane) + block.shape, block.dtype)] + riders.shapes(values),
        scratch_shapes=spread_sems(plane) + riders.sems(),
        compiler_params=pltpu.CompilerParams(collective_id=number, has_side_effects=True),
    )(block, *values)


def fold_kernel(plane, riders, parts, *refs):
    count = len(riders.specs)
    sources, out, outs = refs[:count], refs[count], refs[count + 1 : 2 * count + 1]
    got, sent, last, block, plane_send, plane_recv, line_send, line_recv, own = refs[2 * count + 1 : 2 * count + 10]
    own_sems = len(spread_sems(plane))
    sems, ride = refs[2 * count + 10 : 2 * count + 10 + own_sems], refs[2 * count + 10 + own_sems :]
    me = lax.axis_index("tok")
    line, spot = me // plane, me % plane
    greet(line, spot, plane)
    copies = [pltpu.make_async_copy(parts.at[:, spot], got.at[spot], own.at[0])]
    for k in range(1, plane):
        place = (spot + k) % plane
        copies.append(
            remote(parts.at[:, place], got.at[spot], plane_send.at[k], plane_recv.at[k], line * plane + place)
        )
    for copy in copies:
        copy.start()
    guests = riders.all_copies(sources, outs, ride)
    for copy in guests:
        copy.start()
    for copy in copies:
        copy.wait()
    for z in range(LINES):
        total = got[0, z].astype(jnp.float32)
        for k in range(1, plane):
            total = total + got[k, z].astype(jnp.float32)
        sent[z] = total
    copies = [pltpu.make_async_copy(sent.at[line], last.at[line], own.at[1])]
    for k in range(1, LINES):
        place = (line + k) % LINES
        copies.append(remote(sent.at[place], last.at[line], line_send.at[k], line_recv.at[k], place * plane + spot))
    for copy in copies:
        copy.start()
    for copy in copies:
        copy.wait()
    block[...] = ((last[0] + last[1]) + (last[2] + last[3])).astype(block.dtype)
    spread_steps(plane, block, out, sems)
    for copy in guests:
        copy.wait()


def fold_and_spread(parts, plane, number, specs=(), values=()):
    shape = parts.shape[2:]
    riders = Riders(specs)
    return pl.pallas_call(
        functools.partial(fold_kernel, plane, riders),
        in_specs=[HBM] * (1 + len(values)),
        out_specs=[HBM] * (1 + len(values)),
        out_shape=[jax.ShapeDtypeStruct(parts.shape, parts.dtype)] + riders.shapes(values),
        scratch_shapes=[
            pltpu.VMEM((plane, LINES) + shape, parts.dtype),
            pltpu.VMEM((LINES,) + shape, jnp.float32),
            pltpu.VMEM((LINES,) + shape, jnp.float32),
            pltpu.VMEM(shape, parts.dtype),
        ]
        + [pltpu.SemaphoreType.DMA((plane,))] * 2
        + [pltpu.SemaphoreType.DMA((LINES,))] * 2
        + [pltpu.SemaphoreType.DMA((2,))]
        + spread_sems(plane)
        + riders.sems(),
        compiler_params=pltpu.CompilerParams(collective_id=number, has_side_effects=True, vmem_limit_bytes=60 * 2**20),
    )(parts, *values)


def dot_nt(left, right):
    return lax.dot_general(left, right, (((1,), (1,)), ((), ())), preferred_element_type=jnp.float32)

def dot_nn(left, right):
    return jnp.dot(left, right, preferred_element_type=jnp.float32)

def softplus(v):
    return jnp.maximum(v, 0.0) + jnp.log1p(jnp.exp(-jnp.abs(v)))

def split2(v):
    high = v.astype(jnp.bfloat16)
    return high, (v - high.astype(jnp.float32)).astype(jnp.bfloat16)

def own_token(dtype):
    token = lax.broadcasted_iota(jnp.int32, (GROUP, GROUP * N), 0)
    column = lax.broadcasted_iota(jnp.int32, (GROUP, GROUP * N), 1)
    return (column // N == token).astype(dtype)

def slice_columns(block_ref, cols_s, r, chunk):
    values = block_ref[0, chunk:].astype(jnp.float32)
    for g in range(chunk // GROUP):
        cols_s[r, g] = values[:, g * GROUP : (g + 1) * GROUP]


def lay_out(block_ref, inject_s, read_s, r, chunk):
    token = lax.broadcasted_iota(jnp.int32, (chunk, GROUP * N), 0) % GROUP
    column = lax.broadcasted_iota(jnp.int32, (chunk, GROUP * N), 1)
    mine = column // N == token
    for start, rows_s in ((chunk, inject_s), (chunk + N, read_s)):
        if rows_s is not None:
            rows_s[r] = jnp.where(mine, repeat_columns(block_ref[0, start : start + N]), 0).astype(jnp.bfloat16)


def repeat_columns(values):
    state = lax.broadcasted_iota(jnp.int32, (N, GROUP * N), 0)
    column = lax.broadcasted_iota(jnp.int32, (N, GROUP * N), 1)
    chosen = (column % N == state).astype(jnp.bfloat16)
    product = lax.dot_general(
        values, chosen, (((0,), (0,)), ((), ())), preferred_element_type=jnp.float32
    )
    return product


def fwd_kernel(pair, chunk, riders, f_ref, z_ref, start_ref, *refs):
    count = len(riders.specs)
    block_refs, refs = refs[:pair], refs[pair:]
    stepw_ref, bias_ref, rate_ref, skip_ref = refs[:4]
    sources, (mixed_ref, dz_ref, keep_ref) = refs[4 : 4 + count], refs[4 + count : 7 + count]
    outs, refs = refs[7 + count : 7 + 2 * count], refs[7 + 2 * count :]
    state, step_s, drive_s, scan_s, cols_s, read_s = refs[:6]
    if count:

        @pl.when((pl.program_id(0) == 0) & (pl.program_id(1) == 0))
        def _():
            riders.begin(sources, outs, refs[6:])

    groups = chunk // GROUP
    neg = rate_ref[...] * (-LOG2E)
    @pl.when(pl.program_id(1) == 0)
    def _():
        state[...] = jnp.zeros_like(state)

    for r in range(pair):
        raw = dot_nt(block_refs[r][0, :chunk], stepw_ref[...])
        step = softplus(raw + bias_ref[...])
        slice_columns(block_refs[r], cols_s, r, chunk)
        lay_out(block_refs[r], None, read_s, r, chunk)
        step_s[r] = step + start_ref[r].astype(jnp.float32)
        drive_s[r] = step * f_ref[r].astype(jnp.float32)
        keep_ref[r, 0] = state[r]

    def group(g, hidden):
        hidden = list(hidden)
        held = [[] for _ in range(pair)]
        base = pl.multiple_of(g * GROUP, GROUP)
        cols = [cols_s[r, g] for r in range(pair)]
        for k in range(GROUP):
            for r in range(pair):
                factor = jnp.exp2(step_s[r, pl.ds(base + k, 1), :] * neg)
                hidden[r] = factor * hidden[r] + drive_s[r, pl.ds(base + k, 1), :] * cols[r][:N, k : k + 1]
                held[r].append(hidden[r].astype(jnp.bfloat16))
        for r in range(pair):
            states = jnp.concatenate(held[r], axis=0)
            scan_s[r, pl.ds(base, GROUP), :] = dot_nn(read_s[r, pl.ds(base, GROUP), :], states)
        return tuple(hidden)

    hidden = lax.fori_loop(0, groups, group, tuple(state[r] for r in range(pair)), unroll=groups)
    for r in range(pair):
        state[r] = hidden[r]
        f = f_ref[r].astype(jnp.float32)
        z = z_ref[r].astype(jnp.float32)
        gate = 1.0 / (1.0 + jnp.exp(-z))
        summed = scan_s[r] + skip_ref[...] * f
        mixed_ref[r] = (summed * (z * gate)).astype(jnp.bfloat16)
        dz_ref[r] = summed * (gate * (1.0 + z * (1.0 - gate)))
    if count:

        @pl.when((pl.program_id(0) == pl.num_programs(0) - 1) & (pl.program_id(1) == pl.num_programs(1) - 1))
        def _():
            riders.end(sources, outs, refs[6:])

def bwd_kernel(pair, chunk, riders, f_ref, z_ref, gm_ref, start_ref, *refs):
    block_refs, refs = refs[:pair], refs[pair:]
    stepw_ref, bias_ref, rate_ref, skip_ref, keep_ref = refs[:5]
    refs = refs[5:]
    count = len(riders.specs)
    sources, refs = refs[:count], refs[count:]
    draw_ref, dfm_ref, dinj_ref, dread_ref, drate_ref, dskip_ref, dbias_ref = refs[:7]
    outs, refs = refs[7 : 7 + count], refs[7 + count :]
    carry_s, step_s, drive_s, dscan_s, raw_s, delta_s, a_s, ah_s, h_s, s1_s, s2_s, cols_s, inject_s = refs[:13]
    if count:

        @pl.when((pl.program_id(0) == 0) & (pl.program_id(1) == 0))
        def _():
            riders.begin(sources, outs, refs[13:])

    groups = chunk // GROUP
    rate = rate_ref[...]
    neg = rate * (-LOG2E)
    mine = own_token(jnp.bfloat16)
    mine_f = own_token(jnp.float32)

    @pl.when(pl.program_id(1) == 0)
    def _():
        carry_s[...] = jnp.zeros_like(carry_s)

    @pl.when((pl.program_id(1) == 0) & (pl.program_id(0) == 0))
    def _():
        drate_ref[...] = jnp.zeros_like(drate_ref)
        dskip_ref[...] = jnp.zeros_like(dskip_ref)
        dbias_ref[...] = jnp.zeros_like(dbias_ref)

    for r in range(pair):
        raw = dot_nt(block_refs[r][0, :chunk], stepw_ref[...]) + bias_ref[...]
        slice_columns(block_refs[r], cols_s, r, chunk)
        lay_out(block_refs[r], inject_s, None, r, chunk)
        step = softplus(raw)
        raw_s[r] = raw
        delta_s[r] = step
        step_s[r] = step + start_ref[r].astype(jnp.float32)
        f = f_ref[r].astype(jnp.float32)
        drive_s[r] = step * f
        z = z_ref[r].astype(jnp.float32)
        gate = 1.0 / (1.0 + jnp.exp(-z))
        dscan = gm_ref[r].astype(jnp.float32) * (z * gate)
        dscan_s[r] = dscan
        dskip_ref[...] += jnp.sum(dscan * f, axis=0, keepdims=True)

    def forward(g, hidden):
        hidden = list(hidden)
        base = pl.multiple_of(g * GROUP, GROUP)
        cols = [cols_s[r, g] for r in range(pair)]
        held = [[] for _ in range(pair)]
        for k in range(GROUP):
            for r in range(pair):
                factor = jnp.exp2(step_s[r, pl.ds(base + k, 1), :] * neg)
                kept = factor * hidden[r]
                hidden[r] = kept + drive_s[r, pl.ds(base + k, 1), :] * cols[r][:N, k : k + 1]
                a_s[r, base + k] = factor
                ah_s[r, base + k] = kept
                held[r].append(hidden[r].astype(jnp.bfloat16))
        for r in range(pair):
            h_s[r, g] = jnp.concatenate(held[r], axis=0)
        return tuple(hidden)

    lax.fori_loop(0, groups, forward, tuple(keep_ref[r, 0] for r in range(pair)), unroll=groups)

    def backward(i, carried):
        g = groups - 1 - i
        base = pl.multiple_of(g * GROUP, GROUP)
        ag = list(carried[:pair])
        total = carried[pair]
        cols = [cols_s[r, g] for r in range(pair)]
        gs = [[None] * GROUP for _ in range(pair)]
        qs = [[None] * GROUP for _ in range(pair)]
        for k in reversed(range(GROUP)):
            for r in range(pair):
                grad = dscan_s[r, pl.ds(base + k, 1), :] * cols[r][N:, k : k + 1] + ag[r]
                ag[r] = a_s[r, base + k] * grad
                q = grad * ah_s[r, base + k]
                total = total + delta_s[r, pl.ds(base + k, 1), :] * q
                gs[r][k] = grad.astype(jnp.bfloat16)
                qs[r][k] = (rate * q).astype(jnp.bfloat16)
        for r in range(pair):
            grads = jnp.concatenate(gs[r], axis=0)
            pulls = jnp.concatenate(qs[r], axis=0)
            s1_s[r, pl.ds(base, GROUP), :] = dot_nn(inject_s[r, pl.ds(base, GROUP), :], grads)
            s2_s[r, pl.ds(base, GROUP), :] = dot_nn(mine, pulls)
            dh, dl = split2(dscan_s[r, pl.ds(base, GROUP), :])
            uh, ul = split2(drive_s[r, pl.ds(base, GROUP), :])
            dr = dot_nt(jnp.concatenate([dh, dl], axis=0), h_s[r, g])
            dread_ref[r, pl.ds(g, 1), :] = jnp.sum((dr[:GROUP] + dr[GROUP:]) * mine_f, axis=0, keepdims=True)
            di = dot_nt(jnp.concatenate([uh, ul], axis=0), grads)
            dinj_ref[r, pl.ds(g, 1), :] = jnp.sum((di[:GROUP] + di[GROUP:]) * mine_f, axis=0, keepdims=True)
        return tuple(ag) + (total,)

    out = lax.fori_loop(
        0, groups, backward, tuple(carry_s[r] for r in range(pair)) + (jnp.zeros_like(rate),), unroll=groups
    )
    drate_ref[...] += out[pair]
    for r in range(pair):
        carry_s[r] = out[r]
        f = f_ref[r].astype(jnp.float32)
        draw = (f * s1_s[r] - s2_s[r]) / (1.0 + jnp.exp(-raw_s[r]))
        draw_ref[r] = draw.astype(jnp.bfloat16)
        dbias_ref[...] += jnp.sum(draw, axis=0, keepdims=True)
        dfm_ref[r] = delta_s[r] * s1_s[r] + skip_ref[...] * dscan_s[r]

    if count:

        @pl.when((pl.program_id(0) == pl.num_programs(0) - 1) & (pl.program_id(1) == pl.num_programs(1) - 1))
        def _():
            riders.end(sources, outs, refs[13:])


def specs(pair, chunk, ch, blocks, back, chunks):
    def at(i, j):
        return (i, chunks - 1 - j if back else j)
    tok = pl.BlockSpec((pair, chunk, ch), lambda i, j: at(i, j) + (0,))
    flat = pl.BlockSpec((pair, chunk // GROUP, GROUP * N), lambda i, j: at(i, j) + (0,))
    keep = pl.BlockSpec((pair, 1, N, ch), lambda i, j: at(i, j) + (0, 0))
    def block(r):
        def index(i, j):
            i, j = at(i, j)
            return ((i * pair + r) * chunks + j, 0, 0)
        return pl.BlockSpec((1,) + blocks.shape[1:], index)
    def whole(a):
        return pl.BlockSpec(a.shape, lambda i, j: (0,) * a.ndim)
    return tok, [block(r) for r in range(pair)], flat, keep, whole

def scan_forward(f, z, start, blocks, stepw, bias, rate, skip, rides=(), guests=(), number=None):
    riders = Riders(rides)
    params = dict(collective_id=number, has_side_effects=True) if guests else {}
    chunk = blocks.shape[1] - 2 * N
    rows, length, ch = f.shape
    pair = 2 if rows % 2 == 0 else 1
    chunks = length // chunk
    tok, block_specs, flat, keep, whole = specs(pair, chunk, ch, blocks, False, chunks)
    return pl.pallas_call(
        functools.partial(fwd_kernel, pair, chunk, riders),
        grid=(rows // pair, chunks),
        in_specs=[tok, tok, tok]
        + block_specs
        + [whole(stepw), whole(bias), whole(rate), whole(skip)]
        + [HBM] * len(guests),
        out_specs=[tok, tok, keep] + [HBM] * len(guests),
        out_shape=[jax.ShapeDtypeStruct(f.shape, jnp.bfloat16), jax.ShapeDtypeStruct(f.shape, jnp.float32),
                   jax.ShapeDtypeStruct((rows, chunks, N, ch), jnp.float32)]
        + riders.shapes(guests),
        scratch_shapes=[pltpu.VMEM((pair, N, ch), jnp.float32)] + [pltpu.VMEM((pair, chunk, ch), jnp.float32)] * 3
        + [pltpu.VMEM((pair, chunk // GROUP, 2 * N, GROUP), jnp.float32)]
        + [pltpu.VMEM((pair, chunk, GROUP * N), jnp.bfloat16)]
        + riders.sems(),
        compiler_params=pltpu.CompilerParams(vmem_limit_bytes=60 * 2**20, **params),
        cost_estimate=pl.CostEstimate(flops=4 * 10**10, bytes_accessed=8 * 10**6, transcendentals=0),
    )(f, z, start, *([blocks] * pair), stepw, bias, rate, skip, *guests)

def scan_backward(f, z, gm, start, blocks, stepw, bias, rate, skip, kept, rides=(), guests=(), number=None):
    chunk = blocks.shape[1] - 2 * N
    rows, length, ch = f.shape
    pair = 2 if rows % 2 == 0 else 1
    chunks = length // chunk
    tok, block_specs, flat, keep, whole = specs(pair, chunk, ch, blocks, True, chunks)
    f32 = jnp.float32
    row = jax.ShapeDtypeStruct((1, ch), f32)
    in_specs = [tok, tok, tok, tok] + block_specs + [whole(stepw), whole(bias), whole(rate), whole(skip), keep]
    inj = jax.ShapeDtypeStruct((rows, length // GROUP, GROUP * N), f32)
    out_specs = [tok, tok, flat, flat, whole(rate), whole(row), whole(row)]
    out_shape = [jax.ShapeDtypeStruct(f.shape, jnp.bfloat16), jax.ShapeDtypeStruct(f.shape, f32),
                 jax.ShapeDtypeStruct(inj.shape, f32), jax.ShapeDtypeStruct(inj.shape, f32),
                 jax.ShapeDtypeStruct(rate.shape, f32), row, row]
    scratch = ([pltpu.VMEM((pair, N, ch), f32)] + [pltpu.VMEM((pair, chunk, ch), f32)] * 5
               + [pltpu.VMEM((pair, chunk, N, ch), f32)] * 2
               + [pltpu.VMEM((pair, chunk // GROUP, GROUP * N, ch), jnp.bfloat16)]
               + [pltpu.VMEM((pair, chunk, ch), f32)] * 2
               + [pltpu.VMEM((pair, chunk // GROUP, 2 * N, GROUP), f32)]
               + [pltpu.VMEM((pair, chunk, GROUP * N), jnp.bfloat16)])
    values = (f, z, gm, start, *([blocks] * pair), stepw, bias, rate, skip, kept)
    params = dict(vmem_limit_bytes=60 * 2**20)
    riders = Riders(rides)
    if guests:
        in_specs, out_specs = in_specs + [HBM] * len(guests), out_specs + [HBM] * len(guests)
        out_shape = out_shape + riders.shapes(guests)
        scratch = scratch + riders.sems()
        values = values + tuple(guests)
        params.update(collective_id=number, has_side_effects=True)
    return pl.pallas_call(
        functools.partial(bwd_kernel, pair, chunk, riders),
        grid=(rows // pair, chunks),
        in_specs=in_specs,
        out_specs=out_specs,
        out_shape=out_shape,
        scratch_shapes=scratch,
        compiler_params=pltpu.CompilerParams(**params),
        cost_estimate=pl.CostEstimate(flops=7 * 10**10, bytes_accessed=8 * 10**6, transcendentals=0),
    )(*values)


DEPTH = 4
BATCH = 16


def tile_product_kernel(pairs, steps, transposed, residual, idx_ref, left_ref, pool_ref, *refs):
    if residual:
        res_ref, refs = refs[0], refs[1:]
    out_ref, slots, sems = refs
    side = slots.shape[2]
    total_steps = pairs * steps

    def fetch(step):
        for u in range(BATCH):
            pltpu.make_async_copy(
                pool_ref.at[idx_ref[step * BATCH + u]], slots.at[step % DEPTH, u], sems.at[step % DEPTH]
            ).start()

    for step in range(min(DEPTH - 1, total_steps)):
        fetch(step)

    def one_pair(o, carry):
        total = jnp.zeros((left_ref.shape[1], 2 * side), jnp.float32)
        for k in range(steps):
            step = o * steps + k

            @pl.when(step + DEPTH - 1 < total_steps)
            def _():
                fetch(step + DEPTH - 1)

            slot = step % DEPTH
            pltpu.make_async_copy(slots.at[slot], slots.at[slot], sems.at[slot]).wait()
            for u in range(0, BATCH, 4):
                at = k * (BATCH // 2) + u // 2
                left = jnp.concatenate([left_ref[at], left_ref[at + 1]], axis=1)
                tile = [slots[slot, u + v] for v in range(4)]
                if transposed:
                    right = jnp.concatenate(
                        [jnp.concatenate([tile[0], tile[2]], axis=1), jnp.concatenate([tile[1], tile[3]], axis=1)], axis=0
                    )
                    total += dot_nt(left, right)
                else:
                    right = jnp.concatenate(
                        [jnp.concatenate([tile[0], tile[1]], axis=1), jnp.concatenate([tile[2], tile[3]], axis=1)], axis=0
                    )
                    total += dot_nn(left, right)
        columns = pl.ds(pl.multiple_of(o * 2 * side, side), 2 * side)
        if residual:
            total += res_ref[:, columns].astype(jnp.float32)
        out_ref[:, columns] = total.astype(out_ref.dtype)
        return carry

    lax.fori_loop(0, pairs, one_pair, 0)


def tile_product(left, pool, index, transposed, dtype, residual=None):
    outs, depth = index.shape
    pairs, steps = outs // 2, 2 * depth // BATCH
    side = pool.shape[1]
    tok = left.shape[1]
    vmem = pl.BlockSpec(memory_space=pltpu.VMEM)
    extra = [residual] if residual is not None else []
    order = index.reshape(pairs, 2, depth).transpose(0, 2, 1).reshape(-1).astype(jnp.int32)
    return pl.pallas_call(
        functools.partial(tile_product_kernel, pairs, steps, transposed, residual is not None),
        in_specs=[pl.BlockSpec(memory_space=pltpu.SMEM), vmem, pl.BlockSpec(memory_space=pl.ANY)] + [vmem] * len(extra),
        out_specs=vmem,
        out_shape=jax.ShapeDtypeStruct((tok, outs * side), dtype),
        scratch_shapes=[pltpu.VMEM((DEPTH, BATCH, side, side), pool.dtype), pltpu.SemaphoreType.DMA((DEPTH,))],
        compiler_params=pltpu.CompilerParams(vmem_limit_bytes=40 * 2**20),
        cost_estimate=pl.CostEstimate(
            flops=2 * outs * depth * tok * side * side, bytes_accessed=outs * depth * side * side * 2, transcendentals=0
        ),
    )(order, left, pool, *extra)


def dot_tn(left, right):
    return lax.dot_general(left, right, (((0,), (0,)), ((), ())), preferred_element_type=jnp.float32)


def three(dot, left, right):
    left_axis, right_axis = {dot_nn: (1, 0), dot_nt: (1, 1), dot_tn: (0, 0)}[dot]
    return dot(
        jnp.concatenate([left[0], left[0], left[1]], axis=left_axis),
        jnp.concatenate([right[0], right[1], right[0]], axis=right_axis),
    )


def soap_kernel(sources, many, kind_ref, idx_ref, *refs):
    grad_refs, refs = refs[: sources * many], refs[sources * many :]
    weight_ref, first_ref, second_ref, left_ref, right_ref, lstat_ref, rstat_ref = refs[:7]
    first_out, second_out, weight_out, lstat_out, rstat_out, turned_out, gram_out = refs[7:]
    side = weight_ref.shape[1]
    diagonal = lax.broadcasted_iota(jnp.int32, (side, side), 0) == lax.broadcasted_iota(jnp.int32, (side, side), 1)
    every = range(many)
    grads, lefts, rights = [], [], []
    for u in every:
        kind = kind_ref[pl.program_id(0) * many + u]
        grad = grad_refs[u * sources][0]
        for which in range(1, sources):
            grad = jnp.where(kind == which, grad_refs[u * sources + which][0], grad)
        grads.append(grad)
        lefts.append(split2(left_ref[u]))
        rights.append(split2(right_ref[u]))
    across = [split2(dot_nn(grads[u], rights[u][0]) + dot_nn(grads[u], rights[u][1])) for u in every]
    turned = [three(dot_tn, lefts[u], across[u]) for u in every]
    products = [(dot_nt(grads[u], grads[u]), dot_tn(grads[u], grads[u])) for u in every]
    directions = []
    for u in every:
        first = beta_first * first_ref[u] + (1.0 - beta_first) * turned[u]
        second = beta_second * second_ref[u] + (1.0 - beta_second) * turned[u] * turned[u]
        first_out[u] = first
        second_out[u] = second
        directions.append(split2(
            first / (1.0 - beta_first**STEP) / (jnp.sqrt(second / (1.0 - beta_second**STEP)) + adam_epsilon)
        ))
    renewed = []
    for u in every:
        for which, (stat_ref, basis_ref, basis2, stat_out) in enumerate(
            ((lstat_ref, left_ref, lefts[u], lstat_out), (rstat_ref, right_ref, rights[u], rstat_out))
        ):
            stat = stat_decay * stat_ref[u] + (1.0 - stat_decay) * products[u][which]
            stat_out[u] = stat
            trace = jnp.sum(jnp.sum(jnp.where(diagonal, stat, 0.0), axis=0, keepdims=True), axis=1, keepdims=True)
            value = three(dot_nn, split2(stat), basis2) + (trace / side) * basis_ref[u]
            turned_out[u, which] = value
            renewed.append(split2(value))
    back = [split2(three(dot_nt, directions[u], rights[u])) for u in every]
    for u in every:
        for which in range(2):
            gram_out[u, which] = three(dot_tn, renewed[u * 2 + which], renewed[u * 2 + which])
    for u in every:
        weight = weight_ref[u]
        weight_out[u] = weight - learn_rate * (three(dot_nn, lefts[u], back[u]) + weight_decay * weight)


def soap_tiles(kind, index, grads, weight, first, second, left, right, lstat, rstat, many=4):
    count, side, _ = weight.shape
    one = pl.BlockSpec((many, side, side), lambda s, kind, idx: (s, 0, 0))
    two = pl.BlockSpec((many, 2, side, side), lambda s, kind, idx: (s, 0, 0, 0))

    def picked(u, which):
        def at(s, kind, idx):
            return (jnp.where(kind[s * many + u] == which, idx[s * many + u], 0), 0, 0)

        return pl.BlockSpec((1, side, side), at)

    tile = jax.ShapeDtypeStruct(weight.shape, jnp.float32)
    pairs = jax.ShapeDtypeStruct((count, 2, side, side), jnp.float32)
    sources = len(grads)
    return pl.pallas_call(
        functools.partial(soap_kernel, sources, many),
        grid_spec=pltpu.PrefetchScalarGridSpec(
            num_scalar_prefetch=2,
            grid=(count // many,),
            in_specs=[picked(u, which) for u in range(many) for which in range(sources)] + [one] * 7,
            out_specs=[one] * 5 + [two] * 2,
        ),
        out_shape=[tile] * 5 + [pairs] * 2,
        compiler_params=pltpu.CompilerParams(vmem_limit_bytes=60 * 2**20),
        cost_estimate=pl.CostEstimate(flops=count * 60 * side**3, bytes_accessed=count * 18 * 4 * side**2, transcendentals=0),
    )(kind, index, *(list(grads) * many), weight, first, second, left, right, lstat, rstat)


def renew_kernel(many, turned_ref, inv_ref, left_out, right_out):
    for u in range(many):
        for which, out in ((0, left_out), (1, right_out)):
            out[u] = three(dot_nt, split2(turned_ref[u, which]), split2(inv_ref[u, which]))


def renew_bases(turned, inverse, many=6):
    count, _, side, _ = turned.shape
    one = pl.BlockSpec((many, side, side), lambda s: (s, 0, 0))
    two = pl.BlockSpec((many, 2, side, side), lambda s: (s, 0, 0, 0))
    tile = jax.ShapeDtypeStruct((count, side, side), jnp.float32)
    return pl.pallas_call(
        functools.partial(renew_kernel, many),
        grid=(count // many,),
        in_specs=[two, two],
        out_specs=[one, one],
        out_shape=[tile, tile],
        compiler_params=pltpu.CompilerParams(vmem_limit_bytes=60 * 2**20),
    )(turned, inverse)


def chol_kernel(batch, order, riders, gram_ref, *refs):
    count = len(riders.specs)
    sources, out_ref, outs = refs[:count], refs[count], refs[count + 1 : 2 * count + 1]
    low_ref, inv_ref, piv_ref = refs[2 * count + 1 : 2 * count + 4]
    ride_sems_here = refs[2 * count + 4 :]
    if count:
        riders.begin(sources, outs, ride_sems_here)
    tiles = order // 8
    rows8 = lax.broadcasted_iota(jnp.int32, (8, batch), 0)

    def load_slab(j, carry):
        low_ref[j, pl.ds(0, order), :] = gram_ref[pl.ds(j, batch, stride=order), :].T
        inv_ref[j] = jnp.zeros(inv_ref.shape[1:], jnp.float32)
        return carry

    lax.fori_loop(0, order, load_slab, 0, unroll=8)

    def bcast(ref, j, row):
        return jnp.broadcast_to(ref[j, pl.ds(row, 1), :], (8, batch))

    def block_column(block, carry):
        base = pl.multiple_of(block * 8, 8)

        def updated(tile_rows, seed):
            def one(j, accs):
                mult = [bcast(low_ref, j, base + k) for k in range(8)]
                out = []
                for s, rows in enumerate(tile_rows):
                    piece = low_ref[j, pl.ds(rows, 8), :]
                    out.extend(accs[s * 8 + k] - piece * mult[k] for k in range(8))
                return tuple(out)

            def eight(step, accs):
                for u in range(8):
                    accs = one(step * 8 + u, accs)
                return accs

            return list(lax.fori_loop(0, block, eight, tuple(seed)))

        accs = updated([base], [low_ref[base + k, pl.ds(base, 8), :] for k in range(8)])
        scales = []
        for k in range(8):
            scale = lax.rsqrt(jnp.broadcast_to(accs[k][k : k + 1, :], (8, batch)))
            scales.append(scale)
            accs[k] = jnp.where(rows8 >= k, accs[k] * scale, 0.0)
            for later in range(k + 1, 8):
                accs[later] = accs[later] - accs[k] * jnp.broadcast_to(
                    accs[k][later : later + 1, :], (8, batch)
                )
        for k in range(8):
            low_ref[base + k, pl.ds(base, 8), :] = accs[k]
            piv_ref[base + k] = scales[k]

        def pair(p, carry):
            first = pl.multiple_of(base + 8 + p * 16, 8)
            both = [first, pl.multiple_of(first + 8, 8)]
            accs = updated(
                both, [low_ref[base + k, pl.ds(rows, 8), :] for rows in both for k in range(8)]
            )
            for k in range(8):
                scale = piv_ref[base + k]
                for s in range(2):
                    accs[s * 8 + k] = accs[s * 8 + k] * scale
                for later in range(k + 1, 8):
                    mult = bcast(low_ref, base + k, base + later)
                    for s in range(2):
                        accs[s * 8 + later] = accs[s * 8 + later] - accs[s * 8 + k] * mult
            for s, rows in enumerate(both):
                for k in range(8):
                    low_ref[base + k, pl.ds(rows, 8), :] = accs[s * 8 + k]
            return carry

        lax.fori_loop(0, (tiles - block) // 2, pair, 0)
        return carry

    lax.fori_loop(0, tiles, block_column, 0)

    def block_row(block, carry):
        base = pl.multiple_of(block * 8, 8)

        def finish(accs, both):
            for k in range(8):
                scale = piv_ref[base + k]
                for s in range(len(both)):
                    accs[s * 8 + k] = accs[s * 8 + k] * scale
                for later in range(k + 1, 8):
                    mult = bcast(low_ref, base + k, base + later)
                    for s in range(len(both)):
                        accs[s * 8 + later] = accs[s * 8 + later] - accs[s * 8 + k] * mult
            for s, columns in enumerate(both):
                for k in range(8):
                    inv_ref[base + k, pl.ds(columns, 8), :] = accs[s * 8 + k]

        def pair(p, carry):
            first = pl.multiple_of(p * 16, 8)
            both = [first, pl.multiple_of(first + 8, 8)]

            def eight(step, accs):
                for u in range(8):
                    j = step * 8 + u
                    mult = [bcast(low_ref, j, base + k) for k in range(8)]
                    out = []
                    for s, columns in enumerate(both):
                        piece = inv_ref[j, pl.ds(columns, 8), :]
                        out.extend(accs[s * 8 + k] - piece * mult[k] for k in range(8))
                    accs = tuple(out)
                return accs

            accs = list(lax.fori_loop(
                p * 2, block, eight, (jnp.zeros((8, batch), jnp.float32),) * 16
            ))
            finish(accs, both)
            return carry

        lax.fori_loop(0, (block + 1) // 2, pair, 0)
        odd = block % 2

        def diagonal():
            accs = [jnp.where(rows8 == k, 1.0, 0.0) for k in range(8)]
            finish(accs, [base])

        diagonal()
        return carry

    lax.fori_loop(0, tiles, block_row, 0)

    def store_slab(i, carry):
        out_ref[pl.ds(i, batch, stride=order), :] = inv_ref[i, pl.ds(0, order), :].T
        return carry

    lax.fori_loop(0, order, store_slab, 0, unroll=8)
    if count:
        riders.end(sources, outs, ride_sems_here)

def inverse_factors(gram, rides=(), guests=(), number=None):
    count, pair, order, _ = gram.shape
    batch = count * pair
    riders = Riders(rides)
    params = dict(vmem_limit_bytes=60 * 2**20)
    if guests:
        params.update(collective_id=number, has_side_effects=True)
    vmem = pl.BlockSpec(memory_space=pltpu.VMEM)
    out, *arrived = pl.pallas_call(
        functools.partial(chol_kernel, batch, order, riders),
        out_shape=[jax.ShapeDtypeStruct((batch * order, order), jnp.float32)] + riders.shapes(guests),
        in_specs=[vmem] + [HBM] * len(guests),
        out_specs=[vmem] + [HBM] * len(guests),
        scratch_shapes=[
            pltpu.VMEM((order, order + 8, batch), jnp.float32),
            pltpu.VMEM((order, order + 8, batch), jnp.float32),
            pltpu.VMEM((order, 8, batch), jnp.float32),
        ]
        + riders.sems(),
        compiler_params=pltpu.CompilerParams(**params),
        cost_estimate=pl.CostEstimate(flops=5 * 10**10, bytes_accessed=12 * 10**6, transcendentals=0),
    )(gram.reshape(batch * order, order), *guests)
    return (out.reshape(gram.shape), *arrived)


def norm_joint_kernel(channels, riders, x_ref, gain_ref, weight_ref, *refs):
    count = len(riders.specs)
    sources, (normed_ref, xs_ref, gate_ref) = refs[:count], refs[count : count + 3]
    outs, sems = refs[count + 3 : 2 * count + 3], refs[2 * count + 3 :]
    if count:

        @pl.when(pl.program_id(0) == 0)
        def _():
            riders.begin(sources, outs, sems)

    width = x_ref.shape[2]
    x = x_ref[...].astype(jnp.float32).reshape(-1, width)
    inverse = lax.rsqrt(jnp.mean(x * x, axis=1, keepdims=True) + norm_epsilon)
    normed = (x * inverse * gain_ref[...]).astype(jnp.bfloat16)
    normed_ref[...] = normed
    joint = dot_nn(normed, weight_ref[...]).astype(jnp.bfloat16)
    xs_ref[...] = joint[:, :channels]
    gate_ref[...] = joint[:, channels:]
    if count:

        @pl.when(pl.program_id(0) == pl.num_programs(0) - 1)
        def _():
            riders.end(sources, outs, sems)


def norm_joint(x, gain, weight, rides=(), guests=(), number=None, many=2):
    devices, rows, width = x.shape
    riders = Riders(rides)
    params = dict(collective_id=number, has_side_effects=True) if guests else {}
    tokens, block = devices * rows, many * rows
    channels = weight.shape[1] // 2
    wide = pl.BlockSpec((block, width), lambda i: (i, 0))
    thin = pl.BlockSpec((block, channels), lambda i: (i, 0))
    half = jax.ShapeDtypeStruct((tokens, channels), jnp.bfloat16)
    return pl.pallas_call(
        functools.partial(norm_joint_kernel, channels, riders),
        grid=(tokens // block,),
        in_specs=[
            pl.BlockSpec((many, rows, width), lambda i: (i, 0, 0)),
            pl.BlockSpec((1, width), lambda i: (0, 0)),
            pl.BlockSpec((width, 2 * channels), lambda i: (0, 0)),
        ]
        + [HBM] * len(guests),
        out_specs=[wide, thin, thin] + [HBM] * len(guests),
        out_shape=[jax.ShapeDtypeStruct((tokens, width), jnp.bfloat16), half, half] + riders.shapes(guests),
        scratch_shapes=riders.sems(),
        compiler_params=pltpu.CompilerParams(vmem_limit_bytes=60 * 2**20, **params),
        cost_estimate=pl.CostEstimate(
            flops=4 * tokens * width * channels, bytes_accessed=4 * tokens * width, transcendentals=0
        ),
    )(x, gain, weight, *guests)


def plane_product_kernel(count, many, weight_ref, *refs):
    lefts, out_ref, total_ref = refs[:count], refs[count], refs[count + 1]
    step = pl.program_id(0)
    left = jnp.concatenate([ref[u] for u in range(many) for ref in lefts], axis=1)
    part = dot_nt(left, jnp.concatenate([weight_ref[u] for u in range(many)], axis=1))

    @pl.when(step == 0)
    def _():
        total_ref[...] = part

    @pl.when(step > 0)
    def _():
        total_ref[...] += part

    @pl.when(step == pl.num_programs(0) - 1)
    def _():
        out_ref[...] = total_ref[...].astype(out_ref.dtype)


def plane_product(lefts, weight, block, many=4):
    members, tokens, channels = lefts[0].shape
    rows, width = len(lefts) * channels, weight.shape[1]
    return pl.pallas_call(
        functools.partial(plane_product_kernel, len(lefts), many),
        grid=(members // many,),
        in_specs=[pl.BlockSpec((many, width, rows), lambda p: (p, 0, block))]
        + [pl.BlockSpec((many, tokens, channels), lambda p: (p, 0, 0))] * len(lefts),
        out_specs=pl.BlockSpec((tokens, width), lambda p: (0, 0)),
        out_shape=jax.ShapeDtypeStruct((tokens, width), jnp.bfloat16),
        scratch_shapes=[pltpu.VMEM((tokens, width), jnp.float32)],
        compiler_params=pltpu.CompilerParams(vmem_limit_bytes=60 * 2**20),
        cost_estimate=pl.CostEstimate(
            flops=2 * members * tokens * rows * width, bytes_accessed=2 * members * rows * width, transcendentals=0
        ),
    )(weight, *lefts)


def plane_back_kernel(left_ref, weight_ref, out_ref):
    out_ref[0] = dot_nn(left_ref[...], weight_ref[0]).astype(out_ref.dtype)


def plane_back(left, weight, channels, block):
    members, width, _ = weight.shape
    tokens = left.shape[0]
    return pl.pallas_call(
        plane_back_kernel,
        grid=(members,),
        in_specs=[
            pl.BlockSpec((tokens, width), lambda p: (0, 0)),
            pl.BlockSpec((1, width, channels), lambda p: (p, 0, block)),
        ],
        out_specs=pl.BlockSpec((1, tokens, channels), lambda p: (p, 0, 0)),
        out_shape=jax.ShapeDtypeStruct((members, tokens, channels), jnp.bfloat16),
        compiler_params=pltpu.CompilerParams(vmem_limit_bytes=60 * 2**20),
        cost_estimate=pl.CostEstimate(
            flops=2 * members * tokens * width * channels, bytes_accessed=2 * members * width * channels, transcendentals=0
        ),
    )(left, weight)


def line_product_kernel(left_ref, right_ref, out_ref):
    product = dot_tn(left_ref[0], right_ref[...])
    side = out_ref.shape[3]
    for b in range(out_ref.shape[1]):
        out_ref[0, b] = product[:, b * side : (b + 1) * side].astype(out_ref.dtype)


def line_product(lefts, right, tall):
    members, tokens, channels = lefts.shape
    width = right.shape[1]
    side = width // tall
    return pl.pallas_call(
        line_product_kernel,
        grid=(members,),
        in_specs=[
            pl.BlockSpec((1, tokens, channels), lambda p: (p, 0, 0)),
            pl.BlockSpec((tokens, width), lambda p: (0, 0)),
        ],
        out_specs=pl.BlockSpec((1, tall, channels, side), lambda p: (p, 0, 0, 0)),
        out_shape=jax.ShapeDtypeStruct((members, tall, channels, side), jnp.bfloat16),
        compiler_params=pltpu.CompilerParams(vmem_limit_bytes=60 * 2**20),
        cost_estimate=pl.CostEstimate(
            flops=2 * members * tokens * channels * width, bytes_accessed=4 * members * channels * width, transcendentals=0
        ),
    )(lefts, right)


def plain_three(dot, left, right):
    return dot(left[0], right[0]) + (dot(left[0], right[1]) + dot(left[1], right[0]))


def channel_kernel(weight_ref, grad_ref, first_ref, second_ref, left_ref, right_ref, lstat_ref, rstat_ref,
                   first_out, second_out, weight_out, lstat_out, rstat_out, lturn_out, rturn_out, lgram_out, rgram_out):
    grad = split2(grad_ref[...])
    left, right = split2(left_ref[...]), split2(right_ref[...])
    turned = plain_three(dot_tn, left, split2(plain_three(dot_nn, grad, right)))
    first = beta_first * first_ref[...] + (1.0 - beta_first) * turned
    second = beta_second * second_ref[...] + (1.0 - beta_second) * turned * turned
    first_out[...] = first
    second_out[...] = second
    direction = split2(
        first / (1.0 - beta_first**STEP) / (jnp.sqrt(second / (1.0 - beta_second**STEP)) + adam_epsilon)
    )
    returned = plain_three(dot_nn, left, split2(plain_three(dot_nt, direction, right)))
    weight = weight_ref[...]
    weight_out[...] = weight - learn_rate * (returned + weight_decay * weight)
    for basis_ref, basis, stat_ref, product, stat_out, turn_out, gram_out in (
        (left_ref, left, lstat_ref, plain_three(dot_nt, grad, grad), lstat_out, lturn_out, lgram_out),
        (right_ref, right, rstat_ref, plain_three(dot_tn, grad, grad), rstat_out, rturn_out, rgram_out),
    ):
        order = basis_ref.shape[0]
        diagonal = lax.broadcasted_iota(jnp.int32, (order, order), 0) == lax.broadcasted_iota(
            jnp.int32, (order, order), 1
        )
        stat = stat_decay * stat_ref[...] + (1.0 - stat_decay) * product
        stat_out[...] = stat
        trace = jnp.sum(jnp.sum(jnp.where(diagonal, stat, 0.0), axis=0, keepdims=True), axis=1, keepdims=True)
        value = plain_three(dot_nn, split2(stat), basis) + (trace / order) * basis_ref[...]
        turn_out[...] = value
        value = split2(value)
        gram_out[...] = plain_three(dot_tn, value, value)


def channel_moments(weight, grad, first, second, left, right, lstat, rstat):
    f32 = jnp.float32
    rows = jax.ShapeDtypeStruct(weight.shape, f32)
    small = jax.ShapeDtypeStruct(left.shape, f32)
    large = jax.ShapeDtypeStruct(right.shape, f32)
    return pl.pallas_call(
        channel_kernel,
        out_shape=[rows] * 3 + [small, large] * 3,
        compiler_params=pltpu.CompilerParams(vmem_limit_bytes=60 * 2**20),
        cost_estimate=pl.CostEstimate(flops=8 * 10**9, bytes_accessed=6 * 10**6, transcendentals=0),
    )(weight, grad, first, second, left, right, lstat, rstat)


PANEL = 32


def factor_inverse(block):
    order = block.shape[0]
    rows = lax.broadcasted_iota(jnp.int32, (order, 2 * order), 0)
    columns = lax.broadcasted_iota(jnp.int32, (order, 2 * order), 1)
    both = jnp.concatenate([block, jnp.zeros_like(block)], axis=1) + jnp.where(columns == rows + order, 1.0, 0.0)
    for k in range(order):
        scale = lax.rsqrt(both[k : k + 1, k : k + 1])
        row = both[k : k + 1, :] * scale
        column = both[:, k : k + 1] * scale
        both = jnp.where(rows == k, row, jnp.where(rows > k, both - column * row, both))
    return both[:, order:]


def solve_kernel(count, riders, *refs):
    guests = len(riders.specs)
    grams, sides, refs = refs[:count], refs[count : 2 * count], refs[2 * count :]
    sources, outs, refs = refs[:guests], refs[guests : guests + count], refs[guests + count :]
    arrived, works, ride = refs[:guests], refs[guests : guests + 2 * count], refs[guests + 2 * count :]
    if guests:
        riders.begin(sources, arrived, ride)
    for i in range(count):
        order = grams[i].shape[0]
        gram, side = works[2 * i], works[2 * i + 1]
        gram[...] = grams[i][...]
        side[...] = sides[i][...]
        for start in range(0, order, PANEL):
            stop = start + PANEL
            low = split2(factor_inverse(gram[start:stop, start:stop]))
            upper = split2(plain_three(dot_nn, low, split2(gram[start:stop, :])))
            solved = plain_three(dot_nn, low, split2(side[start:stop, :]))
            outs[i][start:stop, :] = solved
            if stop < order:
                gram[stop:, :] -= plain_three(dot_tn, upper, upper)[stop:]
                side[stop:, :] -= plain_three(dot_tn, upper, split2(solved))[stop:]
    if guests:
        riders.end(sources, arrived, ride)


def solve_factors(grams, sides, rides=(), guests=(), number=None):
    count = len(grams)
    riders = Riders(rides)
    params = dict(vmem_limit_bytes=60 * 2**20)
    if guests:
        params.update(collective_id=number, has_side_effects=True)
    shapes = [jax.ShapeDtypeStruct(s.shape, jnp.float32) for s in sides]
    scratch = []
    for g, s in zip(grams, sides):
        scratch += [pltpu.VMEM(g.shape, jnp.float32), pltpu.VMEM(s.shape, jnp.float32)]
    vmem = pl.BlockSpec(memory_space=pltpu.VMEM)
    return pl.pallas_call(
        functools.partial(solve_kernel, count, riders),
        in_specs=[vmem] * (2 * count) + [HBM] * len(guests),
        out_specs=[vmem] * count + [HBM] * len(guests),
        out_shape=shapes + riders.shapes(guests),
        scratch_shapes=scratch + riders.sems(),
        compiler_params=pltpu.CompilerParams(**params),
        cost_estimate=pl.CostEstimate(flops=4 * 10**10, bytes_accessed=3 * 10**6, transcendentals=0),
    )(*grams, *sides, *guests)


def doc_positions(doc_lengths):
    starts = jnp.cumsum(doc_lengths, axis=1) - doc_lengths
    places = jnp.arange(L, dtype=jnp.int32)
    begun = jnp.where(starts[:, None, :] <= places[None, :, None], starts[:, None, :], 0)
    return places[None, :] - jnp.max(begun, axis=2)


def adam_step(weight, gradient, first, second):
    first_new = beta_first * first + (1.0 - beta_first) * gradient
    second_new = beta_second * second + (1.0 - beta_second) * gradient * gradient
    direction = (
        first_new
        / (1.0 - beta_first**STEP)
        / (jnp.sqrt(second_new / (1.0 - beta_second**STEP)) + adam_epsilon)
    )
    return (first_new, second_new, weight - vector_rate * (direction + weight_decay * weight))


def later(values, lag):
    return jnp.pad(values, ((lag, 0), (0, 0)))[: values.shape[0]]


def sooner(values, lag):
    return jnp.pad(values, ((0, lag), (0, 0)))[lag:]


def conv_pre(xs, taps, offset, place):
    total = offset[None] + taps[K - 1][None] * xs
    for lag in range(1, K):
        total = total + jnp.where(place >= lag, taps[K - 1 - lag][None] * later(xs, lag), 0.0)
    return total


def rank_within(key):
    count = key.shape[0]
    earlier = jnp.arange(count)[None, :] < jnp.arange(count)[:, None]
    return jnp.sum(((key[None, :] == key[:, None]) & earlier).astype(jnp.int32), axis=1)


def table(size, target, chosen, value):
    hit = (target[None, :] == jnp.arange(size)[:, None]) & chosen[None, :]
    return jnp.sum(jnp.where(hit, value[None, :], 0), axis=1)


CAPS = (13, 9)


class Routes:
    def __init__(self, tile_slot, devices, tiles_here, tall, half):
        count = tile_slot.shape[0]
        plane = devices // LINES
        wide = 2 * half
        tile = jnp.arange(count, dtype=jnp.int32)
        output = tile >= tall * wide
        relative = tile - tall * wide
        column = tile % wide
        self.plane = plane
        self.local = tile_slot % tiles_here
        self.owner = tile_slot // tiles_here
        self.target = jnp.where(output, relative // tall, column % half)
        self.kind = jnp.where(output, 2, column // half)
        self.place = jnp.where(output, 2 * tall + relative % tall, column // half * tall + tile // wide)
        self.owner_line, self.owner_spot = self.owner // plane, self.owner % plane
        self.target_line, self.target_spot = self.target // plane, self.target % plane
        self.ways, self.fits = self.settle(CAPS)

    def settle(self, caps):
        odd = self.place % 2 == 1
        for attempt in range(2):
            middle = jnp.where(
                odd, self.owner_line * self.plane + self.target_spot, self.target_line * self.plane + self.owner_spot
            )
            kind = odd.astype(jnp.int32)
            line_key = (self.owner_line * LINES + self.target_line) * self.plane + middle % self.plane
            plane_key = (self.owner_spot * self.plane + self.target_spot) * LINES + middle // self.plane
            ranks = rank_within(line_key * 2 + kind), rank_within(plane_key * 2 + kind)
            full = (ranks[0] >= caps[0]) | (ranks[1] >= caps[1])
            if attempt == 0:
                odd = odd ^ full
        return (odd, middle, *ranks), ~jnp.any(full)

    def spots(self, line_member, spot_member):
        by_line = line_member * CAPS[0] + self.ways[2]
        by_plane = LINES * CAPS[0] + spot_member * CAPS[1] + self.ways[3]
        return by_line, by_plane

    def tables(self, me):
        odd, middle = self.ways[:2]
        size = LINES * CAPS[0] + self.plane * CAPS[1]
        target_line, target_plane = self.spots(self.target_line, self.target_spot)
        owner_line, owner_plane = self.spots(self.owner_line, self.owner_spot)
        first = table(size, jnp.where(odd, target_plane, target_line), self.owner == me, self.local)
        second = table(
            size, jnp.where(odd, target_line, target_plane), middle == me, jnp.where(odd, owner_plane, owner_line)
        )
        landed = jnp.where(odd, owner_line, owner_plane)
        back_first = table(size, jnp.where(odd, owner_line, owner_plane), self.target == me, self.place)
        back_second = table(
            size, jnp.where(odd, owner_plane, owner_line), middle == me, jnp.where(odd, target_line, target_plane)
        )
        back_landed = jnp.where(odd, target_plane, target_line)
        return first, second, landed, back_first, back_second, back_landed


def pick(values, index):
    return values.at[index].get(mode="clip")


def device_groups(devices):
    plane = devices // LINES
    lines = [[z * plane + p for z in range(LINES)] for p in range(plane)]
    planes = [[z * plane + p for p in range(plane)] for z in range(LINES)]
    return lines, planes


def spread(value, devices):
    lines, planes = device_groups(devices)
    plane = devices // LINES
    step = lax.all_to_all(
        jnp.broadcast_to(value, (LINES,) + value.shape), "tok", 0, 0, tiled=True, axis_index_groups=lines
    )
    step = lax.all_to_all(
        jnp.broadcast_to(step, (plane,) + step.shape), "tok", 0, 0, tiled=True, axis_index_groups=planes
    )
    return jnp.swapaxes(step, 0, 1).reshape((devices * value.shape[0],) + value.shape[1:])


def fold(values, devices):
    lines, planes = device_groups(devices)
    plane = devices // LINES
    rows = values.shape[0] // devices
    parts = jnp.swapaxes(values.reshape((LINES, plane, rows) + values.shape[1:]), 0, 1).astype(jnp.bfloat16)
    parts = lax.all_to_all(parts, "tok", 0, 0, tiled=True, axis_index_groups=planes)
    parts = jnp.sum(parts.astype(jnp.float32), axis=0)
    parts = lax.all_to_all(parts, "tok", 0, 0, tiled=True, axis_index_groups=lines)
    return jnp.sum(parts, axis=0)


def core(
    routes,
    fast,
    x_all,
    small_all,
    weights,
    layer_in,
    cotangent,
    doc_lengths,
    tile_slot,
    pool_weight,
    pool_first,
    pool_second,
    pool_left,
    pool_right,
    pool_left_stat,
    pool_right_stat,
    channel_weight,
    channel_first,
    channel_second,
    channel_left,
    channel_right,
    channel_left_stat,
    channel_right_stat,
    norm_gain,
    gain_first,
    gain_second,
    channel_vectors,
    vector_first,
    vector_second,
):
    bf16, f32 = jnp.bfloat16, jnp.float32
    devices = lax.axis_size("tok")
    me = lax.axis_index("tok")
    lines, planes = device_groups(devices)
    plane = devices // LINES
    my_line, my_plane = me // plane, me % plane
    tok_rows, model_width = layer_in.shape
    tokens = tok_rows * devices
    rows = tokens // L
    channels = channel_vectors.shape[1]
    inner_width = channels * devices
    tiles_here, side, _ = pool_weight.shape
    tall = model_width // side
    half = inner_width // side
    wide = 2 * half
    cut = side // channels
    input_tiles = tall * wide
    select_width = channel_weight.shape[1] - R
    gain_here = norm_gain.shape[0]

    gain_float = small_all[:, select_width, :gain_here].reshape(1, model_width).astype(f32)
    select_blocks = small_all[:, :select_width].reshape(half, cut, select_width, channels)
    select_blocks = select_blocks.transpose(0, 2, 1, 3).reshape(half, select_width, side)
    if not fast:
        pool_low = pool_weight.astype(bf16)

    is_out = routes.kind == 2
    if fast:
        input_local, output_local, plane_own, back_first, back_second, back_landed = weights
    else:
        pool_all = lax.all_gather(pool_low, "tok", axis=0, tiled=True)
        columns = me // cut
        input_slots = tile_slot[:input_tiles].reshape(tall, 2, half)
        input_own = jnp.take(
            pool_all, lax.dynamic_index_in_dim(input_slots, columns, 2, False).T.reshape(-1), axis=0
        )
        output_slots = tile_slot[input_tiles:].reshape(half, tall)
        output_own = jnp.take(pool_all, lax.dynamic_index_in_dim(output_slots, columns, 0, False), axis=0)
        offset = me % cut * channels
        input_local = input_own.reshape(2, tall, side, side)
        output_local = output_own
        if cut > 1:
            input_local = lax.dynamic_slice_in_dim(input_local, offset, channels, axis=3)
            output_local = lax.dynamic_slice_in_dim(output_local, offset, channels, axis=1)
        input_local = input_local.transpose(1, 2, 0, 3).reshape(model_width, 2 * channels)
        output_local = output_local.transpose(1, 0, 2).reshape(channels, model_width)

    if fast:
        plane_weight = lax.all_gather(plane_own, "tok", axis=0, axis_index_groups=planes)
        upper, lower = cotangent[: tok_rows // 2], cotangent[tok_rows // 2 :]
        normed_all, xs_low, gates, upper = norm_joint(
            x_all, gain_float, input_local, [("line_gather", plane)], [upper], 11
        )
    else:
        normed_all, xs_low, gates = norm_joint(x_all, gain_float, input_local)
        cotangent_all = lax.all_gather(cotangent, "tok", axis=0, tiled=True)

    def to_tokens(values, number=None):
        lead = values.shape[:-2]
        parts = values.reshape(lead + (devices, tok_rows, channels))
        if fast and number is not None:
            moved = everyone(parts, number)
        else:
            moved = lax.all_to_all(parts, "tok", split_axis=len(lead), concat_axis=len(lead), tiled=True)
        moved = moved.reshape(lead + (half, cut, tok_rows, channels))
        return jnp.swapaxes(moved, -3, -2).reshape(lead + (half, tok_rows, side))

    place = doc_positions(doc_lengths).reshape(-1, 1)
    taps, offset = channel_vectors[:K], channel_vectors[K]
    xs = xs_low.astype(f32)
    filtered = jax.nn.silu(conv_pre(xs, taps, offset, place)).astype(bf16)
    filtered_tokens = to_tokens(filtered, 3)
    block = jnp.concatenate(
        [
            jnp.einsum("gtc,gfc->tf", filtered_tokens, select_blocks[:, :R], preferred_element_type=f32),
            jnp.einsum("gtc,gfc->ft", filtered_tokens, select_blocks[:, R:], preferred_element_type=f32),
        ],
        axis=0,
    ).astype(bf16)
    if fast:
        blocks, lower = spread_blocks(block, plane, 4, [("line_gather", plane)], [lower])
        blocks = blocks.reshape(devices, tok_rows + 2 * N, R)
        cotangent_line = jnp.concatenate([upper, lower], axis=1).reshape(LINES * tok_rows, model_width)
    else:
        blocks = spread(block[None], devices)

    if fast:
        def share(values):
            return values.reshape(LINES, plane, tok_rows, channels)

        def across(blocks, which):
            blocks = [values.reshape(plane, LINES * tok_rows, channels) for values in blocks]
            return plane_product(blocks, plane_weight, which).reshape(LINES, tok_rows, model_width)

    by_row = lambda values: values.reshape((rows, L) + values.shape[1:])
    begins = by_row(jnp.broadcast_to(jnp.where(place == 0, 1e30, 0.0).astype(bf16), (tokens, channels)))
    step_local = channel_weight[:, select_width:].astype(bf16)
    rates = jnp.exp(channel_vectors[K + 2 : K + 2 + N])
    step_bias = channel_vectors[K + 1 : K + 2]
    skip_gain = channel_vectors[K + 2 + N :]
    scan_params = (step_local, step_bias, rates, skip_gain)
    scan_rides, scan_guests = [], []
    if fast:
        back_parts = plane_back(cotangent_line, plane_weight, channels, 2)
        scan_rides = [("plane_back", plane)]
        scan_guests = [back_parts.reshape(plane, LINES, tok_rows, channels)]
    mixed, gate_slope, kept, *arrived = scan_forward(
        by_row(filtered), by_row(gates), begins, blocks, *scan_params, scan_rides, scan_guests, 12
    )
    mixed = mixed.reshape(tokens, channels)
    if fast:
        back_chan = arrived[0].reshape(tokens, channels)
        (mixed_plane,) = exchange([("plane", plane)], [share(mixed)], 7)
    else:
        back_chan = jnp.einsum("td,cd->tc", cotangent_all, output_local, preferred_element_type=f32).astype(bf16)
    back_chan = lax.optimization_barrier(back_chan)
    gate_grad = (back_chan.astype(f32) * gate_slope.reshape(tokens, channels)).astype(bf16)

    def input_parts(grads):
        part = jnp.einsum("td,tc->dc", normed_all, jnp.concatenate(grads, axis=1), preferred_element_type=f32)
        part = part.astype(bf16).reshape(tall, side, len(grads), channels)
        return part.transpose(2, 0, 1, 3)

    def every_input(part):
        every = lax.all_gather(part, "tok", axis=0)
        every = every.reshape(half, cut, tall, side, channels).transpose(0, 2, 3, 1, 4)
        return every.reshape(half * tall, side, side)

    if fast:
        output_shares = line_product(
            mixed_plane.reshape(plane, LINES * tok_rows, channels), cotangent_line, tall
        )
        layer_parts = across([mixed_plane], 2)

    scan_in = (by_row(filtered), by_row(gates), by_row(back_chan), begins, blocks)
    if fast:
        *scan_grads, output_shares, layer_parts = scan_backward(
            *scan_in,
            *scan_params,
            kept,
            [("plane_rows", plane), ("line", plane)],
            [output_shares, layer_parts],
            6,
        )
    else:
        scan_grads = scan_backward(*scan_in, *scan_params, kept)
    draw, filter_mix, inject_grad, read_grad, rate_sum, skip_grad, bias_grad = scan_grads
    draw = draw.reshape(tokens, channels)
    rank_in = blocks[:, :tok_rows].reshape(tokens, R)
    step_grad = jnp.einsum("tc,tr->rc", draw, rank_in, preferred_element_type=f32)
    rank_part = jnp.einsum("tc,cr->tr", draw, step_local, preferred_element_type=f32)
    state_part = jnp.concatenate([inject_grad.reshape(tokens, N), read_grad.reshape(tokens, N)], axis=1)
    if fast:
        parts = jnp.concatenate(
            [
                rank_part.astype(bf16).reshape(devices, tok_rows, R),
                state_part.astype(bf16).reshape(devices, tok_rows, 2 * N).transpose(0, 2, 1),
            ],
            axis=1,
        )
        grad_blocks, gate_plane = fold_and_spread(
            parts.reshape(LINES, plane, tok_rows + 2 * N, R),
            plane,
            5,
            [("plane", plane)],
            [share(gate_grad)],
        )
        grad_blocks = grad_blocks.reshape(devices, tok_rows + 2 * N, R)
        projected_grad_all = jnp.concatenate(
            [
                grad_blocks[:, :tok_rows].reshape(tokens, R),
                grad_blocks[:, tok_rows:].transpose(0, 2, 1).reshape(tokens, 2 * N),
            ],
            axis=1,
        )
    else:
        partial_sums = jnp.concatenate([rank_part, state_part], axis=1)
        projected_grad_all = spread(fold(partial_sums, devices).astype(bf16), devices)
    select_local = channel_weight[:, :select_width].astype(bf16)
    back_filter = jnp.einsum(
        "tf,cf->tc", projected_grad_all, select_local, preferred_element_type=f32
    ).astype(bf16)
    select_grad = jnp.einsum("tc,tf->fc", filtered, projected_grad_all, preferred_element_type=f32)
    pre = conv_pre(xs, taps, offset, place)
    gate = jax.nn.sigmoid(pre)
    dpre = (filter_mix.reshape(tokens, channels) + back_filter.astype(f32)) * (gate * (1.0 + pre * (1.0 - gate)))
    offset_grad = jnp.sum(dpre, axis=0)
    taps_grad = [jnp.sum(dpre * xs, axis=0)]
    xs_grad = taps[K - 1][None] * dpre
    for lag in range(1, K):
        masked = jnp.where(place >= lag, dpre, 0.0)
        xs_grad = xs_grad + taps[K - 1 - lag][None] * sooner(masked, lag)
        taps_grad.insert(0, jnp.sum(masked * later(xs, lag), axis=0))
    xs_grad = xs_grad.astype(bf16)
    input_both = input_parts([xs_grad, gate_grad])
    if fast:
        output_part = jnp.sum(output_shares.astype(f32), axis=0).astype(bf16)
        tiles = jnp.concatenate([input_both.reshape(2 * tall, side, channels), output_part], axis=0)
        route = ("route", plane, *CAPS)
        rides = [route, ("plane", plane)]
        guests = [pick(tiles, back_first), share(xs_grad)]
    else:
        xs_every, gate_every = every_input(input_both[0]), every_input(input_both[1])
        output_part = jnp.einsum("tc,td->cd", mixed, cotangent_all, preferred_element_type=f32).astype(bf16)
        output_every = lax.all_gather(output_part.reshape(channels, tall, side).transpose(1, 0, 2), "tok", axis=0)
        output_every = (
            output_every.reshape(half, cut, tall, channels, side)
            .transpose(0, 2, 1, 3, 4)
            .reshape(half * tall, side, side)
        )
        rides, guests = [], []

    first_c, second_c, weight_c, rstat_c, lstat_c, right_turned, left_turned, right_gram, left_gram = channel_moments(
        channel_weight.T,
        jnp.concatenate([select_grad, step_grad], axis=0),
        channel_first.T,
        channel_second.T,
        channel_right,
        channel_left,
        channel_right_stat,
        channel_left_stat,
    )
    left_c, right_c, *arrived = solve_factors(
        (left_gram, right_gram), (left_turned.T, right_turned.T), rides, guests, 8
    )
    channel_new = (first_c.T, second_c.T, weight_c.T, left_c.T, right_c.T, lstat_c, rstat_c)
    if fast:
        middle, xs_plane = arrived
        (arrived_tiles,) = exchange([route], [pick(middle, back_second)], 9)
        normed_parts = across([xs_plane, gate_plane], 0)
        x_here = x_all.reshape((LINES, plane) + x_all.shape[1:])
        x_here = lax.dynamic_index_in_dim(x_here, me % plane, 1, False).astype(f32)
        root = lax.rsqrt(jnp.mean(x_here * x_here, axis=2, keepdims=True) + norm_epsilon)
        gain_part = jnp.sum(normed_parts.astype(f32) * x_here * root, axis=(0, 1)).reshape(devices, 1, gain_here)
        gain_part = jnp.pad(gain_part, ((0, 0), (0, 7), (0, 128 - gain_here)))
        rides = [("line", plane), ("all", plane)]
        guests = [normed_parts, gain_part]

    own_slot = tile_slot - me * tiles_here
    every_tile = jnp.full(tile_slot.shape, True)
    if fast:
        grads = (arrived_tiles,)
        kind = jnp.zeros((tiles_here,), jnp.int32)
        index = table(tiles_here, own_slot, every_tile, back_landed)
    else:
        grads = (xs_every, gate_every, output_every)
        tile = jnp.arange(tile_slot.shape[0], dtype=jnp.int32)
        kind = table(tiles_here, own_slot, every_tile, routes.kind)
        spot = jnp.where(is_out, tile - input_tiles, tile % wide % half * tall + tile // wide)
        index = table(tiles_here, own_slot, every_tile, spot)
    first_next, second_next, weight_next, lstat_next, rstat_next, turned, gram = soap_tiles(
        kind,
        index,
        grads,
        pool_weight,
        pool_first,
        pool_second,
        pool_left,
        pool_right,
        pool_left_stat,
        pool_right_stat,
    )
    inverse_low, *arrived = inverse_factors(gram, rides, guests, 10)
    left_next, right_next = renew_bases(turned, inverse_low)

    if fast:
        layer_out = (layer_in.astype(f32) + jnp.sum(layer_parts.astype(f32), axis=0)).astype(bf16)
        normed_grad = jnp.sum(arrived[0].astype(f32), axis=0)
    else:
        mixed_tokens = to_tokens(mixed)
        joint_grad = to_tokens(jnp.stack([xs_grad, gate_grad])).reshape(wide, tok_rows, side)
        layer_out = tile_product(
            mixed_tokens, pool_all, tile_slot[input_tiles:].reshape(half, tall).T, False, bf16, layer_in
        )
        normed_grad = tile_product(
            joint_grad, pool_all, tile_slot[:input_tiles].reshape(tall, wide), True, f32
        )
    input_float = layer_in.astype(f32)
    inverse = lax.rsqrt(jnp.mean(input_float * input_float, axis=1, keepdims=True) + norm_epsilon)
    scaled = normed_grad * gain_float
    input_grad = (
        cotangent.astype(f32)
        + inverse * scaled
        - input_float * inverse**3 * jnp.mean(scaled * input_float, axis=1, keepdims=True)
    )
    if fast:
        gain_grad = jnp.sum(arrived[1][:, 0, :gain_here], axis=0)
    else:
        gain_part = jnp.sum(normed_grad * input_float * inverse, axis=0).reshape(devices, gain_here)
        gain_grad = jnp.sum(lax.all_to_all(gain_part, "tok", split_axis=0, concat_axis=0, tiled=True), axis=0)

    gain_new = adam_step(norm_gain, gain_grad, gain_first, gain_second)
    vector_grad = jnp.concatenate(
        [jnp.stack(taps_grad), offset_grad[None], bias_grad, -rates * rate_sum, skip_grad], axis=0
    )
    vector_new = adam_step(channel_vectors, vector_grad, vector_first, vector_second)
    return (
        layer_out,
        input_grad,
        first_next,
        second_next,
        weight_next,
        left_next,
        right_next,
        lstat_next,
        rstat_next,
        *channel_new,
        *gain_new,
        *vector_new,
    )


def shards(*args):
    bf16 = jnp.bfloat16
    devices = lax.axis_size("tok")
    me = lax.axis_index("tok")
    layer_in, tile_slot, pool_weight, channel_weight = args[0], args[3], args[4], args[11]
    norm_gain, channel_vectors = args[18], args[21]
    tok_rows, model_width = layer_in.shape
    tiles_here, side, _ = pool_weight.shape
    tall = model_width // side
    channels = channel_vectors.shape[1]
    x_all = lax.all_gather(layer_in, "tok", axis=0)
    select_width = channel_weight.shape[1] - R
    small = jnp.concatenate(
        [
            channel_weight[:, :select_width].T,
            jnp.pad(norm_gain[None], ((0, 15), (0, channels - norm_gain.shape[0]))),
        ],
        axis=0,
    ).astype(bf16)
    routes = Routes(tile_slot, devices, tiles_here, tall, channels * devices // side)
    if channels != side or devices % LINES:
        small = lax.all_gather(small, "tok", axis=0)
        return core(routes, False, x_all, small, None, *args)
    plane = devices // LINES
    route = ("route", plane, *CAPS)
    first, second, landed, *back = routes.tables(me)
    middle, line_small = exchange(
        [route, ("line_gather", plane)], [pick(pool_weight.astype(bf16), first), small], 1
    )
    last, small = exchange([route, ("plane_gather", plane)], [pick(middle, second), line_small], 2)
    small = jnp.swapaxes(small, 0, 1).reshape((devices,) + small.shape[2:])
    tiles_own = pick(last, table(3 * tall, routes.place, routes.target == me, landed))
    input_own, output_own = tiles_own[: 2 * tall], tiles_own[2 * tall :]
    input_local = input_own.reshape(2, tall, side, side).transpose(1, 2, 0, 3).reshape(model_width, 2 * channels)
    output_local = output_own.transpose(1, 0, 2).reshape(channels, model_width)
    plane_own = jnp.concatenate([input_local, output_own.transpose(0, 2, 1).reshape(model_width, channels)], axis=1)
    weights, small = lax.optimization_barrier(((input_local, output_local, plane_own, *back), small))
    return lax.cond(
        routes.fits, functools.partial(core, routes, True), functools.partial(core, routes, False), x_all, small, weights, *args
    )


def solution(mesh):
    line, flat, cube, column = P("tok"), P("tok", None), P("tok", None, None), P(None, "tok")
    in_specs = (flat, flat, P(), P()) + (cube,) * 7 + (flat,) * 7 + (line,) * 3 + (column,) * 3
    out_specs = (flat, flat) + (cube,) * 7 + (flat,) * 7 + (line,) * 3 + (column,) * 3
    return jax.shard_map(shards, mesh=mesh, in_specs=in_specs, out_specs=out_specs, check_vma=False)
```

```python
import functools

import jax
import jax.numpy as jnp
from jax import lax
from jax.experimental import pallas as pl
from jax.experimental.pallas import tpu as pltpu
from jax.sharding import PartitionSpec as P

N = 16
R = 128
K = 4
L = 2048
STEP = 5
GROUP = 16
LOG2E = 1.4426950408889634

beta_first = 0.5
beta_second = 0.5
stat_decay = 0.5
learn_rate = 0.02
vector_rate = 0.2
weight_decay = 0.01
adam_epsilon = 1e-08
norm_epsilon = 1e-05
highest = lax.Precision.HIGHEST


LINES = 4
MESH = pl.DeviceIdType.MESH


def greet(line, spot, plane):
    barrier = pltpu.get_barrier_semaphore()
    for k in range(1, LINES):
        pl.semaphore_signal(barrier, inc=1, device_id=((line + k) % LINES * plane + spot,), device_id_type=MESH)
    for k in range(1, plane):
        pl.semaphore_signal(barrier, inc=1, device_id=(line * plane + (spot + k) % plane,), device_id_type=MESH)
    pl.semaphore_wait(barrier, LINES + plane - 2)


def greet_all(me, devices):
    barrier = pltpu.get_barrier_semaphore()
    for k in range(1, devices):
        pl.semaphore_signal(barrier, inc=1, device_id=((me + k) % devices,), device_id_type=MESH)
    pl.semaphore_wait(barrier, devices - 1)


def remote(source, target, send, recv, device):
    return pltpu.make_async_remote_copy(
        src_ref=source, dst_ref=target, send_sem=send, recv_sem=recv, device_id=(device,), device_id_type=MESH
    )


def ride_copies(spec, source, out, sems):
    kind, plane = spec[:2]
    me = lax.axis_index("tok")
    line, spot = me // plane, me % plane
    if kind in ("line", "line_gather"):
        send, recv, own = sems
        part = lambda place: source if kind == "line_gather" else source.at[place]
        copies = [pltpu.make_async_copy(part(line), out.at[line], own.at[0])]
        for k in range(1, LINES):
            place = (line + k) % LINES
            copies.append(remote(part(place), out.at[line], send.at[k], recv.at[k], place * plane + spot))
        return copies
    if kind.startswith("plane"):
        send, recv, own = sems
        part = {
            "plane": lambda place: source.at[:, place],
            "plane_gather": lambda place: source,
            "plane_rows": lambda place: source.at[place],
            "plane_back": lambda place: source.at[place],
        }[kind]
        target = out.at[:, spot] if kind == "plane_back" else out.at[spot]
        copies = [pltpu.make_async_copy(part(spot), target, own.at[0])]
        for k in range(1, plane):
            place = (spot + k) % plane
            copies.append(remote(part(place), target, send.at[k], recv.at[k], line * plane + place))
        return copies
    if kind == "all":
        send, recv, own = sems
        devices = LINES * plane
        copies = [pltpu.make_async_copy(source.at[me], out.at[me], own.at[0])]
        for k in range(1, devices):
            target = (me + k) % devices
            copies.append(remote(source.at[target], out.at[me], send.at[k], recv.at[k], target))
        return copies
    cap_line, cap_plane = spec[2:]
    line_send, line_recv, plane_send, plane_recv, own = sems
    start = LINES * cap_line

    def to_line(place):
        return pl.ds(place * cap_line, cap_line)

    def to_plane(place):
        return pl.ds(start + place * cap_plane, cap_plane)

    copies = [
        pltpu.make_async_copy(source.at[to_line(line)], out.at[to_line(line)], own.at[0]),
        pltpu.make_async_copy(source.at[to_plane(spot)], out.at[to_plane(spot)], own.at[1]),
    ]
    for k in range(1, LINES):
        place = (line + k) % LINES
        copies.append(
            remote(source.at[to_line(place)], out.at[to_line(line)], line_send.at[k], line_recv.at[k], place * plane + spot)
        )
    for k in range(1, plane):
        place = (spot + k) % plane
        copies.append(
            remote(source.at[to_plane(place)], out.at[to_plane(spot)], plane_send.at[k], plane_recv.at[k], line * plane + place)
        )
    return copies


def ride_sems(spec):
    kind, plane = spec[:2]
    if kind == "route":
        return (
            [pltpu.SemaphoreType.DMA((LINES,))] * 2
            + [pltpu.SemaphoreType.DMA((plane,))] * 2
            + [pltpu.SemaphoreType.DMA((2,))]
        )
    members = LINES if kind.startswith("line") else plane if kind.startswith("plane") else LINES * plane
    return [pltpu.SemaphoreType.DMA((members,))] * 2 + [pltpu.SemaphoreType.DMA((1,))]


def ride_shape(spec, value):
    kind, plane = spec[:2]
    shape = value.shape
    if kind in ("plane", "plane_back"):
        shape = (shape[1], shape[0]) + shape[2:]
    if kind.endswith("gather"):
        shape = (LINES if kind == "line_gather" else plane,) + shape
    return jax.ShapeDtypeStruct(shape, value.dtype)


class Riders:
    def __init__(self, specs):
        self.specs = tuple(specs)

    def all_copies(self, sources, outs, sems):
        copies, at = [], 0
        for spec, source, out in zip(self.specs, sources, outs):
            count = len(ride_sems(spec))
            copies += ride_copies(spec, source, out, sems[at : at + count])
            at += count
        return copies

    def begin(self, sources, outs, sems):
        plane = self.specs[0][1]
        me = lax.axis_index("tok")
        if any(spec[0] == "all" for spec in self.specs):
            greet_all(me, LINES * plane)
        else:
            greet(me // plane, me % plane, plane)
        for copy in self.all_copies(sources, outs, sems):
            copy.start()

    def end(self, sources, outs, sems):
        for copy in self.all_copies(sources, outs, sems):
            copy.wait()

    def sems(self):
        return [sem for spec in self.specs for sem in ride_sems(spec)]

    def shapes(self, values):
        return [ride_shape(spec, value) for spec, value in zip(self.specs, values)]


def riders_kernel(riders, *refs):
    count = len(riders.specs)
    sources, outs, sems = refs[:count], refs[count : 2 * count], refs[2 * count :]
    riders.begin(sources, outs, sems)
    riders.end(sources, outs, sems)


HBM = pl.BlockSpec(memory_space=pl.ANY)


def exchange(specs, values, number):
    riders = Riders(specs)
    return pl.pallas_call(
        functools.partial(riders_kernel, riders),
        in_specs=[HBM] * len(values),
        out_specs=[HBM] * len(values),
        out_shape=riders.shapes(values),
        scratch_shapes=riders.sems(),
        compiler_params=pltpu.CompilerParams(collective_id=number, has_side_effects=True),
    )(*values)


def everyone_kernel(devices, source, out, send, recv, own):
    me = lax.axis_index("tok")
    greet_all(me, devices)
    copies = [pltpu.make_async_copy(source.at[me], out.at[me], own.at[0])]
    for k in range(1, devices):
        target = (me + k) % devices
        copies.append(remote(source.at[target], out.at[me], send.at[k], recv.at[k], target))
    for copy in copies:
        copy.start()
    for copy in copies:
        copy.wait()


def everyone(values, number):
    devices = values.shape[0]
    return pl.pallas_call(
        functools.partial(everyone_kernel, devices),
        in_specs=[HBM],
        out_specs=HBM,
        out_shape=jax.ShapeDtypeStruct(values.shape, values.dtype),
        scratch_shapes=[pltpu.SemaphoreType.DMA((devices,))] * 2 + [pltpu.SemaphoreType.DMA((1,))],
        compiler_params=pltpu.CompilerParams(collective_id=number, has_side_effects=True),
    )(values)


def spread_steps(plane, block, out, sems, guests=()):
    line_send, line_recv, plane_send, plane_recv, own = sems
    me = lax.axis_index("tok")
    line, spot = me // plane, me % plane
    copies = [pltpu.make_async_copy(block, out.at[line, spot], own.at[0])]
    arrivals = []
    for k in range(1, LINES):
        place = (line + k) % LINES
        arrivals.append(remote(block, out.at[line, spot], line_send.at[k], line_recv.at[k], place * plane + spot))
    for k in range(1, plane):
        place = (spot + k) % plane
        copies.append(
            remote(block, out.at[line, spot], plane_send.at[0, k], plane_recv.at[0, k], line * plane + place)
        )
    for copy in (*arrivals, *copies, *guests):
        copy.start()
    for k in range(1, LINES):
        arrivals[k - 1].wait_recv()
        origin = (line + LINES - k) % LINES
        for j in range(1, plane):
            place = (spot + j) % plane
            copy = remote(
                out.at[origin, spot], out.at[origin, spot], plane_send.at[k, j], plane_recv.at[k, j], line * plane + place
            )
            copy.start()
            copies.append(copy)
    for copy in arrivals:
        copy.wait_send()
    for copy in copies:
        copy.wait()


def spread_sems(plane):
    return (
        [pltpu.SemaphoreType.DMA((LINES,))] * 2
        + [pltpu.SemaphoreType.DMA((LINES, plane))] * 2
        + [pltpu.SemaphoreType.DMA((1,))]
    )


def spread_kernel(plane, riders, block, *refs):
    count, own_sems = len(riders.specs), len(spread_sems(plane))
    sources, out, outs = refs[:count], refs[count], refs[count + 1 : 2 * count + 1]
    sems, ride = refs[2 * count + 1 : 2 * count + 1 + own_sems], refs[2 * count + 1 + own_sems :]
    me = lax.axis_index("tok")
    greet(me // plane, me % plane, plane)
    guests = riders.all_copies(sources, outs, ride)
    spread_steps(plane, block, out, sems, guests)
    for copy in guests:
        copy.wait()


def spread_blocks(block, plane, number, specs=(), values=()):
    riders = Riders(specs)
    return pl.pallas_call(
        functools.partial(spread_kernel, plane, riders),
        in_specs=[HBM] * (1 + len(values)),
        out_specs=[HBM] * (1 + len(values)),
        out_shape=[jax.ShapeDtypeStruct((LINES, plane) + block.shape, block.dtype)] + riders.shapes(values),
        scratch_shapes=spread_sems(plane) + riders.sems(),
        compiler_params=pltpu.CompilerParams(collective_id=number, has_side_effects=True),
    )(block, *values)


def fold_kernel(plane, riders, parts, *refs):
    count = len(riders.specs)
    sources, out, outs = refs[:count], refs[count], refs[count + 1 : 2 * count + 1]
    got, sent, last, block, plane_send, plane_recv, line_send, line_recv, own = refs[2 * count + 1 : 2 * count + 10]
    own_sems = len(spread_sems(plane))
    sems, ride = refs[2 * count + 10 : 2 * count + 10 + own_sems], refs[2 * count + 10 + own_sems :]
    me = lax.axis_index("tok")
    line, spot = me // plane, me % plane
    greet(line, spot, plane)
    copies = [pltpu.make_async_copy(parts.at[:, spot], got.at[spot], own.at[0])]
    for k in range(1, plane):
        place = (spot + k) % plane
        copies.append(
            remote(parts.at[:, place], got.at[spot], plane_send.at[k], plane_recv.at[k], line * plane + place)
        )
    for copy in copies:
        copy.start()
    guests = riders.all_copies(sources, outs, ride)
    for copy in guests:
        copy.start()
    for copy in copies:
        copy.wait()
    for z in range(LINES):
        total = got[0, z].astype(jnp.float32)
        for k in range(1, plane):
            total = total + got[k, z].astype(jnp.float32)
        sent[z] = total
    copies = [pltpu.make_async_copy(sent.at[line], last.at[line], own.at[1])]
    for k in range(1, LINES):
        place = (line + k) % LINES
        copies.append(remote(sent.at[place], last.at[line], line_send.at[k], line_recv.at[k], place * plane + spot))
    for copy in copies:
        copy.start()
    for copy in copies:
        copy.wait()
    block[...] = ((last[0] + last[1]) + (last[2] + last[3])).astype(block.dtype)
    spread_steps(plane, block, out, sems)
    for copy in guests:
        copy.wait()


def fold_and_spread(parts, plane, number, specs=(), values=()):
    shape = parts.shape[2:]
    riders = Riders(specs)
    return pl.pallas_call(
        functools.partial(fold_kernel, plane, riders),
        in_specs=[HBM] * (1 + len(values)),
        out_specs=[HBM] * (1 + len(values)),
        out_shape=[jax.ShapeDtypeStruct(parts.shape, parts.dtype)] + riders.shapes(values),
        scratch_shapes=[
            pltpu.VMEM((plane, LINES) + shape, parts.dtype),
            pltpu.VMEM((LINES,) + shape, jnp.float32),
            pltpu.VMEM((LINES,) + shape, jnp.float32),
            pltpu.VMEM(shape, parts.dtype),
        ]
        + [pltpu.SemaphoreType.DMA((plane,))] * 2
        + [pltpu.SemaphoreType.DMA((LINES,))] * 2
        + [pltpu.SemaphoreType.DMA((2,))]
        + spread_sems(plane)
        + riders.sems(),
        compiler_params=pltpu.CompilerParams(collective_id=number, has_side_effects=True, vmem_limit_bytes=60 * 2**20),
    )(parts, *values)


def dot_nt(left, right):
    return lax.dot_general(left, right, (((1,), (1,)), ((), ())), preferred_element_type=jnp.float32)

def dot_nn(left, right):
    return jnp.dot(left, right, preferred_element_type=jnp.float32)

def softplus(v):
    return jnp.maximum(v, 0.0) + jnp.log1p(jnp.exp(-jnp.abs(v)))

def split2(v):
    high = v.astype(jnp.bfloat16)
    return high, (v - high.astype(jnp.float32)).astype(jnp.bfloat16)

def own_token(dtype):
    token = lax.broadcasted_iota(jnp.int32, (GROUP, GROUP * N), 0)
    column = lax.broadcasted_iota(jnp.int32, (GROUP, GROUP * N), 1)
    return (column // N == token).astype(dtype)

def slice_columns(block_ref, cols_s, r, chunk):
    values = block_ref[0, chunk:].astype(jnp.float32)
    for g in range(chunk // GROUP):
        cols_s[r, g] = values[:, g * GROUP : (g + 1) * GROUP]


def lay_out(block_ref, inject_s, read_s, r, chunk):
    token = lax.broadcasted_iota(jnp.int32, (chunk, GROUP * N), 0) % GROUP
    column = lax.broadcasted_iota(jnp.int32, (chunk, GROUP * N), 1)
    mine = column // N == token
    for start, rows_s in ((chunk, inject_s), (chunk + N, read_s)):
        if rows_s is not None:
            rows_s[r] = jnp.where(mine, repeat_columns(block_ref[0, start : start + N]), 0).astype(jnp.bfloat16)


def repeat_columns(values):
    state = lax.broadcasted_iota(jnp.int32, (N, GROUP * N), 0)
    column = lax.broadcasted_iota(jnp.int32, (N, GROUP * N), 1)
    chosen = (column % N == state).astype(jnp.bfloat16)
    product = lax.dot_general(
        values, chosen, (((0,), (0,)), ((), ())), preferred_element_type=jnp.float32
    )
    return product


def fwd_kernel(pair, chunk, riders, f_ref, z_ref, start_ref, *refs):
    count = len(riders.specs)
    block_refs, refs = refs[:pair], refs[pair:]
    stepw_ref, bias_ref, rate_ref, skip_ref = refs[:4]
    sources, (mixed_ref, dz_ref, keep_ref) = refs[4 : 4 + count], refs[4 + count : 7 + count]
    outs, refs = refs[7 + count : 7 + 2 * count], refs[7 + 2 * count :]
    state, step_s, drive_s, scan_s, cols_s, read_s = refs[:6]
    if count:

        @pl.when((pl.program_id(0) == 0) & (pl.program_id(1) == 0))
        def _():
            riders.begin(sources, outs, refs[6:])

    groups = chunk // GROUP
    neg = rate_ref[...] * (-LOG2E)
    @pl.when(pl.program_id(1) == 0)
    def _():
        state[...] = jnp.zeros_like(state)

    for r in range(pair):
        raw = dot_nt(block_refs[r][0, :chunk], stepw_ref[...])
        step = softplus(raw + bias_ref[...])
        slice_columns(block_refs[r], cols_s, r, chunk)
        lay_out(block_refs[r], None, read_s, r, chunk)
        step_s[r] = step + start_ref[r].astype(jnp.float32)
        drive_s[r] = step * f_ref[r].astype(jnp.float32)
        keep_ref[r, 0] = state[r]

    def group(g, hidden):
        hidden = list(hidden)
        held = [[] for _ in range(pair)]
        base = pl.multiple_of(g * GROUP, GROUP)
        cols = [cols_s[r, g] for r in range(pair)]
        for k in range(GROUP):
            for r in range(pair):
                factor = jnp.exp2(step_s[r, pl.ds(base + k, 1), :] * neg)
                hidden[r] = factor * hidden[r] + drive_s[r, pl.ds(base + k, 1), :] * cols[r][:N, k : k + 1]
                held[r].append(hidden[r].astype(jnp.bfloat16))
        for r in range(pair):
            states = jnp.concatenate(held[r], axis=0)
            scan_s[r, pl.ds(base, GROUP), :] = dot_nn(read_s[r, pl.ds(base, GROUP), :], states)
        return tuple(hidden)

    hidden = lax.fori_loop(0, groups, group, tuple(state[r] for r in range(pair)), unroll=groups)
    for r in range(pair):
        state[r] = hidden[r]
        f = f_ref[r].astype(jnp.float32)
        z = z_ref[r].astype(jnp.float32)
        gate = 1.0 / (1.0 + jnp.exp(-z))
        summed = scan_s[r] + skip_ref[...] * f
        mixed_ref[r] = (summed * (z * gate)).astype(jnp.bfloat16)
        dz_ref[r] = summed * (gate * (1.0 + z * (1.0 - gate)))
    if count:

        @pl.when((pl.program_id(0) == pl.num_programs(0) - 1) & (pl.program_id(1) == pl.num_programs(1) - 1))
        def _():
            riders.end(sources, outs, refs[6:])

def bwd_kernel(pair, chunk, riders, f_ref, z_ref, gm_ref, start_ref, *refs):
    block_refs, refs = refs[:pair], refs[pair:]
    stepw_ref, bias_ref, rate_ref, skip_ref, keep_ref = refs[:5]
    refs = refs[5:]
    count = len(riders.specs)
    sources, refs = refs[:count], refs[count:]
    draw_ref, dfm_ref, dinj_ref, dread_ref, drate_ref, dskip_ref, dbias_ref = refs[:7]
    outs, refs = refs[7 : 7 + count], refs[7 + count :]
    carry_s, step_s, drive_s, dscan_s, raw_s, delta_s, a_s, ah_s, h_s, s1_s, s2_s, cols_s, inject_s = refs[:13]
    if count:

        @pl.when((pl.program_id(0) == 0) & (pl.program_id(1) == 0))
        def _():
            riders.begin(sources, outs, refs[13:])

    groups = chunk // GROUP
    rate = rate_ref[...]
    neg = rate * (-LOG2E)
    mine = own_token(jnp.bfloat16)
    mine_f = own_token(jnp.float32)

    @pl.when(pl.program_id(1) == 0)
    def _():
        carry_s[...] = jnp.zeros_like(carry_s)

    @pl.when((pl.program_id(1) == 0) & (pl.program_id(0) == 0))
    def _():
        drate_ref[...] = jnp.zeros_like(drate_ref)
        dskip_ref[...] = jnp.zeros_like(dskip_ref)
        dbias_ref[...] = jnp.zeros_like(dbias_ref)

    for r in range(pair):
        raw = dot_nt(block_refs[r][0, :chunk], stepw_ref[...]) + bias_ref[...]
        slice_columns(block_refs[r], cols_s, r, chunk)
        lay_out(block_refs[r], inject_s, None, r, chunk)
        step = softplus(raw)
        raw_s[r] = raw
        delta_s[r] = step
        step_s[r] = step + start_ref[r].astype(jnp.float32)
        f = f_ref[r].astype(jnp.float32)
        drive_s[r] = step * f
        z = z_ref[r].astype(jnp.float32)
        gate = 1.0 / (1.0 + jnp.exp(-z))
        dscan = gm_ref[r].astype(jnp.float32) * (z * gate)
        dscan_s[r] = dscan
        dskip_ref[...] += jnp.sum(dscan * f, axis=0, keepdims=True)

    def forward(g, hidden):
        hidden = list(hidden)
        base = pl.multiple_of(g * GROUP, GROUP)
        cols = [cols_s[r, g] for r in range(pair)]
        held = [[] for _ in range(pair)]
        for k in range(GROUP):
            for r in range(pair):
                factor = jnp.exp2(step_s[r, pl.ds(base + k, 1), :] * neg)
                kept = factor * hidden[r]
                hidden[r] = kept + drive_s[r, pl.ds(base + k, 1), :] * cols[r][:N, k : k + 1]
                a_s[r, base + k] = factor
                ah_s[r, base + k] = kept
                held[r].append(hidden[r].astype(jnp.bfloat16))
        for r in range(pair):
            h_s[r, g] = jnp.concatenate(held[r], axis=0)
        return tuple(hidden)

    lax.fori_loop(0, groups, forward, tuple(keep_ref[r, 0] for r in range(pair)), unroll=groups)

    def backward(i, carried):
        g = groups - 1 - i
        base = pl.multiple_of(g * GROUP, GROUP)
        ag = list(carried[:pair])
        total = carried[pair]
        cols = [cols_s[r, g] for r in range(pair)]
        gs = [[None] * GROUP for _ in range(pair)]
        qs = [[None] * GROUP for _ in range(pair)]
        for k in reversed(range(GROUP)):
            for r in range(pair):
                grad = dscan_s[r, pl.ds(base + k, 1), :] * cols[r][N:, k : k + 1] + ag[r]
                ag[r] = a_s[r, base + k] * grad
                q = grad * ah_s[r, base + k]
                total = total + delta_s[r, pl.ds(base + k, 1), :] * q
                gs[r][k] = grad.astype(jnp.bfloat16)
                qs[r][k] = (rate * q).astype(jnp.bfloat16)
        for r in range(pair):
            grads = jnp.concatenate(gs[r], axis=0)
            pulls = jnp.concatenate(qs[r], axis=0)
            s1_s[r, pl.ds(base, GROUP), :] = dot_nn(inject_s[r, pl.ds(base, GROUP), :], grads)
            s2_s[r, pl.ds(base, GROUP), :] = dot_nn(mine, pulls)
            dh, dl = split2(dscan_s[r, pl.ds(base, GROUP), :])
            uh, ul = split2(drive_s[r, pl.ds(base, GROUP), :])
            dr = dot_nt(jnp.concatenate([dh, dl], axis=0), h_s[r, g])
            dread_ref[r, pl.ds(g, 1), :] = jnp.sum((dr[:GROUP] + dr[GROUP:]) * mine_f, axis=0, keepdims=True)
            di = dot_nt(jnp.concatenate([uh, ul], axis=0), grads)
            dinj_ref[r, pl.ds(g, 1), :] = jnp.sum((di[:GROUP] + di[GROUP:]) * mine_f, axis=0, keepdims=True)
        return tuple(ag) + (total,)

    out = lax.fori_loop(
        0, groups, backward, tuple(carry_s[r] for r in range(pair)) + (jnp.zeros_like(rate),), unroll=groups
    )
    drate_ref[...] += out[pair]
    for r in range(pair):
        carry_s[r] = out[r]
        f = f_ref[r].astype(jnp.float32)
        draw = (f * s1_s[r] - s2_s[r]) / (1.0 + jnp.exp(-raw_s[r]))
        draw_ref[r] = draw.astype(jnp.bfloat16)
        dbias_ref[...] += jnp.sum(draw, axis=0, keepdims=True)
        dfm_ref[r] = delta_s[r] * s1_s[r] + skip_ref[...] * dscan_s[r]

    if count:

        @pl.when((pl.program_id(0) == pl.num_programs(0) - 1) & (pl.program_id(1) == pl.num_programs(1) - 1))
        def _():
            riders.end(sources, outs, refs[13:])


def specs(pair, chunk, ch, blocks, back, chunks):
    def at(i, j):
        return (i, chunks - 1 - j if back else j)
    tok = pl.BlockSpec((pair, chunk, ch), lambda i, j: at(i, j) + (0,))
    flat = pl.BlockSpec((pair, chunk // GROUP, GROUP * N), lambda i, j: at(i, j) + (0,))
    keep = pl.BlockSpec((pair, 1, N, ch), lambda i, j: at(i, j) + (0, 0))
    def block(r):
        def index(i, j):
            i, j = at(i, j)
            return ((i * pair + r) * chunks + j, 0, 0)
        return pl.BlockSpec((1,) + blocks.shape[1:], index)
    def whole(a):
        return pl.BlockSpec(a.shape, lambda i, j: (0,) * a.ndim)
    return tok, [block(r) for r in range(pair)], flat, keep, whole

def scan_forward(f, z, start, blocks, stepw, bias, rate, skip, rides=(), guests=(), number=None):
    riders = Riders(rides)
    params = dict(collective_id=number, has_side_effects=True) if guests else {}
    chunk = blocks.shape[1] - 2 * N
    rows, length, ch = f.shape
    pair = 2 if rows % 2 == 0 else 1
    chunks = length // chunk
    tok, block_specs, flat, keep, whole = specs(pair, chunk, ch, blocks, False, chunks)
    return pl.pallas_call(
        functools.partial(fwd_kernel, pair, chunk, riders),
        grid=(rows // pair, chunks),
        in_specs=[tok, tok, tok]
        + block_specs
        + [whole(stepw), whole(bias), whole(rate), whole(skip)]
        + [HBM] * len(guests),
        out_specs=[tok, tok, keep] + [HBM] * len(guests),
        out_shape=[jax.ShapeDtypeStruct(f.shape, jnp.bfloat16), jax.ShapeDtypeStruct(f.shape, jnp.float32),
                   jax.ShapeDtypeStruct((rows, chunks, N, ch), jnp.float32)]
        + riders.shapes(guests),
        scratch_shapes=[pltpu.VMEM((pair, N, ch), jnp.float32)] + [pltpu.VMEM((pair, chunk, ch), jnp.float32)] * 3
        + [pltpu.VMEM((pair, chunk // GROUP, 2 * N, GROUP), jnp.float32)]
        + [pltpu.VMEM((pair, chunk, GROUP * N), jnp.bfloat16)]
        + riders.sems(),
        compiler_params=pltpu.CompilerParams(vmem_limit_bytes=60 * 2**20, **params),
        cost_estimate=pl.CostEstimate(flops=4 * 10**10, bytes_accessed=8 * 10**6, transcendentals=0),
    )(f, z, start, *([blocks] * pair), stepw, bias, rate, skip, *guests)

def scan_backward(f, z, gm, start, blocks, stepw, bias, rate, skip, kept, rides=(), guests=(), number=None):
    chunk = blocks.shape[1] - 2 * N
    rows, length, ch = f.shape
    pair = 2 if rows % 2 == 0 else 1
    chunks = length // chunk
    tok, block_specs, flat, keep, whole = specs(pair, chunk, ch, blocks, True, chunks)
    f32 = jnp.float32
    row = jax.ShapeDtypeStruct((1, ch), f32)
    in_specs = [tok, tok, tok, tok] + block_specs + [whole(stepw), whole(bias), whole(rate), whole(skip), keep]
    inj = jax.ShapeDtypeStruct((rows, length // GROUP, GROUP * N), f32)
    out_specs = [tok, tok, flat, flat, whole(rate), whole(row), whole(row)]
    out_shape = [jax.ShapeDtypeStruct(f.shape, jnp.bfloat16), jax.ShapeDtypeStruct(f.shape, f32),
                 jax.ShapeDtypeStruct(inj.shape, f32), jax.ShapeDtypeStruct(inj.shape, f32),
                 jax.ShapeDtypeStruct(rate.shape, f32), row, row]
    scratch = ([pltpu.VMEM((pair, N, ch), f32)] + [pltpu.VMEM((pair, chunk, ch), f32)] * 5
               + [pltpu.VMEM((pair, chunk, N, ch), f32)] * 2
               + [pltpu.VMEM((pair, chunk // GROUP, GROUP * N, ch), jnp.bfloat16)]
               + [pltpu.VMEM((pair, chunk, ch), f32)] * 2
               + [pltpu.VMEM((pair, chunk // GROUP, 2 * N, GROUP), f32)]
               + [pltpu.VMEM((pair, chunk, GROUP * N), jnp.bfloat16)])
    values = (f, z, gm, start, *([blocks] * pair), stepw, bias, rate, skip, kept)
    params = dict(vmem_limit_bytes=60 * 2**20)
    riders = Riders(rides)
    if guests:
        in_specs, out_specs = in_specs + [HBM] * len(guests), out_specs + [HBM] * len(guests)
        out_shape = out_shape + riders.shapes(guests)
        scratch = scratch + riders.sems()
        values = values + tuple(guests)
        params.update(collective_id=number, has_side_effects=True)
    return pl.pallas_call(
        functools.partial(bwd_kernel, pair, chunk, riders),
        grid=(rows // pair, chunks),
        in_specs=in_specs,
        out_specs=out_specs,
        out_shape=out_shape,
        scratch_shapes=scratch,
        compiler_params=pltpu.CompilerParams(**params),
        cost_estimate=pl.CostEstimate(flops=7 * 10**10, bytes_accessed=8 * 10**6, transcendentals=0),
    )(*values)


DEPTH = 4
BATCH = 16


def tile_product_kernel(pairs, steps, transposed, residual, idx_ref, left_ref, pool_ref, *refs):
    if residual:
        res_ref, refs = refs[0], refs[1:]
    out_ref, slots, sems = refs
    side = slots.shape[2]
    total_steps = pairs * steps

    def fetch(step):
        for u in range(BATCH):
            pltpu.make_async_copy(
                pool_ref.at[idx_ref[step * BATCH + u]], slots.at[step % DEPTH, u], sems.at[step % DEPTH]
            ).start()

    for step in range(min(DEPTH - 1, total_steps)):
        fetch(step)

    def one_pair(o, carry):
        total = jnp.zeros((left_ref.shape[1], 2 * side), jnp.float32)
        for k in range(steps):
            step = o * steps + k

            @pl.when(step + DEPTH - 1 < total_steps)
            def _():
                fetch(step + DEPTH - 1)

            slot = step % DEPTH
            pltpu.make_async_copy(slots.at[slot], slots.at[slot], sems.at[slot]).wait()
            for u in range(0, BATCH, 4):
                at = k * (BATCH // 2) + u // 2
                left = jnp.concatenate([left_ref[at], left_ref[at + 1]], axis=1)
                tile = [slots[slot, u + v] for v in range(4)]
                if transposed:
                    right = jnp.concatenate(
                        [jnp.concatenate([tile[0], tile[2]], axis=1), jnp.concatenate([tile[1], tile[3]], axis=1)], axis=0
                    )
                    total += dot_nt(left, right)
                else:
                    right = jnp.concatenate(
                        [jnp.concatenate([tile[0], tile[1]], axis=1), jnp.concatenate([tile[2], tile[3]], axis=1)], axis=0
                    )
                    total += dot_nn(left, right)
        columns = pl.ds(pl.multiple_of(o * 2 * side, side), 2 * side)
        if residual:
            total += res_ref[:, columns].astype(jnp.float32)
        out_ref[:, columns] = total.astype(out_ref.dtype)
        return carry

    lax.fori_loop(0, pairs, one_pair, 0)


def tile_product(left, pool, index, transposed, dtype, residual=None):
    outs, depth = index.shape
    pairs, steps = outs // 2, 2 * depth // BATCH
    side = pool.shape[1]
    tok = left.shape[1]
    vmem = pl.BlockSpec(memory_space=pltpu.VMEM)
    extra = [residual] if residual is not None else []
    order = index.reshape(pairs, 2, depth).transpose(0, 2, 1).reshape(-1).astype(jnp.int32)
    return pl.pallas_call(
        functools.partial(tile_product_kernel, pairs, steps, transposed, residual is not None),
        in_specs=[pl.BlockSpec(memory_space=pltpu.SMEM), vmem, pl.BlockSpec(memory_space=pl.ANY)] + [vmem] * len(extra),
        out_specs=vmem,
        out_shape=jax.ShapeDtypeStruct((tok, outs * side), dtype),
        scratch_shapes=[pltpu.VMEM((DEPTH, BATCH, side, side), pool.dtype), pltpu.SemaphoreType.DMA((DEPTH,))],
        compiler_params=pltpu.CompilerParams(vmem_limit_bytes=40 * 2**20),
        cost_estimate=pl.CostEstimate(
            flops=2 * outs * depth * tok * side * side, bytes_accessed=outs * depth * side * side * 2, transcendentals=0
        ),
    )(order, left, pool, *extra)


def dot_tn(left, right):
    return lax.dot_general(left, right, (((0,), (0,)), ((), ())), preferred_element_type=jnp.float32)


def three(dot, left, right):
    left_axis, right_axis = {dot_nn: (1, 0), dot_nt: (1, 1), dot_tn: (0, 0)}[dot]
    return dot(
        jnp.concatenate([left[0], left[0], left[1]], axis=left_axis),
        jnp.concatenate([right[0], right[1], right[0]], axis=right_axis),
    )


def soap_kernel(sources, many, kind_ref, idx_ref, *refs):
    grad_refs, refs = refs[: sources * many], refs[sources * many :]
    weight_ref, first_ref, second_ref, left_ref, right_ref, lstat_ref, rstat_ref = refs[:7]
    first_out, second_out, weight_out, lstat_out, rstat_out, turned_out, gram_out = refs[7:]
    side = weight_ref.shape[1]
    diagonal = lax.broadcasted_iota(jnp.int32, (side, side), 0) == lax.broadcasted_iota(jnp.int32, (side, side), 1)
    every = range(many)
    grads, lefts, rights = [], [], []
    for u in every:
        kind = kind_ref[pl.program_id(0) * many + u]
        grad = grad_refs[u * sources][0]
        for which in range(1, sources):
            grad = jnp.where(kind == which, grad_refs[u * sources + which][0], grad)
        grads.append(grad)
        lefts.append(split2(left_ref[u]))
        rights.append(split2(right_ref[u]))
    across = [split2(dot_nn(grads[u], rights[u][0]) + dot_nn(grads[u], rights[u][1])) for u in every]
    turned = [three(dot_tn, lefts[u], across[u]) for u in every]
    products = [(dot_nt(grads[u], grads[u]), dot_tn(grads[u], grads[u])) for u in every]
    directions = []
    for u in every:
        first = beta_first * first_ref[u] + (1.0 - beta_first) * turned[u]
        second = beta_second * second_ref[u] + (1.0 - beta_second) * turned[u] * turned[u]
        first_out[u] = first
        second_out[u] = second
        directions.append(split2(
            first / (1.0 - beta_first**STEP) / (jnp.sqrt(second / (1.0 - beta_second**STEP)) + adam_epsilon)
        ))
    renewed = []
    for u in every:
        for which, (stat_ref, basis_ref, basis2, stat_out) in enumerate(
            ((lstat_ref, left_ref, lefts[u], lstat_out), (rstat_ref, right_ref, rights[u], rstat_out))
        ):
            stat = stat_decay * stat_ref[u] + (1.0 - stat_decay) * products[u][which]
            stat_out[u] = stat
            trace = jnp.sum(jnp.sum(jnp.where(diagonal, stat, 0.0), axis=0, keepdims=True), axis=1, keepdims=True)
            value = three(dot_nn, split2(stat), basis2) + (trace / side) * basis_ref[u]
            turned_out[u, which] = value
            renewed.append(split2(value))
    back = [split2(three(dot_nt, directions[u], rights[u])) for u in every]
    for u in every:
        for which in range(2):
            gram_out[u, which] = three(dot_tn, renewed[u * 2 + which], renewed[u * 2 + which])
    for u in every:
        weight = weight_ref[u]
        weight_out[u] = weight - learn_rate * (three(dot_nn, lefts[u], back[u]) + weight_decay * weight)


def soap_tiles(kind, index, grads, weight, first, second, left, right, lstat, rstat, many=4):
    count, side, _ = weight.shape
    one = pl.BlockSpec((many, side, side), lambda s, kind, idx: (s, 0, 0))
    two = pl.BlockSpec((many, 2, side, side), lambda s, kind, idx: (s, 0, 0, 0))

    def picked(u, which):
        def at(s, kind, idx):
            return (jnp.where(kind[s * many + u] == which, idx[s * many + u], 0), 0, 0)

        return pl.BlockSpec((1, side, side), at)

    tile = jax.ShapeDtypeStruct(weight.shape, jnp.float32)
    pairs = jax.ShapeDtypeStruct((count, 2, side, side), jnp.float32)
    sources = len(grads)
    return pl.pallas_call(
        functools.partial(soap_kernel, sources, many),
        grid_spec=pltpu.PrefetchScalarGridSpec(
            num_scalar_prefetch=2,
            grid=(count // many,),
            in_specs=[picked(u, which) for u in range(many) for which in range(sources)] + [one] * 7,
            out_specs=[one] * 5 + [two] * 2,
        ),
        out_shape=[tile] * 5 + [pairs] * 2,
        compiler_params=pltpu.CompilerParams(vmem_limit_bytes=60 * 2**20),
        cost_estimate=pl.CostEstimate(flops=count * 60 * side**3, bytes_accessed=count * 18 * 4 * side**2, transcendentals=0),
    )(kind, index, *(list(grads) * many), weight, first, second, left, right, lstat, rstat)


def renew_kernel(many, turned_ref, inv_ref, left_out, right_out):
    for u in range(many):
        for which, out in ((0, left_out), (1, right_out)):
            out[u] = three(dot_nt, split2(turned_ref[u, which]), split2(inv_ref[u, which]))


def renew_bases(turned, inverse, many=6):
    count, _, side, _ = turned.shape
    one = pl.BlockSpec((many, side, side), lambda s: (s, 0, 0))
    two = pl.BlockSpec((many, 2, side, side), lambda s: (s, 0, 0, 0))
    tile = jax.ShapeDtypeStruct((count, side, side), jnp.float32)
    return pl.pallas_call(
        functools.partial(renew_kernel, many),
        grid=(count // many,),
        in_specs=[two, two],
        out_specs=[one, one],
        out_shape=[tile, tile],
        compiler_params=pltpu.CompilerParams(vmem_limit_bytes=60 * 2**20),
    )(turned, inverse)


def chol_kernel(batch, order, riders, gram_ref, *refs):
    count = len(riders.specs)
    sources, out_ref, outs = refs[:count], refs[count], refs[count + 1 : 2 * count + 1]
    low_ref, inv_ref, piv_ref = refs[2 * count + 1 : 2 * count + 4]
    ride_sems_here = refs[2 * count + 4 :]
    if count:
        riders.begin(sources, outs, ride_sems_here)
    tiles = order // 8
    rows8 = lax.broadcasted_iota(jnp.int32, (8, batch), 0)

    def load_slab(j, carry):
        low_ref[j, pl.ds(0, order), :] = gram_ref[pl.ds(j, batch, stride=order), :].T
        inv_ref[j] = jnp.zeros(inv_ref.shape[1:], jnp.float32)
        return carry

    lax.fori_loop(0, order, load_slab, 0, unroll=16)

    def bcast(ref, j, row):
        return jnp.broadcast_to(ref[j, pl.ds(row, 1), :], (8, batch))

    def block_column(block, carry):
        base = pl.multiple_of(block * 8, 8)

        def updated(tile_rows, seed):
            def one(j, accs):
                mult = [bcast(low_ref, j, base + k) for k in range(8)]
                out = []
                for s, rows in enumerate(tile_rows):
                    piece = low_ref[j, pl.ds(rows, 8), :]
                    out.extend(accs[s * 8 + k] - piece * mult[k] for k in range(8))
                return tuple(out)

            def eight(step, accs):
                for u in range(8):
                    accs = one(step * 8 + u, accs)
                return accs

            return list(lax.fori_loop(0, block, eight, tuple(seed)))

        accs = updated([base], [low_ref[base + k, pl.ds(base, 8), :] for k in range(8)])
        scales = []
        for k in range(8):
            scale = lax.rsqrt(jnp.broadcast_to(accs[k][k : k + 1, :], (8, batch)))
            scales.append(scale)
            accs[k] = jnp.where(rows8 >= k, accs[k] * scale, 0.0)
            for later in range(k + 1, 8):
                accs[later] = accs[later] - accs[k] * jnp.broadcast_to(
                    accs[k][later : later + 1, :], (8, batch)
                )
        for k in range(8):
            low_ref[base + k, pl.ds(base, 8), :] = accs[k]
            piv_ref[base + k] = scales[k]

        def pair(p, carry):
            first = pl.multiple_of(base + 8 + p * 16, 8)
            both = [first, pl.multiple_of(first + 8, 8)]
            accs = updated(
                both, [low_ref[base + k, pl.ds(rows, 8), :] for rows in both for k in range(8)]
            )
            for k in range(8):
                scale = piv_ref[base + k]
                for s in range(2):
                    accs[s * 8 + k] = accs[s * 8 + k] * scale
                for later in range(k + 1, 8):
                    mult = bcast(low_ref, base + k, base + later)
                    for s in range(2):
                        accs[s * 8 + later] = accs[s * 8 + later] - accs[s * 8 + k] * mult
            for s, rows in enumerate(both):
                for k in range(8):
                    low_ref[base + k, pl.ds(rows, 8), :] = accs[s * 8 + k]
            return carry

        lax.fori_loop(0, (tiles - block) // 2, pair, 0)
        return carry

    lax.fori_loop(0, tiles, block_column, 0)

    def block_row(block, carry):
        base = pl.multiple_of(block * 8, 8)

        def finish(accs, both):
            for k in range(8):
                scale = piv_ref[base + k]
                for s in range(len(both)):
                    accs[s * 8 + k] = accs[s * 8 + k] * scale
                for later in range(k + 1, 8):
                    mult = bcast(low_ref, base + k, base + later)
                    for s in range(len(both)):
                        accs[s * 8 + later] = accs[s * 8 + later] - accs[s * 8 + k] * mult
            for s, columns in enumerate(both):
                for k in range(8):
                    inv_ref[base + k, pl.ds(columns, 8), :] = accs[s * 8 + k]

        def pair(p, carry):
            first = pl.multiple_of(p * 16, 8)
            both = [first, pl.multiple_of(first + 8, 8)]

            def eight(step, accs):
                for u in range(8):
                    j = step * 8 + u
                    mult = [bcast(low_ref, j, base + k) for k in range(8)]
                    out = []
                    for s, columns in enumerate(both):
                        piece = inv_ref[j, pl.ds(columns, 8), :]
                        out.extend(accs[s * 8 + k] - piece * mult[k] for k in range(8))
                    accs = tuple(out)
                return accs

            accs = list(lax.fori_loop(
                p * 2, block, eight, (jnp.zeros((8, batch), jnp.float32),) * 16
            ))
            finish(accs, both)
            return carry

        lax.fori_loop(0, (block + 1) // 2, pair, 0)
        odd = block % 2

        def diagonal():
            accs = [jnp.where(rows8 == k, 1.0, 0.0) for k in range(8)]
            finish(accs, [base])

        diagonal()
        return carry

    lax.fori_loop(0, tiles, block_row, 0)

    def store_slab(i, carry):
        out_ref[pl.ds(i, batch, stride=order), :] = inv_ref[i, pl.ds(0, order), :].T
        return carry

    lax.fori_loop(0, order, store_slab, 0, unroll=16)
    if count:
        riders.end(sources, outs, ride_sems_here)

def inverse_factors(gram, rides=(), guests=(), number=None):
    count, pair, order, _ = gram.shape
    batch = count * pair
    riders = Riders(rides)
    params = dict(vmem_limit_bytes=60 * 2**20)
    if guests:
        params.update(collective_id=number, has_side_effects=True)
    vmem = pl.BlockSpec(memory_space=pltpu.VMEM)
    out, *arrived = pl.pallas_call(
        functools.partial(chol_kernel, batch, order, riders),
        out_shape=[jax.ShapeDtypeStruct((batch * order, order), jnp.float32)] + riders.shapes(guests),
        in_specs=[vmem] + [HBM] * len(guests),
        out_specs=[vmem] + [HBM] * len(guests),
        scratch_shapes=[
            pltpu.VMEM((order, order + 8, batch), jnp.float32),
            pltpu.VMEM((order, order + 8, batch), jnp.float32),
            pltpu.VMEM((order, 8, batch), jnp.float32),
        ]
        + riders.sems(),
        compiler_params=pltpu.CompilerParams(**params),
        cost_estimate=pl.CostEstimate(flops=5 * 10**10, bytes_accessed=12 * 10**6, transcendentals=0),
    )(gram.reshape(batch * order, order), *guests)
    return (out.reshape(gram.shape), *arrived)


def norm_joint_kernel(channels, riders, x_ref, gain_ref, weight_ref, *refs):
    count = len(riders.specs)
    sources, (normed_ref, xs_ref, gate_ref) = refs[:count], refs[count : count + 3]
    outs, sems = refs[count + 3 : 2 * count + 3], refs[2 * count + 3 :]
    if count:

        @pl.when(pl.program_id(0) == 0)
        def _():
            riders.begin(sources, outs, sems)

    width = x_ref.shape[2]
    x = x_ref[...].astype(jnp.float32).reshape(-1, width)
    inverse = lax.rsqrt(jnp.mean(x * x, axis=1, keepdims=True) + norm_epsilon)
    normed = (x * inverse * gain_ref[...]).astype(jnp.bfloat16)
    normed_ref[...] = normed
    joint = dot_nn(normed, weight_ref[...]).astype(jnp.bfloat16)
    xs_ref[...] = joint[:, :channels]
    gate_ref[...] = joint[:, channels:]
    if count:

        @pl.when(pl.program_id(0) == pl.num_programs(0) - 1)
        def _():
            riders.end(sources, outs, sems)


def norm_joint(x, gain, weight, rides=(), guests=(), number=None, many=2):
    devices, rows, width = x.shape
    riders = Riders(rides)
    params = dict(collective_id=number, has_side_effects=True) if guests else {}
    tokens, block = devices * rows, many * rows
    channels = weight.shape[1] // 2
    wide = pl.BlockSpec((block, width), lambda i: (i, 0))
    thin = pl.BlockSpec((block, channels), lambda i: (i, 0))
    half = jax.ShapeDtypeStruct((tokens, channels), jnp.bfloat16)
    return pl.pallas_call(
        functools.partial(norm_joint_kernel, channels, riders),
        grid=(tokens // block,),
        in_specs=[
            pl.BlockSpec((many, rows, width), lambda i: (i, 0, 0)),
            pl.BlockSpec((1, width), lambda i: (0, 0)),
            pl.BlockSpec((width, 2 * channels), lambda i: (0, 0)),
        ]
        + [HBM] * len(guests),
        out_specs=[wide, thin, thin] + [HBM] * len(guests),
        out_shape=[jax.ShapeDtypeStruct((tokens, width), jnp.bfloat16), half, half] + riders.shapes(guests),
        scratch_shapes=riders.sems(),
        compiler_params=pltpu.CompilerParams(vmem_limit_bytes=60 * 2**20, **params),
        cost_estimate=pl.CostEstimate(
            flops=4 * tokens * width * channels, bytes_accessed=4 * tokens * width, transcendentals=0
        ),
    )(x, gain, weight, *guests)


def plane_product_kernel(count, many, riders, weight_ref, *refs):
    guests = len(riders.specs)
    lefts, sources, out_ref = refs[:count], refs[count : count + guests], refs[count + guests]
    outs, total_ref = refs[count + guests + 1 : count + 2 * guests + 1], refs[count + 2 * guests + 1]
    sems = refs[count + 2 * guests + 2 :]
    step = pl.program_id(0)
    if guests:

        @pl.when(step == 0)
        def _():
            riders.begin(sources, outs, sems)

    left = jnp.concatenate([ref[u] for u in range(many) for ref in lefts], axis=1)
    part = dot_nt(left, jnp.concatenate([weight_ref[u] for u in range(many)], axis=1))

    @pl.when(step == 0)
    def _():
        total_ref[...] = part

    @pl.when(step > 0)
    def _():
        total_ref[...] += part

    @pl.when(step == pl.num_programs(0) - 1)
    def _():
        out_ref[...] = total_ref[...].astype(out_ref.dtype)
        if guests:
            riders.end(sources, outs, sems)


def plane_product(lefts, weight, block, rides=(), guests=(), number=None, many=4):
    members, tokens, channels = lefts[0].shape
    rows, width = len(lefts) * channels, weight.shape[1]
    riders = Riders(rides)
    params = dict(collective_id=number, has_side_effects=True) if guests else {}
    out, *arrived = pl.pallas_call(
        functools.partial(plane_product_kernel, len(lefts), many, riders),
        grid=(members // many,),
        in_specs=[pl.BlockSpec((many, width, rows), lambda p: (p, 0, block))]
        + [pl.BlockSpec((many, tokens, channels), lambda p: (p, 0, 0))] * len(lefts)
        + [HBM] * len(guests),
        out_specs=[pl.BlockSpec((tokens, width), lambda p: (0, 0))] + [HBM] * len(guests),
        out_shape=[jax.ShapeDtypeStruct((tokens, width), jnp.bfloat16)] + riders.shapes(guests),
        scratch_shapes=[pltpu.VMEM((tokens, width), jnp.float32)] + riders.sems(),
        compiler_params=pltpu.CompilerParams(vmem_limit_bytes=60 * 2**20, **params),
        cost_estimate=pl.CostEstimate(
            flops=2 * members * tokens * rows * width, bytes_accessed=2 * members * rows * width, transcendentals=0
        ),
    )(weight, *lefts, *guests)
    return (out, *arrived)


def plane_back_kernel(left_ref, weight_ref, out_ref):
    out_ref[0] = dot_nn(left_ref[...], weight_ref[0]).astype(out_ref.dtype)


def plane_back(left, weight, channels, block):
    members, width, _ = weight.shape
    tokens = left.shape[0]
    return pl.pallas_call(
        plane_back_kernel,
        grid=(members,),
        in_specs=[
            pl.BlockSpec((tokens, width), lambda p: (0, 0)),
            pl.BlockSpec((1, width, channels), lambda p: (p, 0, block)),
        ],
        out_specs=pl.BlockSpec((1, tokens, channels), lambda p: (p, 0, 0)),
        out_shape=jax.ShapeDtypeStruct((members, tokens, channels), jnp.bfloat16),
        compiler_params=pltpu.CompilerParams(vmem_limit_bytes=60 * 2**20),
        cost_estimate=pl.CostEstimate(
            flops=2 * members * tokens * width * channels, bytes_accessed=2 * members * width * channels, transcendentals=0
        ),
    )(left, weight)


def line_product_kernel(left_ref, right_ref, out_ref):
    product = dot_tn(left_ref[0], right_ref[...])
    side = out_ref.shape[3]
    for b in range(out_ref.shape[1]):
        out_ref[0, b] = product[:, b * side : (b + 1) * side].astype(out_ref.dtype)


def line_product(lefts, right, tall):
    members, tokens, channels = lefts.shape
    width = right.shape[1]
    side = width // tall
    return pl.pallas_call(
        line_product_kernel,
        grid=(members,),
        in_specs=[
            pl.BlockSpec((1, tokens, channels), lambda p: (p, 0, 0)),
            pl.BlockSpec((tokens, width), lambda p: (0, 0)),
        ],
        out_specs=pl.BlockSpec((1, tall, channels, side), lambda p: (p, 0, 0, 0)),
        out_shape=jax.ShapeDtypeStruct((members, tall, channels, side), jnp.bfloat16),
        compiler_params=pltpu.CompilerParams(vmem_limit_bytes=60 * 2**20),
        cost_estimate=pl.CostEstimate(
            flops=2 * members * tokens * channels * width, bytes_accessed=4 * members * channels * width, transcendentals=0
        ),
    )(lefts, right)


def plain_three(dot, left, right):
    return dot(left[0], right[0]) + (dot(left[0], right[1]) + dot(left[1], right[0]))


def channel_kernel(weight_ref, grad_ref, first_ref, second_ref, left_ref, right_ref, lstat_ref, rstat_ref,
                   first_out, second_out, weight_out, lstat_out, rstat_out, lturn_out, rturn_out, lgram_out, rgram_out):
    grad = split2(grad_ref[...])
    left, right = split2(left_ref[...]), split2(right_ref[...])
    turned = plain_three(dot_tn, left, split2(plain_three(dot_nn, grad, right)))
    first = beta_first * first_ref[...] + (1.0 - beta_first) * turned
    second = beta_second * second_ref[...] + (1.0 - beta_second) * turned * turned
    first_out[...] = first
    second_out[...] = second
    direction = split2(
        first / (1.0 - beta_first**STEP) / (jnp.sqrt(second / (1.0 - beta_second**STEP)) + adam_epsilon)
    )
    returned = plain_three(dot_nn, left, split2(plain_three(dot_nt, direction, right)))
    weight = weight_ref[...]
    weight_out[...] = weight - learn_rate * (returned + weight_decay * weight)
    for basis_ref, basis, stat_ref, product, stat_out, turn_out, gram_out in (
        (left_ref, left, lstat_ref, plain_three(dot_nt, grad, grad), lstat_out, lturn_out, lgram_out),
        (right_ref, right, rstat_ref, plain_three(dot_tn, grad, grad), rstat_out, rturn_out, rgram_out),
    ):
        order = basis_ref.shape[0]
        diagonal = lax.broadcasted_iota(jnp.int32, (order, order), 0) == lax.broadcasted_iota(
            jnp.int32, (order, order), 1
        )
        stat = stat_decay * stat_ref[...] + (1.0 - stat_decay) * product
        stat_out[...] = stat
        trace = jnp.sum(jnp.sum(jnp.where(diagonal, stat, 0.0), axis=0, keepdims=True), axis=1, keepdims=True)
        value = plain_three(dot_nn, split2(stat), basis) + (trace / order) * basis_ref[...]
        turn_out[...] = value
        value = split2(value)
        gram_out[...] = plain_three(dot_tn, value, value)


def channel_moments(weight, grad, first, second, left, right, lstat, rstat):
    f32 = jnp.float32
    rows = jax.ShapeDtypeStruct(weight.shape, f32)
    small = jax.ShapeDtypeStruct(left.shape, f32)
    large = jax.ShapeDtypeStruct(right.shape, f32)
    return pl.pallas_call(
        channel_kernel,
        out_shape=[rows] * 3 + [small, large] * 3,
        compiler_params=pltpu.CompilerParams(vmem_limit_bytes=60 * 2**20),
        cost_estimate=pl.CostEstimate(flops=8 * 10**9, bytes_accessed=6 * 10**6, transcendentals=0),
    )(weight, grad, first, second, left, right, lstat, rstat)


PANEL = 32


def factor_inverse(block):
    order = block.shape[0]
    rows = lax.broadcasted_iota(jnp.int32, (order, 2 * order), 0)
    columns = lax.broadcasted_iota(jnp.int32, (order, 2 * order), 1)
    both = jnp.concatenate([block, jnp.zeros_like(block)], axis=1) + jnp.where(columns == rows + order, 1.0, 0.0)
    for k in range(order):
        scale = lax.rsqrt(both[k : k + 1, k : k + 1])
        row = both[k : k + 1, :] * scale
        column = both[:, k : k + 1] * scale
        both = jnp.where(rows == k, row, jnp.where(rows > k, both - column * row, both))
    return both[:, order:]


def solve_kernel(count, riders, *refs):
    guests = len(riders.specs)
    grams, sides, refs = refs[:count], refs[count : 2 * count], refs[2 * count :]
    sources, outs, refs = refs[:guests], refs[guests : guests + count], refs[guests + count :]
    arrived, works, ride = refs[:guests], refs[guests : guests + 2 * count], refs[guests + 2 * count :]
    if guests:
        riders.begin(sources, arrived, ride)
    for i in range(count):
        order = grams[i].shape[0]
        gram, side = works[2 * i], works[2 * i + 1]
        gram[...] = grams[i][...]
        side[...] = sides[i][...]
        for start in range(0, order, PANEL):
            stop = start + PANEL
            low = split2(factor_inverse(gram[start:stop, start:stop]))
            upper = split2(plain_three(dot_nn, low, split2(gram[start:stop, :])))
            solved = plain_three(dot_nn, low, split2(side[start:stop, :]))
            outs[i][start:stop, :] = solved
            if stop < order:
                gram[stop:, :] -= plain_three(dot_tn, upper, upper)[stop:]
                side[stop:, :] -= plain_three(dot_tn, upper, split2(solved))[stop:]
    if guests:
        riders.end(sources, arrived, ride)


def solve_factors(grams, sides, rides=(), guests=(), number=None):
    count = len(grams)
    riders = Riders(rides)
    params = dict(vmem_limit_bytes=60 * 2**20)
    if guests:
        params.update(collective_id=number, has_side_effects=True)
    shapes = [jax.ShapeDtypeStruct(s.shape, jnp.float32) for s in sides]
    scratch = []
    for g, s in zip(grams, sides):
        scratch += [pltpu.VMEM(g.shape, jnp.float32), pltpu.VMEM(s.shape, jnp.float32)]
    vmem = pl.BlockSpec(memory_space=pltpu.VMEM)
    return pl.pallas_call(
        functools.partial(solve_kernel, count, riders),
        in_specs=[vmem] * (2 * count) + [HBM] * len(guests),
        out_specs=[vmem] * count + [HBM] * len(guests),
        out_shape=shapes + riders.shapes(guests),
        scratch_shapes=scratch + riders.sems(),
        compiler_params=pltpu.CompilerParams(**params),
        cost_estimate=pl.CostEstimate(flops=4 * 10**10, bytes_accessed=3 * 10**6, transcendentals=0),
    )(*grams, *sides, *guests)


def doc_positions(doc_lengths):
    starts = jnp.cumsum(doc_lengths, axis=1) - doc_lengths
    places = jnp.arange(L, dtype=jnp.int32)
    begun = jnp.where(starts[:, None, :] <= places[None, :, None], starts[:, None, :], 0)
    return places[None, :] - jnp.max(begun, axis=2)


def adam_step(weight, gradient, first, second):
    first_new = beta_first * first + (1.0 - beta_first) * gradient
    second_new = beta_second * second + (1.0 - beta_second) * gradient * gradient
    direction = (
        first_new
        / (1.0 - beta_first**STEP)
        / (jnp.sqrt(second_new / (1.0 - beta_second**STEP)) + adam_epsilon)
    )
    return (first_new, second_new, weight - vector_rate * (direction + weight_decay * weight))


def later(values, lag):
    return jnp.pad(values, ((lag, 0), (0, 0)))[: values.shape[0]]


def sooner(values, lag):
    return jnp.pad(values, ((0, lag), (0, 0)))[lag:]


def conv_pre(xs, taps, offset, place):
    total = offset[None] + taps[K - 1][None] * xs
    for lag in range(1, K):
        total = total + jnp.where(place >= lag, taps[K - 1 - lag][None] * later(xs, lag), 0.0)
    return total


def rank_within(key):
    count = key.shape[0]
    earlier = jnp.arange(count)[None, :] < jnp.arange(count)[:, None]
    return jnp.sum(((key[None, :] == key[:, None]) & earlier).astype(jnp.int32), axis=1)


def table(size, target, chosen, value):
    hit = (target[None, :] == jnp.arange(size)[:, None]) & chosen[None, :]
    return jnp.sum(jnp.where(hit, value[None, :], 0), axis=1)


CAPS = (13, 9)


class Routes:
    def __init__(self, tile_slot, devices, tiles_here, tall, half):
        count = tile_slot.shape[0]
        plane = devices // LINES
        wide = 2 * half
        tile = jnp.arange(count, dtype=jnp.int32)
        output = tile >= tall * wide
        relative = tile - tall * wide
        column = tile % wide
        self.plane = plane
        self.local = tile_slot % tiles_here
        self.owner = tile_slot // tiles_here
        self.target = jnp.where(output, relative // tall, column % half)
        self.kind = jnp.where(output, 2, column // half)
        self.place = jnp.where(output, 2 * tall + relative % tall, column // half * tall + tile // wide)
        self.owner_line, self.owner_spot = self.owner // plane, self.owner % plane
        self.target_line, self.target_spot = self.target // plane, self.target % plane
        self.ways, self.fits = self.settle(CAPS)

    def settle(self, caps):
        odd = self.place % 2 == 1
        for attempt in range(2):
            middle = jnp.where(
                odd, self.owner_line * self.plane + self.target_spot, self.target_line * self.plane + self.owner_spot
            )
            kind = odd.astype(jnp.int32)
            line_key = (self.owner_line * LINES + self.target_line) * self.plane + middle % self.plane
            plane_key = (self.owner_spot * self.plane + self.target_spot) * LINES + middle // self.plane
            ranks = rank_within(line_key * 2 + kind), rank_within(plane_key * 2 + kind)
            full = (ranks[0] >= caps[0]) | (ranks[1] >= caps[1])
            if attempt == 0:
                odd = odd ^ full
        return (odd, middle, *ranks), ~jnp.any(full)

    def spots(self, line_member, spot_member):
        by_line = line_member * CAPS[0] + self.ways[2]
        by_plane = LINES * CAPS[0] + spot_member * CAPS[1] + self.ways[3]
        return by_line, by_plane

    def tables(self, me):
        odd, middle = self.ways[:2]
        size = LINES * CAPS[0] + self.plane * CAPS[1]
        target_line, target_plane = self.spots(self.target_line, self.target_spot)
        owner_line, owner_plane = self.spots(self.owner_line, self.owner_spot)
        first = table(size, jnp.where(odd, target_plane, target_line), self.owner == me, self.local)
        second = table(
            size, jnp.where(odd, target_line, target_plane), middle == me, jnp.where(odd, owner_plane, owner_line)
        )
        landed = jnp.where(odd, owner_line, owner_plane)
        back_first = table(size, jnp.where(odd, owner_line, owner_plane), self.target == me, self.place)
        back_second = table(
            size, jnp.where(odd, owner_plane, owner_line), middle == me, jnp.where(odd, target_line, target_plane)
        )
        back_landed = jnp.where(odd, target_plane, target_line)
        return first, second, landed, back_first, back_second, back_landed


def pick(values, index):
    return values.at[index].get(mode="clip")


def device_groups(devices):
    plane = devices // LINES
    lines = [[z * plane + p for z in range(LINES)] for p in range(plane)]
    planes = [[z * plane + p for p in range(plane)] for z in range(LINES)]
    return lines, planes


def spread(value, devices):
    lines, planes = device_groups(devices)
    plane = devices // LINES
    step = lax.all_to_all(
        jnp.broadcast_to(value, (LINES,) + value.shape), "tok", 0, 0, tiled=True, axis_index_groups=lines
    )
    step = lax.all_to_all(
        jnp.broadcast_to(step, (plane,) + step.shape), "tok", 0, 0, tiled=True, axis_index_groups=planes
    )
    return jnp.swapaxes(step, 0, 1).reshape((devices * value.shape[0],) + value.shape[1:])


def fold(values, devices):
    lines, planes = device_groups(devices)
    plane = devices // LINES
    rows = values.shape[0] // devices
    parts = jnp.swapaxes(values.reshape((LINES, plane, rows) + values.shape[1:]), 0, 1).astype(jnp.bfloat16)
    parts = lax.all_to_all(parts, "tok", 0, 0, tiled=True, axis_index_groups=planes)
    parts = jnp.sum(parts.astype(jnp.float32), axis=0)
    parts = lax.all_to_all(parts, "tok", 0, 0, tiled=True, axis_index_groups=lines)
    return jnp.sum(parts, axis=0)


def core(
    routes,
    fast,
    x_all,
    small_all,
    weights,
    layer_in,
    cotangent,
    doc_lengths,
    tile_slot,
    pool_weight,
    pool_first,
    pool_second,
    pool_left,
    pool_right,
    pool_left_stat,
    pool_right_stat,
    channel_weight,
    channel_first,
    channel_second,
    channel_left,
    channel_right,
    channel_left_stat,
    channel_right_stat,
    norm_gain,
    gain_first,
    gain_second,
    channel_vectors,
    vector_first,
    vector_second,
):
    bf16, f32 = jnp.bfloat16, jnp.float32
    devices = lax.axis_size("tok")
    me = lax.axis_index("tok")
    lines, planes = device_groups(devices)
    plane = devices // LINES
    my_line, my_plane = me // plane, me % plane
    tok_rows, model_width = layer_in.shape
    tokens = tok_rows * devices
    rows = tokens // L
    channels = channel_vectors.shape[1]
    inner_width = channels * devices
    tiles_here, side, _ = pool_weight.shape
    tall = model_width // side
    half = inner_width // side
    wide = 2 * half
    cut = side // channels
    input_tiles = tall * wide
    select_width = channel_weight.shape[1] - R
    gain_here = norm_gain.shape[0]

    gain_float = small_all[:, select_width, :gain_here].reshape(1, model_width).astype(f32)
    select_blocks = small_all[:, :select_width].reshape(half, cut, select_width, channels)
    select_blocks = select_blocks.transpose(0, 2, 1, 3).reshape(half, select_width, side)
    if not fast:
        pool_low = pool_weight.astype(bf16)

    is_out = routes.kind == 2
    if fast:
        input_local, output_local, plane_own, back_first, back_second, back_landed = weights
    else:
        pool_all = lax.all_gather(pool_low, "tok", axis=0, tiled=True)
        columns = me // cut
        input_slots = tile_slot[:input_tiles].reshape(tall, 2, half)
        input_own = jnp.take(
            pool_all, lax.dynamic_index_in_dim(input_slots, columns, 2, False).T.reshape(-1), axis=0
        )
        output_slots = tile_slot[input_tiles:].reshape(half, tall)
        output_own = jnp.take(pool_all, lax.dynamic_index_in_dim(output_slots, columns, 0, False), axis=0)
        offset = me % cut * channels
        input_local = input_own.reshape(2, tall, side, side)
        output_local = output_own
        if cut > 1:
            input_local = lax.dynamic_slice_in_dim(input_local, offset, channels, axis=3)
            output_local = lax.dynamic_slice_in_dim(output_local, offset, channels, axis=1)
        input_local = input_local.transpose(1, 2, 0, 3).reshape(model_width, 2 * channels)
        output_local = output_local.transpose(1, 0, 2).reshape(channels, model_width)

    if fast:
        plane_weight = lax.all_gather(plane_own, "tok", axis=0, axis_index_groups=planes)
        upper, lower = cotangent[: tok_rows // 2], cotangent[tok_rows // 2 :]
        normed_all, xs_low, gates, upper = norm_joint(
            x_all, gain_float, input_local, [("line_gather", plane)], [upper], 11
        )
    else:
        normed_all, xs_low, gates = norm_joint(x_all, gain_float, input_local)
        cotangent_all = lax.all_gather(cotangent, "tok", axis=0, tiled=True)

    def to_tokens(values, number=None):
        lead = values.shape[:-2]
        parts = values.reshape(lead + (devices, tok_rows, channels))
        if fast and number is not None:
            moved = everyone(parts, number)
        else:
            moved = lax.all_to_all(parts, "tok", split_axis=len(lead), concat_axis=len(lead), tiled=True)
        moved = moved.reshape(lead + (half, cut, tok_rows, channels))
        return jnp.swapaxes(moved, -3, -2).reshape(lead + (half, tok_rows, side))

    place = doc_positions(doc_lengths).reshape(-1, 1)
    taps, offset = channel_vectors[:K], channel_vectors[K]
    xs = xs_low.astype(f32)
    filtered = jax.nn.silu(conv_pre(xs, taps, offset, place)).astype(bf16)
    filtered_tokens = to_tokens(filtered, 3)
    block = jnp.concatenate(
        [
            jnp.einsum("gtc,gfc->tf", filtered_tokens, select_blocks[:, :R], preferred_element_type=f32),
            jnp.einsum("gtc,gfc->ft", filtered_tokens, select_blocks[:, R:], preferred_element_type=f32),
        ],
        axis=0,
    ).astype(bf16)
    if fast:
        blocks, lower = spread_blocks(block, plane, 4, [("line_gather", plane)], [lower])
        blocks = blocks.reshape(devices, tok_rows + 2 * N, R)
        cotangent_line = jnp.concatenate([upper, lower], axis=1).reshape(LINES * tok_rows, model_width)
    else:
        blocks = spread(block[None], devices)

    if fast:
        def share(values):
            return values.reshape(LINES, plane, tok_rows, channels)

        def across(blocks, which, *riding):
            blocks = [values.reshape(plane, LINES * tok_rows, channels) for values in blocks]
            product, *arrived = plane_product(blocks, plane_weight, which, *riding)
            return (product.reshape(LINES, tok_rows, model_width), *arrived)

    by_row = lambda values: values.reshape((rows, L) + values.shape[1:])
    begins = by_row(jnp.broadcast_to(jnp.where(place == 0, 1e30, 0.0).astype(bf16), (tokens, channels)))
    step_local = channel_weight[:, select_width:].astype(bf16)
    rates = jnp.exp(channel_vectors[K + 2 : K + 2 + N])
    step_bias = channel_vectors[K + 1 : K + 2]
    skip_gain = channel_vectors[K + 2 + N :]
    scan_params = (step_local, step_bias, rates, skip_gain)
    scan_rides, scan_guests = [], []
    if fast:
        back_parts = plane_back(cotangent_line, plane_weight, channels, 2)
        scan_rides = [("plane_back", plane)]
        scan_guests = [back_parts.reshape(plane, LINES, tok_rows, channels)]
    mixed, gate_slope, kept, *arrived = scan_forward(
        by_row(filtered), by_row(gates), begins, blocks, *scan_params, scan_rides, scan_guests, 12
    )
    mixed = mixed.reshape(tokens, channels)
    if fast:
        back_chan = arrived[0].reshape(tokens, channels)
        (mixed_plane,) = exchange([("plane", plane)], [share(mixed)], 7)
    else:
        back_chan = jnp.einsum("td,cd->tc", cotangent_all, output_local, preferred_element_type=f32).astype(bf16)
    back_chan = lax.optimization_barrier(back_chan)
    gate_grad = (back_chan.astype(f32) * gate_slope.reshape(tokens, channels)).astype(bf16)

    def input_parts(grads):
        part = jnp.einsum("td,tc->dc", normed_all, jnp.concatenate(grads, axis=1), preferred_element_type=f32)
        part = part.astype(bf16).reshape(tall, side, len(grads), channels)
        return part.transpose(2, 0, 1, 3)

    def every_input(part):
        every = lax.all_gather(part, "tok", axis=0)
        every = every.reshape(half, cut, tall, side, channels).transpose(0, 2, 3, 1, 4)
        return every.reshape(half * tall, side, side)

    if fast:
        output_shares = line_product(
            mixed_plane.reshape(plane, LINES * tok_rows, channels), cotangent_line, tall
        )
        (layer_parts,) = across([mixed_plane], 2)

    scan_in = (by_row(filtered), by_row(gates), by_row(back_chan), begins, blocks)
    if fast:
        *scan_grads, output_shares, layer_parts = scan_backward(
            *scan_in,
            *scan_params,
            kept,
            [("plane_rows", plane), ("line", plane)],
            [output_shares, layer_parts],
            6,
        )
    else:
        scan_grads = scan_backward(*scan_in, *scan_params, kept)
    draw, filter_mix, inject_grad, read_grad, rate_sum, skip_grad, bias_grad = scan_grads
    draw = draw.reshape(tokens, channels)
    rank_in = blocks[:, :tok_rows].reshape(tokens, R)
    step_grad = jnp.einsum("tc,tr->rc", draw, rank_in, preferred_element_type=f32)
    rank_part = jnp.einsum("tc,cr->tr", draw, step_local, preferred_element_type=f32)
    state_part = jnp.concatenate([inject_grad.reshape(tokens, N), read_grad.reshape(tokens, N)], axis=1)
    if fast:
        parts = jnp.concatenate(
            [
                rank_part.astype(bf16).reshape(devices, tok_rows, R),
                state_part.astype(bf16).reshape(devices, tok_rows, 2 * N).transpose(0, 2, 1),
            ],
            axis=1,
        )
        grad_blocks, gate_plane = fold_and_spread(
            parts.reshape(LINES, plane, tok_rows + 2 * N, R),
            plane,
            5,
            [("plane", plane)],
            [share(gate_grad)],
        )
        grad_blocks = grad_blocks.reshape(devices, tok_rows + 2 * N, R)
        projected_grad_all = jnp.concatenate(
            [
                grad_blocks[:, :tok_rows].reshape(tokens, R),
                grad_blocks[:, tok_rows:].transpose(0, 2, 1).reshape(tokens, 2 * N),
            ],
            axis=1,
        )
    else:
        partial_sums = jnp.concatenate([rank_part, state_part], axis=1)
        projected_grad_all = spread(fold(partial_sums, devices).astype(bf16), devices)
    select_local = channel_weight[:, :select_width].astype(bf16)
    back_filter = jnp.einsum(
        "tf,cf->tc", projected_grad_all, select_local, preferred_element_type=f32
    ).astype(bf16)
    select_grad = jnp.einsum("tc,tf->fc", filtered, projected_grad_all, preferred_element_type=f32)
    pre = conv_pre(xs, taps, offset, place)
    gate = jax.nn.sigmoid(pre)
    dpre = (filter_mix.reshape(tokens, channels) + back_filter.astype(f32)) * (gate * (1.0 + pre * (1.0 - gate)))
    offset_grad = jnp.sum(dpre, axis=0)
    taps_grad = [jnp.sum(dpre * xs, axis=0)]
    xs_grad = taps[K - 1][None] * dpre
    for lag in range(1, K):
        masked = jnp.where(place >= lag, dpre, 0.0)
        xs_grad = xs_grad + taps[K - 1 - lag][None] * sooner(masked, lag)
        taps_grad.insert(0, jnp.sum(masked * later(xs, lag), axis=0))
    xs_grad = xs_grad.astype(bf16)
    input_both = input_parts([xs_grad, gate_grad])
    if fast:
        output_part = jnp.sum(output_shares.astype(f32), axis=0).astype(bf16)
        tiles = jnp.concatenate([input_both.reshape(2 * tall, side, channels), output_part], axis=0)
        route = ("route", plane, *CAPS)
        rides = [route, ("plane", plane)]
        guests = [pick(tiles, back_first), share(xs_grad)]
    else:
        xs_every, gate_every = every_input(input_both[0]), every_input(input_both[1])
        output_part = jnp.einsum("tc,td->cd", mixed, cotangent_all, preferred_element_type=f32).astype(bf16)
        output_every = lax.all_gather(output_part.reshape(channels, tall, side).transpose(1, 0, 2), "tok", axis=0)
        output_every = (
            output_every.reshape(half, cut, tall, channels, side)
            .transpose(0, 2, 1, 3, 4)
            .reshape(half * tall, side, side)
        )
        rides, guests = [], []

    first_c, second_c, weight_c, rstat_c, lstat_c, right_turned, left_turned, right_gram, left_gram = channel_moments(
        channel_weight.T,
        jnp.concatenate([select_grad, step_grad], axis=0),
        channel_first.T,
        channel_second.T,
        channel_right,
        channel_left,
        channel_right_stat,
        channel_left_stat,
    )
    left_c, right_c, *arrived = solve_factors(
        (left_gram, right_gram), (left_turned.T, right_turned.T), rides, guests, 8
    )
    channel_new = (first_c.T, second_c.T, weight_c.T, left_c.T, right_c.T, lstat_c, rstat_c)
    if fast:
        middle, xs_plane = arrived
        normed_parts, arrived_tiles = across(
            [xs_plane, gate_plane], 0, [route], [pick(middle, back_second)], 9
        )
        x_here = x_all.reshape((LINES, plane) + x_all.shape[1:])
        x_here = lax.dynamic_index_in_dim(x_here, me % plane, 1, False).astype(f32)
        root = lax.rsqrt(jnp.mean(x_here * x_here, axis=2, keepdims=True) + norm_epsilon)
        gain_part = jnp.sum(normed_parts.astype(f32) * x_here * root, axis=(0, 1)).reshape(devices, 1, gain_here)
        gain_part = jnp.pad(gain_part, ((0, 0), (0, 7), (0, 128 - gain_here)))
        rides = [("line", plane), ("all", plane)]
        guests = [normed_parts, gain_part]

    own_slot = tile_slot - me * tiles_here
    every_tile = jnp.full(tile_slot.shape, True)
    if fast:
        grads = (arrived_tiles,)
        kind = jnp.zeros((tiles_here,), jnp.int32)
        index = table(tiles_here, own_slot, every_tile, back_landed)
    else:
        grads = (xs_every, gate_every, output_every)
        tile = jnp.arange(tile_slot.shape[0], dtype=jnp.int32)
        kind = table(tiles_here, own_slot, every_tile, routes.kind)
        spot = jnp.where(is_out, tile - input_tiles, tile % wide % half * tall + tile // wide)
        index = table(tiles_here, own_slot, every_tile, spot)
    first_next, second_next, weight_next, lstat_next, rstat_next, turned, gram = soap_tiles(
        kind,
        index,
        grads,
        pool_weight,
        pool_first,
        pool_second,
        pool_left,
        pool_right,
        pool_left_stat,
        pool_right_stat,
    )
    inverse_low, *arrived = inverse_factors(gram, rides, guests, 10)
    left_next, right_next = renew_bases(turned, inverse_low)

    if fast:
        layer_out = (layer_in.astype(f32) + jnp.sum(layer_parts.astype(f32), axis=0)).astype(bf16)
        normed_grad = jnp.sum(arrived[0].astype(f32), axis=0)
    else:
        mixed_tokens = to_tokens(mixed)
        joint_grad = to_tokens(jnp.stack([xs_grad, gate_grad])).reshape(wide, tok_rows, side)
        layer_out = tile_product(
            mixed_tokens, pool_all, tile_slot[input_tiles:].reshape(half, tall).T, False, bf16, layer_in
        )
        normed_grad = tile_product(
            joint_grad, pool_all, tile_slot[:input_tiles].reshape(tall, wide), True, f32
        )
    input_float = layer_in.astype(f32)
    inverse = lax.rsqrt(jnp.mean(input_float * input_float, axis=1, keepdims=True) + norm_epsilon)
    scaled = normed_grad * gain_float
    input_grad = (
        cotangent.astype(f32)
        + inverse * scaled
        - input_float * inverse**3 * jnp.mean(scaled * input_float, axis=1, keepdims=True)
    )
    if fast:
        gain_grad = jnp.sum(arrived[1][:, 0, :gain_here], axis=0)
    else:
        gain_part = jnp.sum(normed_grad * input_float * inverse, axis=0).reshape(devices, gain_here)
        gain_grad = jnp.sum(lax.all_to_all(gain_part, "tok", split_axis=0, concat_axis=0, tiled=True), axis=0)

    gain_new = adam_step(norm_gain, gain_grad, gain_first, gain_second)
    vector_grad = jnp.concatenate(
        [jnp.stack(taps_grad), offset_grad[None], bias_grad, -rates * rate_sum, skip_grad], axis=0
    )
    vector_new = adam_step(channel_vectors, vector_grad, vector_first, vector_second)
    return (
        layer_out,
        input_grad,
        first_next,
        second_next,
        weight_next,
        left_next,
        right_next,
        lstat_next,
        rstat_next,
        *channel_new,
        *gain_new,
        *vector_new,
    )


def shards(*args):
    bf16 = jnp.bfloat16
    devices = lax.axis_size("tok")
    me = lax.axis_index("tok")
    layer_in, tile_slot, pool_weight, channel_weight = args[0], args[3], args[4], args[11]
    norm_gain, channel_vectors = args[18], args[21]
    tok_rows, model_width = layer_in.shape
    tiles_here, side, _ = pool_weight.shape
    tall = model_width // side
    channels = channel_vectors.shape[1]
    x_all = lax.all_gather(layer_in, "tok", axis=0)
    select_width = channel_weight.shape[1] - R
    small = jnp.concatenate(
        [
            channel_weight[:, :select_width].T,
            jnp.pad(norm_gain[None], ((0, 15), (0, channels - norm_gain.shape[0]))),
        ],
        axis=0,
    ).astype(bf16)
    routes = Routes(tile_slot, devices, tiles_here, tall, channels * devices // side)
    if channels != side or devices % LINES:
        small = lax.all_gather(small, "tok", axis=0)
        return core(routes, False, x_all, small, None, *args)
    plane = devices // LINES
    route = ("route", plane, *CAPS)
    first, second, landed, *back = routes.tables(me)
    middle, line_small = exchange(
        [route, ("line_gather", plane)], [pick(pool_weight.astype(bf16), first), small], 1
    )
    last, small = exchange([route, ("plane_gather", plane)], [pick(middle, second), line_small], 2)
    small = jnp.swapaxes(small, 0, 1).reshape((devices,) + small.shape[2:])
    tiles_own = pick(last, table(3 * tall, routes.place, routes.target == me, landed))
    input_own, output_own = tiles_own[: 2 * tall], tiles_own[2 * tall :]
    input_local = input_own.reshape(2, tall, side, side).transpose(1, 2, 0, 3).reshape(model_width, 2 * channels)
    output_local = output_own.transpose(1, 0, 2).reshape(channels, model_width)
    plane_own = jnp.concatenate([input_local, output_own.transpose(0, 2, 1).reshape(model_width, channels)], axis=1)
    weights, small = lax.optimization_barrier(((input_local, output_local, plane_own, *back), small))
    return lax.cond(
        routes.fits, functools.partial(core, routes, True), functools.partial(core, routes, False), x_all, small, weights, *args
    )


def solution(mesh):
    line, flat, cube, column = P("tok"), P("tok", None), P("tok", None, None), P(None, "tok")
    in_specs = (flat, flat, P(), P()) + (cube,) * 7 + (flat,) * 7 + (line,) * 3 + (column,) * 3
    out_specs = (flat, flat) + (cube,) * 7 + (flat,) * 7 + (line,) * 3 + (column,) * 3
    return jax.shard_map(shards, mesh=mesh, in_specs=in_specs, out_specs=out_specs, check_vma=False)
```

```python
import functools

import jax
import jax.numpy as jnp
from jax import lax
from jax.experimental import pallas as pl
from jax.experimental.pallas import tpu as pltpu
from jax.sharding import PartitionSpec as P

N = 16
R = 128
K = 4
L = 2048
STEP = 5
GROUP = 16
LOG2E = 1.4426950408889634

beta_first = 0.5
beta_second = 0.5
stat_decay = 0.5
learn_rate = 0.02
vector_rate = 0.2
weight_decay = 0.01
adam_epsilon = 1e-08
norm_epsilon = 1e-05
highest = lax.Precision.HIGHEST


LINES = 4
MESH = pl.DeviceIdType.MESH


def signal_members(line, spot, plane):
    barrier = pltpu.get_barrier_semaphore()
    for k in range(1, LINES):
        pl.semaphore_signal(barrier, inc=1, device_id=((line + k) % LINES * plane + spot,), device_id_type=MESH)
    for k in range(1, plane):
        pl.semaphore_signal(barrier, inc=1, device_id=(line * plane + (spot + k) % plane,), device_id_type=MESH)
    return LINES + plane - 2


def signal_all(me, devices):
    barrier = pltpu.get_barrier_semaphore()
    for k in range(1, devices):
        pl.semaphore_signal(barrier, inc=1, device_id=((me + k) % devices,), device_id_type=MESH)
    return devices - 1


def greet(line, spot, plane):
    pl.semaphore_wait(pltpu.get_barrier_semaphore(), signal_members(line, spot, plane))


def remote(source, target, send, recv, device):
    return pltpu.make_async_remote_copy(
        src_ref=source, dst_ref=target, send_sem=send, recv_sem=recv, device_id=(device,), device_id_type=MESH
    )


def ride_copies(spec, source, out, sems):
    kind, plane = spec[:2]
    me = lax.axis_index("tok")
    line, spot = me // plane, me % plane
    if kind in ("line", "line_gather"):
        send, recv, own = sems
        part = lambda place: source if kind == "line_gather" else source.at[place]
        copies = [pltpu.make_async_copy(part(line), out.at[line], own.at[0])]
        for k in range(1, LINES):
            place = (line + k) % LINES
            copies.append(remote(part(place), out.at[line], send.at[k], recv.at[k], place * plane + spot))
        return copies
    if kind.startswith("plane"):
        send, recv, own = sems
        part = {
            "plane": lambda place: source.at[:, place],
            "plane_gather": lambda place: source,
            "plane_rows": lambda place: source.at[place],
            "plane_back": lambda place: source.at[place],
        }[kind]
        target = out.at[:, spot] if kind == "plane_back" else out.at[spot]
        copies = [pltpu.make_async_copy(part(spot), target, own.at[0])]
        for k in range(1, plane):
            place = (spot + k) % plane
            copies.append(remote(part(place), target, send.at[k], recv.at[k], line * plane + place))
        return copies
    if kind == "all":
        send, recv, own = sems
        devices = LINES * plane
        copies = [pltpu.make_async_copy(source.at[me], out.at[me], own.at[0])]
        for k in range(1, devices):
            target = (me + k) % devices
            copies.append(remote(source.at[target], out.at[me], send.at[k], recv.at[k], target))
        return copies
    cap_line, cap_plane = spec[2:]
    line_send, line_recv, plane_send, plane_recv, own = sems
    start = LINES * cap_line

    def to_line(place):
        return pl.ds(place * cap_line, cap_line)

    def to_plane(place):
        return pl.ds(start + place * cap_plane, cap_plane)

    copies = [
        pltpu.make_async_copy(source.at[to_line(line)], out.at[to_line(line)], own.at[0]),
        pltpu.make_async_copy(source.at[to_plane(spot)], out.at[to_plane(spot)], own.at[1]),
    ]
    for k in range(1, LINES):
        place = (line + k) % LINES
        copies.append(
            remote(source.at[to_line(place)], out.at[to_line(line)], line_send.at[k], line_recv.at[k], place * plane + spot)
        )
    for k in range(1, plane):
        place = (spot + k) % plane
        copies.append(
            remote(source.at[to_plane(place)], out.at[to_plane(spot)], plane_send.at[k], plane_recv.at[k], line * plane + place)
        )
    return copies


def ride_sems(spec):
    kind, plane = spec[:2]
    if kind == "route":
        return (
            [pltpu.SemaphoreType.DMA((LINES,))] * 2
            + [pltpu.SemaphoreType.DMA((plane,))] * 2
            + [pltpu.SemaphoreType.DMA((2,))]
        )
    members = LINES if kind.startswith("line") else plane if kind.startswith("plane") else LINES * plane
    return [pltpu.SemaphoreType.DMA((members,))] * 2 + [pltpu.SemaphoreType.DMA((1,))]


def ride_shape(spec, value):
    kind, plane = spec[:2]
    shape = value.shape
    if kind in ("plane", "plane_back"):
        shape = (shape[1], shape[0]) + shape[2:]
    if kind.endswith("gather"):
        shape = (LINES if kind == "line_gather" else plane,) + shape
    return jax.ShapeDtypeStruct(shape, value.dtype)


class Riders:
    def __init__(self, specs):
        self.specs = tuple(specs)

    def all_copies(self, sources, outs, sems):
        copies, at = [], 0
        for spec, source, out in zip(self.specs, sources, outs):
            count = len(ride_sems(spec))
            copies += ride_copies(spec, source, out, sems[at : at + count])
            at += count
        return copies

    def hello(self):
        plane = self.specs[0][1]
        me = lax.axis_index("tok")
        if any(spec[0] == "all" for spec in self.specs):
            return signal_all(me, LINES * plane)
        return signal_members(me // plane, me % plane, plane)

    def start(self, greetings, sources, outs, sems):
        pl.semaphore_wait(pltpu.get_barrier_semaphore(), greetings)
        for copy in self.all_copies(sources, outs, sems):
            copy.start()

    def begin(self, sources, outs, sems):
        self.start(self.hello(), sources, outs, sems)

    def end(self, sources, outs, sems):
        for copy in self.all_copies(sources, outs, sems):
            copy.wait()

    def sems(self):
        return [sem for spec in self.specs for sem in ride_sems(spec)]

    def shapes(self, values):
        return [ride_shape(spec, value) for spec, value in zip(self.specs, values)]


def riders_kernel(riders, *refs):
    count = len(riders.specs)
    sources, outs, sems = refs[:count], refs[count : 2 * count], refs[2 * count :]
    riders.begin(sources, outs, sems)
    riders.end(sources, outs, sems)


HBM = pl.BlockSpec(memory_space=pl.ANY)


def exchange(specs, values, number):
    riders = Riders(specs)
    return pl.pallas_call(
        functools.partial(riders_kernel, riders),
        in_specs=[HBM] * len(values),
        out_specs=[HBM] * len(values),
        out_shape=riders.shapes(values),
        scratch_shapes=riders.sems(),
        compiler_params=pltpu.CompilerParams(collective_id=number, has_side_effects=True),
    )(*values)


def everyone_kernel(devices, source, out, send, recv, own):
    me = lax.axis_index("tok")
    pl.semaphore_wait(pltpu.get_barrier_semaphore(), signal_all(me, devices))
    copies = [pltpu.make_async_copy(source.at[me], out.at[me], own.at[0])]
    for k in range(1, devices):
        target = (me + k) % devices
        copies.append(remote(source.at[target], out.at[me], send.at[k], recv.at[k], target))
    for copy in copies:
        copy.start()
    for copy in copies:
        copy.wait()


def everyone(values, number):
    devices = values.shape[0]
    return pl.pallas_call(
        functools.partial(everyone_kernel, devices),
        in_specs=[HBM],
        out_specs=HBM,
        out_shape=jax.ShapeDtypeStruct(values.shape, values.dtype),
        scratch_shapes=[pltpu.SemaphoreType.DMA((devices,))] * 2 + [pltpu.SemaphoreType.DMA((1,))],
        compiler_params=pltpu.CompilerParams(collective_id=number, has_side_effects=True),
    )(values)


def spread_steps(plane, block, out, sems, guests=()):
    line_send, line_recv, plane_send, plane_recv, own = sems
    me = lax.axis_index("tok")
    line, spot = me // plane, me % plane
    copies = [pltpu.make_async_copy(block, out.at[line, spot], own.at[0])]
    arrivals = []
    for k in range(1, LINES):
        place = (line + k) % LINES
        arrivals.append(remote(block, out.at[line, spot], line_send.at[k], line_recv.at[k], place * plane + spot))
    for k in range(1, plane):
        place = (spot + k) % plane
        copies.append(
            remote(block, out.at[line, spot], plane_send.at[0, k], plane_recv.at[0, k], line * plane + place)
        )
    for copy in (*arrivals, *copies, *guests):
        copy.start()
    for k in range(1, LINES):
        arrivals[k - 1].wait_recv()
        origin = (line + LINES - k) % LINES
        for j in range(1, plane):
            place = (spot + j) % plane
            copy = remote(
                out.at[origin, spot], out.at[origin, spot], plane_send.at[k, j], plane_recv.at[k, j], line * plane + place
            )
            copy.start()
            copies.append(copy)
    for copy in arrivals:
        copy.wait_send()
    for copy in copies:
        copy.wait()


def spread_sems(plane):
    return (
        [pltpu.SemaphoreType.DMA((LINES,))] * 2
        + [pltpu.SemaphoreType.DMA((LINES, plane))] * 2
        + [pltpu.SemaphoreType.DMA((1,))]
    )


def spread_kernel(plane, riders, block, *refs):
    count, own_sems = len(riders.specs), len(spread_sems(plane))
    sources, out, outs = refs[:count], refs[count], refs[count + 1 : 2 * count + 1]
    sems, ride = refs[2 * count + 1 : 2 * count + 1 + own_sems], refs[2 * count + 1 + own_sems :]
    me = lax.axis_index("tok")
    greet(me // plane, me % plane, plane)
    guests = riders.all_copies(sources, outs, ride)
    spread_steps(plane, block, out, sems, guests)
    for copy in guests:
        copy.wait()


def spread_blocks(block, plane, number, specs=(), values=()):
    riders = Riders(specs)
    return pl.pallas_call(
        functools.partial(spread_kernel, plane, riders),
        in_specs=[HBM] * (1 + len(values)),
        out_specs=[HBM] * (1 + len(values)),
        out_shape=[jax.ShapeDtypeStruct((LINES, plane) + block.shape, block.dtype)] + riders.shapes(values),
        scratch_shapes=spread_sems(plane) + riders.sems(),
        compiler_params=pltpu.CompilerParams(collective_id=number, has_side_effects=True),
    )(block, *values)


def fold_kernel(plane, riders, parts, *refs):
    count = len(riders.specs)
    sources, out, outs = refs[:count], refs[count], refs[count + 1 : 2 * count + 1]
    got, sent, last, block, plane_send, plane_recv, line_send, line_recv, own = refs[2 * count + 1 : 2 * count + 10]
    own_sems = len(spread_sems(plane))
    sems, ride = refs[2 * count + 10 : 2 * count + 10 + own_sems], refs[2 * count + 10 + own_sems :]
    me = lax.axis_index("tok")
    line, spot = me // plane, me % plane
    greet(line, spot, plane)
    copies = [pltpu.make_async_copy(parts.at[:, spot], got.at[spot], own.at[0])]
    for k in range(1, plane):
        place = (spot + k) % plane
        copies.append(
            remote(parts.at[:, place], got.at[spot], plane_send.at[k], plane_recv.at[k], line * plane + place)
        )
    for copy in copies:
        copy.start()
    guests = riders.all_copies(sources, outs, ride)
    for copy in guests:
        copy.start()
    for copy in copies:
        copy.wait()
    for z in range(LINES):
        total = got[0, z].astype(jnp.float32)
        for k in range(1, plane):
            total = total + got[k, z].astype(jnp.float32)
        sent[z] = total
    copies = [pltpu.make_async_copy(sent.at[line], last.at[line], own.at[1])]
    for k in range(1, LINES):
        place = (line + k) % LINES
        copies.append(remote(sent.at[place], last.at[line], line_send.at[k], line_recv.at[k], place * plane + spot))
    for copy in copies:
        copy.start()
    for copy in copies:
        copy.wait()
    block[...] = ((last[0] + last[1]) + (last[2] + last[3])).astype(block.dtype)
    spread_steps(plane, block, out, sems)
    for copy in guests:
        copy.wait()


def fold_and_spread(parts, plane, number, specs=(), values=()):
    shape = parts.shape[2:]
    riders = Riders(specs)
    return pl.pallas_call(
        functools.partial(fold_kernel, plane, riders),
        in_specs=[HBM] * (1 + len(values)),
        out_specs=[HBM] * (1 + len(values)),
        out_shape=[jax.ShapeDtypeStruct(parts.shape, parts.dtype)] + riders.shapes(values),
        scratch_shapes=[
            pltpu.VMEM((plane, LINES) + shape, parts.dtype),
            pltpu.VMEM((LINES,) + shape, jnp.float32),
            pltpu.VMEM((LINES,) + shape, jnp.float32),
            pltpu.VMEM(shape, parts.dtype),
        ]
        + [pltpu.SemaphoreType.DMA((plane,))] * 2
        + [pltpu.SemaphoreType.DMA((LINES,))] * 2
        + [pltpu.SemaphoreType.DMA((2,))]
        + spread_sems(plane)
        + riders.sems(),
        compiler_params=pltpu.CompilerParams(collective_id=number, has_side_effects=True, vmem_limit_bytes=60 * 2**20),
    )(parts, *values)


def dot_nt(left, right):
    return lax.dot_general(left, right, (((1,), (1,)), ((), ())), preferred_element_type=jnp.float32)

def dot_nn(left, right):
    return jnp.dot(left, right, preferred_element_type=jnp.float32)

def softplus(v):
    return jnp.maximum(v, 0.0) + jnp.log1p(jnp.exp(-jnp.abs(v)))

def split2(v):
    high = v.astype(jnp.bfloat16)
    return high, (v - high.astype(jnp.float32)).astype(jnp.bfloat16)

def own_token(dtype):
    token = lax.broadcasted_iota(jnp.int32, (GROUP, GROUP * N), 0)
    column = lax.broadcasted_iota(jnp.int32, (GROUP, GROUP * N), 1)
    return (column // N == token).astype(dtype)

def slice_columns(block_ref, cols_s, r, chunk):
    values = block_ref[0, chunk:].astype(jnp.float32)
    for g in range(chunk // GROUP):
        cols_s[r, g] = values[:, g * GROUP : (g + 1) * GROUP]


def lay_out(block_ref, inject_s, read_s, r, chunk):
    token = lax.broadcasted_iota(jnp.int32, (chunk, GROUP * N), 0) % GROUP
    column = lax.broadcasted_iota(jnp.int32, (chunk, GROUP * N), 1)
    mine = column // N == token
    for start, rows_s in ((chunk, inject_s), (chunk + N, read_s)):
        if rows_s is not None:
            rows_s[r] = jnp.where(mine, repeat_columns(block_ref[0, start : start + N]), 0).astype(jnp.bfloat16)


def repeat_columns(values):
    state = lax.broadcasted_iota(jnp.int32, (N, GROUP * N), 0)
    column = lax.broadcasted_iota(jnp.int32, (N, GROUP * N), 1)
    chosen = (column % N == state).astype(jnp.bfloat16)
    product = lax.dot_general(
        values, chosen, (((0,), (0,)), ((), ())), preferred_element_type=jnp.float32
    )
    return product


def fwd_kernel(pair, chunk, riders, f_ref, z_ref, start_ref, *refs):
    count = len(riders.specs)
    block_refs, refs = refs[:pair], refs[pair:]
    stepw_ref, bias_ref, rate_ref, skip_ref = refs[:4]
    sources, (mixed_ref, dz_ref, keep_ref) = refs[4 : 4 + count], refs[4 + count : 7 + count]
    outs, refs = refs[7 + count : 7 + 2 * count], refs[7 + 2 * count :]
    state, step_s, drive_s, scan_s, cols_s, read_s = refs[:6]
    if count:

        @pl.when((pl.program_id(0) == 0) & (pl.program_id(1) == 0))
        def _():
            riders.begin(sources, outs, refs[6:])

    groups = chunk // GROUP
    neg = rate_ref[...] * (-LOG2E)
    @pl.when(pl.program_id(1) == 0)
    def _():
        state[...] = jnp.zeros_like(state)

    for r in range(pair):
        raw = dot_nt(block_refs[r][0, :chunk], stepw_ref[...])
        step = softplus(raw + bias_ref[...])
        slice_columns(block_refs[r], cols_s, r, chunk)
        lay_out(block_refs[r], None, read_s, r, chunk)
        step_s[r] = step + start_ref[r].astype(jnp.float32)
        drive_s[r] = step * f_ref[r].astype(jnp.float32)
        keep_ref[r, 0] = state[r]

    def group(g, hidden):
        hidden = list(hidden)
        held = [[] for _ in range(pair)]
        base = pl.multiple_of(g * GROUP, GROUP)
        cols = [cols_s[r, g] for r in range(pair)]
        for k in range(GROUP):
            for r in range(pair):
                factor = jnp.exp2(step_s[r, pl.ds(base + k, 1), :] * neg)
                hidden[r] = factor * hidden[r] + drive_s[r, pl.ds(base + k, 1), :] * cols[r][:N, k : k + 1]
                held[r].append(hidden[r].astype(jnp.bfloat16))
        for r in range(pair):
            states = jnp.concatenate(held[r], axis=0)
            scan_s[r, pl.ds(base, GROUP), :] = dot_nn(read_s[r, pl.ds(base, GROUP), :], states)
        return tuple(hidden)

    hidden = lax.fori_loop(0, groups, group, tuple(state[r] for r in range(pair)), unroll=groups)
    for r in range(pair):
        state[r] = hidden[r]
        f = f_ref[r].astype(jnp.float32)
        z = z_ref[r].astype(jnp.float32)
        gate = 1.0 / (1.0 + jnp.exp(-z))
        summed = scan_s[r] + skip_ref[...] * f
        mixed_ref[r] = (summed * (z * gate)).astype(jnp.bfloat16)
        dz_ref[r] = summed * (gate * (1.0 + z * (1.0 - gate)))
    if count:

        @pl.when((pl.program_id(0) == pl.num_programs(0) - 1) & (pl.program_id(1) == pl.num_programs(1) - 1))
        def _():
            riders.end(sources, outs, refs[6:])

def bwd_kernel(pair, chunk, riders, f_ref, z_ref, gm_ref, start_ref, *refs):
    block_refs, refs = refs[:pair], refs[pair:]
    stepw_ref, bias_ref, rate_ref, skip_ref, keep_ref = refs[:5]
    refs = refs[5:]
    count = len(riders.specs)
    sources, refs = refs[:count], refs[count:]
    draw_ref, dfm_ref, dinj_ref, dread_ref, drate_ref, dskip_ref, dbias_ref = refs[:7]
    outs, refs = refs[7 : 7 + count], refs[7 + count :]
    carry_s, step_s, drive_s, dscan_s, raw_s, delta_s, a_s, ah_s, h_s, s1_s, s2_s, cols_s, inject_s = refs[:13]
    if count:

        @pl.when((pl.program_id(0) == 0) & (pl.program_id(1) == 0))
        def _():
            riders.begin(sources, outs, refs[13:])

    groups = chunk // GROUP
    rate = rate_ref[...]
    neg = rate * (-LOG2E)
    mine = own_token(jnp.bfloat16)
    mine_f = own_token(jnp.float32)

    @pl.when(pl.program_id(1) == 0)
    def _():
        carry_s[...] = jnp.zeros_like(carry_s)

    @pl.when((pl.program_id(1) == 0) & (pl.program_id(0) == 0))
    def _():
        drate_ref[...] = jnp.zeros_like(drate_ref)
        dskip_ref[...] = jnp.zeros_like(dskip_ref)
        dbias_ref[...] = jnp.zeros_like(dbias_ref)

    for r in range(pair):
        raw = dot_nt(block_refs[r][0, :chunk], stepw_ref[...]) + bias_ref[...]
        slice_columns(block_refs[r], cols_s, r, chunk)
        lay_out(block_refs[r], inject_s, None, r, chunk)
        step = softplus(raw)
        raw_s[r] = raw
        delta_s[r] = step
        step_s[r] = step + start_ref[r].astype(jnp.float32)
        f = f_ref[r].astype(jnp.float32)
        drive_s[r] = step * f
        z = z_ref[r].astype(jnp.float32)
        gate = 1.0 / (1.0 + jnp.exp(-z))
        dscan = gm_ref[r].astype(jnp.float32) * (z * gate)
        dscan_s[r] = dscan
        dskip_ref[...] += jnp.sum(dscan * f, axis=0, keepdims=True)

    def forward(g, hidden):
        hidden = list(hidden)
        base = pl.multiple_of(g * GROUP, GROUP)
        cols = [cols_s[r, g] for r in range(pair)]
        held = [[] for _ in range(pair)]
        for k in range(GROUP):
            for r in range(pair):
                factor = jnp.exp2(step_s[r, pl.ds(base + k, 1), :] * neg)
                kept = factor * hidden[r]
                hidden[r] = kept + drive_s[r, pl.ds(base + k, 1), :] * cols[r][:N, k : k + 1]
                a_s[r, base + k] = factor
                ah_s[r, base + k] = kept
                held[r].append(hidden[r].astype(jnp.bfloat16))
        for r in range(pair):
            h_s[r, g] = jnp.concatenate(held[r], axis=0)
        return tuple(hidden)

    lax.fori_loop(0, groups, forward, tuple(keep_ref[r, 0] for r in range(pair)), unroll=groups)

    def backward(i, carried):
        g = groups - 1 - i
        base = pl.multiple_of(g * GROUP, GROUP)
        ag = list(carried[:pair])
        total = carried[pair]
        cols = [cols_s[r, g] for r in range(pair)]
        gs = [[None] * GROUP for _ in range(pair)]
        qs = [[None] * GROUP for _ in range(pair)]
        for k in reversed(range(GROUP)):
            for r in range(pair):
                grad = dscan_s[r, pl.ds(base + k, 1), :] * cols[r][N:, k : k + 1] + ag[r]
                ag[r] = a_s[r, base + k] * grad
                q = grad * ah_s[r, base + k]
                total = total + delta_s[r, pl.ds(base + k, 1), :] * q
                gs[r][k] = grad.astype(jnp.bfloat16)
                qs[r][k] = (rate * q).astype(jnp.bfloat16)
        for r in range(pair):
            grads = jnp.concatenate(gs[r], axis=0)
            pulls = jnp.concatenate(qs[r], axis=0)
            s1_s[r, pl.ds(base, GROUP), :] = dot_nn(inject_s[r, pl.ds(base, GROUP), :], grads)
            s2_s[r, pl.ds(base, GROUP), :] = dot_nn(mine, pulls)
            dh, dl = split2(dscan_s[r, pl.ds(base, GROUP), :])
            uh, ul = split2(drive_s[r, pl.ds(base, GROUP), :])
            dr = dot_nt(jnp.concatenate([dh, dl], axis=0), h_s[r, g])
            dread_ref[r, pl.ds(g, 1), :] = jnp.sum((dr[:GROUP] + dr[GROUP:]) * mine_f, axis=0, keepdims=True)
            di = dot_nt(jnp.concatenate([uh, ul], axis=0), grads)
            dinj_ref[r, pl.ds(g, 1), :] = jnp.sum((di[:GROUP] + di[GROUP:]) * mine_f, axis=0, keepdims=True)
        return tuple(ag) + (total,)

    out = lax.fori_loop(
        0, groups, backward, tuple(carry_s[r] for r in range(pair)) + (jnp.zeros_like(rate),), unroll=groups
    )
    drate_ref[...] += out[pair]
    for r in range(pair):
        carry_s[r] = out[r]
        f = f_ref[r].astype(jnp.float32)
        draw = (f * s1_s[r] - s2_s[r]) / (1.0 + jnp.exp(-raw_s[r]))
        draw_ref[r] = draw.astype(jnp.bfloat16)
        dbias_ref[...] += jnp.sum(draw, axis=0, keepdims=True)
        dfm_ref[r] = delta_s[r] * s1_s[r] + skip_ref[...] * dscan_s[r]

    if count:

        @pl.when((pl.program_id(0) == pl.num_programs(0) - 1) & (pl.program_id(1) == pl.num_programs(1) - 1))
        def _():
            riders.end(sources, outs, refs[13:])


def specs(pair, chunk, ch, blocks, back, chunks):
    def at(i, j):
        return (i, chunks - 1 - j if back else j)
    tok = pl.BlockSpec((pair, chunk, ch), lambda i, j: at(i, j) + (0,))
    flat = pl.BlockSpec((pair, chunk // GROUP, GROUP * N), lambda i, j: at(i, j) + (0,))
    keep = pl.BlockSpec((pair, 1, N, ch), lambda i, j: at(i, j) + (0, 0))
    def block(r):
        def index(i, j):
            i, j = at(i, j)
            return ((i * pair + r) * chunks + j, 0, 0)
        return pl.BlockSpec((1,) + blocks.shape[1:], index)
    def whole(a):
        return pl.BlockSpec(a.shape, lambda i, j: (0,) * a.ndim)
    return tok, [block(r) for r in range(pair)], flat, keep, whole

def scan_forward(f, z, start, blocks, stepw, bias, rate, skip, rides=(), guests=(), number=None):
    riders = Riders(rides)
    params = dict(collective_id=number, has_side_effects=True) if guests else {}
    chunk = blocks.shape[1] - 2 * N
    rows, length, ch = f.shape
    pair = 2 if rows % 2 == 0 else 1
    chunks = length // chunk
    tok, block_specs, flat, keep, whole = specs(pair, chunk, ch, blocks, False, chunks)
    return pl.pallas_call(
        functools.partial(fwd_kernel, pair, chunk, riders),
        grid=(rows // pair, chunks),
        in_specs=[tok, tok, tok]
        + block_specs
        + [whole(stepw), whole(bias), whole(rate), whole(skip)]
        + [HBM] * len(guests),
        out_specs=[tok, tok, keep] + [HBM] * len(guests),
        out_shape=[jax.ShapeDtypeStruct(f.shape, jnp.bfloat16), jax.ShapeDtypeStruct(f.shape, jnp.float32),
                   jax.ShapeDtypeStruct((rows, chunks, N, ch), jnp.float32)]
        + riders.shapes(guests),
        scratch_shapes=[pltpu.VMEM((pair, N, ch), jnp.float32)] + [pltpu.VMEM((pair, chunk, ch), jnp.float32)] * 3
        + [pltpu.VMEM((pair, chunk // GROUP, 2 * N, GROUP), jnp.float32)]
        + [pltpu.VMEM((pair, chunk, GROUP * N), jnp.bfloat16)]
        + riders.sems(),
        compiler_params=pltpu.CompilerParams(vmem_limit_bytes=60 * 2**20, **params),
        cost_estimate=pl.CostEstimate(flops=4 * 10**10, bytes_accessed=8 * 10**6, transcendentals=0),
    )(f, z, start, *([blocks] * pair), stepw, bias, rate, skip, *guests)

def scan_backward(f, z, gm, start, blocks, stepw, bias, rate, skip, kept, rides=(), guests=(), number=None):
    chunk = blocks.shape[1] - 2 * N
    rows, length, ch = f.shape
    pair = 2 if rows % 2 == 0 else 1
    chunks = length // chunk
    tok, block_specs, flat, keep, whole = specs(pair, chunk, ch, blocks, True, chunks)
    f32 = jnp.float32
    row = jax.ShapeDtypeStruct((1, ch), f32)
    in_specs = [tok, tok, tok, tok] + block_specs + [whole(stepw), whole(bias), whole(rate), whole(skip), keep]
    inj = jax.ShapeDtypeStruct((rows, length // GROUP, GROUP * N), f32)
    out_specs = [tok, tok, flat, flat, whole(rate), whole(row), whole(row)]
    out_shape = [jax.ShapeDtypeStruct(f.shape, jnp.bfloat16), jax.ShapeDtypeStruct(f.shape, f32),
                 jax.ShapeDtypeStruct(inj.shape, f32), jax.ShapeDtypeStruct(inj.shape, f32),
                 jax.ShapeDtypeStruct(rate.shape, f32), row, row]
    scratch = ([pltpu.VMEM((pair, N, ch), f32)] + [pltpu.VMEM((pair, chunk, ch), f32)] * 5
               + [pltpu.VMEM((pair, chunk, N, ch), f32)] * 2
               + [pltpu.VMEM((pair, chunk // GROUP, GROUP * N, ch), jnp.bfloat16)]
               + [pltpu.VMEM((pair, chunk, ch), f32)] * 2
               + [pltpu.VMEM((pair, chunk // GROUP, 2 * N, GROUP), f32)]
               + [pltpu.VMEM((pair, chunk, GROUP * N), jnp.bfloat16)])
    values = (f, z, gm, start, *([blocks] * pair), stepw, bias, rate, skip, kept)
    params = dict(vmem_limit_bytes=60 * 2**20)
    riders = Riders(rides)
    if guests:
        in_specs, out_specs = in_specs + [HBM] * len(guests), out_specs + [HBM] * len(guests)
        out_shape = out_shape + riders.shapes(guests)
        scratch = scratch + riders.sems()
        values = values + tuple(guests)
        params.update(collective_id=number, has_side_effects=True)
    return pl.pallas_call(
        functools.partial(bwd_kernel, pair, chunk, riders),
        grid=(rows // pair, chunks),
        in_specs=in_specs,
        out_specs=out_specs,
        out_shape=out_shape,
        scratch_shapes=scratch,
        compiler_params=pltpu.CompilerParams(**params),
        cost_estimate=pl.CostEstimate(flops=7 * 10**10, bytes_accessed=8 * 10**6, transcendentals=0),
    )(*values)


DEPTH = 4
BATCH = 16


def tile_product_kernel(pairs, steps, transposed, residual, idx_ref, left_ref, pool_ref, *refs):
    if residual:
        res_ref, refs = refs[0], refs[1:]
    out_ref, slots, sems = refs
    side = slots.shape[2]
    total_steps = pairs * steps

    def fetch(step):
        for u in range(BATCH):
            pltpu.make_async_copy(
                pool_ref.at[idx_ref[step * BATCH + u]], slots.at[step % DEPTH, u], sems.at[step % DEPTH]
            ).start()

    for step in range(min(DEPTH - 1, total_steps)):
        fetch(step)

    def one_pair(o, carry):
        total = jnp.zeros((left_ref.shape[1], 2 * side), jnp.float32)
        for k in range(steps):
            step = o * steps + k

            @pl.when(step + DEPTH - 1 < total_steps)
            def _():
                fetch(step + DEPTH - 1)

            slot = step % DEPTH
            pltpu.make_async_copy(slots.at[slot], slots.at[slot], sems.at[slot]).wait()
            for u in range(0, BATCH, 4):
                at = k * (BATCH // 2) + u // 2
                left = jnp.concatenate([left_ref[at], left_ref[at + 1]], axis=1)
                tile = [slots[slot, u + v] for v in range(4)]
                if transposed:
                    right = jnp.concatenate(
                        [jnp.concatenate([tile[0], tile[2]], axis=1), jnp.concatenate([tile[1], tile[3]], axis=1)], axis=0
                    )
                    total += dot_nt(left, right)
                else:
                    right = jnp.concatenate(
                        [jnp.concatenate([tile[0], tile[1]], axis=1), jnp.concatenate([tile[2], tile[3]], axis=1)], axis=0
                    )
                    total += dot_nn(left, right)
        columns = pl.ds(pl.multiple_of(o * 2 * side, side), 2 * side)
        if residual:
            total += res_ref[:, columns].astype(jnp.float32)
        out_ref[:, columns] = total.astype(out_ref.dtype)
        return carry

    lax.fori_loop(0, pairs, one_pair, 0)


def tile_product(left, pool, index, transposed, dtype, residual=None):
    outs, depth = index.shape
    pairs, steps = outs // 2, 2 * depth // BATCH
    side = pool.shape[1]
    tok = left.shape[1]
    vmem = pl.BlockSpec(memory_space=pltpu.VMEM)
    extra = [residual] if residual is not None else []
    order = index.reshape(pairs, 2, depth).transpose(0, 2, 1).reshape(-1).astype(jnp.int32)
    return pl.pallas_call(
        functools.partial(tile_product_kernel, pairs, steps, transposed, residual is not None),
        in_specs=[pl.BlockSpec(memory_space=pltpu.SMEM), vmem, pl.BlockSpec(memory_space=pl.ANY)] + [vmem] * len(extra),
        out_specs=vmem,
        out_shape=jax.ShapeDtypeStruct((tok, outs * side), dtype),
        scratch_shapes=[pltpu.VMEM((DEPTH, BATCH, side, side), pool.dtype), pltpu.SemaphoreType.DMA((DEPTH,))],
        compiler_params=pltpu.CompilerParams(vmem_limit_bytes=40 * 2**20),
        cost_estimate=pl.CostEstimate(
            flops=2 * outs * depth * tok * side * side, bytes_accessed=outs * depth * side * side * 2, transcendentals=0
        ),
    )(order, left, pool, *extra)


def dot_tn(left, right):
    return lax.dot_general(left, right, (((0,), (0,)), ((), ())), preferred_element_type=jnp.float32)


def three(dot, left, right):
    left_axis, right_axis = {dot_nn: (1, 0), dot_nt: (1, 1), dot_tn: (0, 0)}[dot]
    return dot(
        jnp.concatenate([left[0], left[0], left[1]], axis=left_axis),
        jnp.concatenate([right[0], right[1], right[0]], axis=right_axis),
    )


def soap_kernel(sources, many, kind_ref, idx_ref, *refs):
    grad_refs, refs = refs[: sources * many], refs[sources * many :]
    weight_ref, first_ref, second_ref, left_ref, right_ref, lstat_ref, rstat_ref = refs[:7]
    first_out, second_out, weight_out, lstat_out, rstat_out, turned_out, gram_out = refs[7:]
    side = weight_ref.shape[1]
    diagonal = lax.broadcasted_iota(jnp.int32, (side, side), 0) == lax.broadcasted_iota(jnp.int32, (side, side), 1)
    every = range(many)
    grads, lefts, rights = [], [], []
    for u in every:
        kind = kind_ref[pl.program_id(0) * many + u]
        grad = grad_refs[u * sources][0]
        for which in range(1, sources):
            grad = jnp.where(kind == which, grad_refs[u * sources + which][0], grad)
        grads.append(grad)
        lefts.append(split2(left_ref[u]))
        rights.append(split2(right_ref[u]))
    across = [split2(dot_nn(grads[u], rights[u][0]) + dot_nn(grads[u], rights[u][1])) for u in every]
    turned = [three(dot_tn, lefts[u], across[u]) for u in every]
    products = [(dot_nt(grads[u], grads[u]), dot_tn(grads[u], grads[u])) for u in every]
    directions = []
    for u in every:
        first = beta_first * first_ref[u] + (1.0 - beta_first) * turned[u]
        second = beta_second * second_ref[u] + (1.0 - beta_second) * turned[u] * turned[u]
        first_out[u] = first
        second_out[u] = second
        directions.append(split2(
            first / (1.0 - beta_first**STEP) / (jnp.sqrt(second / (1.0 - beta_second**STEP)) + adam_epsilon)
        ))
    renewed = []
    for u in every:
        for which, (stat_ref, basis_ref, basis2, stat_out) in enumerate(
            ((lstat_ref, left_ref, lefts[u], lstat_out), (rstat_ref, right_ref, rights[u], rstat_out))
        ):
            stat = stat_decay * stat_ref[u] + (1.0 - stat_decay) * products[u][which]
            stat_out[u] = stat
            trace = jnp.sum(jnp.sum(jnp.where(diagonal, stat, 0.0), axis=0, keepdims=True), axis=1, keepdims=True)
            value = three(dot_nn, split2(stat), basis2) + (trace / side) * basis_ref[u]
            turned_out[u, which] = value
            renewed.append(split2(value))
    back = [split2(three(dot_nt, directions[u], rights[u])) for u in every]
    for u in every:
        for which in range(2):
            gram_out[u, which] = three(dot_tn, renewed[u * 2 + which], renewed[u * 2 + which])
    for u in every:
        weight = weight_ref[u]
        weight_out[u] = weight - learn_rate * (three(dot_nn, lefts[u], back[u]) + weight_decay * weight)


def soap_tiles(kind, index, grads, weight, first, second, left, right, lstat, rstat, many=4):
    count, side, _ = weight.shape
    one = pl.BlockSpec((many, side, side), lambda s, kind, idx: (s, 0, 0))
    two = pl.BlockSpec((many, 2, side, side), lambda s, kind, idx: (s, 0, 0, 0))

    def picked(u, which):
        def at(s, kind, idx):
            return (jnp.where(kind[s * many + u] == which, idx[s * many + u], 0), 0, 0)

        return pl.BlockSpec((1, side, side), at)

    tile = jax.ShapeDtypeStruct(weight.shape, jnp.float32)
    pairs = jax.ShapeDtypeStruct((count, 2, side, side), jnp.float32)
    sources = len(grads)
    return pl.pallas_call(
        functools.partial(soap_kernel, sources, many),
        grid_spec=pltpu.PrefetchScalarGridSpec(
            num_scalar_prefetch=2,
            grid=(count // many,),
            in_specs=[picked(u, which) for u in range(many) for which in range(sources)] + [one] * 7,
            out_specs=[one] * 5 + [two] * 2,
        ),
        out_shape=[tile] * 5 + [pairs] * 2,
        compiler_params=pltpu.CompilerParams(vmem_limit_bytes=60 * 2**20),
        cost_estimate=pl.CostEstimate(flops=count * 60 * side**3, bytes_accessed=count * 18 * 4 * side**2, transcendentals=0),
    )(kind, index, *(list(grads) * many), weight, first, second, left, right, lstat, rstat)


def renew_kernel(many, turned_ref, inv_ref, left_out, right_out):
    for u in range(many):
        for which, out in ((0, left_out), (1, right_out)):
            out[u] = three(dot_nt, split2(turned_ref[u, which]), split2(inv_ref[u, which]))


def renew_bases(turned, inverse, many=12):
    count, _, side, _ = turned.shape
    one = pl.BlockSpec((many, side, side), lambda s: (s, 0, 0))
    two = pl.BlockSpec((many, 2, side, side), lambda s: (s, 0, 0, 0))
    tile = jax.ShapeDtypeStruct((count, side, side), jnp.float32)
    return pl.pallas_call(
        functools.partial(renew_kernel, many),
        grid=(count // many,),
        in_specs=[two, two],
        out_specs=[one, one],
        out_shape=[tile, tile],
        compiler_params=pltpu.CompilerParams(vmem_limit_bytes=60 * 2**20),
    )(turned, inverse)


def chol_kernel(batch, order, riders, gram_ref, *refs):
    count = len(riders.specs)
    sources, out_ref, outs = refs[:count], refs[count], refs[count + 1 : 2 * count + 1]
    low_ref, inv_ref, piv_ref = refs[2 * count + 1 : 2 * count + 4]
    ride_sems_here = refs[2 * count + 4 :]
    if count:
        greetings = riders.hello()
    tiles = order // 8
    rows8 = lax.broadcasted_iota(jnp.int32, (8, batch), 0)

    def load_slab(j, carry):
        low_ref[j, pl.ds(0, order), :] = gram_ref[pl.ds(j, batch, stride=order), :].T
        inv_ref[j] = jnp.zeros(inv_ref.shape[1:], jnp.float32)
        return carry

    lax.fori_loop(0, order, load_slab, 0, unroll=16)
    if count:
        riders.start(greetings, sources, outs, ride_sems_here)

    def bcast(ref, j, row):
        return jnp.broadcast_to(ref[j, pl.ds(row, 1), :], (8, batch))

    def block_column(block, carry):
        base = pl.multiple_of(block * 8, 8)

        def updated(tile_rows, seed):
            def one(j, accs):
                mult = [bcast(low_ref, j, base + k) for k in range(8)]
                out = []
                for s, rows in enumerate(tile_rows):
                    piece = low_ref[j, pl.ds(rows, 8), :]
                    out.extend(accs[s * 8 + k] - piece * mult[k] for k in range(8))
                return tuple(out)

            def eight(step, accs):
                for u in range(8):
                    accs = one(step * 8 + u, accs)
                return accs

            return list(lax.fori_loop(0, block, eight, tuple(seed)))

        accs = updated([base], [low_ref[base + k, pl.ds(base, 8), :] for k in range(8)])
        scales = []
        for k in range(8):
            scale = lax.rsqrt(jnp.broadcast_to(accs[k][k : k + 1, :], (8, batch)))
            scales.append(scale)
            accs[k] = jnp.where(rows8 >= k, accs[k] * scale, 0.0)
            for later in range(k + 1, 8):
                accs[later] = accs[later] - accs[k] * jnp.broadcast_to(
                    accs[k][later : later + 1, :], (8, batch)
                )
        for k in range(8):
            low_ref[base + k, pl.ds(base, 8), :] = accs[k]
            piv_ref[base + k] = scales[k]

        def pair(p, carry):
            first = pl.multiple_of(base + 8 + p * 16, 8)
            both = [first, pl.multiple_of(first + 8, 8)]
            accs = updated(
                both, [low_ref[base + k, pl.ds(rows, 8), :] for rows in both for k in range(8)]
            )
            for k in range(8):
                scale = piv_ref[base + k]
                for s in range(2):
                    accs[s * 8 + k] = accs[s * 8 + k] * scale
                for later in range(k + 1, 8):
                    mult = bcast(low_ref, base + k, base + later)
                    for s in range(2):
                        accs[s * 8 + later] = accs[s * 8 + later] - accs[s * 8 + k] * mult
            for s, rows in enumerate(both):
                for k in range(8):
                    low_ref[base + k, pl.ds(rows, 8), :] = accs[s * 8 + k]
            return carry

        lax.fori_loop(0, (tiles - block) // 2, pair, 0)
        return carry

    lax.fori_loop(0, tiles, block_column, 0)

    def block_row(block, carry):
        base = pl.multiple_of(block * 8, 8)

        def finish(accs, both):
            for k in range(8):
                scale = piv_ref[base + k]
                for s in range(len(both)):
                    accs[s * 8 + k] = accs[s * 8 + k] * scale
                for later in range(k + 1, 8):
                    mult = bcast(low_ref, base + k, base + later)
                    for s in range(len(both)):
                        accs[s * 8 + later] = accs[s * 8 + later] - accs[s * 8 + k] * mult
            for s, columns in enumerate(both):
                for k in range(8):
                    inv_ref[base + k, pl.ds(columns, 8), :] = accs[s * 8 + k]

        def pair(p, carry):
            first = pl.multiple_of(p * 16, 8)
            both = [first, pl.multiple_of(first + 8, 8)]

            def eight(step, accs):
                for u in range(8):
                    j = step * 8 + u
                    mult = [bcast(low_ref, j, base + k) for k in range(8)]
                    out = []
                    for s, columns in enumerate(both):
                        piece = inv_ref[j, pl.ds(columns, 8), :]
                        out.extend(accs[s * 8 + k] - piece * mult[k] for k in range(8))
                    accs = tuple(out)
                return accs

            accs = list(lax.fori_loop(
                p * 2, block, eight, (jnp.zeros((8, batch), jnp.float32),) * 16
            ))
            finish(accs, both)
            return carry

        lax.fori_loop(0, (block + 1) // 2, pair, 0)
        odd = block % 2

        def diagonal():
            accs = [jnp.where(rows8 == k, 1.0, 0.0) for k in range(8)]
            finish(accs, [base])

        diagonal()
        return carry

    lax.fori_loop(0, tiles, block_row, 0)

    def store_slab(i, carry):
        out_ref[pl.ds(i, batch, stride=order), :] = inv_ref[i, pl.ds(0, order), :].T
        return carry

    lax.fori_loop(0, order, store_slab, 0, unroll=16)
    if count:
        riders.end(sources, outs, ride_sems_here)

def inverse_factors(gram, rides=(), guests=(), number=None):
    count, pair, order, _ = gram.shape
    batch = count * pair
    riders = Riders(rides)
    params = dict(vmem_limit_bytes=60 * 2**20)
    if guests:
        params.update(collective_id=number, has_side_effects=True)
    vmem = pl.BlockSpec(memory_space=pltpu.VMEM)
    out, *arrived = pl.pallas_call(
        functools.partial(chol_kernel, batch, order, riders),
        out_shape=[jax.ShapeDtypeStruct((batch * order, order), jnp.float32)] + riders.shapes(guests),
        in_specs=[vmem] + [HBM] * len(guests),
        out_specs=[vmem] + [HBM] * len(guests),
        scratch_shapes=[
            pltpu.VMEM((order, order + 8, batch), jnp.float32),
            pltpu.VMEM((order, order + 8, batch), jnp.float32),
            pltpu.VMEM((order, 8, batch), jnp.float32),
        ]
        + riders.sems(),
        compiler_params=pltpu.CompilerParams(**params),
        cost_estimate=pl.CostEstimate(flops=5 * 10**10, bytes_accessed=12 * 10**6, transcendentals=0),
    )(gram.reshape(batch * order, order), *guests)
    return (out.reshape(gram.shape), *arrived)


def norm_joint_kernel(channels, riders, x_ref, gain_ref, weight_ref, *refs):
    count = len(riders.specs)
    sources, (normed_ref, xs_ref, gate_ref) = refs[:count], refs[count : count + 3]
    outs, sems = refs[count + 3 : 2 * count + 3], refs[2 * count + 3 :]
    if count:

        @pl.when(pl.program_id(0) == 0)
        def _():
            riders.begin(sources, outs, sems)

    width = x_ref.shape[2]
    x = x_ref[...].astype(jnp.float32).reshape(-1, width)
    inverse = lax.rsqrt(jnp.mean(x * x, axis=1, keepdims=True) + norm_epsilon)
    normed = (x * inverse * gain_ref[...]).astype(jnp.bfloat16)
    normed_ref[...] = normed
    joint = dot_nn(normed, weight_ref[...]).astype(jnp.bfloat16)
    xs_ref[...] = joint[:, :channels]
    gate_ref[...] = joint[:, channels:]
    if count:

        @pl.when(pl.program_id(0) == pl.num_programs(0) - 1)
        def _():
            riders.end(sources, outs, sems)


def norm_joint(x, gain, weight, rides=(), guests=(), number=None, many=2):
    devices, rows, width = x.shape
    riders = Riders(rides)
    params = dict(collective_id=number, has_side_effects=True) if guests else {}
    tokens, block = devices * rows, many * rows
    channels = weight.shape[1] // 2
    wide = pl.BlockSpec((block, width), lambda i: (i, 0))
    thin = pl.BlockSpec((block, channels), lambda i: (i, 0))
    half = jax.ShapeDtypeStruct((tokens, channels), jnp.bfloat16)
    return pl.pallas_call(
        functools.partial(norm_joint_kernel, channels, riders),
        grid=(tokens // block,),
        in_specs=[
            pl.BlockSpec((many, rows, width), lambda i: (i, 0, 0)),
            pl.BlockSpec((1, width), lambda i: (0, 0)),
            pl.BlockSpec((width, 2 * channels), lambda i: (0, 0)),
        ]
        + [HBM] * len(guests),
        out_specs=[wide, thin, thin] + [HBM] * len(guests),
        out_shape=[jax.ShapeDtypeStruct((tokens, width), jnp.bfloat16), half, half] + riders.shapes(guests),
        scratch_shapes=riders.sems(),
        compiler_params=pltpu.CompilerParams(vmem_limit_bytes=60 * 2**20, **params),
        cost_estimate=pl.CostEstimate(
            flops=4 * tokens * width * channels, bytes_accessed=4 * tokens * width, transcendentals=0
        ),
    )(x, gain, weight, *guests)


def plane_product_kernel(count, many, riders, weight_ref, *refs):
    guests = len(riders.specs)
    lefts, sources, out_ref = refs[:count], refs[count : count + guests], refs[count + guests]
    outs, total_ref = refs[count + guests + 1 : count + 2 * guests + 1], refs[count + 2 * guests + 1]
    sems = refs[count + 2 * guests + 2 :]
    step = pl.program_id(0)
    if guests:

        @pl.when(step == 0)
        def _():
            riders.begin(sources, outs, sems)

    left = jnp.concatenate([ref[u] for u in range(many) for ref in lefts], axis=1)
    part = dot_nt(left, jnp.concatenate([weight_ref[u] for u in range(many)], axis=1))

    @pl.when(step == 0)
    def _():
        total_ref[...] = part

    @pl.when(step > 0)
    def _():
        total_ref[...] += part

    @pl.when(step == pl.num_programs(0) - 1)
    def _():
        out_ref[...] = total_ref[...].astype(out_ref.dtype)
        if guests:
            riders.end(sources, outs, sems)


def plane_product(lefts, weight, block, rides=(), guests=(), number=None, many=4):
    members, tokens, channels = lefts[0].shape
    rows, width = len(lefts) * channels, weight.shape[1]
    riders = Riders(rides)
    params = dict(collective_id=number, has_side_effects=True) if guests else {}
    out, *arrived = pl.pallas_call(
        functools.partial(plane_product_kernel, len(lefts), many, riders),
        grid=(members // many,),
        in_specs=[pl.BlockSpec((many, width, rows), lambda p: (p, 0, block))]
        + [pl.BlockSpec((many, tokens, channels), lambda p: (p, 0, 0))] * len(lefts)
        + [HBM] * len(guests),
        out_specs=[pl.BlockSpec((tokens, width), lambda p: (0, 0))] + [HBM] * len(guests),
        out_shape=[jax.ShapeDtypeStruct((tokens, width), jnp.bfloat16)] + riders.shapes(guests),
        scratch_shapes=[pltpu.VMEM((tokens, width), jnp.float32)] + riders.sems(),
        compiler_params=pltpu.CompilerParams(vmem_limit_bytes=60 * 2**20, **params),
        cost_estimate=pl.CostEstimate(
            flops=2 * members * tokens * rows * width, bytes_accessed=2 * members * rows * width, transcendentals=0
        ),
    )(weight, *lefts, *guests)
    return (out, *arrived)


def plane_back_kernel(left_ref, weight_ref, out_ref):
    out_ref[0] = dot_nn(left_ref[...], weight_ref[0]).astype(out_ref.dtype)


def plane_back(left, weight, channels, block):
    members, width, _ = weight.shape
    tokens = left.shape[0]
    return pl.pallas_call(
        plane_back_kernel,
        grid=(members,),
        in_specs=[
            pl.BlockSpec((tokens, width), lambda p: (0, 0)),
            pl.BlockSpec((1, width, channels), lambda p: (p, 0, block)),
        ],
        out_specs=pl.BlockSpec((1, tokens, channels), lambda p: (p, 0, 0)),
        out_shape=jax.ShapeDtypeStruct((members, tokens, channels), jnp.bfloat16),
        compiler_params=pltpu.CompilerParams(vmem_limit_bytes=60 * 2**20),
        cost_estimate=pl.CostEstimate(
            flops=2 * members * tokens * width * channels, bytes_accessed=2 * members * width * channels, transcendentals=0
        ),
    )(left, weight)


def line_product_kernel(left_ref, right_ref, out_ref):
    product = dot_tn(left_ref[0], right_ref[...])
    side = out_ref.shape[3]
    for b in range(out_ref.shape[1]):
        out_ref[0, b] = product[:, b * side : (b + 1) * side].astype(out_ref.dtype)


def line_product(lefts, right, tall):
    members, tokens, channels = lefts.shape
    width = right.shape[1]
    side = width // tall
    return pl.pallas_call(
        line_product_kernel,
        grid=(members,),
        in_specs=[
            pl.BlockSpec((1, tokens, channels), lambda p: (p, 0, 0)),
            pl.BlockSpec((tokens, width), lambda p: (0, 0)),
        ],
        out_specs=pl.BlockSpec((1, tall, channels, side), lambda p: (p, 0, 0, 0)),
        out_shape=jax.ShapeDtypeStruct((members, tall, channels, side), jnp.bfloat16),
        compiler_params=pltpu.CompilerParams(vmem_limit_bytes=60 * 2**20),
        cost_estimate=pl.CostEstimate(
            flops=2 * members * tokens * channels * width, bytes_accessed=4 * members * channels * width, transcendentals=0
        ),
    )(lefts, right)


def plain_three(dot, left, right):
    return dot(left[0], right[0]) + (dot(left[0], right[1]) + dot(left[1], right[0]))


def channel_kernel(weight_ref, grad_ref, first_ref, second_ref, left_ref, right_ref, lstat_ref, rstat_ref,
                   first_out, second_out, weight_out, lstat_out, rstat_out, lturn_out, rturn_out, lgram_out, rgram_out):
    grad = split2(grad_ref[...])
    left, right = split2(left_ref[...]), split2(right_ref[...])
    turned = plain_three(dot_tn, left, split2(plain_three(dot_nn, grad, right)))
    first = beta_first * first_ref[...] + (1.0 - beta_first) * turned
    second = beta_second * second_ref[...] + (1.0 - beta_second) * turned * turned
    first_out[...] = first
    second_out[...] = second
    direction = split2(
        first / (1.0 - beta_first**STEP) / (jnp.sqrt(second / (1.0 - beta_second**STEP)) + adam_epsilon)
    )
    returned = plain_three(dot_nn, left, split2(plain_three(dot_nt, direction, right)))
    weight = weight_ref[...]
    weight_out[...] = weight - learn_rate * (returned + weight_decay * weight)
    for basis_ref, basis, stat_ref, product, stat_out, turn_out, gram_out in (
        (left_ref, left, lstat_ref, plain_three(dot_nt, grad, grad), lstat_out, lturn_out, lgram_out),
        (right_ref, right, rstat_ref, plain_three(dot_tn, grad, grad), rstat_out, rturn_out, rgram_out),
    ):
        order = basis_ref.shape[0]
        diagonal = lax.broadcasted_iota(jnp.int32, (order, order), 0) == lax.broadcasted_iota(
            jnp.int32, (order, order), 1
        )
        stat = stat_decay * stat_ref[...] + (1.0 - stat_decay) * product
        stat_out[...] = stat
        trace = jnp.sum(jnp.sum(jnp.where(diagonal, stat, 0.0), axis=0, keepdims=True), axis=1, keepdims=True)
        value = plain_three(dot_nn, split2(stat), basis) + (trace / order) * basis_ref[...]
        turn_out[...] = value
        value = split2(value)
        gram_out[...] = plain_three(dot_tn, value, value)


def channel_moments(weight, grad, first, second, left, right, lstat, rstat):
    f32 = jnp.float32
    rows = jax.ShapeDtypeStruct(weight.shape, f32)
    small = jax.ShapeDtypeStruct(left.shape, f32)
    large = jax.ShapeDtypeStruct(right.shape, f32)
    return pl.pallas_call(
        channel_kernel,
        out_shape=[rows] * 3 + [small, large] * 3,
        compiler_params=pltpu.CompilerParams(vmem_limit_bytes=60 * 2**20),
        cost_estimate=pl.CostEstimate(flops=8 * 10**9, bytes_accessed=6 * 10**6, transcendentals=0),
    )(weight, grad, first, second, left, right, lstat, rstat)


PANEL = 32


def factor_inverse(block):
    order = block.shape[0]
    rows = lax.broadcasted_iota(jnp.int32, (order, 2 * order), 0)
    columns = lax.broadcasted_iota(jnp.int32, (order, 2 * order), 1)
    both = jnp.concatenate([block, jnp.zeros_like(block)], axis=1) + jnp.where(columns == rows + order, 1.0, 0.0)
    for k in range(order):
        scale = lax.rsqrt(both[k : k + 1, k : k + 1])
        row = both[k : k + 1, :] * scale
        column = both[:, k : k + 1] * scale
        both = jnp.where(rows == k, row, jnp.where(rows > k, both - column * row, both))
    return both[:, order:]


def solve_kernel(count, riders, *refs):
    guests = len(riders.specs)
    grams, sides, refs = refs[:count], refs[count : 2 * count], refs[2 * count :]
    sources, outs, refs = refs[:guests], refs[guests : guests + count], refs[guests + count :]
    arrived, works, ride = refs[:guests], refs[guests : guests + 2 * count], refs[guests + 2 * count :]
    if guests:
        riders.begin(sources, arrived, ride)
    for i in range(count):
        order = grams[i].shape[0]
        gram, side = works[2 * i], works[2 * i + 1]
        gram[...] = grams[i][...]
        side[...] = sides[i][...]
        for start in range(0, order, PANEL):
            stop = start + PANEL
            low = split2(factor_inverse(gram[start:stop, start:stop]))
            upper = split2(plain_three(dot_nn, low, split2(gram[start:stop, :])))
            solved = plain_three(dot_nn, low, split2(side[start:stop, :]))
            outs[i][start:stop, :] = solved
            if stop < order:
                gram[stop:, :] -= plain_three(dot_tn, upper, upper)[stop:]
                side[stop:, :] -= plain_three(dot_tn, upper, split2(solved))[stop:]
    if guests:
        riders.end(sources, arrived, ride)


def solve_factors(grams, sides, rides=(), guests=(), number=None):
    count = len(grams)
    riders = Riders(rides)
    params = dict(vmem_limit_bytes=60 * 2**20)
    if guests:
        params.update(collective_id=number, has_side_effects=True)
    shapes = [jax.ShapeDtypeStruct(s.shape, jnp.float32) for s in sides]
    scratch = []
    for g, s in zip(grams, sides):
        scratch += [pltpu.VMEM(g.shape, jnp.float32), pltpu.VMEM(s.shape, jnp.float32)]
    vmem = pl.BlockSpec(memory_space=pltpu.VMEM)
    return pl.pallas_call(
        functools.partial(solve_kernel, count, riders),
        in_specs=[vmem] * (2 * count) + [HBM] * len(guests),
        out_specs=[vmem] * count + [HBM] * len(guests),
        out_shape=shapes + riders.shapes(guests),
        scratch_shapes=scratch + riders.sems(),
        compiler_params=pltpu.CompilerParams(**params),
        cost_estimate=pl.CostEstimate(flops=4 * 10**10, bytes_accessed=3 * 10**6, transcendentals=0),
    )(*grams, *sides, *guests)


def doc_positions(doc_lengths):
    starts = jnp.cumsum(doc_lengths, axis=1) - doc_lengths
    places = jnp.arange(L, dtype=jnp.int32)
    begun = jnp.where(starts[:, None, :] <= places[None, :, None], starts[:, None, :], 0)
    return places[None, :] - jnp.max(begun, axis=2)


def adam_step(weight, gradient, first, second):
    first_new = beta_first * first + (1.0 - beta_first) * gradient
    second_new = beta_second * second + (1.0 - beta_second) * gradient * gradient
    direction = (
        first_new
        / (1.0 - beta_first**STEP)
        / (jnp.sqrt(second_new / (1.0 - beta_second**STEP)) + adam_epsilon)
    )
    return (first_new, second_new, weight - vector_rate * (direction + weight_decay * weight))


def later(values, lag):
    return jnp.pad(values, ((lag, 0), (0, 0)))[: values.shape[0]]


def sooner(values, lag):
    return jnp.pad(values, ((0, lag), (0, 0)))[lag:]


def conv_pre(xs, taps, offset, place):
    total = offset[None] + taps[K - 1][None] * xs
    for lag in range(1, K):
        total = total + jnp.where(place >= lag, taps[K - 1 - lag][None] * later(xs, lag), 0.0)
    return total


def rank_within(key):
    count = key.shape[0]
    earlier = jnp.arange(count)[None, :] < jnp.arange(count)[:, None]
    return jnp.sum(((key[None, :] == key[:, None]) & earlier).astype(jnp.int32), axis=1)


def table(size, target, chosen, value):
    hit = (target[None, :] == jnp.arange(size)[:, None]) & chosen[None, :]
    return jnp.sum(jnp.where(hit, value[None, :], 0), axis=1)


CAPS = (13, 9)


class Routes:
    def __init__(self, tile_slot, devices, tiles_here, tall, half):
        count = tile_slot.shape[0]
        plane = devices // LINES
        wide = 2 * half
        tile = jnp.arange(count, dtype=jnp.int32)
        output = tile >= tall * wide
        relative = tile - tall * wide
        column = tile % wide
        self.plane = plane
        self.local = tile_slot % tiles_here
        self.owner = tile_slot // tiles_here
        self.target = jnp.where(output, relative // tall, column % half)
        self.kind = jnp.where(output, 2, column // half)
        self.place = jnp.where(output, 2 * tall + relative % tall, column // half * tall + tile // wide)
        self.owner_line, self.owner_spot = self.owner // plane, self.owner % plane
        self.target_line, self.target_spot = self.target // plane, self.target % plane
        self.ways, self.fits = self.settle(CAPS)

    def settle(self, caps):
        odd = self.place % 2 == 1
        for attempt in range(2):
            middle = jnp.where(
                odd, self.owner_line * self.plane + self.target_spot, self.target_line * self.plane + self.owner_spot
            )
            kind = odd.astype(jnp.int32)
            line_key = (self.owner_line * LINES + self.target_line) * self.plane + middle % self.plane
            plane_key = (self.owner_spot * self.plane + self.target_spot) * LINES + middle // self.plane
            ranks = rank_within(line_key * 2 + kind), rank_within(plane_key * 2 + kind)
            full = (ranks[0] >= caps[0]) | (ranks[1] >= caps[1])
            if attempt == 0:
                odd = odd ^ full
        return (odd, middle, *ranks), ~jnp.any(full)

    def spots(self, line_member, spot_member):
        by_line = line_member * CAPS[0] + self.ways[2]
        by_plane = LINES * CAPS[0] + spot_member * CAPS[1] + self.ways[3]
        return by_line, by_plane

    def tables(self, me):
        odd, middle = self.ways[:2]
        size = LINES * CAPS[0] + self.plane * CAPS[1]
        target_line, target_plane = self.spots(self.target_line, self.target_spot)
        owner_line, owner_plane = self.spots(self.owner_line, self.owner_spot)
        first = table(size, jnp.where(odd, target_plane, target_line), self.owner == me, self.local)
        second = table(
            size, jnp.where(odd, target_line, target_plane), middle == me, jnp.where(odd, owner_plane, owner_line)
        )
        landed = jnp.where(odd, owner_line, owner_plane)
        back_first = table(size, jnp.where(odd, owner_line, owner_plane), self.target == me, self.place)
        back_second = table(
            size, jnp.where(odd, owner_plane, owner_line), middle == me, jnp.where(odd, target_line, target_plane)
        )
        back_landed = jnp.where(odd, target_plane, target_line)
        return first, second, landed, back_first, back_second, back_landed


def pick(values, index):
    return values.at[index].get(mode="clip")


def device_groups(devices):
    plane = devices // LINES
    lines = [[z * plane + p for z in range(LINES)] for p in range(plane)]
    planes = [[z * plane + p for p in range(plane)] for z in range(LINES)]
    return lines, planes


def spread(value, devices):
    lines, planes = device_groups(devices)
    plane = devices // LINES
    step = lax.all_to_all(
        jnp.broadcast_to(value, (LINES,) + value.shape), "tok", 0, 0, tiled=True, axis_index_groups=lines
    )
    step = lax.all_to_all(
        jnp.broadcast_to(step, (plane,) + step.shape), "tok", 0, 0, tiled=True, axis_index_groups=planes
    )
    return jnp.swapaxes(step, 0, 1).reshape((devices * value.shape[0],) + value.shape[1:])


def fold(values, devices):
    lines, planes = device_groups(devices)
    plane = devices // LINES
    rows = values.shape[0] // devices
    parts = jnp.swapaxes(values.reshape((LINES, plane, rows) + values.shape[1:]), 0, 1).astype(jnp.bfloat16)
    parts = lax.all_to_all(parts, "tok", 0, 0, tiled=True, axis_index_groups=planes)
    parts = jnp.sum(parts.astype(jnp.float32), axis=0)
    parts = lax.all_to_all(parts, "tok", 0, 0, tiled=True, axis_index_groups=lines)
    return jnp.sum(parts, axis=0)


def core(
    routes,
    fast,
    x_all,
    small_all,
    weights,
    layer_in,
    cotangent,
    doc_lengths,
    tile_slot,
    pool_weight,
    pool_first,
    pool_second,
    pool_left,
    pool_right,
    pool_left_stat,
    pool_right_stat,
    channel_weight,
    channel_first,
    channel_second,
    channel_left,
    channel_right,
    channel_left_stat,
    channel_right_stat,
    norm_gain,
    gain_first,
    gain_second,
    channel_vectors,
    vector_first,
    vector_second,
):
    bf16, f32 = jnp.bfloat16, jnp.float32
    devices = lax.axis_size("tok")
    me = lax.axis_index("tok")
    lines, planes = device_groups(devices)
    plane = devices // LINES
    my_line, my_plane = me // plane, me % plane
    tok_rows, model_width = layer_in.shape
    tokens = tok_rows * devices
    rows = tokens // L
    channels = channel_vectors.shape[1]
    inner_width = channels * devices
    tiles_here, side, _ = pool_weight.shape
    tall = model_width // side
    half = inner_width // side
    wide = 2 * half
    cut = side // channels
    input_tiles = tall * wide
    select_width = channel_weight.shape[1] - R
    gain_here = norm_gain.shape[0]

    gain_float = small_all[:, select_width, :gain_here].reshape(1, model_width).astype(f32)
    select_blocks = small_all[:, :select_width].reshape(half, cut, select_width, channels)
    select_blocks = select_blocks.transpose(0, 2, 1, 3).reshape(half, select_width, side)
    if not fast:
        pool_low = pool_weight.astype(bf16)

    is_out = routes.kind == 2
    if fast:
        input_local, output_local, plane_own, back_first, back_second, back_landed = weights
    else:
        pool_all = lax.all_gather(pool_low, "tok", axis=0, tiled=True)
        columns = me // cut
        input_slots = tile_slot[:input_tiles].reshape(tall, 2, half)
        input_own = jnp.take(
            pool_all, lax.dynamic_index_in_dim(input_slots, columns, 2, False).T.reshape(-1), axis=0
        )
        output_slots = tile_slot[input_tiles:].reshape(half, tall)
        output_own = jnp.take(pool_all, lax.dynamic_index_in_dim(output_slots, columns, 0, False), axis=0)
        offset = me % cut * channels
        input_local = input_own.reshape(2, tall, side, side)
        output_local = output_own
        if cut > 1:
            input_local = lax.dynamic_slice_in_dim(input_local, offset, channels, axis=3)
            output_local = lax.dynamic_slice_in_dim(output_local, offset, channels, axis=1)
        input_local = input_local.transpose(1, 2, 0, 3).reshape(model_width, 2 * channels)
        output_local = output_local.transpose(1, 0, 2).reshape(channels, model_width)

    if fast:
        plane_weight = lax.all_gather(plane_own, "tok", axis=0, axis_index_groups=planes)
        upper, lower = cotangent[: tok_rows // 2], cotangent[tok_rows // 2 :]
        normed_all, xs_low, gates, upper = norm_joint(
            x_all, gain_float, input_local, [("line_gather", plane)], [upper], 11
        )
    else:
        normed_all, xs_low, gates = norm_joint(x_all, gain_float, input_local)
        cotangent_all = lax.all_gather(cotangent, "tok", axis=0, tiled=True)

    def to_tokens(values, number=None):
        lead = values.shape[:-2]
        parts = values.reshape(lead + (devices, tok_rows, channels))
        if fast and number is not None:
            moved = everyone(parts, number)
        else:
            moved = lax.all_to_all(parts, "tok", split_axis=len(lead), concat_axis=len(lead), tiled=True)
        moved = moved.reshape(lead + (half, cut, tok_rows, channels))
        return jnp.swapaxes(moved, -3, -2).reshape(lead + (half, tok_rows, side))

    place = doc_positions(doc_lengths).reshape(-1, 1)
    taps, offset = channel_vectors[:K], channel_vectors[K]
    xs = xs_low.astype(f32)
    filtered = jax.nn.silu(conv_pre(xs, taps, offset, place)).astype(bf16)
    filtered_tokens = to_tokens(filtered, 3)
    block = jnp.concatenate(
        [
            jnp.einsum("gtc,gfc->tf", filtered_tokens, select_blocks[:, :R], preferred_element_type=f32),
            jnp.einsum("gtc,gfc->ft", filtered_tokens, select_blocks[:, R:], preferred_element_type=f32),
        ],
        axis=0,
    ).astype(bf16)
    if fast:
        blocks, lower = spread_blocks(block, plane, 4, [("line_gather", plane)], [lower])
        blocks = blocks.reshape(devices, tok_rows + 2 * N, R)
        cotangent_line = jnp.concatenate([upper, lower], axis=1).reshape(LINES * tok_rows, model_width)
    else:
        blocks = spread(block[None], devices)

    if fast:
        def share(values):
            return values.reshape(LINES, plane, tok_rows, channels)

        def across(blocks, which, *riding):
            blocks = [values.reshape(plane, LINES * tok_rows, channels) for values in blocks]
            product, *arrived = plane_product(blocks, plane_weight, which, *riding)
            return (product.reshape(LINES, tok_rows, model_width), *arrived)

    by_row = lambda values: values.reshape((rows, L) + values.shape[1:])
    begins = by_row(jnp.broadcast_to(jnp.where(place == 0, 1e30, 0.0).astype(bf16), (tokens, channels)))
    step_local = channel_weight[:, select_width:].astype(bf16)
    rates = jnp.exp(channel_vectors[K + 2 : K + 2 + N])
    step_bias = channel_vectors[K + 1 : K + 2]
    skip_gain = channel_vectors[K + 2 + N :]
    scan_params = (step_local, step_bias, rates, skip_gain)
    scan_rides, scan_guests = [], []
    if fast:
        back_parts = plane_back(cotangent_line, plane_weight, channels, 2)
        scan_rides = [("plane_back", plane)]
        scan_guests = [back_parts.reshape(plane, LINES, tok_rows, channels)]
    mixed, gate_slope, kept, *arrived = scan_forward(
        by_row(filtered), by_row(gates), begins, blocks, *scan_params, scan_rides, scan_guests, 12
    )
    mixed = mixed.reshape(tokens, channels)
    if fast:
        back_chan = arrived[0].reshape(tokens, channels)
        (mixed_plane,) = exchange([("plane", plane)], [share(mixed)], 7)
    else:
        back_chan = jnp.einsum("td,cd->tc", cotangent_all, output_local, preferred_element_type=f32).astype(bf16)
    back_chan = lax.optimization_barrier(back_chan)
    gate_grad = (back_chan.astype(f32) * gate_slope.reshape(tokens, channels)).astype(bf16)

    def input_parts(grads):
        part = jnp.einsum("td,tc->dc", normed_all, jnp.concatenate(grads, axis=1), preferred_element_type=f32)
        part = part.astype(bf16).reshape(tall, side, len(grads), channels)
        return part.transpose(2, 0, 1, 3)

    def every_input(part):
        every = lax.all_gather(part, "tok", axis=0)
        every = every.reshape(half, cut, tall, side, channels).transpose(0, 2, 3, 1, 4)
        return every.reshape(half * tall, side, side)

    if fast:
        output_shares = line_product(
            mixed_plane.reshape(plane, LINES * tok_rows, channels), cotangent_line, tall
        )
        (layer_parts,) = across([mixed_plane], 2)

    scan_in = (by_row(filtered), by_row(gates), by_row(back_chan), begins, blocks)
    if fast:
        *scan_grads, output_shares, layer_parts = scan_backward(
            *scan_in,
            *scan_params,
            kept,
            [("plane_rows", plane), ("line", plane)],
            [output_shares, layer_parts],
            6,
        )
    else:
        scan_grads = scan_backward(*scan_in, *scan_params, kept)
    draw, filter_mix, inject_grad, read_grad, rate_sum, skip_grad, bias_grad = scan_grads
    draw = draw.reshape(tokens, channels)
    rank_in = blocks[:, :tok_rows].reshape(tokens, R)
    step_grad = jnp.einsum("tc,tr->rc", draw, rank_in, preferred_element_type=f32)
    rank_part = jnp.einsum("tc,cr->tr", draw, step_local, preferred_element_type=f32)
    state_part = jnp.concatenate([inject_grad.reshape(tokens, N), read_grad.reshape(tokens, N)], axis=1)
    if fast:
        parts = jnp.concatenate(
            [
                rank_part.astype(bf16).reshape(devices, tok_rows, R),
                state_part.astype(bf16).reshape(devices, tok_rows, 2 * N).transpose(0, 2, 1),
            ],
            axis=1,
        )
        (grad_blocks,) = fold_and_spread(
            parts.reshape(LINES, plane, tok_rows + 2 * N, R),
            plane,
            5,
        )
        grad_blocks = grad_blocks.reshape(devices, tok_rows + 2 * N, R)
        projected_grad_all = jnp.concatenate(
            [
                grad_blocks[:, :tok_rows].reshape(tokens, R),
                grad_blocks[:, tok_rows:].transpose(0, 2, 1).reshape(tokens, 2 * N),
            ],
            axis=1,
        )
    else:
        partial_sums = jnp.concatenate([rank_part, state_part], axis=1)
        projected_grad_all = spread(fold(partial_sums, devices).astype(bf16), devices)
    select_local = channel_weight[:, :select_width].astype(bf16)
    back_filter = jnp.einsum(
        "tf,cf->tc", projected_grad_all, select_local, preferred_element_type=f32
    ).astype(bf16)
    select_grad = jnp.einsum("tc,tf->fc", filtered, projected_grad_all, preferred_element_type=f32)
    pre = conv_pre(xs, taps, offset, place)
    gate = jax.nn.sigmoid(pre)
    dpre = (filter_mix.reshape(tokens, channels) + back_filter.astype(f32)) * (gate * (1.0 + pre * (1.0 - gate)))
    offset_grad = jnp.sum(dpre, axis=0)
    taps_grad = [jnp.sum(dpre * xs, axis=0)]
    xs_grad = taps[K - 1][None] * dpre
    for lag in range(1, K):
        masked = jnp.where(place >= lag, dpre, 0.0)
        xs_grad = xs_grad + taps[K - 1 - lag][None] * sooner(masked, lag)
        taps_grad.insert(0, jnp.sum(masked * later(xs, lag), axis=0))
    xs_grad = xs_grad.astype(bf16)
    input_both = input_parts([xs_grad, gate_grad])
    if fast:
        output_part = jnp.sum(output_shares.astype(f32), axis=0).astype(bf16)
        tiles = jnp.concatenate([input_both.reshape(2 * tall, side, channels), output_part], axis=0)
        route = ("route", plane, *CAPS)
        rides = [route, ("plane", plane), ("plane", plane)]
        guests = [pick(tiles, back_first), share(xs_grad), share(gate_grad)]
    else:
        xs_every, gate_every = every_input(input_both[0]), every_input(input_both[1])
        output_part = jnp.einsum("tc,td->cd", mixed, cotangent_all, preferred_element_type=f32).astype(bf16)
        output_every = lax.all_gather(output_part.reshape(channels, tall, side).transpose(1, 0, 2), "tok", axis=0)
        output_every = (
            output_every.reshape(half, cut, tall, channels, side)
            .transpose(0, 2, 1, 3, 4)
            .reshape(half * tall, side, side)
        )
        rides, guests = [], []

    first_c, second_c, weight_c, rstat_c, lstat_c, right_turned, left_turned, right_gram, left_gram = channel_moments(
        channel_weight.T,
        jnp.concatenate([select_grad, step_grad], axis=0),
        channel_first.T,
        channel_second.T,
        channel_right,
        channel_left,
        channel_right_stat,
        channel_left_stat,
    )
    left_c, right_c, *arrived = solve_factors(
        (left_gram, right_gram), (left_turned.T, right_turned.T), rides, guests, 8
    )
    channel_new = (first_c.T, second_c.T, weight_c.T, left_c.T, right_c.T, lstat_c, rstat_c)
    if fast:
        middle, xs_plane, gate_plane = arrived
        normed_parts, arrived_tiles = across(
            [xs_plane, gate_plane], 0, [route], [pick(middle, back_second)], 9
        )
        x_here = x_all.reshape((LINES, plane) + x_all.shape[1:])
        x_here = lax.dynamic_index_in_dim(x_here, me % plane, 1, False).astype(f32)
        root = lax.rsqrt(jnp.mean(x_here * x_here, axis=2, keepdims=True) + norm_epsilon)
        gain_part = jnp.sum(normed_parts.astype(f32) * x_here * root, axis=(0, 1)).reshape(devices, 1, gain_here)
        gain_part = jnp.pad(gain_part, ((0, 0), (0, 7), (0, 128 - gain_here)))
        rides = [("line", plane), ("all", plane)]
        guests = [normed_parts, gain_part]

    own_slot = tile_slot - me * tiles_here
    every_tile = jnp.full(tile_slot.shape, True)
    if fast:
        grads = (arrived_tiles,)
        kind = jnp.zeros((tiles_here,), jnp.int32)
        index = table(tiles_here, own_slot, every_tile, back_landed)
    else:
        grads = (xs_every, gate_every, output_every)
        tile = jnp.arange(tile_slot.shape[0], dtype=jnp.int32)
        kind = table(tiles_here, own_slot, every_tile, routes.kind)
        spot = jnp.where(is_out, tile - input_tiles, tile % wide % half * tall + tile // wide)
        index = table(tiles_here, own_slot, every_tile, spot)
    first_next, second_next, weight_next, lstat_next, rstat_next, turned, gram = soap_tiles(
        kind,
        index,
        grads,
        pool_weight,
        pool_first,
        pool_second,
        pool_left,
        pool_right,
        pool_left_stat,
        pool_right_stat,
    )
    inverse_low, *arrived = inverse_factors(gram, rides, guests, 10)
    left_next, right_next = renew_bases(turned, inverse_low)

    if fast:
        layer_out = (layer_in.astype(f32) + jnp.sum(layer_parts.astype(f32), axis=0)).astype(bf16)
        normed_grad = jnp.sum(arrived[0].astype(f32), axis=0)
    else:
        mixed_tokens = to_tokens(mixed)
        joint_grad = to_tokens(jnp.stack([xs_grad, gate_grad])).reshape(wide, tok_rows, side)
        layer_out = tile_product(
            mixed_tokens, pool_all, tile_slot[input_tiles:].reshape(half, tall).T, False, bf16, layer_in
        )
        normed_grad = tile_product(
            joint_grad, pool_all, tile_slot[:input_tiles].reshape(tall, wide), True, f32
        )
    input_float = layer_in.astype(f32)
    inverse = lax.rsqrt(jnp.mean(input_float * input_float, axis=1, keepdims=True) + norm_epsilon)
    scaled = normed_grad * gain_float
    input_grad = (
        cotangent.astype(f32)
        + inverse * scaled
        - input_float * inverse**3 * jnp.mean(scaled * input_float, axis=1, keepdims=True)
    )
    if fast:
        gain_grad = jnp.sum(arrived[1][:, 0, :gain_here], axis=0)
    else:
        gain_part = jnp.sum(normed_grad * input_float * inverse, axis=0).reshape(devices, gain_here)
        gain_grad = jnp.sum(lax.all_to_all(gain_part, "tok", split_axis=0, concat_axis=0, tiled=True), axis=0)

    gain_new = adam_step(norm_gain, gain_grad, gain_first, gain_second)
    vector_grad = jnp.concatenate(
        [jnp.stack(taps_grad), offset_grad[None], bias_grad, -rates * rate_sum, skip_grad], axis=0
    )
    vector_new = adam_step(channel_vectors, vector_grad, vector_first, vector_second)
    return (
        layer_out,
        input_grad,
        first_next,
        second_next,
        weight_next,
        left_next,
        right_next,
        lstat_next,
        rstat_next,
        *channel_new,
        *gain_new,
        *vector_new,
    )


def shards(*args):
    bf16 = jnp.bfloat16
    devices = lax.axis_size("tok")
    me = lax.axis_index("tok")
    layer_in, tile_slot, pool_weight, channel_weight = args[0], args[3], args[4], args[11]
    norm_gain, channel_vectors = args[18], args[21]
    tok_rows, model_width = layer_in.shape
    tiles_here, side, _ = pool_weight.shape
    tall = model_width // side
    channels = channel_vectors.shape[1]
    x_all = lax.all_gather(layer_in, "tok", axis=0)
    select_width = channel_weight.shape[1] - R
    small = jnp.concatenate(
        [
            channel_weight[:, :select_width].T,
            jnp.pad(norm_gain[None], ((0, 15), (0, channels - norm_gain.shape[0]))),
        ],
        axis=0,
    ).astype(bf16)
    routes = Routes(tile_slot, devices, tiles_here, tall, channels * devices // side)
    if channels != side or devices % LINES:
        small = lax.all_gather(small, "tok", axis=0)
        return core(routes, False, x_all, small, None, *args)
    plane = devices // LINES
    route = ("route", plane, *CAPS)
    first, second, landed, *back = routes.tables(me)
    middle, line_small = exchange(
        [route, ("line_gather", plane)], [pick(pool_weight.astype(bf16), first), small], 1
    )
    last, small = exchange([route, ("plane_gather", plane)], [pick(middle, second), line_small], 2)
    small = jnp.swapaxes(small, 0, 1).reshape((devices,) + small.shape[2:])
    tiles_own = pick(last, table(3 * tall, routes.place, routes.target == me, landed))
    input_own, output_own = tiles_own[: 2 * tall], tiles_own[2 * tall :]
    input_local = input_own.reshape(2, tall, side, side).transpose(1, 2, 0, 3).reshape(model_width, 2 * channels)
    output_local = output_own.transpose(1, 0, 2).reshape(channels, model_width)
    plane_own = jnp.concatenate([input_local, output_own.transpose(0, 2, 1).reshape(model_width, channels)], axis=1)
    weights, small = lax.optimization_barrier(((input_local, output_local, plane_own, *back), small))
    return lax.cond(
        routes.fits, functools.partial(core, routes, True), functools.partial(core, routes, False), x_all, small, weights, *args
    )


def solution(mesh):
    line, flat, cube, column = P("tok"), P("tok", None), P("tok", None, None), P(None, "tok")
    in_specs = (flat, flat, P(), P()) + (cube,) * 7 + (flat,) * 7 + (line,) * 3 + (column,) * 3
    out_specs = (flat, flat) + (cube,) * 7 + (flat,) * 7 + (line,) * 3 + (column,) * 3
    return jax.shard_map(shards, mesh=mesh, in_specs=in_specs, out_specs=out_specs, check_vma=False)
```
